32 devices in a mesh: dp: 8 (over y, x, core), tensor: 4 (over z).
Axes of the slice: x: 2, y: 2, z: 4, core: 2. Of those that a mesh axis runs over, the one named last changes fastest.
Arguments:
- inputs: bfloat16 [12288, 1536], P(('dp', 'tensor')), may hold values from -6 to 6
- cotangent: bfloat16 [12288, 1536], P(('dp', 'tensor')), may hold values from -6 to 6
- seq_lengths: int32 [8, 3], P('dp'), may hold values from 1 to 1154, 1536 in all within a row
- norm_gain: float32 [1536], replicated, may hold values from 0.5 to 1.5
- w_z: bfloat16 [1536, 3072], P('dp', 'tensor'), may hold values from -0.15625 to 0.15625
- w_x: bfloat16 [1536, 3072], P('dp', 'tensor'), may hold values from -0.15625 to 0.15625
- w_bc: bfloat16 [1536, 256], P('dp'), may hold values from -0.15625 to 0.15625
- w_dt: bfloat16 [1536, 48], P('dp', 'tensor'), may hold values from -0.15625 to 0.15625
- conv_x: float32 [4, 3072], P(None, 'tensor'), may hold values from -3 to 3
- conv_x_bias: float32 [3072], P('tensor'), may hold values from -3 to 3
- conv_bc: float32 [4, 256], replicated, may hold values from -3 to 3
- conv_bc_bias: float32 [256], replicated, may hold values from -3 to 3
- dt_bias: float32 [48], P('tensor'), may hold values from -7 to -1
- a_log: float32 [48], P('tensor'), may hold values from -1 to 2
- d_skip: float32 [48], P('tensor'), may hold values from 0.5 to 1.5
- gate_gain: float32 [3072], P('tensor'), may hold values from 0.5 to 1.5
- w_out: bfloat16 [3072, 1536], P('tensor', 'dp'), may hold values from -0.109375 to 0.109375
Outputs:
- outputs: bfloat16 [12288, 1536], P(('dp', 'tensor'))
- grad_inputs: bfloat16 [12288, 1536], P(('dp', 'tensor'))
- grad_norm_gain: float32 [1536], replicated
- grad_w_z: float32 [1536, 3072], P('dp', 'tensor')
- grad_w_x: float32 [1536, 3072], P('dp', 'tensor')
- grad_w_bc: float32 [1536, 256], P('dp')
- grad_w_dt: float32 [1536, 48], P('dp', 'tensor')
- grad_conv_x: float32 [4, 3072], P(None, 'tensor')
- grad_conv_x_bias: float32 [3072], P('tensor')
- grad_conv_bc: float32 [4, 256], replicated
- grad_conv_bc_bias: float32 [256], replicated
- grad_dt_bias: float32 [48], P('tensor')
- grad_a_log: float32 [48], P('tensor')
- grad_d_skip: float32 [48], P('tensor')
- grad_gate_gain: float32 [3072], P('tensor')
- grad_w_out: float32 [3072, 1536], P('tensor', 'dp')
The draws below stay inside these ranges and needn't reach their ends.
Inputs may be any that keep to these rules, and one draw needn't show every extreme that they name: `seq_lengths`: each row lists the lengths of the sequences of one group in token order; they sum to 1536, and the largest is exactly 1154.
All inputs are finite; a program needn't handle non-finite values.
Results may differ from the reference program's by a relative error of at most 0.019.
Values may be sent and summed in bfloat16 or wider, within the bound.
A program may use at most 384 MiB of HBM per device.

```python
import math
from functools import partial
import jax
import jax.numpy as jnp
import numpy as np
from jax import lax

D = 1536
HEADS = 48
HEADDIM = 64
STATE = 128
KCONV = 4
SPAN = 256
SEQ_TOK_DEV = 384
SEQS = 3
INNER = 3072
GROUP = 1536
TOKENS = 12288
LONGEST = 1154
N_DP = 8
N_TENSOR = 4


def block_levels(stream_key, dims, cuts, least, largest):
    level = 1.0
    for position, parts in cuts:
        draws = jax.random.uniform(jax.random.fold_in(jax.random.fold_in(stream_key, 6), position), (parts,), jnp.float32, least / len(cuts), largest / len(cuts))
        level = level * jnp.repeat(jnp.exp(draws), dims[position] // parts).reshape((-1,) + (1,) * (len(dims) - 1 - position))
    return level


def split_up(amount, total, reach, lean):
    portions = [(1 << 20) // math.isqrt(standing ** lean) + 1 for standing in range(2, amount + 1)]
    surplus, counts = total - reach - (amount - 1), [1] * (amount - 1)
    while surplus > 0:
        free = [i for i in range(amount - 1) if counts[i] < reach]
        whole, left = sum([portions[i] for i in free]), surplus
        for i in free:
            more = min(reach - counts[i], max(1, left * portions[i] // whole), surplus)
            counts[i] = counts[i] + more
            surplus = surplus - more
    return np.array([reach] + counts)


def uneven_parts(stream_key, number_of, total, limit, skew):
    if number_of == 2:
        one = jax.random.randint(stream_key, (), max(1, total - limit), min(limit, total - 1) + 1)
        return jnp.stack([one, total - one])
    lengths = jnp.asarray(split_up(number_of, total, limit, skew), jnp.int32)
    pairs = (number_of - 1) // 2
    source_of, taker = lengths[1:1 + 2 * pairs:2], lengths[2:2 + 2 * pairs:2]
    margin = jnp.minimum(source_of - 1, limit - taker)
    moved = jax.random.randint(jax.random.fold_in(stream_key, 1), (pairs,), 0, 1 << 20) % (margin + 1)
    lengths = lengths.at[1:1 + 2 * pairs:2].set(source_of - moved).at[2:2 + 2 * pairs:2].set(taker + moved)
    return lengths[jax.random.permutation(jax.random.fold_in(stream_key, 2), number_of)]


def bell_draw(own_key, dims, scale, reach, split=(), kind=jnp.bfloat16):
    entries = scale * jax.random.normal(own_key, dims, jnp.float32)
    if split:
        entries = entries * block_levels(own_key, dims, split, -0.22, 0.18)
    return jnp.clip(entries, -reach, reach).astype(kind)


def setup_inputs(seed: int = 0) -> dict:
    arg_keys = jax.random.split(jax.random.key(seed), 18)
    return {
        "inputs": bell_draw(arg_keys[0], (TOKENS, D), 1.0, 6.0, ((0, 32),)),
        "cotangent": bell_draw(arg_keys[1], (TOKENS, D), 1.0, 6.0, ((0, 32),)),
        "seq_lengths": jax.vmap(lambda own: uneven_parts(own, SEQS, GROUP, LONGEST, 1))(jax.random.split(arg_keys[2], N_DP)).reshape((N_DP, SEQS)).astype(jnp.int32),
        "norm_gain": jnp.clip(1.0 + 0.1 * jax.random.normal(arg_keys[3], (D,), jnp.float32), 0.5, 1.5),
        "w_z": bell_draw(arg_keys[4], (D, INNER), D ** -0.5, 0.15625, ((0, 8), (1, 4))),
        "w_x": bell_draw(arg_keys[5], (D, INNER), D ** -0.5, 0.15625, ((0, 8), (1, 4))),
        "w_bc": bell_draw(arg_keys[6], (D, 2 * STATE), D ** -0.5, 0.15625, ((0, 8),)),
        "w_dt": bell_draw(arg_keys[7], (D, HEADS), D ** -0.5, 0.15625, ((0, 8), (1, 4))),
        "conv_x": bell_draw(arg_keys[8], (KCONV, INNER), KCONV ** -0.5, 3.0, ((1, 4),), jnp.float32),
        "conv_x_bias": bell_draw(arg_keys[9], (INNER,), 0.5, 3.0, ((0, 4),), jnp.float32),
        "conv_bc": bell_draw(arg_keys[10], (KCONV, 2 * STATE), KCONV ** -0.5, 3.0, (), jnp.float32),
        "conv_bc_bias": bell_draw(arg_keys[11], (2 * STATE,), 0.5, 3.0, (), jnp.float32),
        "dt_bias": jnp.clip(-7.0 + 6.0 * jax.random.uniform(arg_keys[12], (HEADS,), jnp.float32) ** block_levels(arg_keys[12], (HEADS,), ((0, 4),), -0.2, 0.2), -7.0, -1.0),
        "a_log": jnp.clip(-1.0 + 3.0 * jax.random.uniform(arg_keys[13], (HEADS,), jnp.float32) ** block_levels(arg_keys[13], (HEADS,), ((0, 4),), -0.2, 0.2), -1.0, 2.0),
        "d_skip": jnp.clip(0.5 + 1.0 * jax.random.uniform(arg_keys[14], (HEADS,), jnp.float32) ** block_levels(arg_keys[14], (HEADS,), ((0, 4),), -0.2, 0.2), 0.5, 1.5),
        "gate_gain": jnp.clip(1.0 + 0.1 * jax.random.normal(arg_keys[15], (INNER,), jnp.float32), 0.5, 1.5),
        "w_out": bell_draw(arg_keys[16], (INNER, D), INNER ** -0.5, 0.109375, ((0, 4), (1, 8))),
    }


epsilon = 1e-05
highest = lax.Precision.HIGHEST

@jax.custom_vjp
def low(v):
    return lax.optimization_barrier(v.astype(jnp.bfloat16)).astype(jnp.float32)

@jax.custom_vjp
def low_back(v):
    return v

def low_keep(v):
    return (low(v), None)

def low_pass(kept, grad):
    return (grad,)

def back_keep(v):
    return (v, None)

def back_low(kept, grad):
    return (low(grad),)
low.defvjp(low_keep, low_pass)
low_back.defvjp(back_keep, back_low)

def silu(values):
    return values * jax.nn.sigmoid(values)

def segments_of(lengths_row, count):
    ends = jnp.cumsum(lengths_row).astype(jnp.int32)
    places = jnp.arange(count, dtype=jnp.int32)
    return lax.optimization_barrier(jnp.sum((ends[None, :] <= places[:, None]).astype(jnp.int32), axis=1)).astype(jnp.int32)

def causal_conv(values, kernel, bias_row, segment):
    running = bias_row[None, :] + kernel[0][None, :] * values
    for offset in range(1, kernel.shape[0]):
        moved = jnp.concatenate([jnp.zeros((offset, values.shape[1]), values.dtype), values[:-offset]], axis=0)
        moved_seg = jnp.concatenate([jnp.full((offset,), -1, jnp.int32), segment[:-offset]])
        keep_mask = (moved_seg == segment).astype(values.dtype)
        running = running + kernel[offset][None, :] * moved * keep_mask[:, None]
    return running

def block_step(rate, carry, block):
    state_now, prev_segment = carry
    x_block, b_block, c_block, step_block, seg_block = block
    length = x_block.shape[0]
    log_decay = jnp.cumsum(step_block * rate[None, :], axis=0)
    places = jnp.arange(length, dtype=jnp.int32)
    visible = (places[:, None] >= places[None, :]) & (seg_block[:, None] == seg_block[None, :])
    gaps = log_decay[:, None, :] - log_decay[None, :, :]
    decays = jnp.where(visible[:, :, None], jnp.exp(jnp.where(visible[:, :, None], gaps, 0.0)), 0.0)
    intersection = jnp.dot(c_block, b_block.T, precision=highest)
    mixing = intersection[:, :, None] * decays * step_block[None, :, :]
    local_part = jnp.einsum('tsh,shp->thp', mixing, x_block, precision=highest)
    carry_mask = (seg_block == prev_segment).astype(jnp.float32)
    state_read = jnp.einsum('tn,hpn->thp', c_block, state_now, precision=highest)
    state_part = state_read * (carry_mask[:, None] * jnp.exp(log_decay))[:, :, None]
    last_seg = seg_block[length - 1]
    tail_weight = (seg_block == last_seg).astype(jnp.float32)[:, None] * jnp.exp(log_decay[length - 1][None, :] - log_decay) * step_block
    fresh_state = jnp.einsum('sh,shp,sn->hpn', tail_weight, x_block, b_block, precision=highest)
    kept_state = (prev_segment == last_seg).astype(jnp.float32) * jnp.exp(log_decay[length - 1])
    new_state = fresh_state + kept_state[:, None, None] * state_now
    return ((new_state, last_seg), local_part + state_part)

def run_scan(heads_x, b_map, c_map, steps_dt, segment, rate):
    count, heads, width = heads_x.shape
    blocks = count // SPAN
    pieces = (heads_x.reshape(blocks, SPAN, heads, width), b_map.reshape(blocks, SPAN, -1), c_map.reshape(blocks, SPAN, -1), steps_dt.reshape(blocks, SPAN, heads), segment.reshape(blocks, SPAN))
    begin = (jnp.zeros((heads, width, b_map.shape[1]), jnp.float32), jnp.int32(-1))
    _, ys = lax.scan(jax.checkpoint(partial(block_step, rate)), begin, pieces)
    return ys.reshape(count, heads, width)

def layer(params, tokens, segment):
    norm_gain, w_z, w_x, w_bc, w_dt, conv_x, conv_x_bias, conv_bc, conv_bc_bias, dt_bias, a_log, d_skip, gate_gain, w_out = params
    count = tokens.shape[0]
    scale = lax.rsqrt(lax.optimization_barrier(jnp.mean(tokens * tokens, axis=1, keepdims=True)) + epsilon)
    normed = low(tokens * scale * norm_gain[None, :])
    width_block = INNER // N_TENSOR
    head_block = HEADS // N_TENSOR
    token_places = jnp.arange(count, dtype=jnp.int32)
    z_parts = []
    x_parts = []
    dt_parts = []
    bc_input = jnp.zeros_like(normed)
    for block_index in range(N_TENSOR):
        normed_view = low_back(normed)
        low_col = block_index * width_block
        z_parts.append(jnp.dot(normed_view, w_z[:, low_col:low_col + width_block], precision=highest))
        x_parts.append(jnp.dot(normed_view, w_x[:, low_col:low_col + width_block], precision=highest))
        head_col = block_index * head_block
        dt_parts.append(jnp.dot(normed_view, w_dt[:, head_col:head_col + head_block], precision=highest))
        owner_mask = (token_places // SEQ_TOK_DEV == block_index).astype(jnp.float32)[:, None]
        bc_input = bc_input + owner_mask * normed_view
    zgate = low_back(jnp.concatenate(z_parts, axis=1))
    xpre = low_back(jnp.concatenate(x_parts, axis=1))
    dtraw = low_back(jnp.concatenate(dt_parts, axis=1))
    bcpre = low_back(jnp.dot(bc_input, w_bc, precision=highest))
    scanned = low(silu(causal_conv(xpre, conv_x, conv_x_bias, segment)))
    maps = low(silu(causal_conv(bcpre, conv_bc, conv_bc_bias, segment)))
    b_map = maps[:, :STATE]
    c_map = maps[:, STATE:]
    steps_dt = jax.nn.softplus(dtraw + dt_bias[None, :])
    rate = -jnp.exp(a_log)
    heads_x = scanned.reshape(count, HEADS, HEADDIM)
    result = run_scan(heads_x, b_map, c_map, steps_dt, segment, rate) + d_skip[None, :, None] * heads_x
    gated = result.reshape(count, INNER) * silu(zgate)
    gscale = lax.rsqrt(lax.optimization_barrier(jnp.mean(gated * gated, axis=1, keepdims=True)) + epsilon)
    mixed = low(gated * gscale * gate_gain[None, :])
    branch = jnp.zeros_like(tokens)
    for block_index in range(N_TENSOR):
        low_col = block_index * width_block
        branch = branch + low(jnp.dot(mixed[:, low_col:low_col + width_block], w_out[low_col:low_col + width_block, :], precision=highest))
    return tokens + branch

def reference(inputs, cotangent, seq_lengths, norm_gain, w_z, w_x, w_bc, w_dt, conv_x, conv_x_bias, conv_bc, conv_bc_bias, dt_bias, a_log, d_skip, gate_gain, w_out):
    params = tuple((item.astype(jnp.float32) for item in (norm_gain, w_z, w_x, w_bc, w_dt, conv_x, conv_x_bias, conv_bc, conv_bc_bias, dt_bias, a_log, d_skip, gate_gain, w_out)))
    group_x = inputs.astype(jnp.float32).reshape(N_DP, GROUP, D)
    group_c = cotangent.astype(jnp.float32).reshape(N_DP, GROUP, D)

    def one_group(totals, block):
        tokens, upstream, lengths_row = block
        segment = segments_of(lengths_row, GROUP)
        result, pull = jax.vjp(lambda given, values: layer(given, values, segment), params, tokens)
        grads, grad_tokens = pull(upstream)
        totals = jax.tree.map(lambda left, right: left + right, totals, grads)
        return (totals, (result.astype(jnp.bfloat16), grad_tokens.astype(jnp.bfloat16)))
    zero_grads = jax.tree.map(jnp.zeros_like, params)
    totals, (results, grad_tokens) = lax.scan(one_group, zero_grads, (group_x, group_c, seq_lengths))
    return (results.reshape(TOKENS, D), grad_tokens.reshape(TOKENS, D), totals[0], totals[1], totals[2], totals[3], totals[4], totals[5], totals[6], totals[7], totals[8], totals[9], totals[10], totals[11], totals[12], totals[13])
```

```python
from functools import partial

import jax
import jax.numpy as jnp
from jax import lax
from jax.experimental import pallas as pl
from jax.experimental.pallas import tpu as pltpu
from jax.sharding import PartitionSpec as P

SPAN = 256
HALO = 16
LANES = 128
LOG2E = 1.4426950408889634
EPS = 1e-05
FAR = -1e30
HIGH = lax.Precision.HIGHEST
F32 = jnp.float32
BF16 = jnp.bfloat16
VMEM_BYTES = 60 * 1024 * 1024


def nn(a, b):
    return jnp.dot(a, b, preferred_element_type=F32)


def nt(a, b):
    return lax.dot_general(a, b, (((1,), (1,)), ((), ())), preferred_element_type=F32)


def tn(a, b):
    return lax.dot_general(a, b, (((0,), (0,)), ((), ())), preferred_element_type=F32)


def sigmoid(v):
    return 1.0 / (1.0 + jnp.exp(-v))


def iota(shape, axis):
    return lax.broadcasted_iota(jnp.int32, shape, axis)


def seg_at(sc, pos):
    found = (pos >= sc[0]).astype(jnp.int32)
    for i in range(1, 3):
        found = found + (pos >= sc[i]).astype(jnp.int32)
    return jnp.where(pos < 0, -1, found)


def same_as_behind(sc, pos, offset):
    return (seg_at(sc, pos - offset) == seg_at(sc, pos)).astype(F32)


def head_map(cols, start, dtype=BF16, both=True):
    k = iota((LANES, cols), 0)
    if both:
        k = k & 63
    head = (iota((LANES, cols), 1) + start) >> 6
    return (k == head).astype(dtype)


def expand(values, mapping):
    high = values.astype(BF16).astype(F32)
    low = values - high
    return nn((high + pltpu.roll(low, 64, axis=1)).astype(BF16), mapping)


def assemble(me, rows, parts, refs, scratch):
    for (order, low), ref in zip(parts, refs):
        for i, v in enumerate(order):
            start = pl.multiple_of((me ^ v) * rows, 16)
            scratch[pl.ds(start, rows), low : low + ref.shape[2]] = ref[i]


def whole():
    return pl.BlockSpec(memory_space=pltpu.VMEM)


def scalars():
    return pl.BlockSpec(memory_space=pltpu.SMEM)


def params():
    return pltpu.CompilerParams(vmem_limit_bytes=VMEM_BYTES)


def cost(flops, nbytes):
    return pl.CostEstimate(flops=int(flops), bytes_accessed=int(nbytes), transcendentals=0)


def maps_body(parts, rows, ha, sc, tok, taps, bias, dtb, alog, *rest):
    n = len(parts)
    refs, outs = rest[:n], rest[n : n + 9]
    wscr = rest[n + 9]
    pre_o, bc_o, dtin_o, dt_o, lc_o, lr_o, em_o, et_o, kd_o = outs
    count = bc_o.shape[0]
    chunks = count // SPAN
    assemble(sc[4], rows, parts, refs, wscr)
    pre_o[...] = nn(tok[...], wscr[:, LANES:])
    base = sc[3]
    pos = base + iota((count, 1), 0)
    acc = bias[...] + taps[0:1, :] * pre_o[HALO : HALO + count, :]
    for j in range(1, 4):
        acc = acc + taps[j : j + 1, :] * pre_o[HALO - j : HALO - j + count, :] * same_as_behind(sc, pos, j)
    bc_o[...] = (acc * sigmoid(acc)).astype(BF16)
    dtin = nn(tok[HALO:, :], wscr[:, :LANES]) + dtb[...]
    steps = jnp.maximum(dtin, 0.0) + jnp.log1p(jnp.exp(-jnp.abs(dtin)))
    scaled = steps * (-jnp.exp(alog[...]) * LOG2E)
    lane = iota((1, LANES), 1)
    keep = (lane < ha).astype(F32)

    def block(v, b):
        if b:
            v = pltpu.roll(v, LANES - ha, axis=1)
        return v * keep

    for b in range(2):
        dtin_o[b] = block(dtin, b)
        dt_o[b] = block(steps, b)
    tri = (iota((SPAN, SPAN), 0) >= iota((SPAN, SPAN), 1)).astype(F32)
    gone = []
    for c in range(chunks):
        span = slice(c * SPAN, (c + 1) * SPAN)
        logs = jnp.dot(tri, scaled[span, :], precision=HIGH, preferred_element_type=F32)
        first, last = base + c * SPAN - 1, base + (c + 1) * SPAN - 1
        here = base + c * SPAN + iota((SPAN, 1), 0)
        seg = seg_at(sc, here)
        seg_first, seg_last = seg_at(sc, first), seg_at(sc, last)
        starts = (seg == seg_first).astype(F32)
        ends = (seg == seg_last).astype(F32)
        final = logs[SPAN - 1 : SPAN, :]
        lead = starts * jnp.exp2(logs)
        tail = ends * jnp.exp2(final - logs)
        kept = jnp.where(seg_first == seg_last, 1.0, 0.0).astype(F32)
        gone.append(kept * jnp.exp2(final))
        for b in range(2):
            mine = block(logs, b)
            lc_o[b, span, :] = mine
            lr_o[b, :, span] = mine.T[:16, :]
            em_o[b, span, :] = block(lead, b)
            et_o[b, span, :] = block(tail, b)
    ones = jnp.ones((1, LANES), F32)
    ahead_of, behind_of = [ones], [ones]
    for c in range(chunks - 1):
        ahead_of.append(ahead_of[-1] * gone[c])
        behind_of.append(behind_of[-1] * gone[chunks - 1 - c])
    behind_of = behind_of[::-1]
    fill = [jnp.zeros((1, LANES), F32)] * (8 - chunks)
    table = jnp.concatenate(gone + fill + ahead_of + fill + behind_of + fill, axis=0)
    for b in range(2):
        kd_o[b] = block(table, b)


def run_maps(sc, tok, taps, bias, dtb, alog, pieces, rows, ha):
    parts, refs = pieces
    total, width = tok.shape
    count = total - HALO
    small = sum(r.shape[2] for r, p in zip(refs, parts) if p[0][0] == 0)
    per_block = jax.ShapeDtypeStruct((2, count, LANES), F32)
    return pl.pallas_call(
        partial(maps_body, parts, rows, ha),
        out_shape=(
            jax.ShapeDtypeStruct((total, 2 * LANES), F32),
            jax.ShapeDtypeStruct((count, 2 * LANES), BF16),
            per_block,
            per_block,
            per_block,
            jax.ShapeDtypeStruct((2, 16, count), F32),
            per_block,
            per_block,
            jax.ShapeDtypeStruct((2, 24, LANES), F32),
        ),
        in_specs=[scalars()] + [whole()] * (5 + len(refs)),
        out_specs=[whole()] * 9,
        scratch_shapes=[pltpu.VMEM((width, small), BF16)],
        compiler_params=params(),
        cost_estimate=cost(2 * total * width * 512, 8e6),
        name="maps",
    )(sc, tok, taps, bias, dtb, alog, *refs)


def xpath_body(parts, rows, ig, sc, tok, taps, bias, bc, dt, et, kd, *rest):
    n = len(parts)
    refs = rest[:n]
    pre_o, xs_o, st_o, fin_o, wscr = rest[n:]
    count, cols = xs_o.shape
    j = pl.program_id(0)

    @pl.when(j == 0)
    def _():
        assemble(sc[4], rows, parts, refs, wscr)

    at = pl.multiple_of(j * cols, cols)
    pre_o[...] = nn(tok[...], wscr[:, pl.ds(at, cols)])
    mapping = head_map(cols, lax.rem(at, ig))
    state = jnp.zeros((LANES, cols), F32)
    gone = expand(kd[0], mapping)
    for c in range(count // SPAN):
        low = c * SPAN
        pos = sc[3] + low + iota((SPAN, 1), 0)
        acc = bias[...] + taps[0:1, :] * pre_o[HALO + low : HALO + low + SPAN, :]
        for k in range(1, 4):
            acc = acc + taps[k : k + 1, :] * pre_o[HALO + low - k : HALO + low - k + SPAN, :] * same_as_behind(sc, pos, k)
        xs = (acc * sigmoid(acc)).astype(BF16)
        xs_o[low : low + SPAN, :] = xs
        weight = expand(dt[0, low : low + SPAN, :] * et[0, low : low + SPAN, :], mapping)
        st_o[c] = state
        state = gone[c : c + 1, :] * state + tn(bc[low : low + SPAN, :LANES], (xs.astype(F32) * weight).astype(BF16))
    fin_o[...] = state.astype(BF16)


def col_tile(ig):
    return 256 if ig % 256 == 0 else 128


def run_xpath(sc, tok, taps, bias, bc, dt, et, kd, pieces, rows, ig):
    parts, refs = pieces
    total, width = tok.shape
    count = total - HALO
    inner = 2 * ig
    cols = col_tile(ig)
    chunks = count // SPAN
    per_block = pl.BlockSpec((1, count, LANES), lambda j: (j * cols // ig, 0, 0))
    return pl.pallas_call(
        partial(xpath_body, parts, rows, ig),
        grid=(inner // cols,),
        out_shape=(
            jax.ShapeDtypeStruct((total, inner), F32),
            jax.ShapeDtypeStruct((count, inner), BF16),
            jax.ShapeDtypeStruct((chunks, LANES, inner), F32),
            jax.ShapeDtypeStruct((LANES, inner), BF16),
        ),
        in_specs=[
            scalars(),
            whole(),
            pl.BlockSpec((4, cols), lambda j: (0, j)),
            pl.BlockSpec((1, cols), lambda j: (0, j)),
            whole(),
            per_block,
            per_block,
            pl.BlockSpec((1, 24, LANES), lambda j: (j * cols // ig, 0, 0)),
        ]
        + [whole()] * len(refs),
        out_specs=(
            pl.BlockSpec((total, cols), lambda j: (0, j)),
            pl.BlockSpec((count, cols), lambda j: (0, j)),
            pl.BlockSpec((chunks, LANES, cols), lambda j: (0, 0, j)),
            pl.BlockSpec((LANES, cols), lambda j: (0, j)),
        ),
        scratch_shapes=[pltpu.VMEM((width, inner), BF16)],
        compiler_params=params(),
        cost_estimate=cost(2.4 * total * width * inner, 20e6),
        name="xpath",
    )(sc, tok, taps, bias, bc, dt, et, kd, *refs)


def proj_body(parts, rows, sc, x, *rest):
    n = len(parts)
    out, wscr = rest[n:]
    cols = out.shape[1]
    j = pl.program_id(0)

    @pl.when(j == 0)
    def _():
        assemble(sc[4], rows, parts, rest[:n], wscr)

    skip = x.shape[0] - out.shape[0]
    out[...] = nn(x[skip:, :], wscr[:, pl.ds(pl.multiple_of(j * cols, cols), cols)])


def run_proj(sc, x, pieces, rows, inner, count):
    parts, refs = pieces
    width = x.shape[1]
    cols = 256
    return pl.pallas_call(
        partial(proj_body, parts, rows),
        grid=(inner // cols,),
        out_shape=jax.ShapeDtypeStruct((count, inner), F32),
        in_specs=[scalars()] + [whole()] * (1 + len(refs)),
        out_specs=pl.BlockSpec((count, cols), lambda j: (0, j)),
        scratch_shapes=[pltpu.VMEM((width, inner), BF16)],
        compiler_params=params(),
        cost_estimate=cost(2 * count * width * inner, 12e6),
        name="proj",
    )(sc, x, *refs)


def back_body(parts, rows, sc, x, *rest):
    n = len(parts)
    out, wscr = rest[n:]
    cols = out.shape[1]
    j = pl.program_id(0)

    @pl.when(j == 0)
    def _():
        assemble(sc[4], rows, parts, rest[:n], wscr)

    out[...] = nt(x[...], wscr[pl.ds(pl.multiple_of(j * cols, cols), cols), :]).astype(BF16)


def run_back(sc, x, pieces, rows, width):
    parts, refs = pieces
    count, inner = x.shape
    cols = 256
    return pl.pallas_call(
        partial(back_body, parts, rows),
        grid=(width // cols,),
        out_shape=jax.ShapeDtypeStruct((count, width), BF16),
        in_specs=[scalars()] + [whole()] * (1 + len(refs)),
        out_specs=pl.BlockSpec((count, cols), lambda j: (0, j)),
        scratch_shapes=[pltpu.VMEM((width, inner), BF16)],
        compiler_params=params(),
        cost_estimate=cost(2 * count * width * inner, 10e6),
        name="back",
    )(sc, x, *refs)


def grad_body(rows, sc, x, y, own, oth, scr):
    skip = x.shape[0] - y.shape[0]
    scr[...] = tn(x[skip:, :], y[...]).astype(BF16)
    me = sc[4]
    for v in range(2 * own.shape[0]):
        block = scr[pl.ds(pl.multiple_of((me ^ v) * rows, 16), rows), :]
        if v & 1:
            oth[v >> 1] = block
        else:
            own[v >> 1] = block


def run_grad(sc, x, y, rows):
    width = x.shape[1]
    count, inner = y.shape
    cols = 256 if inner % 256 == 0 else 128
    half = width // rows // 2
    shape = jax.ShapeDtypeStruct((half, rows, inner), BF16)
    spec = pl.BlockSpec((half, rows, cols), lambda j: (0, 0, j))
    return pl.pallas_call(
        partial(grad_body, rows),
        grid=(inner // cols,),
        out_shape=(shape, shape),
        in_specs=[scalars(), whole(), pl.BlockSpec((count, cols), lambda j: (0, j))],
        out_specs=(spec, spec),
        scratch_shapes=[pltpu.VMEM((width, cols), BF16)],
        compiler_params=params(),
        cost_estimate=cost(2 * count * width * inner, 10e6),
        name="grad",
    )(sc, x, y)


def scan_body(sc, xs, bc, dt, lc, lr, em, kd, st, sin, z, dm, skip, gain, y_o, stat_o, cb, off):
    c, b = pl.program_id(0), pl.program_id(1)
    cols = xs.shape[1]

    @pl.when(b == 0)
    def _():
        cb[...] = nt(bc[:, LANES:], bc[:, :LANES])
        start = sc[3] + c * SPAN
        t, s = iota((SPAN, SPAN), 0), iota((SPAN, SPAN), 1)
        seen = (t >= s) & (seg_at(sc, start + t) == seg_at(sc, start + s))
        off[...] = jnp.where(seen, 0.0, FAR)
        stat_o[...] = jnp.zeros_like(stat_o)

    mapping = head_map(cols, 0)
    scaled = (xs[...].astype(F32) * expand(dt[0], mapping)).astype(BF16)
    carry = expand(kd[0, 8:16, :], mapping)
    rows8 = (iota((8, 1), 0) == c).astype(F32)
    state = st[0] + jnp.sum(carry * rows8, axis=0, keepdims=True) * sin[...].astype(F32)
    far = nn(bc[:, LANES:], state.astype(BF16)) * expand(em[0], mapping) + skip[...] * xs[...].astype(F32)
    lane = iota((1, LANES), 1)
    sides = [(lane < 64).astype(BF16), (lane >= 64).astype(BF16)]
    half = SPAN // 2
    square = jnp.zeros((SPAN, 1), F32)
    cross = jnp.zeros((SPAN, 1), F32)
    for k in range(cols // LANES):
        at = slice(k * LANES, (k + 1) * LANES)
        pair = scaled[:, at]
        top = far[:half, at]
        low = far[half:, at]
        for side in range(2):
            h = 2 * k + side
            operand = pair * sides[side]
            column = lc[0, :, h : h + 1]
            row = lr[0, h : h + 1, :]
            w_top = cb[:half, :half] * jnp.exp2(column[:half] - row[:, :half] + off[:half, :half])
            top = top + nn(w_top.astype(BF16), operand[:half, :])
            w_low = cb[half:, :] * jnp.exp2(column[half:] - row + off[half:, :])
            low = low + nn(w_low.astype(BF16), operand)
        out = jnp.concatenate([top, low], axis=0)
        y_o[:, at] = out
        gate = z[:, at]
        gated = out * (gate * sigmoid(gate))
        square = square + jnp.sum(gated * gated, axis=1, keepdims=True)
        cross = cross + jnp.sum(gated * (dm[:, at] * gain[:, at]), axis=1, keepdims=True)
    stat_o[...] += jnp.where(lane == 0, square, 0.0) + jnp.where(lane == 1, cross, 0.0)


def run_scan(sc, xs, bc, dt, lc, lr, em, kd, st, sin, z, dm, skip, gain, ig):
    count, inner = xs.shape
    chunks = count // SPAN
    tile = pl.BlockSpec((SPAN, ig), lambda c, b: (c, b))
    per_block = pl.BlockSpec((1, SPAN, LANES), lambda c, b: (b, c, 0))
    row = pl.BlockSpec((1, ig), lambda c, b: (0, b))
    return pl.pallas_call(
        scan_body,
        grid=(chunks, 2),
        out_shape=(
            jax.ShapeDtypeStruct((count, inner), F32),
            jax.ShapeDtypeStruct((count, LANES), F32),
        ),
        in_specs=[
            scalars(),
            tile,
            pl.BlockSpec((SPAN, 2 * LANES), lambda c, b: (c, 0)),
            per_block,
            per_block,
            pl.BlockSpec((1, 16, SPAN), lambda c, b: (b, 0, c)),
            per_block,
            pl.BlockSpec((1, 24, LANES), lambda c, b: (b, 0, 0)),
            pl.BlockSpec((1, LANES, ig), lambda c, b: (c, 0, b)),
            pl.BlockSpec((LANES, ig), lambda c, b: (0, b)),
            tile,
            tile,
            row,
            row,
        ],
        out_specs=(tile, pl.BlockSpec((SPAN, LANES), lambda c, b: (c, 0))),
        scratch_shapes=[pltpu.VMEM((SPAN, SPAN), F32), pltpu.VMEM((SPAN, SPAN), F32)],
        compiler_params=params(),
        cost_estimate=cost(6e9, 20e6),
        name="scan",
    )(sc, xs, bc, dt, lc, lr, em, kd, st, sin, z, dm, skip, gain)


def gate_body(ig, inner_all, sc, y, z, dm, stat_a, stat_b, xs, gain, bc, em, kd, mixed_o, dz_o, dy_o, sums_o, ds_o, first_o):
    count, cols = y.shape
    at = pl.program_id(0) * cols
    mapping = head_map(cols, lax.rem(at, ig))
    gone = expand(kd[0], mapping)
    grad = jnp.zeros((LANES, cols), F32)
    by_gain = jnp.zeros((1, cols), F32)
    by_skip = jnp.zeros((1, cols), F32)
    for c in range(count // SPAN - 1, -1, -1):
        span = slice(c * SPAN, (c + 1) * SPAN)
        stat = stat_a[span, :] + stat_b[span, :]
        scale = lax.rsqrt(stat[:, 0:1] / inner_all + EPS)
        pull = scale * scale * scale * stat[:, 1:2] / inner_all
        gate = z[span, :]
        sig = sigmoid(gate)
        act = gate * sig
        out = y[span, :]
        gated = out * act
        normal = gated * scale
        mixed_o[span, :] = (normal * gain[...]).astype(BF16)
        upstream = dm[span, :]
        by_gain = by_gain + jnp.sum(upstream * normal, axis=0, keepdims=True)
        dgated = scale * (upstream * gain[...]) - gated * pull
        dz_o[span, :] = (dgated * out * (sig * (1.0 + gate * (1.0 - sig)))).astype(BF16)
        dy = dgated * act
        by_skip = by_skip + jnp.sum(dy * xs[span, :].astype(F32), axis=0, keepdims=True)
        dy_o[span, :] = dy.astype(BF16)
        ds_o[c] = grad
        lead = (dy * expand(em[0, span, :], mapping)).astype(BF16)
        grad = gone[c : c + 1, :] * grad + tn(bc[span, LANES:], lead)
    first_o[...] = grad.astype(BF16)
    sums_o[...] = jnp.concatenate([by_gain, by_skip, jnp.zeros((6, cols), F32)], axis=0)


def run_gate(sc, y, z, dm, stat_a, stat_b, xs, gain, bc, em, kd, ig, inner_all):
    count, inner = y.shape
    cols = col_tile(ig)
    chunks = count // SPAN
    tile = pl.BlockSpec((count, cols), lambda j: (0, j))
    low = jax.ShapeDtypeStruct((count, inner), BF16)
    return pl.pallas_call(
        partial(gate_body, ig, inner_all),
        grid=(inner // cols,),
        out_shape=(
            low,
            low,
            low,
            jax.ShapeDtypeStruct((8, inner), F32),
            jax.ShapeDtypeStruct((chunks, LANES, inner), F32),
            jax.ShapeDtypeStruct((LANES, inner), BF16),
        ),
        in_specs=[
            scalars(),
            tile,
            tile,
            tile,
            whole(),
            whole(),
            tile,
            pl.BlockSpec((1, cols), lambda j: (0, j)),
            whole(),
            pl.BlockSpec((1, count, LANES), lambda j: (j * cols // ig, 0, 0)),
            pl.BlockSpec((1, 24, LANES), lambda j: (j * cols // ig, 0, 0)),
        ],
        out_specs=(
            tile,
            tile,
            tile,
            pl.BlockSpec((8, cols), lambda j: (0, j)),
            pl.BlockSpec((chunks, LANES, cols), lambda j: (0, 0, j)),
            pl.BlockSpec((LANES, cols), lambda j: (0, j)),
        ),
        compiler_params=params(),
        cost_estimate=cost(4e9, 30e6),
        name="gate",
    )(sc, y, z, dm, stat_a, stat_b, xs, gain, bc, em, kd)


def pull_body(
    ha, sc, xs, dy, bc, dtin, dt, lc, lr, em, et, kd, st, sin, ds, dsin, pre, taps, bias, skip, alog,
    dx_o, dbc_o, ddt_o, csum_o, hsum_o, cbt, off, dcb, ahead, dxi, rsum,
):
    b, step = pl.program_id(0), pl.program_id(1)
    chunks = pl.num_programs(1)
    c = chunks - 1 - step
    cols = xs.shape[1]
    half = SPAN // 2
    start = sc[3] + c * SPAN
    b_map, c_map = bc[:, :LANES], bc[:, LANES:]
    cbt[...] = nt(b_map, c_map)
    s, t = iota((SPAN, SPAN), 0), iota((SPAN, SPAN), 1)
    seen = (t >= s) & (seg_at(sc, start + t) == seg_at(sc, start + s))
    off[...] = jnp.where(seen, 0.0, FAR)
    dcb[...] = jnp.zeros_like(dcb)

    @pl.when(step == 0)
    def _():
        ahead[...] = jnp.zeros_like(ahead)
        csum_o[...] = jnp.zeros_like(csum_o)
        hsum_o[...] = jnp.zeros_like(hsum_o)
        rsum[...] = jnp.zeros_like(rsum)

    mapping = head_map(cols, 0)
    single = head_map(cols, 0, both=False)
    lane = iota((1, LANES), 1)
    sides = [(lane < 64).astype(BF16), (lane >= 64).astype(BF16)]
    steps = dt[0]
    steps_wide = expand(steps, mapping)
    xf = xs[...].astype(F32)
    scaled = (xf * steps_wide).astype(BF16)
    dyl = dy[...]
    csums = jnp.zeros((SPAN, LANES), F32)
    for k in range(cols // LANES):
        at = slice(k * LANES, (k + 1) * LANES)
        x_pair, dy_pair = scaled[:, at], dyl[:, at]
        top = jnp.zeros((half, LANES), F32)
        low = jnp.zeros((half, LANES), F32)
        for side in range(2):
            h = 2 * k + side
            x_one = x_pair * sides[side]
            dy_one = dy_pair * sides[side]
            column = lc[0, :, h : h + 1]
            row = lr[0, h : h + 1, :]
            decay = jnp.exp2(row - column[:half] + off[:half, :])
            top = top + nn((cbt[:half, :] * decay).astype(BF16), dy_one)
            share = nt(x_one[:half, :], dy_pair) * decay
            dcb[:half, :] += share
            both = share * cbt[:half, :]
            row_sum = jnp.sum(both, axis=0, keepdims=True)
            col_top = jnp.sum(both, axis=1, keepdims=True)
            decay = jnp.exp2(row[:, half:] - column[half:] + off[half:, half:])
            low = low + nn((cbt[half:, half:] * decay).astype(BF16), dy_one[half:, :])
            share = nt(x_one[half:, :], dy_pair[half:, :]) * decay
            dcb[half:, half:] += share
            both = share * cbt[half:, half:]
            rsum[h : h + 1, :half] = row_sum[:, :half]
            rsum[h : h + 1, half:] = row_sum[:, half:] + jnp.sum(both, axis=0, keepdims=True)
            col_low = jnp.sum(both, axis=1, keepdims=True)
            csums = csums + jnp.where(lane == h, jnp.concatenate([col_top, col_low], axis=0), 0.0)
        dxi[:half, at] = top
        dxi[half:, at] = low
    lead_wide = expand(em[0], mapping)
    tail_wide = expand(et[0], mapping)
    decays = expand(kd[0], mapping)
    pick = (iota((8, 1), 0) == c).astype(F32)
    state = st[0] + jnp.sum(decays[8:16] * pick, axis=0, keepdims=True) * sin[...].astype(F32)
    dstate = ds[0] + jnp.sum(decays[16:24] * pick, axis=0, keepdims=True) * dsin[...].astype(F32)
    state_l, dstate_l = state.astype(BF16), dstate.astype(BF16)
    dyf = dyl.astype(F32)
    led = dyf * lead_wide
    read = nn(c_map, state_l)
    dx_far = nn(b_map, dstate_l) * tail_wide
    db = nn(dcb[...].astype(BF16), c_map) + nt((scaled.astype(F32) * tail_wide).astype(BF16), dstate_l)
    dc = tn(dcb[...].astype(BF16), b_map) + nt(led.astype(BF16), state_l)
    rows_here = pl.ds(pl.multiple_of(c * SPAN, SPAN), SPAN)

    @pl.when(b == 0)
    def _():
        dbc_o[rows_here, :LANES] = db
        dbc_o[rows_here, LANES:] = dc

    @pl.when(b > 0)
    def _():
        dbc_o[rows_here, :LANES] += db
        dbc_o[rows_here, LANES:] += dc

    near = dxi[...]
    from_near = nt((xf * near).astype(BF16), single)
    from_far = nt((xf * dx_far).astype(BF16), single)
    reads = nt((led * read).astype(BF16), single)
    crossing = jnp.sum(state * dstate, axis=0, keepdims=True)
    held = lax.dot_general(
        jnp.broadcast_to(crossing, (8, cols)),
        single.astype(F32),
        (((1,), (1,)), ((), ())),
        precision=HIGH,
        preferred_element_type=F32,
    )[0:1, :]
    held = held * jnp.sum(kd[0, 0:8, :] * pick, axis=0, keepdims=True)
    lower = (s > t).astype(F32)
    upper = (s <= t).astype(F32)
    dlog = (
        jnp.dot(upper, rsum[...].T - csums + reads, precision=HIGH, preferred_element_type=F32)
        + jnp.dot(lower, steps * from_far, precision=HIGH, preferred_element_type=F32)
        + held
    )
    rate = -jnp.exp(alog[0])
    dstep = from_near + from_far + dlog * rate
    ddt = dstep * sigmoid(dtin[0]) * (lane < ha).astype(F32)
    ddt_o[0] = ddt
    hsum_o[0, 0:1, :] += jnp.sum(ddt, axis=0, keepdims=True)
    hsum_o[0, 1:2, :] += jnp.sum(dlog * steps * rate, axis=0, keepdims=True)

    dxs = (near + dx_far) * steps_wide + dyf * skip[...]
    window = pre[pl.ds(pl.multiple_of(c * SPAN, SPAN), SPAN + HALO), :]
    pos = start + iota((SPAN, 1), 0)
    masks = [same_as_behind(sc, pos, j) for j in range(4)]
    lagged = [window[HALO:, :]]
    for j in range(1, 4):
        lagged.append(pltpu.roll(window, j, axis=0)[HALO:, :] * masks[j])
    conv = bias[...]
    for j in range(4):
        conv = conv + taps[j : j + 1, :] * lagged[j]
    sig = sigmoid(conv)
    dconv = dxs * (sig * (1.0 + conv * (1.0 - sig)))
    sums = [jnp.sum(dconv * lagged[j], axis=0, keepdims=True) for j in range(4)]
    sums.append(jnp.sum(dconv, axis=0, keepdims=True))
    csum_o[...] += jnp.concatenate(sums + [jnp.zeros((3, cols), F32)], axis=0)
    dpre = taps[0:1, :] * dconv
    place = iota((SPAN + 8, 1), 0)
    edge = jnp.zeros((HALO, cols), F32)
    blank = jnp.zeros((8, cols), F32)
    for j in range(1, 4):
        masked = dconv * masks[j]
        longer = jnp.concatenate([masked, ahead[8 * (j - 1) : 8 * j, :]], axis=0)
        dpre = dpre + taps[j : j + 1, :] * pltpu.roll(longer, SPAN + 8 - j, axis=0)[:SPAN, :]
        first = masked[:8, :]
        ahead[8 * (j - 1) : 8 * j, :] = first
        before = pltpu.roll(jnp.concatenate([blank, blank, first], axis=0), 24 - j, axis=0)[:HALO, :]
        edge = edge + taps[j : j + 1, :] * before
    dx_o[pl.ds(pl.multiple_of(HALO + c * SPAN, HALO), SPAN), :] = dpre.astype(BF16)

    @pl.when(c == 0)
    def _():
        dx_o[:HALO, :] = edge.astype(BF16)


def run_pull(sc, xs, dy, bc, dtin, dt, lc, lr, em, et, kd, st, sin, ds, dsin, pre, taps, bias, skip, alog, ha, ig):
    count, inner = xs.shape
    total = count + HALO
    chunks = count // SPAN

    def rev(step):
        return chunks - 1 - step

    tile = pl.BlockSpec((SPAN, ig), lambda b, i: (rev(i), b))
    per_block = pl.BlockSpec((1, SPAN, LANES), lambda b, i: (b, rev(i), 0))
    states = pl.BlockSpec((1, LANES, ig), lambda b, i: (rev(i), 0, b))
    edge = pl.BlockSpec((LANES, ig), lambda b, i: (0, b))
    row = pl.BlockSpec((1, ig), lambda b, i: (0, b))
    full = pl.BlockSpec((total, ig), lambda b, i: (0, b))
    return pl.pallas_call(
        partial(pull_body, ha),
        grid=(2, chunks),
        out_shape=(
            jax.ShapeDtypeStruct((total, inner), BF16),
            jax.ShapeDtypeStruct((count, 2 * LANES), F32),
            jax.ShapeDtypeStruct((2, count, LANES), F32),
            jax.ShapeDtypeStruct((8, inner), F32),
            jax.ShapeDtypeStruct((2, 8, LANES), F32),
        ),
        in_specs=[
            scalars(),
            tile,
            tile,
            pl.BlockSpec((SPAN, 2 * LANES), lambda b, i: (rev(i), 0)),
            per_block,
            per_block,
            per_block,
            pl.BlockSpec((1, 16, SPAN), lambda b, i: (b, 0, rev(i))),
            per_block,
            per_block,
            pl.BlockSpec((1, 24, LANES), lambda b, i: (b, 0, 0)),
            states,
            edge,
            states,
            edge,
            full,
            pl.BlockSpec((4, ig), lambda b, i: (0, b)),
            row,
            row,
            pl.BlockSpec((1, 1, LANES), lambda b, i: (b, 0, 0)),
        ],
        out_specs=(
            full,
            pl.BlockSpec((count, 2 * LANES), lambda b, i: (0, 0)),
            per_block,
            pl.BlockSpec((8, ig), lambda b, i: (0, b)),
            pl.BlockSpec((1, 8, LANES), lambda b, i: (b, 0, 0)),
        ),
        scratch_shapes=[
            pltpu.VMEM((SPAN, SPAN), F32),
            pltpu.VMEM((SPAN, SPAN), F32),
            pltpu.VMEM((SPAN, SPAN), F32),
            pltpu.VMEM((24, ig), F32),
            pltpu.VMEM((SPAN, ig), F32),
            pltpu.VMEM((LANES, SPAN), F32),
        ],
        compiler_params=params(),
        cost_estimate=cost(16e9, 30e6),
        name="pull",
    )(sc, xs, dy, bc, dtin, dt, lc, lr, em, et, kd, st, sin, ds, dsin, pre, taps, bias, skip, alog)


def small_body(ha, sc, own, oth, pre, taps, bias, ddt, out, sums_o, scr):
    count = own.shape[0]
    total = count + HALO
    lane = iota((1, LANES), 1)
    steps = ddt[0] + pltpu.roll(ddt[1], ha, axis=1)
    out[:HALO, :] = jnp.zeros((HALO, 3 * LANES), BF16)
    out[HALO:, :LANES] = steps.astype(BF16)
    upstream = own[...].astype(F32) + oth[...].astype(F32)
    pos = sc[3] + iota((count, 1), 0)
    masks = [same_as_behind(sc, pos, j) for j in range(4)]
    lagged = [pre[HALO - j : HALO - j + count, :] * masks[j] for j in range(4)]
    lagged[0] = pre[HALO:, :]
    conv = bias[...]
    for j in range(4):
        conv = conv + taps[j : j + 1, :] * lagged[j]
    sig = sigmoid(conv)
    dconv = upstream * (sig * (1.0 + conv * (1.0 - sig)))
    sums = [jnp.sum(dconv * lagged[j], axis=0, keepdims=True) for j in range(4)]
    sums.append(jnp.sum(dconv, axis=0, keepdims=True))
    sums_o[...] = jnp.concatenate(sums + [jnp.zeros((3, 2 * LANES), F32)], axis=0)
    scr[...] = jnp.zeros_like(scr)
    dpre = jnp.zeros((total, 2 * LANES), F32)
    for j in range(4):
        scr[HALO : HALO + count, :] = dconv * masks[j] if j else dconv
        dpre = dpre + taps[j : j + 1, :] * scr[j : j + total, :]
    out[:, LANES:] = dpre.astype(BF16)


def run_small(sc, own, oth, pre, taps, bias, ddt, ha):
    count = own.shape[0]
    total = count + HALO
    return pl.pallas_call(
        partial(small_body, ha),
        out_shape=(
            jax.ShapeDtypeStruct((total, 3 * LANES), BF16),
            jax.ShapeDtypeStruct((8, 2 * LANES), F32),
        ),
        in_specs=[scalars()] + [whole()] * 6,
        out_specs=[whole()] * 2,
        scratch_shapes=[pltpu.VMEM((total + 8, 2 * LANES), F32)],
        compiler_params=params(),
        cost_estimate=cost(1e8, 4e6),
        name="small",
    )(sc, own, oth, pre, taps, bias, ddt)


def dnorm_body(lists, rows, share, sc, dz, dx, dsmall, tok, *rest):
    counts = [len(parts) for parts in lists]
    total_refs = sum(counts)
    refs = rest[:total_refs]
    out, sums, scr_z, scr_x, scr_s = rest[total_refs:]
    cols = out.shape[1]
    j = pl.program_id(0)

    @pl.when(j == 0)
    def _():
        low = 0
        for parts, scr in zip(lists, (scr_z, scr_x, scr_s)):
            assemble(sc[4], rows, parts, refs[low : low + len(parts)], scr)
            low += len(parts)

    at = pl.ds(pl.multiple_of(j * cols, cols), cols)
    w_s = scr_s[at, :]
    value = (
        nt(dx[...], scr_x[at, :])
        + nt(dsmall[:, :LANES], w_s[:, :LANES])
        + nt(dsmall[:, LANES:], w_s[:, LANES:]) * share
    )
    from_z = nt(dz[...], scr_z[at, :])
    top = value[:HALO, :]
    rest_v = value[HALO:, :] + from_z
    out[:HALO, :] = top.astype(BF16)
    out[HALO:, :] = rest_v.astype(BF16)
    total = jnp.sum(top * tok[:HALO, :].astype(F32), axis=0, keepdims=True) + jnp.sum(
        rest_v * tok[HALO:, :].astype(F32), axis=0, keepdims=True
    )
    sums[...] = jnp.broadcast_to(total, sums.shape)


def run_dnorm(sc, dz, dx, dsmall, tok, pieces_z, pieces_x, pieces_s, rows, share):
    total, width = tok.shape
    inner = dx.shape[1]
    cols = 256
    lists = [pieces_z[0], pieces_x[0], pieces_s[0]]
    refs = [*pieces_z[1], *pieces_x[1], *pieces_s[1]]
    return pl.pallas_call(
        partial(dnorm_body, lists, rows, share),
        grid=(width // cols,),
        out_shape=(
            jax.ShapeDtypeStruct((total, width), BF16),
            jax.ShapeDtypeStruct((8, width), F32),
        ),
        in_specs=[scalars(), whole(), whole(), whole(), pl.BlockSpec((total, cols), lambda j: (0, j))]
        + [whole()] * len(refs),
        out_specs=(
            pl.BlockSpec((total, cols), lambda j: (0, j)),
            pl.BlockSpec((8, cols), lambda j: (0, j)),
        ),
        scratch_shapes=[
            pltpu.VMEM((width, inner), BF16),
            pltpu.VMEM((width, inner), BF16),
            pltpu.VMEM((width, 3 * LANES), BF16),
        ],
        compiler_params=params(),
        cost_estimate=cost(2 * total * width * (2 * inner + 384), 20e6),
        name="dnorm",
    )(sc, dz, dx, dsmall, tok, *refs)


def swap(value, bit, size):
    return lax.ppermute(value, "dp", [(i, i ^ bit) for i in range(size)])


def link_bits(size):
    bits = []
    bit = 2
    while bit < size:
        bits.append(bit)
        bit *= 2
    return bits


def gather_rows(shard, split, size):
    parts, refs = [], []
    bits = link_bits(size)
    for low, high, order in ((0, split, bits), (split, shard.shape[1], bits[::-1])):
        held, names = shard[None, :, low:high], [0]
        stacks = []
        for position, bit in enumerate(order):
            got = swap(held, bit, size)
            new = [v ^ bit for v in names]
            if position + 1 < len(order):
                held, names = jnp.concatenate([held, got], axis=0), names + new
            else:
                stacks = [(held, names), (got, new)]
        for stack, named in stacks:
            parts.append((tuple(named), low))
            refs.append(stack)
        for stack, named in stacks:
            parts.append((tuple(v ^ 1 for v in named), low))
            refs.append(swap(stack, 1, size))
    return parts, refs


def scatter_rows(own, oth, split, size):
    got = swap(oth, 1, size)
    outs = []
    bits = link_bits(size)
    for low, high, order in ((0, split, bits), (split, own.shape[2], bits[::-1])):
        held = {2 * u: own[u, :, low:high].astype(F32) + got[u, :, low:high].astype(F32) for u in range(own.shape[0])}
        for bit in order:
            away = sorted(v for v in held if v & bit)
            stay = sorted(v for v in held if not v & bit)
            arrived = swap(jnp.stack([held[v].astype(BF16) for v in away]), bit, size)
            held = {v: held[v] + arrived[i].astype(F32) for i, v in enumerate(stay)}
        outs.append(held[0].astype(BF16))
    return outs


def to_heads(shard, parts, lower):
    hp = parts // 2
    first = [(2 * p, p) for p in range(hp)] + [(2 * (p - hp) + 1, p) for p in range(hp, parts)]
    second = [(2 * p + 1, p) for p in range(hp)] + [(2 * (p - hp), p) for p in range(hp, parts)]
    one, two = lax.ppermute(shard, "tensor", first), lax.ppermute(shard, "tensor", second)
    return jnp.where(lower, one, two), jnp.where(lower, two, one)


def from_heads(block_a, block_b, parts, lower):
    hp = parts // 2
    first = [(p, 2 * p) for p in range(hp)] + [(p, 2 * (p - hp) + 1) for p in range(hp, parts)]
    second = [(p, 2 * p + 1) for p in range(hp)] + [(p, 2 * (p - hp)) for p in range(hp, parts)]
    one = lax.ppermute(jnp.where(lower, block_a, block_b), "tensor", first)
    two = lax.ppermute(jnp.where(lower, block_b, block_a), "tensor", second)
    return one.astype(F32) + two.astype(F32)


def half_groups(parts):
    hp = parts // 2
    return [list(range(hp)), list(range(hp, parts))]


def half_gather(value, parts, place):
    hp = parts // 2
    if hp != 2:
        return lax.all_gather(value, "tensor", axis=0, tiled=True, axis_index_groups=half_groups(parts))
    other = lax.ppermute(value, "tensor", [(p, p ^ 1) for p in range(parts)])
    return jnp.where(
        place == 0, jnp.concatenate([value, other], axis=0), jnp.concatenate([other, value], axis=0)
    )


def half_other(value, parts):
    hp = parts // 2
    total = jnp.zeros(value.shape, F32)
    for shift in range(1, hp):
        pairs = [(p, (p // hp) * hp + (p % hp + shift) % hp) for p in range(parts)]
        total = total + lax.ppermute(value, "tensor", pairs).astype(F32)
    return total if hp > 2 else lax.ppermute(value, "tensor", [(p, p ^ 1) for p in range(parts)])


def half_scatter(value, parts, place):
    hp = parts // 2
    rows = value.shape[0] // hp
    mine = lax.dynamic_slice_in_dim(value, place * rows, rows, 0)
    total = mine.astype(F32)
    for shift in range(1, hp):
        pairs = [(p, (p // hp) * hp + (p % hp + shift) % hp) for p in range(parts)]
        away = lax.dynamic_slice_in_dim(value, lax.rem(place + shift, hp) * rows, rows, 0)
        total = total + lax.ppermute(away, "tensor", pairs).astype(F32)
    return total


def sum_dp(value, size):
    bit = 1
    while bit < size:
        value = value + swap(value, bit, size)
        bit *= 2
    return value


def sum_tensor(value, parts):
    bit = 1
    while bit < parts:
        value = value + lax.ppermute(value, "tensor", [(p, p ^ bit) for p in range(parts)])
        bit *= 2
    return value


def after(value, *others):
    return lax.optimization_barrier((value, *others))[0]


def local(
    inputs,
    cotangent,
    seq_lengths,
    norm_gain,
    w_z,
    w_x,
    w_bc,
    w_dt,
    conv_x,
    conv_x_bias,
    conv_bc,
    conv_bc_bias,
    dt_bias,
    a_log,
    d_skip,
    gate_gain,
    w_out,
):
    local_rows, width = inputs.shape
    parts = lax.axis_size("tensor")
    size = lax.axis_size("dp")
    hp = parts // 2
    position = lax.axis_index("tensor")
    me = lax.axis_index("dp")
    lower = position < hp
    place = lax.rem(position, hp)
    count = local_rows * hp
    ha = dt_bias.shape[0]
    ig = w_z.shape[1]
    inner = 2 * ig
    inner_all = ig * parts
    rows = w_z.shape[0]
    head_width = ig // ha

    ends = [seq_lengths[0, 0], seq_lengths[0, 0] + seq_lengths[0, 1]]
    ends.append(ends[1] + seq_lengths[0, 2])
    base = jnp.where(lower, 0, count)
    sc = jnp.stack([*ends, base, me, position, position, position]).astype(jnp.int32)

    def pad(v, to):
        return jnp.pad(v, [(0, 0)] * (v.ndim - 1) + [(0, to - v.shape[-1])])

    heads_row = jnp.concatenate([pad(dt_bias, LANES), pad(a_log, LANES), pad(d_skip, LANES)])
    table = jnp.concatenate(
        [conv_x, conv_x_bias[None], gate_gain[None], jnp.repeat(d_skip, head_width)[None], pad(heads_row, ig)[None]]
    )
    par_a, par_b = to_heads(table, parts, lower)
    wide = jnp.concatenate([par_a, par_b], axis=1)
    taps_x, bias_x, gain, skip = wide[0:4], wide[4:5], wide[5:6], wide[6:7]
    dtb = jnp.concatenate([par_a[7, :ha], par_b[7, :ha], jnp.zeros((LANES - 2 * ha,), F32)])[None]
    alog = jnp.concatenate([par_a[7, LANES : LANES + ha], par_b[7, LANES : LANES + ha], jnp.zeros((LANES - 2 * ha,), F32)])[None]
    alog_blocks = jnp.stack([par_a[7, LANES : 2 * LANES], par_b[7, LANES : 2 * LANES]])[:, None, :]

    dt_a, dt_b = to_heads(w_dt, parts, lower)
    small = jnp.concatenate([dt_a, dt_b, jnp.zeros((rows, LANES - 2 * ha), BF16), w_bc], axis=1)
    p_small = gather_rows(small, LANES, size)
    x_a, x_b = to_heads(w_x, parts, lower)
    p_x = gather_rows(jnp.concatenate([x_a, x_b], axis=1), ig, size)
    z_a, z_b = to_heads(after(w_z, x_a), parts, lower)
    p_z = gather_rows(jnp.concatenate([z_a, z_b], axis=1), ig, size)
    o_a, o_b = to_heads(after(w_out, z_a).T, parts, lower)
    p_o = gather_rows(jnp.concatenate([o_a, o_b], axis=1), ig, size)

    input_f = inputs.astype(F32)
    in_scale = lax.rsqrt(jnp.mean(input_f * input_f, axis=1, keepdims=True) + EPS)
    normed = (input_f * in_scale * norm_gain[None, :]).astype(BF16)
    halo = jnp.zeros((HALO, width), BF16)
    for k in range(hp):
        halo = halo + lax.ppermute(normed[local_rows - HALO :], "tensor", [(hp - 1, hp + k)])
    tok = jnp.concatenate([halo, half_gather(normed, parts, place)], axis=0)
    pulled = half_gather(after(cotangent, tok), parts, place)

    pre_bc, bc, dtin, dt, lc, lr, em, et, kd = run_maps(
        sc, tok, conv_bc, conv_bc_bias[None], dtb, alog, p_small, rows, ha
    )
    pre_x, xs, st, fin = run_xpath(sc, tok, taps_x, bias_x, bc, dt, et, kd, p_x, rows, ig)
    forward = [(p, p + hp) for p in range(hp)]
    sin = lax.ppermute(fin, "tensor", forward)
    z = run_proj(sc, tok, p_z, rows, inner, count)
    dm = run_proj(sc, pulled, p_o, rows, inner, count)
    y, stat = run_scan(sc, xs, bc, dt, lc, lr, em, kd, st, sin, z, dm, skip, gain, ig)
    stat_other = half_other(stat, parts)
    mixed, dz, dy, gate_sums, ds, dfirst = run_gate(
        sc, y, z, dm, stat, stat_other, xs, gain, bc, em, kd, ig, inner_all
    )
    dsin = lax.ppermute(dfirst, "tensor", [(p + hp, p) for p in range(hp)])
    branch = run_back(sc, mixed, p_o, rows, width)
    outputs = (input_f + half_scatter(branch, parts, place)).astype(BF16)
    gw_o = run_grad(sc, pulled, mixed, rows)
    gw_z = run_grad(sc, tok, dz, rows)
    dx, dbc, ddt, conv_sums, head_sums = run_pull(
        sc, xs, dy, bc, dtin, dt, lc, lr, em, et, kd, st, sin, ds, dsin, pre_x, taps_x, bias_x, skip,
        alog_blocks, ha, ig,
    )
    dbc_low = dbc.astype(BF16)
    dbc_other = half_other(dbc_low, parts)
    gw_x = run_grad(sc, tok, dx, rows)
    dsmall, bc_sums = run_small(sc, dbc_low, dbc_other, pre_bc, conv_bc, conv_bc_bias[None], ddt, ha)
    dn, norm_sums = run_dnorm(sc, dz, dx, dsmall, tok, p_z, p_x, p_small, rows, 1.0 / hp)
    gw_s = run_grad(sc, tok, dsmall, rows)

    dn_own = half_scatter(dn[HALO:], parts, place)
    edge = jnp.zeros((HALO, width), F32)
    for k in range(hp):
        edge = edge + lax.ppermute(dn[:HALO], "tensor", [(hp + k, hp - 1)]).astype(F32)
    dn_own = dn_own + jnp.concatenate([jnp.zeros((local_rows - HALO, width), F32), edge], axis=0)
    dnorm_side = dn_own * norm_gain[None, :]
    grad_inputs = (
        in_scale * dnorm_side
        - input_f
        * (in_scale * in_scale * in_scale)
        * (jnp.sum(dnorm_side * input_f, axis=1, keepdims=True) / width)
        + cotangent.astype(F32)
    ).astype(BF16)

    grad_w_out = from_heads(*scatter_rows(*gw_o, ig, size), parts, lower).T
    grad_w_z = from_heads(*scatter_rows(*gw_z, ig, size), parts, lower)
    grad_w_x = from_heads(*scatter_rows(*gw_x, ig, size), parts, lower)
    s_dt, s_bc = scatter_rows(*gw_s, LANES, size)
    grad_w_dt = from_heads(s_dt[:, :ha], s_dt[:, ha : 2 * ha], parts, lower)
    grad_w_bc = s_bc.astype(F32) + lax.ppermute(
        s_bc, "tensor", [(p, (p + hp) % parts) for p in range(parts)]
    ).astype(F32)

    heads_row = pad(head_sums[:, :2].reshape(2, 2 * LANES), ig).reshape(1, inner)
    chan = jnp.concatenate([conv_sums[:5], gate_sums[:2], heads_row])
    rep = jnp.concatenate([(norm_sums[0] / norm_gain), bc_sums[:5].reshape(-1) / hp])
    chan = sum_dp(chan, size)
    chan = from_heads(chan[:, :ig], chan[:, ig:], parts, lower)
    rep = sum_tensor(sum_dp(rep.reshape(-1, LANES), size), parts).reshape(-1)
    rep_bc = rep[width:].reshape(5, -1)
    return (
        outputs,
        grad_inputs,
        rep[:width],
        grad_w_z,
        grad_w_x,
        grad_w_bc,
        grad_w_dt,
        chan[:4],
        chan[4],
        rep_bc[:4],
        rep_bc[4],
        chan[7, :ha],
        chan[7, LANES : LANES + ha],
        jnp.sum(chan[6].reshape(ha, head_width), axis=1),
        chan[5],
        grad_w_out,
    )


def solution(mesh):
    tokens = P(("dp", "tensor"), None)
    matrix = P("dp", "tensor")
    heads = P("tensor")
    return jax.shard_map(
        local,
        mesh=mesh,
        in_specs=(
            tokens,
            tokens,
            P("dp", None),
            P(),
            matrix,
            matrix,
            P("dp", None),
            matrix,
            P(None, "tensor"),
            heads,
            P(),
            P(),
            heads,
            heads,
            heads,
            heads,
            P("tensor", "dp"),
        ),
        out_specs=(
            tokens,
            tokens,
            P(),
            matrix,
            matrix,
            P("dp", None),
            matrix,
            P(None, "tensor"),
            heads,
            P(),
            P(),
            heads,
            heads,
            heads,
            heads,
            P("tensor", "dp"),
        ),
        check_vma=False,
    )
```

```python
from functools import partial

import jax
import jax.numpy as jnp
from jax import lax
from jax.experimental import pallas as pl
from jax.experimental.pallas import tpu as pltpu
from jax.sharding import PartitionSpec as P

SPAN = 256
HALO = 16
LANES = 128
LOG2E = 1.4426950408889634
EPS = 1e-05
FAR = -1e30
HIGH = lax.Precision.HIGHEST
F32 = jnp.float32
BF16 = jnp.bfloat16
VMEM_BYTES = 60 * 1024 * 1024


def nn(a, b):
    return jnp.dot(a, b, preferred_element_type=F32)


def nt(a, b):
    return lax.dot_general(a, b, (((1,), (1,)), ((), ())), preferred_element_type=F32)


def tn(a, b):
    return lax.dot_general(a, b, (((0,), (0,)), ((), ())), preferred_element_type=F32)


def sigmoid(v):
    return 1.0 / (1.0 + jnp.exp(-v))


def iota(shape, axis):
    return lax.broadcasted_iota(jnp.int32, shape, axis)


def seg_at(sc, pos):
    found = (pos >= sc[0]).astype(jnp.int32)
    for i in range(1, 3):
        found = found + (pos >= sc[i]).astype(jnp.int32)
    return jnp.where(pos < 0, -1, found)


def same_as_behind(sc, pos, offset):
    return (seg_at(sc, pos - offset) == seg_at(sc, pos)).astype(F32)


def head_map(cols, start, dtype=BF16, both=True):
    k = iota((LANES, cols), 0)
    if both:
        k = k & 63
    head = (iota((LANES, cols), 1) + start) >> 6
    return (k == head).astype(dtype)


def expand(values, mapping):
    high = values.astype(BF16).astype(F32)
    low = values - high
    return nn((high + pltpu.roll(low, 64, axis=1)).astype(BF16), mapping)


def whole():
    return pl.BlockSpec(memory_space=pltpu.VMEM)


def scalars():
    return pl.BlockSpec(memory_space=pltpu.SMEM)


def params():
    return pltpu.CompilerParams(vmem_limit_bytes=VMEM_BYTES)


def cost(flops, nbytes):
    return pl.CostEstimate(flops=int(flops), bytes_accessed=int(nbytes), transcendentals=0)


def col_tile(ig):
    return 256 if ig % 256 == 0 else 128


def flip(me, v):
    out = me
    bit = 1
    while bit <= v:
        if v & bit:
            out = out + bit - 2 * bit * lax.rem(me // bit, 2)
        bit *= 2
    return out


def link_bits(size):
    bits = []
    bit = 2
    while bit < size:
        bits.append(bit)
        bit *= 2
    return bits


def remote(src, dst, send, recv, **where):
    return pltpu.make_async_remote_copy(
        src_ref=src, dst_ref=dst, send_sem=send, recv_sem=recv, device_id=where, device_id_type=pl.DeviceIdType.MESH
    )


def greet(size, parts):
    me, p = lax.axis_index("dp"), lax.axis_index("tensor")
    barrier = pltpu.get_barrier_semaphore()
    bits = [1] + link_bits(size)
    for bit in bits:
        pl.semaphore_signal(barrier, inc=1, device_id={"dp": flip(me, bit)}, device_id_type=pl.DeviceIdType.MESH)
    for shift in range(1, parts):
        pl.semaphore_signal(
            barrier, inc=1, device_id={"tensor": lax.rem(p + shift, parts)}, device_id_type=pl.DeviceIdType.MESH
        )
    pl.semaphore_wait(barrier, len(bits) + parts - 1)


class ToHeads:
    def __init__(self, k, src, place_of, parts, send, recv, own):
        self.p = lax.axis_index("tensor")
        self.hp = parts // 2
        self.k, self.src, self.place_of = k, src, place_of
        self.send, self.recv, self.own = send, recv, own

    def copy(self, i, side, to):
        return remote(
            self.src, self.place_of(side), self.send.at[2 * self.k + i], self.recv.at[2 * self.k + side], tensor=to
        )

    def local(self, side):
        return pltpu.make_async_copy(self.src, self.place_of(side), self.own.at[self.k])

    def targets(self):
        return [self.p // 2, self.p // 2 + self.hp]

    def start(self):
        side = lax.rem(self.p, 2)
        for i, to in enumerate(self.targets()):

            @pl.when(to != self.p)
            def _(i=i, to=to):
                self.copy(i, side, to).start()

            @pl.when(to == self.p)
            def _():
                self.local(side).start()

    def wait(self):
        q = lax.rem(self.p, self.hp)
        for side in range(2):
            source = 2 * q + side

            @pl.when(source != self.p)
            def _(side=side):
                self.copy(0, side, self.p // 2).wait_recv()

            @pl.when(source == self.p)
            def _(side=side):
                self.local(side).wait()

    def finish(self):
        side = lax.rem(self.p, 2)
        for i, to in enumerate(self.targets()):

            @pl.when(to != self.p)
            def _(i=i, to=to):
                self.copy(i, side, to).wait_send()


class Gather:
    def __init__(self, k, ref, split, rows, size, send, recv):
        self.me = lax.axis_index("dp")
        self.k, self.ref, self.rows, self.size = k, ref, rows, size
        bits = link_bits(size)
        self.orders = [bits, bits[::-1]]
        self.cols = [slice(0, split), slice(split, ref.shape[1])]
        self.send, self.recv = send, recv
        self.sent = []

    def block(self, half, v):
        start = pl.multiple_of(flip(self.me, v) * self.rows, 16)
        cols = self.cols[half]
        return self.ref.at[pl.ds(start, self.rows), pl.ds(cols.start, cols.stop - cols.start)]

    def copy(self, half, v, bit):
        n = bit.bit_length() - 1
        here = self.block(half, v)
        return remote(
            here,
            here,
            self.send.at[self.k, half, v * self.size.bit_length() + n],
            self.recv.at[self.k, half, v ^ bit],
            dp=flip(self.me, bit),
        )

    def push(self, half, v, bits):
        for bit in bits:
            self.copy(half, v, bit).start()
            self.sent.append((half, v, bit))

    def arrive(self, half, v):
        here = self.block(half, v)
        remote(
            here,
            here,
            self.send.at[self.k, half, 0],
            self.recv.at[self.k, half, v],
            dp=flip(self.me, 1),
        ).wait_recv()

    def start(self):
        for half in range(2):
            self.push(half, 0, self.orders[half])
        for half in range(2):
            self.push(half, 0, [1])

    def stage(self, s):
        for half in range(2):
            order = self.orders[half]
            names = [0]
            for bit in order[:s]:
                names = names + [v ^ bit for v in names]
            for v in sorted(n ^ order[s] for n in names):
                self.arrive(half, v)
                self.push(half, v, order[s + 1 :])
                self.push(half, v, [1])

    def stages(self):
        return len(self.orders[0])

    def cores(self):
        for half in range(2):
            for v in range(1, self.size, 2):
                self.arrive(half, v)

    def finish(self):
        for half, v, bit in self.sent:
            self.copy(half, v, bit).wait_send()


def first_body(
    size, parts, rows, ha, ig,
    ends, inputs, cot, ngain, w_x, w_z, w_o, w_bc, w_dt, table, taps_bc, bias_bc,
    tok_h, pulled_h, wx_h, wz_h, wo_h, ws_h, par_h, pre_h, bc_h, dtin_h, dt_h, lc_h, lr_h, em_h, et_h, kd_h,
    prex_h, xs_h, st_h, sin_h, z_h, dm_h,
    tok, pulled, wx, wz, wo, ws, par, pre, bc, dtin, dt, lc, lr, em, et, kd, st, stage, xs_stage, fin, sin,
    zs, zr, zo, gs, gr, ts, tr, cs, cr, hs, hr, ss, sr, local, outs, tiles,
):
    p = lax.axis_index("tensor")
    me = lax.axis_index("dp")
    hp = parts // 2
    place = lax.rem(p, hp)
    half = p // hp
    inner = 2 * ig
    local_rows, width = inputs.shape
    count = local_rows * hp
    total = count + HALO
    base = half * count
    own_rows = pl.multiple_of(place * local_rows, 16)

    def mates():
        return [(s, half * hp + lax.rem(place + s, hp)) for s in range(1, hp)]

    def my_rows():
        return pl.ds(pl.multiple_of(me * rows, 16), rows)

    def wide(ref, cols):
        return lambda side: ref.at[my_rows(), pl.ds(pl.multiple_of(side * cols, LANES), cols)]

    emitted = []

    def emit(src, dst):
        copy = pltpu.make_async_copy(src, dst, outs.at[len(emitted)])
        copy.start()
        emitted.append(copy)

    greet(size, parts)
    to_table = ToHeads(0, table, lambda side: par.at[:, pl.ds(pl.multiple_of(side * ig, LANES), ig)], parts, zs, zr, zo)
    to_dt = ToHeads(1, w_dt, wide(ws, LANES), parts, zs, zr, zo)
    to_x = ToHeads(2, w_x, wide(wx, ig), parts, zs, zr, zo)
    to_z = ToHeads(3, w_z, wide(wz, ig), parts, zs, zr, zo)
    to_o = ToHeads(4, w_o, wide(wo, ig), parts, zs, zr, zo)
    to_dt.start()
    to_x.start()
    to_table.start()
    bc_copy = pltpu.make_async_copy(w_bc, ws.at[my_rows(), pl.ds(2 * LANES, 2 * LANES)], local.at[0])
    bc_copy.start()
    cot_copy = pltpu.make_async_copy(cot, pulled.at[pl.ds(own_rows, local_rows)], local.at[1])
    cot_copy.start()

    values = inputs[...].astype(F32)
    scale = lax.rsqrt(jnp.mean(values * values, axis=1, keepdims=True) + EPS)
    mine = pl.ds(pl.multiple_of(HALO + own_rows, 16), local_rows)
    tok[mine, :] = (values * scale * ngain[...]).astype(BF16)

    def tok_copy(s, to):
        return remote(tok.at[mine], tok.at[mine], ts.at[s], tr.at[s], tensor=to)

    def tok_arrive(s):
        there = pl.ds(pl.multiple_of(HALO + lax.rem(place + hp - s, hp) * local_rows, 16), local_rows)
        remote(tok.at[there], tok.at[there], ts.at[s], tr.at[s], tensor=p).wait_recv()

    def cot_copy_to(s, to):
        return remote(cot, pulled.at[pl.ds(own_rows, local_rows)], cs.at[s], cr.at[s], tensor=to)

    def cot_arrive(s):
        there = pl.ds(pl.multiple_of(lax.rem(place + hp - s, hp) * local_rows, 16), local_rows)
        remote(pulled.at[there], pulled.at[there], cs.at[s], cr.at[s], tensor=p).wait_recv()

    def halo_copy(k):
        return remote(tok.at[pl.ds(total - HALO, HALO)], tok.at[pl.ds(0, HALO)], hs.at[k], hr.at[0], tensor=hp + k)

    for s, to in mates():
        tok_copy(s, to).start()

    @pl.when(p == hp - 1)
    def _():
        for k in range(hp):
            halo_copy(k).start()

    @pl.when(half == 0)
    def _():
        tok[:HALO, :] = jnp.zeros((HALO, width), BF16)

    to_z.start()
    to_o.start()
    for s, to in mates():
        cot_copy_to(s, to).start()

    g_s = Gather(0, ws, 2 * LANES, rows, size, gs, gr)
    g_x = Gather(1, wx, ig, rows, size, gs, gr)
    g_z = Gather(2, wz, ig, rows, size, gs, gr)
    g_o = Gather(3, wo, ig, rows, size, gs, gr)
    stages = g_x.stages()
    to_dt.wait()
    bc_copy.wait()
    g_s.start()
    to_x.wait()
    g_x.start()
    for s in range(stages):
        g_s.stage(s)
        g_x.stage(s)
        if s == 0:
            to_z.wait()
            g_z.start()
    g_s.cores()
    for s, _ in mates():
        tok_arrive(s)

    @pl.when(half == 1)
    def _():
        halo_copy(0).wait_recv()

    emit(tok, tok_h)
    emit(ws, ws_h)

    pre[...] = nn(tok[...], ws[:, 2 * LANES :])
    emit(pre, pre_h)
    pos = base + iota((count, 1), 0)
    acc = bias_bc[...] + taps_bc[0:1, :] * pre[HALO : HALO + count, :]
    for j in range(1, 4):
        acc = acc + taps_bc[j : j + 1, :] * pre[HALO - j : HALO - j + count, :] * same_as_behind(ends, pos, j)
    bc[...] = (acc * sigmoid(acc)).astype(BF16)
    emit(bc, bc_h)
    to_table.wait()
    emit(par, par_h)
    keep = (iota((1, LANES), 1) < ha).astype(F32)
    tri = (iota((SPAN, SPAN), 0) >= iota((SPAN, SPAN), 1)).astype(F32)
    chunks = count // SPAN
    for b in range(2):
        heads = par[7:8, b * ig : b * ig + 2 * LANES]
        dtraw = nn(tok[HALO:, :], ws[:, b * LANES : (b + 1) * LANES])
        shifted = (dtraw + heads[:, :LANES]) * keep
        steps = (jnp.maximum(shifted, 0.0) + jnp.log1p(jnp.exp(-jnp.abs(shifted)))) * keep
        dtin[b] = shifted
        dt[b] = steps
        scaled = steps * (-jnp.exp(heads[:, LANES:]) * LOG2E)
        gone = []
        for c in range(chunks):
            span = slice(c * SPAN, (c + 1) * SPAN)
            logs = jnp.dot(tri, scaled[span, :], precision=HIGH, preferred_element_type=F32)
            first, last = base + c * SPAN - 1, base + (c + 1) * SPAN - 1
            here = base + c * SPAN + iota((SPAN, 1), 0)
            seg = seg_at(ends, here)
            seg_first, seg_last = seg_at(ends, first), seg_at(ends, last)
            final = logs[SPAN - 1 : SPAN, :]
            gone.append(jnp.where(seg_first == seg_last, 1.0, 0.0).astype(F32) * jnp.exp2(final) * keep)
            lc[b, span, :] = logs
            lr[b, :, span] = logs.T[:16, :]
            em[b, span, :] = (seg == seg_first).astype(F32) * jnp.exp2(logs) * keep
            et[b, span, :] = (seg == seg_last).astype(F32) * jnp.exp2(final - logs) * keep
        ahead_of, behind_of = [keep], [keep]
        for c in range(chunks - 1):
            ahead_of.append(ahead_of[-1] * gone[c])
            behind_of.append(behind_of[-1] * gone[chunks - 1 - c])
        behind_of = behind_of[::-1]
        fill = [jnp.zeros((1, LANES), F32)] * (8 - chunks)
        kd[b] = jnp.concatenate(gone + fill + ahead_of + fill + behind_of + fill, axis=0)
    for src, dst in ((dtin, dtin_h), (dt, dt_h), (lc, lc_h), (lr, lr_h), (em, em_h), (et, et_h), (kd, kd_h)):
        emit(src, dst)

    g_x.cores()
    emit(wx, wx_h)
    to_o.wait()
    g_z.stage(0)
    g_o.start()

    cols = col_tile(ig)

    def tile_out(kind, slot, j):
        at = pl.ds(pl.multiple_of(j * cols, cols), cols)
        if kind == 0:
            return pltpu.make_async_copy(stage.at[slot], prex_h.at[:, at], tiles.at[0, slot])
        if kind == 1:
            return pltpu.make_async_copy(xs_stage.at[slot], xs_h.at[:, at], tiles.at[1, slot])
        rows_of = stage.at[slot, pl.ds(0, count)]
        return pltpu.make_async_copy(rows_of, (z_h if kind == 2 else dm_h).at[:, at], tiles.at[kind, slot])

    def xpath(j, carry):
        slot = lax.rem(j, 2)

        @pl.when(j >= 2)
        def _():
            tile_out(0, slot, j).wait()
            tile_out(1, slot, j).wait()

        at = pl.multiple_of(j * cols, cols)
        lanes = pl.ds(at, cols)
        b = at // ig
        stage[slot] = nn(tok[...], wx[:, lanes])
        mapping = head_map(cols, lax.rem(at, ig))
        state = jnp.zeros((LANES, cols), F32)
        decay = expand(kd[b], mapping)
        taps, bias = par[0:4, lanes], par[4:5, lanes]
        for c in range(chunks):
            low = c * SPAN
            here = base + low + iota((SPAN, 1), 0)
            window = stage[slot, low : low + SPAN + HALO, :]
            conv = bias + taps[0:1, :] * window[HALO:, :]
            for k in range(1, 4):
                lag = pltpu.roll(window, k, axis=0)[HALO:, :]
                conv = conv + taps[k : k + 1, :] * lag * same_as_behind(ends, here, k)
            xs = (conv * sigmoid(conv)).astype(BF16)
            xs_stage[slot, low : low + SPAN, :] = xs
            weight = expand(dt[b, low : low + SPAN, :] * et[b, low : low + SPAN, :], mapping)
            st[c, :, lanes] = state
            fresh = tn(bc[low : low + SPAN, :LANES], (xs.astype(F32) * weight).astype(BF16))
            state = decay[c : c + 1, :] * state + fresh
        fin[:, lanes] = state.astype(BF16)
        tile_out(0, slot, j).start()
        tile_out(1, slot, j).start()
        return carry

    def project(kind, x, skip, w):
        def step(j, carry):
            slot = lax.rem(j, 2)

            @pl.when(j >= 2)
            def _():
                tile_out(kind, slot, j).wait()

            lanes = pl.ds(pl.multiple_of(j * cols, cols), cols)
            stage[slot, :count, :] = nn(x[skip:, :], w[:, lanes])
            tile_out(kind, slot, j).start()
            return carry

        return step

    tiles_all = inner // cols
    middle = tiles_all // 2

    def drain(kind):
        for j in range(tiles_all - 2, tiles_all):
            tile_out(kind, j % 2, j).wait()

    lax.fori_loop(0, middle, xpath, 0)
    for s in range(1, stages):
        g_z.stage(s)
    lax.fori_loop(middle, tiles_all, xpath, 0)
    emit(st, st_h)

    def state_copy():
        return remote(fin, sin, ss.at[0], sr.at[0], tensor=lax.rem(p + hp, parts))

    @pl.when(half == 0)
    def _():
        state_copy().start()

    drain(0)
    drain(1)
    g_z.cores()
    emit(wz, wz_h)
    lax.fori_loop(0, middle, project(2, tok, HALO, wz), 0)
    for s in range(stages):
        g_o.stage(s)
    lax.fori_loop(middle, tiles_all, project(2, tok, HALO, wz), 0)
    drain(2)
    for s, _ in mates():
        cot_arrive(s)
    cot_copy.wait()
    emit(pulled, pulled_h)
    g_o.cores()
    emit(wo, wo_h)
    lax.fori_loop(0, tiles_all, project(3, pulled, 0, wo), 0)

    @pl.when(half == 1)
    def _():
        state_copy().wait_recv()

    @pl.when(half == 0)
    def _():
        sin[...] = jnp.zeros_like(sin)

    emit(sin, sin_h)
    drain(3)
    for item in (to_table, to_dt, to_x, to_z, to_o, g_s, g_x, g_z, g_o):
        item.finish()
    for s, to in mates():
        tok_copy(s, to).wait_send()
        cot_copy_to(s, to).wait_send()

    @pl.when(p == hp - 1)
    def _():
        for k in range(hp):
            halo_copy(k).wait_send()

    @pl.when(half == 0)
    def _():
        state_copy().wait_send()

    for copy in emitted:
        copy.wait()


def run_first(ends, inputs, cot, ngain, w_x, w_z, w_o, w_bc, w_dt, table, taps_bc, bias_bc, size, parts, ha):
    local_rows, width = inputs.shape
    rows, ig = w_x.shape
    inner = 2 * ig
    hp = parts // 2
    count = local_rows * hp
    total = count + HALO
    chunks = count // SPAN
    cols = col_tile(ig)
    shape = jax.ShapeDtypeStruct
    per_block = shape((2, count, LANES), F32)
    outs = (
        shape((total, width), BF16),
        shape((count, width), BF16),
        shape((width, inner), BF16),
        shape((width, inner), BF16),
        shape((width, inner), BF16),
        shape((width, 4 * LANES), BF16),
        shape((8, inner), F32),
        shape((total, 2 * LANES), F32),
        shape((count, 2 * LANES), BF16),
        per_block,
        per_block,
        per_block,
        shape((2, 16, count), F32),
        per_block,
        per_block,
        shape((2, 24, LANES), F32),
        shape((total, inner), F32),
        shape((count, inner), BF16),
        shape((chunks, LANES, inner), F32),
        shape((LANES, inner), BF16),
        shape((count, inner), F32),
        shape((count, inner), F32),
    )
    anywhere = pl.BlockSpec(memory_space=pl.ANY)
    dma = pltpu.SemaphoreType.DMA
    nbits = size.bit_length()
    scratch = [pltpu.VMEM(o.shape, o.dtype) for o in outs[:16]]
    scratch += [
        pltpu.VMEM((chunks, LANES, inner), F32),
        pltpu.VMEM((2, total, cols), F32),
        pltpu.VMEM((2, count, cols), BF16),
        pltpu.VMEM((LANES, inner), BF16),
        pltpu.VMEM((LANES, inner), BF16),
        dma((10,)),
        dma((10,)),
        dma((5,)),
        dma((4, 2, size * nbits)),
        dma((4, 2, size)),
        dma((hp,)),
        dma((hp,)),
        dma((hp,)),
        dma((hp,)),
        dma((hp,)),
        dma((1,)),
        dma((1,)),
        dma((1,)),
        dma((2,)),
        dma((24,)),
        dma((4, 2)),
    ]
    return pl.pallas_call(
        partial(first_body, size, parts, rows, ha, ig),
        out_shape=outs,
        in_specs=[scalars(), whole(), anywhere, whole(), anywhere, anywhere, anywhere, anywhere, anywhere, anywhere]
        + [whole()] * 2,
        out_specs=[anywhere] * len(outs),
        scratch_shapes=scratch,
        compiler_params=pltpu.CompilerParams(vmem_limit_bytes=VMEM_BYTES, collective_id=0, has_side_effects=True),
        cost_estimate=cost(2 * total * width * (3 * inner + 512), 60e6),
        name="first",
    )(ends, inputs, cot, ngain, w_x, w_z, w_o, w_bc, w_dt, table, taps_bc, bias_bc)


def back_body(x, w, out):
    out[...] = nt(x[...], w[...]).astype(BF16)


def run_back(x, w):
    count, inner = x.shape
    width = w.shape[0]
    cols = 256
    return pl.pallas_call(
        back_body,
        grid=(width // cols,),
        out_shape=jax.ShapeDtypeStruct((count, width), BF16),
        in_specs=[whole(), pl.BlockSpec((cols, inner), lambda j: (j, 0))],
        out_specs=pl.BlockSpec((count, cols), lambda j: (0, j)),
        compiler_params=params(),
        cost_estimate=cost(2 * count * width * inner, 10e6),
        name="back",
    )(x, w)


def grad_body(rows, sc, x, y, own, oth, scr):
    skip = x.shape[0] - y.shape[0]
    scr[...] = tn(x[skip:, :], y[...]).astype(BF16)
    me = sc[4]
    for v in range(2 * own.shape[0]):
        block = scr[pl.ds(pl.multiple_of((me ^ v) * rows, 16), rows), :]
        if v & 1:
            oth[v >> 1] = block
        else:
            own[v >> 1] = block


def run_grad(sc, x, y, rows):
    width = x.shape[1]
    count, inner = y.shape
    cols = 256 if inner % 256 == 0 else 128
    half = width // rows // 2
    shape = jax.ShapeDtypeStruct((half, rows, inner), BF16)
    spec = pl.BlockSpec((half, rows, cols), lambda j: (0, 0, j))
    return pl.pallas_call(
        partial(grad_body, rows),
        grid=(inner // cols,),
        out_shape=(shape, shape),
        in_specs=[scalars(), whole(), pl.BlockSpec((count, cols), lambda j: (0, j))],
        out_specs=(spec, spec),
        scratch_shapes=[pltpu.VMEM((width, cols), BF16)],
        compiler_params=params(),
        cost_estimate=cost(2 * count * width * inner, 10e6),
        name="grad",
    )(sc, x, y)


def scan_body(sc, xs, bc, dt, lc, lr, em, kd, st, sin, z, dm, skip, gain, y_o, stat_o, cb, off):
    c, b = pl.program_id(0), pl.program_id(1)
    cols = xs.shape[1]

    @pl.when(b == 0)
    def _():
        cb[...] = nt(bc[:, LANES:], bc[:, :LANES])
        start = sc[3] + c * SPAN
        t, s = iota((SPAN, SPAN), 0), iota((SPAN, SPAN), 1)
        seen = (t >= s) & (seg_at(sc, start + t) == seg_at(sc, start + s))
        off[...] = jnp.where(seen, 0.0, FAR)
        stat_o[...] = jnp.zeros_like(stat_o)

    mapping = head_map(cols, 0)
    scaled = (xs[...].astype(F32) * expand(dt[0], mapping)).astype(BF16)
    carry = expand(kd[0, 8:16, :], mapping)
    rows8 = (iota((8, 1), 0) == c).astype(F32)
    state = st[0] + jnp.sum(carry * rows8, axis=0, keepdims=True) * sin[...].astype(F32)
    far = nn(bc[:, LANES:], state.astype(BF16)) * expand(em[0], mapping) + skip[...] * xs[...].astype(F32)
    lane = iota((1, LANES), 1)
    sides = [(lane < 64).astype(BF16), (lane >= 64).astype(BF16)]
    half = SPAN // 2
    square = jnp.zeros((SPAN, 1), F32)
    cross = jnp.zeros((SPAN, 1), F32)
    for k in range(cols // LANES):
        at = slice(k * LANES, (k + 1) * LANES)
        pair = scaled[:, at]
        top = far[:half, at]
        low = far[half:, at]
        for side in range(2):
            h = 2 * k + side
            operand = pair * sides[side]
            column = lc[0, :, h : h + 1]
            row = lr[0, h : h + 1, :]
            w_top = cb[:half, :half] * jnp.exp2(column[:half] - row[:, :half] + off[:half, :half])
            top = top + nn(w_top.astype(BF16), operand[:half, :])
            w_low = cb[half:, :] * jnp.exp2(column[half:] - row + off[half:, :])
            low = low + nn(w_low.astype(BF16), operand)
        out = jnp.concatenate([top, low], axis=0)
        y_o[:, at] = out
        gate = z[:, at]
        gated = out * (gate * sigmoid(gate))
        square = square + jnp.sum(gated * gated, axis=1, keepdims=True)
        cross = cross + jnp.sum(gated * (dm[:, at] * gain[:, at]), axis=1, keepdims=True)
    stat_o[...] += jnp.where(lane == 0, square, 0.0) + jnp.where(lane == 1, cross, 0.0)


def run_scan(sc, xs, bc, dt, lc, lr, em, kd, st, sin, z, dm, skip, gain, ig):
    count, inner = xs.shape
    chunks = count // SPAN
    tile = pl.BlockSpec((SPAN, ig), lambda c, b: (c, b))
    per_block = pl.BlockSpec((1, SPAN, LANES), lambda c, b: (b, c, 0))
    row = pl.BlockSpec((1, ig), lambda c, b: (0, b))
    return pl.pallas_call(
        scan_body,
        grid=(chunks, 2),
        out_shape=(
            jax.ShapeDtypeStruct((count, inner), F32),
            jax.ShapeDtypeStruct((count, LANES), F32),
        ),
        in_specs=[
            scalars(),
            tile,
            pl.BlockSpec((SPAN, 2 * LANES), lambda c, b: (c, 0)),
            per_block,
            per_block,
            pl.BlockSpec((1, 16, SPAN), lambda c, b: (b, 0, c)),
            per_block,
            pl.BlockSpec((1, 24, LANES), lambda c, b: (b, 0, 0)),
            pl.BlockSpec((1, LANES, ig), lambda c, b: (c, 0, b)),
            pl.BlockSpec((LANES, ig), lambda c, b: (0, b)),
            tile,
            tile,
            row,
            row,
        ],
        out_specs=(tile, pl.BlockSpec((SPAN, LANES), lambda c, b: (c, 0))),
        scratch_shapes=[pltpu.VMEM((SPAN, SPAN), F32), pltpu.VMEM((SPAN, SPAN), F32)],
        compiler_params=params(),
        cost_estimate=cost(6e9, 20e6),
        name="scan",
    )(sc, xs, bc, dt, lc, lr, em, kd, st, sin, z, dm, skip, gain)


def gate_body(ig, inner_all, sc, y, z, dm, stat_a, stat_b, xs, gain, bc, em, kd, mixed_o, dz_o, dy_o, sums_o, ds_o, first_o):
    count, cols = y.shape
    at = pl.program_id(0) * cols
    mapping = head_map(cols, lax.rem(at, ig))
    gone = expand(kd[0], mapping)
    grad = jnp.zeros((LANES, cols), F32)
    by_gain = jnp.zeros((1, cols), F32)
    by_skip = jnp.zeros((1, cols), F32)
    for c in range(count // SPAN - 1, -1, -1):
        span = slice(c * SPAN, (c + 1) * SPAN)
        stat = stat_a[span, :] + stat_b[span, :]
        scale = lax.rsqrt(stat[:, 0:1] / inner_all + EPS)
        pull = scale * scale * scale * stat[:, 1:2] / inner_all
        gate = z[span, :]
        sig = sigmoid(gate)
        act = gate * sig
        out = y[span, :]
        gated = out * act
        normal = gated * scale
        mixed_o[span, :] = (normal * gain[...]).astype(BF16)
        upstream = dm[span, :]
        by_gain = by_gain + jnp.sum(upstream * normal, axis=0, keepdims=True)
        dgated = scale * (upstream * gain[...]) - gated * pull
        dz_o[span, :] = (dgated * out * (sig * (1.0 + gate * (1.0 - sig)))).astype(BF16)
        dy = dgated * act
        by_skip = by_skip + jnp.sum(dy * xs[span, :].astype(F32), axis=0, keepdims=True)
        dy_o[span, :] = dy.astype(BF16)
        ds_o[c] = grad
        lead = (dy * expand(em[0, span, :], mapping)).astype(BF16)
        grad = gone[c : c + 1, :] * grad + tn(bc[span, LANES:], lead)
    first_o[...] = grad.astype(BF16)
    sums_o[...] = jnp.concatenate([by_gain, by_skip, jnp.zeros((6, cols), F32)], axis=0)


def run_gate(sc, y, z, dm, stat_a, stat_b, xs, gain, bc, em, kd, ig, inner_all):
    count, inner = y.shape
    cols = col_tile(ig)
    chunks = count // SPAN
    tile = pl.BlockSpec((count, cols), lambda j: (0, j))
    low = jax.ShapeDtypeStruct((count, inner), BF16)
    return pl.pallas_call(
        partial(gate_body, ig, inner_all),
        grid=(inner // cols,),
        out_shape=(
            low,
            low,
            low,
            jax.ShapeDtypeStruct((8, inner), F32),
            jax.ShapeDtypeStruct((chunks, LANES, inner), F32),
            jax.ShapeDtypeStruct((LANES, inner), BF16),
        ),
        in_specs=[
            scalars(),
            tile,
            tile,
            tile,
            whole(),
            whole(),
            tile,
            pl.BlockSpec((1, cols), lambda j: (0, j)),
            whole(),
            pl.BlockSpec((1, count, LANES), lambda j: (j * cols // ig, 0, 0)),
            pl.BlockSpec((1, 24, LANES), lambda j: (j * cols // ig, 0, 0)),
        ],
        out_specs=(
            tile,
            tile,
            tile,
            pl.BlockSpec((8, cols), lambda j: (0, j)),
            pl.BlockSpec((chunks, LANES, cols), lambda j: (0, 0, j)),
            pl.BlockSpec((LANES, cols), lambda j: (0, j)),
        ),
        compiler_params=params(),
        cost_estimate=cost(4e9, 30e6),
        name="gate",
    )(sc, y, z, dm, stat_a, stat_b, xs, gain, bc, em, kd)


def pull_body(
    ha, sc, xs, dy, bc, dtin, dt, lc, lr, em, et, kd, st, sin, ds, dsin, pre, taps, bias, skip, alog,
    dx_o, dbc_o, ddt_o, csum_o, hsum_o, cbt, off, dcb, ahead, dxi, rsum,
):
    b, step = pl.program_id(0), pl.program_id(1)
    chunks = pl.num_programs(1)
    c = chunks - 1 - step
    cols = xs.shape[1]
    half = SPAN // 2
    start = sc[3] + c * SPAN
    b_map, c_map = bc[:, :LANES], bc[:, LANES:]
    cbt[...] = nt(b_map, c_map)
    s, t = iota((SPAN, SPAN), 0), iota((SPAN, SPAN), 1)
    seen = (t >= s) & (seg_at(sc, start + t) == seg_at(sc, start + s))
    off[...] = jnp.where(seen, 0.0, FAR)
    dcb[...] = jnp.zeros_like(dcb)

    @pl.when(step == 0)
    def _():
        ahead[...] = jnp.zeros_like(ahead)
        csum_o[...] = jnp.zeros_like(csum_o)
        hsum_o[...] = jnp.zeros_like(hsum_o)
        rsum[...] = jnp.zeros_like(rsum)

    mapping = head_map(cols, 0)
    single = head_map(cols, 0, both=False)
    lane = iota((1, LANES), 1)
    sides = [(lane < 64).astype(BF16), (lane >= 64).astype(BF16)]
    steps = dt[0]
    steps_wide = expand(steps, mapping)
    xf = xs[...].astype(F32)
    scaled = (xf * steps_wide).astype(BF16)
    dyl = dy[...]
    csums = jnp.zeros((SPAN, LANES), F32)
    for k in range(cols // LANES):
        at = slice(k * LANES, (k + 1) * LANES)
        x_pair, dy_pair = scaled[:, at], dyl[:, at]
        top = jnp.zeros((half, LANES), F32)
        low = jnp.zeros((half, LANES), F32)
        for side in range(2):
            h = 2 * k + side
            x_one = x_pair * sides[side]
            dy_one = dy_pair * sides[side]
            column = lc[0, :, h : h + 1]
            row = lr[0, h : h + 1, :]
            decay = jnp.exp2(row - column[:half] + off[:half, :])
            top = top + nn((cbt[:half, :] * decay).astype(BF16), dy_one)
            share = nt(x_one[:half, :], dy_pair) * decay
            dcb[:half, :] += share
            both = share * cbt[:half, :]
            row_sum = jnp.sum(both, axis=0, keepdims=True)
            col_top = jnp.sum(both, axis=1, keepdims=True)
            decay = jnp.exp2(row[:, half:] - column[half:] + off[half:, half:])
            low = low + nn((cbt[half:, half:] * decay).astype(BF16), dy_one[half:, :])
            share = nt(x_one[half:, :], dy_pair[half:, :]) * decay
            dcb[half:, half:] += share
            both = share * cbt[half:, half:]
            rsum[h : h + 1, :half] = row_sum[:, :half]
            rsum[h : h + 1, half:] = row_sum[:, half:] + jnp.sum(both, axis=0, keepdims=True)
            col_low = jnp.sum(both, axis=1, keepdims=True)
            csums = csums + jnp.where(lane == h, jnp.concatenate([col_top, col_low], axis=0), 0.0)
        dxi[:half, at] = top
        dxi[half:, at] = low
    lead_wide = expand(em[0], mapping)
    tail_wide = expand(et[0], mapping)
    decays = expand(kd[0], mapping)
    pick = (iota((8, 1), 0) == c).astype(F32)
    state = st[0] + jnp.sum(decays[8:16] * pick, axis=0, keepdims=True) * sin[...].astype(F32)
    dstate = ds[0] + jnp.sum(decays[16:24] * pick, axis=0, keepdims=True) * dsin[...].astype(F32)
    state_l, dstate_l = state.astype(BF16), dstate.astype(BF16)
    dyf = dyl.astype(F32)
    led = dyf * lead_wide
    read = nn(c_map, state_l)
    dx_far = nn(b_map, dstate_l) * tail_wide
    db = nn(dcb[...].astype(BF16), c_map) + nt((scaled.astype(F32) * tail_wide).astype(BF16), dstate_l)
    dc = tn(dcb[...].astype(BF16), b_map) + nt(led.astype(BF16), state_l)
    rows_here = pl.ds(pl.multiple_of(c * SPAN, SPAN), SPAN)

    @pl.when(b == 0)
    def _():
        dbc_o[rows_here, :LANES] = db
        dbc_o[rows_here, LANES:] = dc

    @pl.when(b > 0)
    def _():
        dbc_o[rows_here, :LANES] += db
        dbc_o[rows_here, LANES:] += dc

    near = dxi[...]
    from_near = nt((xf * near).astype(BF16), single)
    from_far = nt((xf * dx_far).astype(BF16), single)
    reads = nt((led * read).astype(BF16), single)
    crossing = jnp.sum(state * dstate, axis=0, keepdims=True)
    held = lax.dot_general(
        jnp.broadcast_to(crossing, (8, cols)),
        single.astype(F32),
        (((1,), (1,)), ((), ())),
        precision=HIGH,
        preferred_element_type=F32,
    )[0:1, :]
    held = held * jnp.sum(kd[0, 0:8, :] * pick, axis=0, keepdims=True)
    lower = (s > t).astype(F32)
    upper = (s <= t).astype(F32)
    dlog = (
        jnp.dot(upper, rsum[...].T - csums + reads, precision=HIGH, preferred_element_type=F32)
        + jnp.dot(lower, steps * from_far, precision=HIGH, preferred_element_type=F32)
        + held
    )
    rate = -jnp.exp(alog[0])
    dstep = from_near + from_far + dlog * rate
    ddt = dstep * sigmoid(dtin[0]) * (lane < ha).astype(F32)
    ddt_o[0] = ddt
    hsum_o[0, 0:1, :] += jnp.sum(ddt, axis=0, keepdims=True)
    hsum_o[0, 1:2, :] += jnp.sum(dlog * steps * rate, axis=0, keepdims=True)

    dxs = (near + dx_far) * steps_wide + dyf * skip[...]
    window = pre[pl.ds(pl.multiple_of(c * SPAN, SPAN), SPAN + HALO), :]
    pos = start + iota((SPAN, 1), 0)
    masks = [same_as_behind(sc, pos, j) for j in range(4)]
    lagged = [window[HALO:, :]]
    for j in range(1, 4):
        lagged.append(pltpu.roll(window, j, axis=0)[HALO:, :] * masks[j])
    conv = bias[...]
    for j in range(4):
        conv = conv + taps[j : j + 1, :] * lagged[j]
    sig = sigmoid(conv)
    dconv = dxs * (sig * (1.0 + conv * (1.0 - sig)))
    sums = [jnp.sum(dconv * lagged[j], axis=0, keepdims=True) for j in range(4)]
    sums.append(jnp.sum(dconv, axis=0, keepdims=True))
    csum_o[...] += jnp.concatenate(sums + [jnp.zeros((3, cols), F32)], axis=0)
    dpre = taps[0:1, :] * dconv
    place = iota((SPAN + 8, 1), 0)
    edge = jnp.zeros((HALO, cols), F32)
    blank = jnp.zeros((8, cols), F32)
    for j in range(1, 4):
        masked = dconv * masks[j]
        longer = jnp.concatenate([masked, ahead[8 * (j - 1) : 8 * j, :]], axis=0)
        dpre = dpre + taps[j : j + 1, :] * pltpu.roll(longer, SPAN + 8 - j, axis=0)[:SPAN, :]
        first = masked[:8, :]
        ahead[8 * (j - 1) : 8 * j, :] = first
        before = pltpu.roll(jnp.concatenate([blank, blank, first], axis=0), 24 - j, axis=0)[:HALO, :]
        edge = edge + taps[j : j + 1, :] * before
    dx_o[pl.ds(pl.multiple_of(HALO + c * SPAN, HALO), SPAN), :] = dpre.astype(BF16)

    @pl.when(c == 0)
    def _():
        dx_o[:HALO, :] = edge.astype(BF16)


def run_pull(sc, xs, dy, bc, dtin, dt, lc, lr, em, et, kd, st, sin, ds, dsin, pre, taps, bias, skip, alog, ha, ig):
    count, inner = xs.shape
    total = count + HALO
    chunks = count // SPAN

    def rev(step):
        return chunks - 1 - step

    tile = pl.BlockSpec((SPAN, ig), lambda b, i: (rev(i), b))
    per_block = pl.BlockSpec((1, SPAN, LANES), lambda b, i: (b, rev(i), 0))
    states = pl.BlockSpec((1, LANES, ig), lambda b, i: (rev(i), 0, b))
    edge = pl.BlockSpec((LANES, ig), lambda b, i: (0, b))
    row = pl.BlockSpec((1, ig), lambda b, i: (0, b))
    full = pl.BlockSpec((total, ig), lambda b, i: (0, b))
    return pl.pallas_call(
        partial(pull_body, ha),
        grid=(2, chunks),
        out_shape=(
            jax.ShapeDtypeStruct((total, inner), BF16),
            jax.ShapeDtypeStruct((count, 2 * LANES), F32),
            jax.ShapeDtypeStruct((2, count, LANES), F32),
            jax.ShapeDtypeStruct((8, inner), F32),
            jax.ShapeDtypeStruct((2, 8, LANES), F32),
        ),
        in_specs=[
            scalars(),
            tile,
            tile,
            pl.BlockSpec((SPAN, 2 * LANES), lambda b, i: (rev(i), 0)),
            per_block,
            per_block,
            per_block,
            pl.BlockSpec((1, 16, SPAN), lambda b, i: (b, 0, rev(i))),
            per_block,
            per_block,
            pl.BlockSpec((1, 24, LANES), lambda b, i: (b, 0, 0)),
            states,
            edge,
            states,
            edge,
            full,
            pl.BlockSpec((4, ig), lambda b, i: (0, b)),
            row,
            row,
            pl.BlockSpec((1, 1, LANES), lambda b, i: (b, 0, 0)),
        ],
        out_specs=(
            full,
            pl.BlockSpec((count, 2 * LANES), lambda b, i: (0, 0)),
            per_block,
            pl.BlockSpec((8, ig), lambda b, i: (0, b)),
            pl.BlockSpec((1, 8, LANES), lambda b, i: (b, 0, 0)),
        ),
        scratch_shapes=[
            pltpu.VMEM((SPAN, SPAN), F32),
            pltpu.VMEM((SPAN, SPAN), F32),
            pltpu.VMEM((SPAN, SPAN), F32),
            pltpu.VMEM((24, ig), F32),
            pltpu.VMEM((SPAN, ig), F32),
            pltpu.VMEM((LANES, SPAN), F32),
        ],
        compiler_params=params(),
        cost_estimate=cost(16e9, 30e6),
        name="pull",
    )(sc, xs, dy, bc, dtin, dt, lc, lr, em, et, kd, st, sin, ds, dsin, pre, taps, bias, skip, alog)


def small_body(sc, own, oth, pre, taps, bias, ddt, out, sums_o, scr):
    count = own.shape[0]
    total = count + HALO
    out[:HALO, :] = jnp.zeros((HALO, 4 * LANES), BF16)
    out[HALO:, :LANES] = ddt[0].astype(BF16)
    out[HALO:, LANES : 2 * LANES] = ddt[1].astype(BF16)
    upstream = own[...].astype(F32) + oth[...].astype(F32)
    pos = sc[3] + iota((count, 1), 0)
    masks = [same_as_behind(sc, pos, j) for j in range(4)]
    lagged = [pre[HALO - j : HALO - j + count, :] * masks[j] for j in range(4)]
    lagged[0] = pre[HALO:, :]
    conv = bias[...]
    for j in range(4):
        conv = conv + taps[j : j + 1, :] * lagged[j]
    sig = sigmoid(conv)
    dconv = upstream * (sig * (1.0 + conv * (1.0 - sig)))
    sums = [jnp.sum(dconv * lagged[j], axis=0, keepdims=True) for j in range(4)]
    sums.append(jnp.sum(dconv, axis=0, keepdims=True))
    sums_o[...] = jnp.concatenate(sums + [jnp.zeros((3, 2 * LANES), F32)], axis=0)
    scr[...] = jnp.zeros_like(scr)
    dpre = jnp.zeros((total, 2 * LANES), F32)
    for j in range(4):
        scr[HALO : HALO + count, :] = dconv * masks[j] if j else dconv
        dpre = dpre + taps[j : j + 1, :] * scr[j : j + total, :]
    out[:, 2 * LANES :] = dpre.astype(BF16)


def run_small(sc, own, oth, pre, taps, bias, ddt):
    count = own.shape[0]
    total = count + HALO
    return pl.pallas_call(
        small_body,
        out_shape=(
            jax.ShapeDtypeStruct((total, 4 * LANES), BF16),
            jax.ShapeDtypeStruct((8, 2 * LANES), F32),
        ),
        in_specs=[scalars()] + [whole()] * 6,
        out_specs=[whole()] * 2,
        scratch_shapes=[pltpu.VMEM((total + 8, 2 * LANES), F32)],
        compiler_params=params(),
        cost_estimate=cost(1e8, 4e6),
        name="small",
    )(sc, own, oth, pre, taps, bias, ddt)


def dnorm_body(share, dz, dx, dsmall, tok, w_z, w_x, w_s, out, sums):
    value = (
        nt(dx[...], w_x[...])
        + nt(dsmall[:, : 2 * LANES], w_s[:, : 2 * LANES])
        + nt(dsmall[:, 2 * LANES :], w_s[:, 2 * LANES :]) * share
    )
    from_z = nt(dz[...], w_z[...])
    top = value[:HALO, :]
    rest_v = value[HALO:, :] + from_z
    out[:HALO, :] = top.astype(BF16)
    out[HALO:, :] = rest_v.astype(BF16)
    total = jnp.sum(top * tok[:HALO, :].astype(F32), axis=0, keepdims=True) + jnp.sum(
        rest_v * tok[HALO:, :].astype(F32), axis=0, keepdims=True
    )
    sums[...] = jnp.broadcast_to(total, sums.shape)


def run_dnorm(dz, dx, dsmall, tok, w_z, w_x, w_s, share):
    total, width = tok.shape
    inner = dx.shape[1]
    cols = 256
    return pl.pallas_call(
        partial(dnorm_body, share),
        grid=(width // cols,),
        out_shape=(
            jax.ShapeDtypeStruct((total, width), BF16),
            jax.ShapeDtypeStruct((8, width), F32),
        ),
        in_specs=[
            whole(),
            whole(),
            whole(),
            pl.BlockSpec((total, cols), lambda j: (0, j)),
            pl.BlockSpec((cols, inner), lambda j: (j, 0)),
            pl.BlockSpec((cols, inner), lambda j: (j, 0)),
            pl.BlockSpec((cols, 4 * LANES), lambda j: (j, 0)),
        ],
        out_specs=(
            pl.BlockSpec((total, cols), lambda j: (0, j)),
            pl.BlockSpec((8, cols), lambda j: (0, j)),
        ),
        compiler_params=params(),
        cost_estimate=cost(2 * total * width * (2 * inner + 384), 20e6),
        name="dnorm",
    )(dz, dx, dsmall, tok, w_z, w_x, w_s)


def swap(value, bit, size):
    return lax.ppermute(value, "dp", [(i, i ^ bit) for i in range(size)])


def scatter_rows(own, oth, split, size):
    got = swap(oth, 1, size)
    outs = []
    bits = link_bits(size)
    for low, high, order in ((0, split, bits), (split, own.shape[2], bits[::-1])):
        held = {2 * u: own[u, :, low:high].astype(F32) + got[u, :, low:high].astype(F32) for u in range(own.shape[0])}
        for bit in order:
            away = sorted(v for v in held if v & bit)
            stay = sorted(v for v in held if not v & bit)
            arrived = swap(jnp.stack([held[v].astype(BF16) for v in away]), bit, size)
            held = {v: held[v] + arrived[i].astype(F32) for i, v in enumerate(stay)}
        outs.append(held[0].astype(BF16))
    return outs


def from_heads(block_a, block_b, parts, lower):
    hp = parts // 2
    first = [(p, 2 * p) for p in range(hp)] + [(p, 2 * (p - hp) + 1) for p in range(hp, parts)]
    second = [(p, 2 * p + 1) for p in range(hp)] + [(p, 2 * (p - hp)) for p in range(hp, parts)]
    one = lax.ppermute(jnp.where(lower, block_a, block_b), "tensor", first)
    two = lax.ppermute(jnp.where(lower, block_b, block_a), "tensor", second)
    return one.astype(F32) + two.astype(F32)


def half_other(value, parts):
    hp = parts // 2
    total = jnp.zeros(value.shape, F32)
    for shift in range(1, hp):
        pairs = [(p, (p // hp) * hp + (p % hp + shift) % hp) for p in range(parts)]
        total = total + lax.ppermute(value, "tensor", pairs).astype(F32)
    return total if hp > 2 else lax.ppermute(value, "tensor", [(p, p ^ 1) for p in range(parts)])


def half_scatter(value, parts, place):
    hp = parts // 2
    rows = value.shape[0] // hp
    mine = lax.dynamic_slice_in_dim(value, place * rows, rows, 0)
    total = mine.astype(F32)
    for shift in range(1, hp):
        pairs = [(p, (p // hp) * hp + (p % hp + shift) % hp) for p in range(parts)]
        away = lax.dynamic_slice_in_dim(value, lax.rem(place + shift, hp) * rows, rows, 0)
        total = total + lax.ppermute(away, "tensor", pairs).astype(F32)
    return total


def sum_dp(value, size):
    bit = 1
    while bit < size:
        value = value + swap(value, bit, size)
        bit *= 2
    return value


def sum_tensor(value, parts):
    bit = 1
    while bit < parts:
        value = value + lax.ppermute(value, "tensor", [(p, p ^ bit) for p in range(parts)])
        bit *= 2
    return value


def local(
    inputs,
    cotangent,
    seq_lengths,
    norm_gain,
    w_z,
    w_x,
    w_bc,
    w_dt,
    conv_x,
    conv_x_bias,
    conv_bc,
    conv_bc_bias,
    dt_bias,
    a_log,
    d_skip,
    gate_gain,
    w_out,
):
    local_rows, width = inputs.shape
    parts = lax.axis_size("tensor")
    size = lax.axis_size("dp")
    hp = parts // 2
    position = lax.axis_index("tensor")
    me = lax.axis_index("dp")
    lower = position < hp
    place = lax.rem(position, hp)
    count = local_rows * hp
    ha = dt_bias.shape[0]
    ig = w_z.shape[1]
    inner = 2 * ig
    inner_all = ig * parts
    rows = w_z.shape[0]
    head_width = ig // ha

    ends = [seq_lengths[0, 0], seq_lengths[0, 0] + seq_lengths[0, 1]]
    ends.append(ends[1] + seq_lengths[0, 2])
    base = jnp.where(lower, 0, count)
    sc = jnp.stack([*ends, base, me, position, position, position]).astype(jnp.int32)

    def pad(v, to):
        return jnp.pad(v, [(0, 0)] * (v.ndim - 1) + [(0, to - v.shape[-1])])

    heads_row = jnp.concatenate([pad(dt_bias, LANES), pad(a_log, LANES)])
    table = jnp.concatenate(
        [conv_x, conv_x_bias[None], gate_gain[None], jnp.repeat(d_skip, head_width)[None], pad(heads_row, ig)[None]]
    )
    (
        tok, pulled, wx, wz, wo, ws, par, pre_bc, bc, dtin, dt, lc, lr, em, et, kd, pre_x, xs, st, sin, z, dm,
    ) = run_first(
        sc, inputs, cotangent, norm_gain[None], w_x, w_z, w_out.T, w_bc, pad(w_dt, LANES), table, conv_bc,
        conv_bc_bias[None], size, parts, ha,
    )
    taps_x, bias_x, gain, skip = par[0:4], par[4:5], par[5:6], par[6:7]
    alog_blocks = jnp.stack([par[7, LANES : 2 * LANES], par[7, ig + LANES : ig + 2 * LANES]])[:, None, :]
    input_f = inputs.astype(F32)
    in_scale = lax.rsqrt(jnp.mean(input_f * input_f, axis=1, keepdims=True) + EPS)
    y, stat = run_scan(sc, xs, bc, dt, lc, lr, em, kd, st, sin, z, dm, skip, gain, ig)
    stat_other = half_other(stat, parts)
    mixed, dz, dy, gate_sums, ds, dfirst = run_gate(
        sc, y, z, dm, stat, stat_other, xs, gain, bc, em, kd, ig, inner_all
    )
    dsin = lax.ppermute(dfirst, "tensor", [(p + hp, p) for p in range(hp)])
    branch = run_back(mixed, wo)
    outputs = (input_f + half_scatter(branch, parts, place)).astype(BF16)
    gw_o = run_grad(sc, pulled, mixed, rows)
    gw_z = run_grad(sc, tok, dz, rows)
    dx, dbc, ddt, conv_sums, head_sums = run_pull(
        sc, xs, dy, bc, dtin, dt, lc, lr, em, et, kd, st, sin, ds, dsin, pre_x, taps_x, bias_x, skip,
        alog_blocks, ha, ig,
    )
    dbc_low = dbc.astype(BF16)
    dbc_other = half_other(dbc_low, parts)
    gw_x = run_grad(sc, tok, dx, rows)
    dsmall, bc_sums = run_small(sc, dbc_low, dbc_other, pre_bc, conv_bc, conv_bc_bias[None], ddt)
    dn, norm_sums = run_dnorm(dz, dx, dsmall, tok, wz, wx, ws, 1.0 / hp)
    gw_s = run_grad(sc, tok, dsmall, rows)

    dn_own = half_scatter(dn[HALO:], parts, place)
    edge = jnp.zeros((HALO, width), F32)
    for k in range(hp):
        edge = edge + lax.ppermute(dn[:HALO], "tensor", [(hp + k, hp - 1)]).astype(F32)
    dn_own = dn_own + jnp.concatenate([jnp.zeros((local_rows - HALO, width), F32), edge], axis=0)
    dnorm_side = dn_own * norm_gain[None, :]
    grad_inputs = (
        in_scale * dnorm_side
        - input_f
        * (in_scale * in_scale * in_scale)
        * (jnp.sum(dnorm_side * input_f, axis=1, keepdims=True) / width)
        + cotangent.astype(F32)
    ).astype(BF16)

    grad_w_out = from_heads(*scatter_rows(*gw_o, ig, size), parts, lower).T
    grad_w_z = from_heads(*scatter_rows(*gw_z, ig, size), parts, lower)
    grad_w_x = from_heads(*scatter_rows(*gw_x, ig, size), parts, lower)
    s_dt, s_bc = scatter_rows(*gw_s, 2 * LANES, size)
    grad_w_dt = from_heads(s_dt[:, :ha], s_dt[:, LANES : LANES + ha], parts, lower)
    grad_w_bc = s_bc.astype(F32) + lax.ppermute(
        s_bc, "tensor", [(p, (p + hp) % parts) for p in range(parts)]
    ).astype(F32)

    heads_row = pad(head_sums[:, :2].reshape(2, 2 * LANES), ig).reshape(1, inner)
    chan = jnp.concatenate([conv_sums[:5], gate_sums[:2], heads_row])
    rep = jnp.concatenate([(norm_sums[0] / norm_gain), bc_sums[:5].reshape(-1) / hp])
    chan = sum_dp(chan, size)
    chan = from_heads(chan[:, :ig], chan[:, ig:], parts, lower)
    rep = sum_tensor(sum_dp(rep.reshape(-1, LANES), size), parts).reshape(-1)
    rep_bc = rep[width:].reshape(5, -1)
    return (
        outputs,
        grad_inputs,
        rep[:width],
        grad_w_z,
        grad_w_x,
        grad_w_bc,
        grad_w_dt,
        chan[:4],
        chan[4],
        rep_bc[:4],
        rep_bc[4],
        chan[7, :ha],
        chan[7, LANES : LANES + ha],
        jnp.sum(chan[6].reshape(ha, head_width), axis=1),
        chan[5],
        grad_w_out,
    )


def solution(mesh):
    tokens = P(("dp", "tensor"), None)
    matrix = P("dp", "tensor")
    heads = P("tensor")
    return jax.shard_map(
        local,
        mesh=mesh,
        in_specs=(
            tokens,
            tokens,
            P("dp", None),
            P(),
            matrix,
            matrix,
            P("dp", None),
            matrix,
            P(None, "tensor"),
            heads,
            P(),
            P(),
            heads,
            heads,
            heads,
            heads,
            P("tensor", "dp"),
        ),
        out_specs=(
            tokens,
            tokens,
            P(),
            matrix,
            matrix,
            P("dp", None),
            matrix,
            P(None, "tensor"),
            heads,
            P(),
            P(),
            heads,
            heads,
            heads,
            heads,
            P("tensor", "dp"),
        ),
        check_vma=False,
    )
```

```python
from functools import partial

import jax
import jax.numpy as jnp
from jax import lax
from jax.experimental import pallas as pl
from jax.experimental.pallas import tpu as pltpu
from jax.sharding import PartitionSpec as P

SPAN = 256
HALO = 16
LANES = 128
LOG2E = 1.4426950408889634
EPS = 1e-05
FAR = -1e30
HIGH = lax.Precision.HIGHEST
F32 = jnp.float32
BF16 = jnp.bfloat16
VMEM_BYTES = 60 * 1024 * 1024


def nn(a, b):
    return jnp.dot(a, b, preferred_element_type=F32)


def nt(a, b):
    return lax.dot_general(a, b, (((1,), (1,)), ((), ())), preferred_element_type=F32)


def tn(a, b):
    return lax.dot_general(a, b, (((0,), (0,)), ((), ())), preferred_element_type=F32)


def sigmoid(v):
    return 1.0 / (1.0 + jnp.exp(-v))


def iota(shape, axis):
    return lax.broadcasted_iota(jnp.int32, shape, axis)


def seg_at(sc, pos):
    found = (pos >= sc[0]).astype(jnp.int32)
    for i in range(1, 3):
        found = found + (pos >= sc[i]).astype(jnp.int32)
    return jnp.where(pos < 0, -1, found)


def same_as_behind(sc, pos, offset):
    return (seg_at(sc, pos - offset) == seg_at(sc, pos)).astype(F32)


def head_map(cols, start, dtype=BF16, both=True):
    k = iota((LANES, cols), 0)
    if both:
        k = k & 63
    head = (iota((LANES, cols), 1) + start) >> 6
    return (k == head).astype(dtype)


def expand(values, mapping):
    high = values.astype(BF16).astype(F32)
    low = values - high
    return nn((high + pltpu.roll(low, 64, axis=1)).astype(BF16), mapping)


def whole():
    return pl.BlockSpec(memory_space=pltpu.VMEM)


def scalars():
    return pl.BlockSpec(memory_space=pltpu.SMEM)


def params():
    return pltpu.CompilerParams(vmem_limit_bytes=VMEM_BYTES)


def cost(flops, nbytes):
    return pl.CostEstimate(flops=int(flops), bytes_accessed=int(nbytes), transcendentals=0)


def col_tile(ig):
    return 256 if ig % 256 == 0 else 128


def flip(me, v):
    out = me
    bit = 1
    while bit <= v:
        if v & bit:
            out = out + bit - 2 * bit * lax.rem(me // bit, 2)
        bit *= 2
    return out


def link_bits(size):
    bits = []
    bit = 2
    while bit < size:
        bits.append(bit)
        bit *= 2
    return bits


def remote(src, dst, send, recv, **where):
    return pltpu.make_async_remote_copy(
        src_ref=src, dst_ref=dst, send_sem=send, recv_sem=recv, device_id=where, device_id_type=pl.DeviceIdType.MESH
    )


def greet(size, parts):
    me, p = lax.axis_index("dp"), lax.axis_index("tensor")
    barrier = pltpu.get_barrier_semaphore()
    bits = [1] + link_bits(size)
    for bit in bits:
        pl.semaphore_signal(barrier, inc=1, device_id={"dp": flip(me, bit)}, device_id_type=pl.DeviceIdType.MESH)
    for shift in range(1, parts):
        pl.semaphore_signal(
            barrier, inc=1, device_id={"tensor": lax.rem(p + shift, parts)}, device_id_type=pl.DeviceIdType.MESH
        )
    pl.semaphore_wait(barrier, len(bits) + parts - 1)


class ToHeads:
    def __init__(self, k, src, place_of, parts, send, recv, own):
        self.p = lax.axis_index("tensor")
        self.hp = parts // 2
        self.k, self.src, self.place_of = k, src, place_of
        self.send, self.recv, self.own = send, recv, own

    def copy(self, i, side, to):
        return remote(
            self.src, self.place_of(side), self.send.at[2 * self.k + i], self.recv.at[2 * self.k + side], tensor=to
        )

    def local(self, side):
        return pltpu.make_async_copy(self.src, self.place_of(side), self.own.at[self.k])

    def targets(self):
        return [self.p // 2, self.p // 2 + self.hp]

    def start(self):
        side = lax.rem(self.p, 2)
        for i, to in enumerate(self.targets()):

            @pl.when(to != self.p)
            def _(i=i, to=to):
                self.copy(i, side, to).start()

            @pl.when(to == self.p)
            def _():
                self.local(side).start()

    def wait(self):
        q = lax.rem(self.p, self.hp)
        for side in range(2):
            source = 2 * q + side

            @pl.when(source != self.p)
            def _(side=side):
                self.copy(0, side, self.p // 2).wait_recv()

            @pl.when(source == self.p)
            def _(side=side):
                self.local(side).wait()

    def finish(self):
        side = lax.rem(self.p, 2)
        for i, to in enumerate(self.targets()):

            @pl.when(to != self.p)
            def _(i=i, to=to):
                self.copy(i, side, to).wait_send()


class Gather:
    def __init__(self, k, ref, split, rows, size, send, recv):
        self.me = lax.axis_index("dp")
        self.k, self.ref, self.rows, self.size = k, ref, rows, size
        bits = link_bits(size)
        self.orders = [bits, bits[::-1]]
        self.cols = [slice(0, split), slice(split, ref.shape[1])]
        self.send, self.recv = send, recv
        self.sent = []

    def block(self, half, v):
        start = pl.multiple_of(flip(self.me, v) * self.rows, 16)
        cols = self.cols[half]
        return self.ref.at[pl.ds(start, self.rows), pl.ds(cols.start, cols.stop - cols.start)]

    def copy(self, half, v, bit):
        n = bit.bit_length() - 1
        here = self.block(half, v)
        return remote(
            here,
            here,
            self.send.at[self.k, half, v * self.size.bit_length() + n],
            self.recv.at[self.k, half, v ^ bit],
            dp=flip(self.me, bit),
        )

    def push(self, half, v, bits):
        for bit in bits:
            self.copy(half, v, bit).start()
            self.sent.append((half, v, bit))

    def arrive(self, half, v):
        here = self.block(half, v)
        remote(
            here,
            here,
            self.send.at[self.k, half, 0],
            self.recv.at[self.k, half, v],
            dp=flip(self.me, 1),
        ).wait_recv()

    def start(self):
        for half in range(2):
            self.push(half, 0, self.orders[half])
        for half in range(2):
            self.push(half, 0, [1])

    def stage(self, s):
        for half in range(2):
            order = self.orders[half]
            names = [0]
            for bit in order[:s]:
                names = names + [v ^ bit for v in names]
            for v in sorted(n ^ order[s] for n in names):
                self.arrive(half, v)
                self.push(half, v, order[s + 1 :])
                self.push(half, v, [1])

    def stages(self):
        return len(self.orders[0])

    def cores(self):
        for half in range(2):
            for v in range(1, self.size, 2):
                self.arrive(half, v)

    def finish(self):
        for half, v, bit in self.sent:
            self.copy(half, v, bit).wait_send()


class Scatter:
    def __init__(self, k, source, acc, own, size, core_buf, link_buf, cs, cr, ls, lr):
        self.me = lax.axis_index("dp")
        self.k, self.source, self.acc, self.own, self.size = k, source, acc, own, size
        self.core_buf, self.link_buf = core_buf, link_buf
        self.cs, self.cr, self.ls, self.lr = cs, cr, ls, lr
        bits = link_bits(size)
        self.orders = [bits, bits[::-1]]
        self.sent = []

    def core(self, half, u):
        return remote(
            self.source(half, 2 * u + 1),
            self.core_buf[half].at[u],
            self.cs.at[self.k, half, u],
            self.cr.at[self.k, half, u],
            dp=flip(self.me, 1),
        )

    def start(self, half):
        for u in range(self.size // 2):
            self.core(half, u).start()
            if self.own is not None:
                self.own(half, u).start()

    def add(self, half, u, other):
        ref = self.acc(half, u)
        ref[...] = (ref[...].astype(F32) + other[...].astype(F32)).astype(BF16)

    def fold_core(self, half):
        for u in range(self.size // 2):
            self.core(half, u).wait_recv()
            if self.own is not None:
                self.own(half, u).wait()
            self.add(half, u, self.core_buf[half].at[u])

    def plan(self, half, s):
        order = self.orders[half]
        held, slot = list(range(0, self.size, 2)), 0
        for i, bit in enumerate(order):
            away = [v for v in held if v & bit]
            stay = [v for v in held if not v & bit]
            if i == s:
                return bit, away, stay, slot
            held, slot = stay, slot + len(stay)

    def link(self, half, s, i):
        bit, away, stay, slot = self.plan(half, s)
        n = slot + stay.index(away[i] ^ bit)
        return remote(
            self.acc(half, away[i] >> 1),
            self.link_buf[half].at[n],
            self.ls.at[self.k, half, n],
            self.lr.at[self.k, half, n],
            dp=flip(self.me, bit),
        )

    def send(self, half, s):
        for i in range(len(self.plan(half, s)[1])):
            self.link(half, s, i).start()

    def fold(self, half, s):
        bit, away, stay, slot = self.plan(half, s)
        for i in range(len(away)):
            self.link(half, s, i).wait_recv()
        for i, v in enumerate(stay):
            self.add(half, v >> 1, self.link_buf[half].at[slot + i])

    def stages(self):
        return len(self.orders[0])

    def finish(self):
        for half in range(2):
            for u in range(self.size // 2):
                self.core(half, u).wait_send()
            for s in range(self.stages()):
                for i in range(len(self.plan(half, s)[1])):
                    self.link(half, s, i).wait_send()


class FromHeads:
    def __init__(self, k, block, slots, parts, send, recv, own):
        self.p = lax.axis_index("tensor")
        self.hp = parts // 2
        self.k, self.block, self.slots = k, block, slots
        self.send, self.recv, self.own = send, recv, own
        self.half = self.p // self.hp
        self.q = lax.rem(self.p, self.hp)

    def copy(self, side, slot):
        return remote(
            self.block(side),
            self.slots.at[slot],
            self.send.at[2 * self.k + side],
            self.recv.at[2 * self.k + slot],
            tensor=2 * self.q + side,
        )

    def local(self, side, slot):
        return pltpu.make_async_copy(self.block(side), self.slots.at[slot], self.own.at[self.k])

    def start(self, side):
        to = 2 * self.q + side

        @pl.when(to != self.p)
        def _():
            self.copy(side, self.half).start()

        @pl.when(to == self.p)
        def _():
            self.local(side, self.half).start()

    def wait(self):
        for slot in range(2):
            source = self.p // 2 + slot * self.hp

            @pl.when(source != self.p)
            def _(slot=slot):
                self.copy(0, slot).wait_recv()

            @pl.when(source == self.p)
            def _(slot=slot):
                self.local(0, slot).wait()

    def finish(self):
        for side in range(2):

            @pl.when(2 * self.q + side != self.p)
            def _(side=side):
                self.copy(side, self.half).wait_send()


class Butterfly:
    def __init__(self, k, ref, slots, steps, send, recv):
        self.k, self.ref, self.slots, self.steps = k, ref, slots, steps
        self.send, self.recv = send, recv

    def copy(self, i):
        axis, bit = self.steps[i]
        return remote(
            self.ref,
            self.slots.at[i],
            self.send.at[self.k, i],
            self.recv.at[self.k, i],
            **{axis: flip(lax.axis_index(axis), bit)},
        )

    def push(self, i):
        self.copy(i).start()

    def fold(self, i):
        self.copy(i).wait()
        self.ref[...] += self.slots[i]


def sharded_rows(ref, me, v, rows, cols):
    start = pl.multiple_of(flip(me, v) * rows, 16)
    return ref.at[pl.ds(start, rows), pl.ds(cols[0], cols[1] - cols[0])]


def halves(split, total):
    return [(0, split), (split, total)]


def first_body(
    size, parts, rows, ha, ig,
    ends, inputs, cot, ngain, w_x, w_z, w_o, w_bc, w_dt, table, taps_bc, bias_bc,
    tok_h, pulled_h, wx_h, wz_h, wo_h, ws_h, par_h, pre_h, bc_h, dtin_h, dt_h, lc_h, lr_h, em_h, et_h, kd_h,
    prex_h, xs_h, st_h, sin_h, z_h, dm_h,
    tok, pulled, wx, wz, wo, ws, par, pre, bc, dtin, dt, lc, lr, em, et, kd, st, stage, xs_stage, fin, sin,
    zs, zr, zo, gs, gr, ts, tr, cs, cr, hs, hr, ss, sr, local, outs, tiles,
):
    p = lax.axis_index("tensor")
    me = lax.axis_index("dp")
    hp = parts // 2
    place = lax.rem(p, hp)
    half = p // hp
    inner = 2 * ig
    local_rows, width = inputs.shape
    count = local_rows * hp
    total = count + HALO
    base = half * count
    own_rows = pl.multiple_of(place * local_rows, 16)

    def mates():
        return [(s, half * hp + lax.rem(place + s, hp)) for s in range(1, hp)]

    def my_rows():
        return pl.ds(pl.multiple_of(me * rows, 16), rows)

    def wide(ref, cols):
        return lambda side: ref.at[my_rows(), pl.ds(pl.multiple_of(side * cols, LANES), cols)]

    emitted = []

    def emit(src, dst):
        copy = pltpu.make_async_copy(src, dst, outs.at[len(emitted)])
        copy.start()
        emitted.append(copy)

    greet(size, parts)
    to_table = ToHeads(0, table, lambda side: par.at[:, pl.ds(pl.multiple_of(side * ig, LANES), ig)], parts, zs, zr, zo)
    to_dt = ToHeads(1, w_dt, wide(ws, LANES), parts, zs, zr, zo)
    to_x = ToHeads(2, w_x, wide(wx, ig), parts, zs, zr, zo)
    to_z = ToHeads(3, w_z, wide(wz, ig), parts, zs, zr, zo)
    to_o = ToHeads(4, w_o, wide(wo, ig), parts, zs, zr, zo)
    to_dt.start()
    to_x.start()
    to_table.start()
    bc_copy = pltpu.make_async_copy(w_bc, ws.at[my_rows(), pl.ds(2 * LANES, 2 * LANES)], local.at[0])
    bc_copy.start()
    cot_copy = pltpu.make_async_copy(cot, pulled.at[pl.ds(own_rows, local_rows)], local.at[1])
    cot_copy.start()

    values = inputs[...].astype(F32)
    scale = lax.rsqrt(jnp.mean(values * values, axis=1, keepdims=True) + EPS)
    mine = pl.ds(pl.multiple_of(HALO + own_rows, 16), local_rows)
    tok[mine, :] = (values * scale * ngain[...]).astype(BF16)

    def tok_copy(s, to):
        return remote(tok.at[mine], tok.at[mine], ts.at[s], tr.at[s], tensor=to)

    def tok_arrive(s):
        there = pl.ds(pl.multiple_of(HALO + lax.rem(place + hp - s, hp) * local_rows, 16), local_rows)
        remote(tok.at[there], tok.at[there], ts.at[s], tr.at[s], tensor=p).wait_recv()

    def cot_copy_to(s, to):
        return remote(cot, pulled.at[pl.ds(own_rows, local_rows)], cs.at[s], cr.at[s], tensor=to)

    def cot_arrive(s):
        there = pl.ds(pl.multiple_of(lax.rem(place + hp - s, hp) * local_rows, 16), local_rows)
        remote(pulled.at[there], pulled.at[there], cs.at[s], cr.at[s], tensor=p).wait_recv()

    def halo_copy(k):
        return remote(tok.at[pl.ds(total - HALO, HALO)], tok.at[pl.ds(0, HALO)], hs.at[k], hr.at[0], tensor=hp + k)

    for s, to in mates():
        tok_copy(s, to).start()

    @pl.when(p == hp - 1)
    def _():
        for k in range(hp):
            halo_copy(k).start()

    @pl.when(half == 0)
    def _():
        tok[:HALO, :] = jnp.zeros((HALO, width), BF16)

    to_z.start()
    to_o.start()
    for s, to in mates():
        cot_copy_to(s, to).start()

    g_s = Gather(0, ws, 2 * LANES, rows, size, gs, gr)
    g_x = Gather(1, wx, ig, rows, size, gs, gr)
    g_z = Gather(2, wz, ig, rows, size, gs, gr)
    g_o = Gather(3, wo, ig, rows, size, gs, gr)
    stages = g_x.stages()
    to_dt.wait()
    bc_copy.wait()
    g_s.start()
    to_x.wait()
    g_x.start()
    for s in range(stages):
        g_s.stage(s)
        g_x.stage(s)
        if s == 0:
            to_z.wait()
            g_z.start()
    g_s.cores()
    for s, _ in mates():
        tok_arrive(s)

    @pl.when(half == 1)
    def _():
        halo_copy(0).wait_recv()

    emit(tok, tok_h)
    emit(ws, ws_h)

    pre[...] = nn(tok[...], ws[:, 2 * LANES :])
    emit(pre, pre_h)
    pos = base + iota((count, 1), 0)
    acc = bias_bc[...] + taps_bc[0:1, :] * pre[HALO : HALO + count, :]
    for j in range(1, 4):
        acc = acc + taps_bc[j : j + 1, :] * pre[HALO - j : HALO - j + count, :] * same_as_behind(ends, pos, j)
    bc[...] = (acc * sigmoid(acc)).astype(BF16)
    emit(bc, bc_h)
    to_table.wait()
    emit(par, par_h)
    keep = (iota((1, LANES), 1) < ha).astype(F32)
    tri = (iota((SPAN, SPAN), 0) >= iota((SPAN, SPAN), 1)).astype(F32)
    chunks = count // SPAN
    for b in range(2):
        heads = par[7:8, b * ig : b * ig + 2 * LANES]
        dtraw = nn(tok[HALO:, :], ws[:, b * LANES : (b + 1) * LANES])
        shifted = (dtraw + heads[:, :LANES]) * keep
        steps = (jnp.maximum(shifted, 0.0) + jnp.log1p(jnp.exp(-jnp.abs(shifted)))) * keep
        dtin[b] = shifted
        dt[b] = steps
        scaled = steps * (-jnp.exp(heads[:, LANES:]) * LOG2E)
        gone = []
        for c in range(chunks):
            span = slice(c * SPAN, (c + 1) * SPAN)
            logs = jnp.dot(tri, scaled[span, :], precision=HIGH, preferred_element_type=F32)
            first, last = base + c * SPAN - 1, base + (c + 1) * SPAN - 1
            here = base + c * SPAN + iota((SPAN, 1), 0)
            seg = seg_at(ends, here)
            seg_first, seg_last = seg_at(ends, first), seg_at(ends, last)
            final = logs[SPAN - 1 : SPAN, :]
            gone.append(jnp.where(seg_first == seg_last, 1.0, 0.0).astype(F32) * jnp.exp2(final) * keep)
            lc[b, span, :] = logs
            lr[b, :, span] = logs.T[:16, :]
            em[b, span, :] = (seg == seg_first).astype(F32) * jnp.exp2(logs) * keep
            et[b, span, :] = (seg == seg_last).astype(F32) * jnp.exp2(final - logs) * keep
        ahead_of, behind_of = [keep], [keep]
        for c in range(chunks - 1):
            ahead_of.append(ahead_of[-1] * gone[c])
            behind_of.append(behind_of[-1] * gone[chunks - 1 - c])
        behind_of = behind_of[::-1]
        fill = [jnp.zeros((1, LANES), F32)] * (8 - chunks)
        kd[b] = jnp.concatenate(gone + fill + ahead_of + fill + behind_of + fill, axis=0)
    for src, dst in ((dtin, dtin_h), (dt, dt_h), (lc, lc_h), (lr, lr_h), (em, em_h), (et, et_h), (kd, kd_h)):
        emit(src, dst)

    g_x.cores()
    emit(wx, wx_h)
    to_o.wait()
    g_z.stage(0)
    g_o.start()

    cols = col_tile(ig)

    def tile_out(kind, slot, j):
        at = pl.ds(pl.multiple_of(j * cols, cols), cols)
        if kind == 0:
            return pltpu.make_async_copy(stage.at[slot], prex_h.at[:, at], tiles.at[0, slot])
        if kind == 1:
            return pltpu.make_async_copy(xs_stage.at[slot], xs_h.at[:, at], tiles.at[1, slot])
        rows_of = stage.at[slot, pl.ds(0, count)]
        return pltpu.make_async_copy(rows_of, (z_h if kind == 2 else dm_h).at[:, at], tiles.at[kind, slot])

    def xpath(j, carry):
        slot = lax.rem(j, 2)

        @pl.when(j >= 2)
        def _():
            tile_out(0, slot, j).wait()
            tile_out(1, slot, j).wait()

        at = pl.multiple_of(j * cols, cols)
        lanes = pl.ds(at, cols)
        b = at // ig
        stage[slot] = nn(tok[...], wx[:, lanes])
        mapping = head_map(cols, lax.rem(at, ig))
        state = jnp.zeros((LANES, cols), F32)
        decay = expand(kd[b], mapping)
        taps, bias = par[0:4, lanes], par[4:5, lanes]
        for c in range(chunks):
            low = c * SPAN
            here = base + low + iota((SPAN, 1), 0)
            window = stage[slot, low : low + SPAN + HALO, :]
            conv = bias + taps[0:1, :] * window[HALO:, :]
            for k in range(1, 4):
                lag = pltpu.roll(window, k, axis=0)[HALO:, :]
                conv = conv + taps[k : k + 1, :] * lag * same_as_behind(ends, here, k)
            xs = (conv * sigmoid(conv)).astype(BF16)
            xs_stage[slot, low : low + SPAN, :] = xs
            weight = expand(dt[b, low : low + SPAN, :] * et[b, low : low + SPAN, :], mapping)
            st[c, :, lanes] = state
            fresh = tn(bc[low : low + SPAN, :LANES], (xs.astype(F32) * weight).astype(BF16))
            state = decay[c : c + 1, :] * state + fresh
        fin[:, lanes] = state.astype(BF16)
        tile_out(0, slot, j).start()
        tile_out(1, slot, j).start()
        return carry

    def project(kind, x, skip, w):
        def step(j, carry):
            slot = lax.rem(j, 2)

            @pl.when(j >= 2)
            def _():
                tile_out(kind, slot, j).wait()

            lanes = pl.ds(pl.multiple_of(j * cols, cols), cols)
            stage[slot, :count, :] = nn(x[skip:, :], w[:, lanes])
            tile_out(kind, slot, j).start()
            return carry

        return step

    tiles_all = inner // cols
    middle = tiles_all // 2

    def drain(kind):
        for j in range(tiles_all - 2, tiles_all):
            tile_out(kind, j % 2, j).wait()

    lax.fori_loop(0, middle, xpath, 0)
    for s in range(1, stages):
        g_z.stage(s)
    lax.fori_loop(middle, tiles_all, xpath, 0)
    emit(st, st_h)

    def state_copy():
        return remote(fin, sin, ss.at[0], sr.at[0], tensor=lax.rem(p + hp, parts))

    @pl.when(half == 0)
    def _():
        state_copy().start()

    drain(0)
    drain(1)
    g_z.cores()
    emit(wz, wz_h)
    lax.fori_loop(0, middle, project(2, tok, HALO, wz), 0)
    for s in range(stages):
        g_o.stage(s)
    lax.fori_loop(middle, tiles_all, project(2, tok, HALO, wz), 0)
    drain(2)
    for s, _ in mates():
        cot_arrive(s)
    cot_copy.wait()
    emit(pulled, pulled_h)
    g_o.cores()
    emit(wo, wo_h)
    lax.fori_loop(0, tiles_all, project(3, pulled, 0, wo), 0)

    @pl.when(half == 1)
    def _():
        state_copy().wait_recv()

    @pl.when(half == 0)
    def _():
        sin[...] = jnp.zeros_like(sin)

    emit(sin, sin_h)
    drain(3)
    for item in (to_table, to_dt, to_x, to_z, to_o, g_s, g_x, g_z, g_o):
        item.finish()
    for s, to in mates():
        tok_copy(s, to).wait_send()
        cot_copy_to(s, to).wait_send()

    @pl.when(p == hp - 1)
    def _():
        for k in range(hp):
            halo_copy(k).wait_send()

    @pl.when(half == 0)
    def _():
        state_copy().wait_send()

    for copy in emitted:
        copy.wait()


def run_first(ends, inputs, cot, ngain, w_x, w_z, w_o, w_bc, w_dt, table, taps_bc, bias_bc, size, parts, ha):
    local_rows, width = inputs.shape
    rows, ig = w_x.shape
    inner = 2 * ig
    hp = parts // 2
    count = local_rows * hp
    total = count + HALO
    chunks = count // SPAN
    cols = col_tile(ig)
    shape = jax.ShapeDtypeStruct
    per_block = shape((2, count, LANES), F32)
    outs = (
        shape((total, width), BF16),
        shape((count, width), BF16),
        shape((width, inner), BF16),
        shape((width, inner), BF16),
        shape((width, inner), BF16),
        shape((width, 4 * LANES), BF16),
        shape((8, inner), F32),
        shape((total, 2 * LANES), F32),
        shape((count, 2 * LANES), BF16),
        per_block,
        per_block,
        per_block,
        shape((2, 16, count), F32),
        per_block,
        per_block,
        shape((2, 24, LANES), F32),
        shape((total, inner), F32),
        shape((count, inner), BF16),
        shape((chunks, LANES, inner), F32),
        shape((LANES, inner), BF16),
        shape((count, inner), F32),
        shape((count, inner), F32),
    )
    anywhere = pl.BlockSpec(memory_space=pl.ANY)
    dma = pltpu.SemaphoreType.DMA
    nbits = size.bit_length()
    scratch = [pltpu.VMEM(o.shape, o.dtype) for o in outs[:16]]
    scratch += [
        pltpu.VMEM((chunks, LANES, inner), F32),
        pltpu.VMEM((2, total, cols), F32),
        pltpu.VMEM((2, count, cols), BF16),
        pltpu.VMEM((LANES, inner), BF16),
        pltpu.VMEM((LANES, inner), BF16),
        dma((10,)),
        dma((10,)),
        dma((5,)),
        dma((4, 2, size * nbits)),
        dma((4, 2, size)),
        dma((hp,)),
        dma((hp,)),
        dma((hp,)),
        dma((hp,)),
        dma((hp,)),
        dma((1,)),
        dma((1,)),
        dma((1,)),
        dma((2,)),
        dma((24,)),
        dma((4, 2)),
    ]
    return pl.pallas_call(
        partial(first_body, size, parts, rows, ha, ig),
        out_shape=outs,
        in_specs=[scalars(), whole(), anywhere, whole(), anywhere, anywhere, anywhere, anywhere, anywhere, anywhere]
        + [whole()] * 2,
        out_specs=[anywhere] * len(outs),
        scratch_shapes=scratch,
        compiler_params=pltpu.CompilerParams(vmem_limit_bytes=VMEM_BYTES, collective_id=0, has_side_effects=True),
        cost_estimate=cost(2 * total * width * (3 * inner + 512), 60e6),
        name="first",
    )(ends, inputs, cot, ngain, w_x, w_z, w_o, w_bc, w_dt, table, taps_bc, bias_bc)


def grad_body(x, y, out):
    skip = x.shape[0] - y.shape[0]
    out[...] = tn(x[skip:, :], y[...]).astype(BF16)


def run_grad(x, y):
    width = x.shape[1]
    count, inner = y.shape
    cols = 256 if inner % 256 == 0 else 128
    return pl.pallas_call(
        grad_body,
        grid=(inner // cols,),
        out_shape=jax.ShapeDtypeStruct((width, inner), BF16),
        in_specs=[whole(), pl.BlockSpec((count, cols), lambda j: (0, j))],
        out_specs=pl.BlockSpec((width, cols), lambda j: (0, j)),
        compiler_params=params(),
        cost_estimate=cost(2 * count * width * inner, 10e6),
        name="grad",
    )(x, y)


def scan_body(
    size, parts, sc, xs, bc, dt, lc, lr, em, kd, st, sin, z, dm, skip, gain, y_o, stat_o, cb, off, stat, mine, theirs, ss, sr
):
    c, b = pl.program_id(0), pl.program_id(1)
    cols = xs.shape[1]
    p = lax.axis_index("tensor")
    hp = parts // 2
    count = stat.shape[0]
    base = (p // hp) * count
    rows_here = pl.ds(pl.multiple_of(c * SPAN, SPAN), SPAN)

    @pl.when((c == 0) & (b == 0))
    def _():
        greet(size, parts)

    @pl.when(b == 0)
    def _():
        cb[...] = nt(bc[:, LANES:], bc[:, :LANES])
        start = base + c * SPAN
        t, s = iota((SPAN, SPAN), 0), iota((SPAN, SPAN), 1)
        seen = (t >= s) & (seg_at(sc, start + t) == seg_at(sc, start + s))
        off[...] = jnp.where(seen, 0.0, FAR)
        stat[rows_here, :] = jnp.zeros((SPAN, LANES), F32)

    mapping = head_map(cols, 0)
    scaled = (xs[...].astype(F32) * expand(dt[0], mapping)).astype(BF16)
    carry = expand(kd[0, 8:16, :], mapping)
    rows8 = (iota((8, 1), 0) == c).astype(F32)
    state = st[0] + jnp.sum(carry * rows8, axis=0, keepdims=True) * sin[...].astype(F32)
    far = nn(bc[:, LANES:], state.astype(BF16)) * expand(em[0], mapping) + skip[...] * xs[...].astype(F32)
    lane = iota((1, LANES), 1)
    sides = [(lane < 64).astype(BF16), (lane >= 64).astype(BF16)]
    half = SPAN // 2
    square = jnp.zeros((SPAN, 1), F32)
    cross = jnp.zeros((SPAN, 1), F32)
    for k in range(cols // LANES):
        at = slice(k * LANES, (k + 1) * LANES)
        pair = scaled[:, at]
        top = far[:half, at]
        low = far[half:, at]
        for side in range(2):
            h = 2 * k + side
            operand = pair * sides[side]
            column = lc[0, :, h : h + 1]
            row = lr[0, h : h + 1, :]
            w_top = cb[:half, :half] * jnp.exp2(column[:half] - row[:, :half] + off[:half, :half])
            top = top + nn(w_top.astype(BF16), operand[:half, :])
            w_low = cb[half:, :] * jnp.exp2(column[half:] - row + off[half:, :])
            low = low + nn(w_low.astype(BF16), operand)
        out = jnp.concatenate([top, low], axis=0)
        y_o[:, at] = out
        gate = z[:, at]
        gated = out * (gate * sigmoid(gate))
        square = square + jnp.sum(gated * gated, axis=1, keepdims=True)
        cross = cross + jnp.sum(gated * (dm[:, at] * gain[:, at]), axis=1, keepdims=True)
    stat[rows_here, :] += jnp.where(lane == 0, square, 0.0) + jnp.where(lane == 1, cross, 0.0)

    @pl.when((c == pl.num_programs(0) - 1) & (b == 1))
    def _():
        mine[...] = stat[...].T[:8, :]

        def copy(s):
            to = (p // hp) * hp + lax.rem(lax.rem(p, hp) + s, hp)
            return remote(mine, theirs.at[s - 1], ss.at[s - 1], sr.at[s - 1], tensor=to)

        for s in range(1, hp):
            copy(s).start()
        for s in range(1, hp):
            copy(s).wait()
        total = mine[...]
        for s in range(1, hp):
            total = total + theirs[s - 1]
        stat_o[...] = jnp.concatenate([total, jnp.zeros((LANES - 8, count), F32)], axis=0).T


def run_scan(sc, xs, bc, dt, lc, lr, em, kd, st, sin, z, dm, skip, gain, ig, size, parts):
    count, inner = xs.shape
    chunks = count // SPAN
    tile = pl.BlockSpec((SPAN, ig), lambda c, b: (c, b))
    per_block = pl.BlockSpec((1, SPAN, LANES), lambda c, b: (b, c, 0))
    row = pl.BlockSpec((1, ig), lambda c, b: (0, b))
    return pl.pallas_call(
        partial(scan_body, size, parts),
        grid=(chunks, 2),
        out_shape=(
            jax.ShapeDtypeStruct((count, inner), F32),
            jax.ShapeDtypeStruct((count, LANES), F32),
        ),
        in_specs=[
            scalars(),
            tile,
            pl.BlockSpec((SPAN, 2 * LANES), lambda c, b: (c, 0)),
            per_block,
            per_block,
            pl.BlockSpec((1, 16, SPAN), lambda c, b: (b, 0, c)),
            per_block,
            pl.BlockSpec((1, 24, LANES), lambda c, b: (b, 0, 0)),
            pl.BlockSpec((1, LANES, ig), lambda c, b: (c, 0, b)),
            pl.BlockSpec((LANES, ig), lambda c, b: (0, b)),
            tile,
            tile,
            row,
            row,
        ],
        out_specs=(tile, pl.BlockSpec((count, LANES), lambda c, b: (0, 0))),
        scratch_shapes=[
            pltpu.VMEM((SPAN, SPAN), F32),
            pltpu.VMEM((SPAN, SPAN), F32),
            pltpu.VMEM((count, LANES), F32),
            pltpu.VMEM((8, count), F32),
            pltpu.VMEM((parts // 2 - 1, 8, count), F32),
            pltpu.SemaphoreType.DMA((parts // 2 - 1,)),
            pltpu.SemaphoreType.DMA((parts // 2 - 1,)),
        ],
        compiler_params=pltpu.CompilerParams(vmem_limit_bytes=VMEM_BYTES, collective_id=2, has_side_effects=True),
        cost_estimate=cost(6e9, 20e6),
        name="scan",
    )(sc, xs, bc, dt, lc, lr, em, kd, st, sin, z, dm, skip, gain)


def gate_body(ig, inner_all, sc, y, z, dm, stats, xs, gain, bc, em, kd, mixed_o, dz_o, dy_o, sums_o, ds_o, first_o):
    count, cols = y.shape
    at = pl.program_id(0) * cols
    mapping = head_map(cols, lax.rem(at, ig))
    gone = expand(kd[0], mapping)
    grad = jnp.zeros((LANES, cols), F32)
    by_gain = jnp.zeros((1, cols), F32)
    by_skip = jnp.zeros((1, cols), F32)
    for c in range(count // SPAN - 1, -1, -1):
        span = slice(c * SPAN, (c + 1) * SPAN)
        stat = stats[span, :]
        scale = lax.rsqrt(stat[:, 0:1] / inner_all + EPS)
        pull = scale * scale * scale * stat[:, 1:2] / inner_all
        gate = z[span, :]
        sig = sigmoid(gate)
        act = gate * sig
        out = y[span, :]
        gated = out * act
        normal = gated * scale
        mixed_o[span, :] = (normal * gain[...]).astype(BF16)
        upstream = dm[span, :]
        by_gain = by_gain + jnp.sum(upstream * normal, axis=0, keepdims=True)
        dgated = scale * (upstream * gain[...]) - gated * pull
        dz_o[span, :] = (dgated * out * (sig * (1.0 + gate * (1.0 - sig)))).astype(BF16)
        dy = dgated * act
        by_skip = by_skip + jnp.sum(dy * xs[span, :].astype(F32), axis=0, keepdims=True)
        dy_o[span, :] = dy.astype(BF16)
        ds_o[c] = grad
        lead = (dy * expand(em[0, span, :], mapping)).astype(BF16)
        grad = gone[c : c + 1, :] * grad + tn(bc[span, LANES:], lead)
    first_o[...] = grad.astype(BF16)
    sums_o[...] = jnp.concatenate([by_gain, by_skip, jnp.zeros((6, cols), F32)], axis=0)


def run_gate(sc, y, z, dm, stat, xs, gain, bc, em, kd, ig, inner_all):
    count, inner = y.shape
    cols = col_tile(ig)
    chunks = count // SPAN
    tile = pl.BlockSpec((count, cols), lambda j: (0, j))
    low = jax.ShapeDtypeStruct((count, inner), BF16)
    return pl.pallas_call(
        partial(gate_body, ig, inner_all),
        grid=(inner // cols,),
        out_shape=(
            low,
            low,
            low,
            jax.ShapeDtypeStruct((8, inner), F32),
            jax.ShapeDtypeStruct((chunks, LANES, inner), F32),
            jax.ShapeDtypeStruct((LANES, inner), BF16),
        ),
        in_specs=[
            scalars(),
            tile,
            tile,
            tile,
            whole(),
            tile,
            pl.BlockSpec((1, cols), lambda j: (0, j)),
            whole(),
            pl.BlockSpec((1, count, LANES), lambda j: (j * cols // ig, 0, 0)),
            pl.BlockSpec((1, 24, LANES), lambda j: (j * cols // ig, 0, 0)),
        ],
        out_specs=(
            tile,
            tile,
            tile,
            pl.BlockSpec((8, cols), lambda j: (0, j)),
            pl.BlockSpec((chunks, LANES, cols), lambda j: (0, 0, j)),
            pl.BlockSpec((LANES, cols), lambda j: (0, j)),
        ),
        compiler_params=params(),
        cost_estimate=cost(4e9, 30e6),
        name="gate",
    )(sc, y, z, dm, stat, xs, gain, bc, em, kd)


def pull_body(
    size, parts, ha, wrows,
    sc, xs, dy, bc, dtin, dt, lc, lr, em, et, kd, st, sin, ds, pre, taps, bias, skip, alog,
    first, inputs, mixed_h, wo_h, gz_h, go_h,
    dx_o, dbc_o, ddt_o, csum_o, hsum_o, out_o, gz_o, go_o,
    cbt, off, dcb, ahead, dxi, rsum, dsin, mixed, wo, branch, arrived,
    zacc, oacc, zcore, ocore, zlink, olink, zz, oz,
    loads, zls, ols, ccs, ccr, cls, clr, hs, hr, ho, ds_s, ds_r, bs, br,
):
    b, step = pl.program_id(0), pl.program_id(1)
    chunks = pl.num_programs(1)
    c = chunks - 1 - step
    cols = xs.shape[1]
    half = SPAN // 2
    p = lax.axis_index("tensor")
    me = lax.axis_index("dp")
    hp = parts // 2
    place = lax.rem(p, hp)
    part = p // hp
    count = dbc_o.shape[0]
    local_rows = inputs.shape[0]
    start = part * count + c * SPAN
    n = b * chunks + step

    def scatter(k, src, acc, core_buf, link_buf, own_sem):
        columns = halves(cols, 2 * cols)
        return Scatter(
            k,
            lambda h, v: sharded_rows(src, me, v, wrows, columns[h]),
            lambda h, u: acc.at[u, :, pl.ds(columns[h][0], cols)],
            lambda h, u: pltpu.make_async_copy(
                sharded_rows(src, me, 2 * u, wrows, columns[h]),
                acc.at[u, :, pl.ds(columns[h][0], cols)],
                own_sem.at[h, u],
            ),
            size, core_buf, link_buf, ccs, ccr, cls, clr,
        )

    scat_o = scatter(0, go_h, oacc, ocore, olink, ols)
    scat_z = scatter(1, gz_h, zacc, zcore, zlink, zls)
    home_o = FromHeads(0, lambda side: oacc.at[0, :, pl.ds(side * cols, cols)], oz, parts, hs, hr, ho)
    home_z = FromHeads(1, lambda side: zacc.at[0, :, pl.ds(side * cols, cols)], zz, parts, hs, hr, ho)
    stages = scat_o.stages()

    def mates():
        return [(s, part * hp + lax.rem(place + s, hp)) for s in range(1, hp)]

    def grad_state():
        return remote(first, dsin, ds_s.at[0], ds_r.at[0], tensor=lax.rem(p + hp, parts))

    def branch_copy(s, to):
        rows_to = pl.ds(pl.multiple_of(lax.rem(place + s, hp) * local_rows, 16), local_rows)
        return remote(branch.at[rows_to], arrived.at[s - 1], bs.at[s - 1], br.at[s - 1], tensor=to)

    @pl.when(n == 0)
    def _():
        greet(size, parts)
        load_mixed = pltpu.make_async_copy(mixed_h, mixed, loads.at[0])
        load_wo = pltpu.make_async_copy(wo_h, wo, loads.at[1])
        load_mixed.start()
        load_wo.start()

        @pl.when(part == 1)
        def _():
            grad_state().start()

        for h in range(2):
            scat_o.start(h)
        for h in range(2):
            scat_z.start(h)
        load_mixed.wait()
        load_wo.wait()

        def out_tile(j, carry):
            at = pl.ds(pl.multiple_of(j * SPAN, SPAN), SPAN)
            branch[:, at] = nt(mixed[...], wo[at, :]).astype(BF16)
            return carry

        lax.fori_loop(0, wo.shape[0] // SPAN, out_tile, 0)
        for s, to in mates():
            branch_copy(s, to).start()
        for h in range(2):
            scat_o.fold_core(h)
            scat_o.send(h, 0)

        @pl.when(part == 0)
        def _():
            grad_state().wait_recv()

        @pl.when(part == 1)
        def _():
            dsin[...] = jnp.zeros_like(dsin)

    @pl.when(n == 1)
    def _():
        for h in range(2):
            scat_z.fold_core(h)
            scat_z.send(h, 0)

    @pl.when(n == 3)
    def _():
        for s in range(stages - 1):
            for h in range(2):
                scat_o.fold(h, s)
                scat_o.send(h, s + 1)

    @pl.when(n == 4)
    def _():
        for s in range(stages - 1):
            for h in range(2):
                scat_z.fold(h, s)
                scat_z.send(h, s + 1)

    @pl.when(n == 5)
    def _():
        for h in range(2):
            scat_o.fold(h, stages - 1)
            home_o.start(h)

    b_map, c_map = bc[:, :LANES], bc[:, LANES:]
    cbt[...] = nt(b_map, c_map)
    s, t = iota((SPAN, SPAN), 0), iota((SPAN, SPAN), 1)
    seen = (t >= s) & (seg_at(sc, start + t) == seg_at(sc, start + s))
    off[...] = jnp.where(seen, 0.0, FAR)
    dcb[...] = jnp.zeros_like(dcb)

    @pl.when(step == 0)
    def _():
        ahead[...] = jnp.zeros_like(ahead)
        csum_o[...] = jnp.zeros_like(csum_o)
        hsum_o[...] = jnp.zeros_like(hsum_o)
        rsum[...] = jnp.zeros_like(rsum)

    mapping = head_map(cols, 0)
    single = head_map(cols, 0, both=False)
    lane = iota((1, LANES), 1)
    sides = [(lane < 64).astype(BF16), (lane >= 64).astype(BF16)]
    steps = dt[0]
    steps_wide = expand(steps, mapping)
    xf = xs[...].astype(F32)
    scaled = (xf * steps_wide).astype(BF16)
    dyl = dy[...]
    csums = jnp.zeros((SPAN, LANES), F32)
    for k in range(cols // LANES):
        at = slice(k * LANES, (k + 1) * LANES)
        x_pair, dy_pair = scaled[:, at], dyl[:, at]
        top = jnp.zeros((half, LANES), F32)
        low = jnp.zeros((half, LANES), F32)
        for side in range(2):
            h = 2 * k + side
            x_one = x_pair * sides[side]
            dy_one = dy_pair * sides[side]
            column = lc[0, :, h : h + 1]
            row = lr[0, h : h + 1, :]
            decay = jnp.exp2(row - column[:half] + off[:half, :])
            top = top + nn((cbt[:half, :] * decay).astype(BF16), dy_one)
            share = nt(x_one[:half, :], dy_pair) * decay
            dcb[:half, :] += share
            both = share * cbt[:half, :]
            row_sum = jnp.sum(both, axis=0, keepdims=True)
            col_top = jnp.sum(both, axis=1, keepdims=True)
            decay = jnp.exp2(row[:, half:] - column[half:] + off[half:, half:])
            low = low + nn((cbt[half:, half:] * decay).astype(BF16), dy_one[half:, :])
            share = nt(x_one[half:, :], dy_pair[half:, :]) * decay
            dcb[half:, half:] += share
            both = share * cbt[half:, half:]
            rsum[h : h + 1, :half] = row_sum[:, :half]
            rsum[h : h + 1, half:] = row_sum[:, half:] + jnp.sum(both, axis=0, keepdims=True)
            col_low = jnp.sum(both, axis=1, keepdims=True)
            csums = csums + jnp.where(lane == h, jnp.concatenate([col_top, col_low], axis=0), 0.0)
        dxi[:half, at] = top
        dxi[half:, at] = low
    lead_wide = expand(em[0], mapping)
    tail_wide = expand(et[0], mapping)
    decays = expand(kd[0], mapping)
    pick = (iota((8, 1), 0) == c).astype(F32)
    state = st[0] + jnp.sum(decays[8:16] * pick, axis=0, keepdims=True) * sin[...].astype(F32)
    dstate = ds[0] + jnp.sum(decays[16:24] * pick, axis=0, keepdims=True) * dsin[:, pl.ds(pl.multiple_of(b * cols, cols), cols)].astype(F32)
    state_l, dstate_l = state.astype(BF16), dstate.astype(BF16)
    dyf = dyl.astype(F32)
    led = dyf * lead_wide
    read = nn(c_map, state_l)
    dx_far = nn(b_map, dstate_l) * tail_wide
    db = nn(dcb[...].astype(BF16), c_map) + nt((scaled.astype(F32) * tail_wide).astype(BF16), dstate_l)
    dc = tn(dcb[...].astype(BF16), b_map) + nt(led.astype(BF16), state_l)
    rows_here = pl.ds(pl.multiple_of(c * SPAN, SPAN), SPAN)

    @pl.when(b == 0)
    def _():
        dbc_o[rows_here, :LANES] = db
        dbc_o[rows_here, LANES:] = dc

    @pl.when(b > 0)
    def _():
        dbc_o[rows_here, :LANES] += db
        dbc_o[rows_here, LANES:] += dc

    near = dxi[...]
    from_near = nt((xf * near).astype(BF16), single)
    from_far = nt((xf * dx_far).astype(BF16), single)
    reads = nt((led * read).astype(BF16), single)
    crossing = jnp.sum(state * dstate, axis=0, keepdims=True)
    held = lax.dot_general(
        jnp.broadcast_to(crossing, (8, cols)),
        single.astype(F32),
        (((1,), (1,)), ((), ())),
        precision=HIGH,
        preferred_element_type=F32,
    )[0:1, :]
    held = held * jnp.sum(kd[0, 0:8, :] * pick, axis=0, keepdims=True)
    lower = (s > t).astype(F32)
    upper = (s <= t).astype(F32)
    dlog = (
        jnp.dot(upper, rsum[...].T - csums + reads, precision=HIGH, preferred_element_type=F32)
        + jnp.dot(lower, steps * from_far, precision=HIGH, preferred_element_type=F32)
        + held
    )
    rate = -jnp.exp(alog[0])
    dstep = from_near + from_far + dlog * rate
    ddt = dstep * sigmoid(dtin[0]) * (lane < ha).astype(F32)
    ddt_o[0] = ddt
    hsum_o[0, 0:1, :] += jnp.sum(ddt, axis=0, keepdims=True)
    hsum_o[0, 1:2, :] += jnp.sum(dlog * steps * rate, axis=0, keepdims=True)

    dxs = (near + dx_far) * steps_wide + dyf * skip[...]
    window = pre[pl.ds(pl.multiple_of(c * SPAN, SPAN), SPAN + HALO), :]
    pos = start + iota((SPAN, 1), 0)
    masks = [same_as_behind(sc, pos, j) for j in range(4)]
    lagged = [window[HALO:, :]]
    for j in range(1, 4):
        lagged.append(pltpu.roll(window, j, axis=0)[HALO:, :] * masks[j])
    conv = bias[...]
    for j in range(4):
        conv = conv + taps[j : j + 1, :] * lagged[j]
    sig = sigmoid(conv)
    dconv = dxs * (sig * (1.0 + conv * (1.0 - sig)))
    sums = [jnp.sum(dconv * lagged[j], axis=0, keepdims=True) for j in range(4)]
    sums.append(jnp.sum(dconv, axis=0, keepdims=True))
    csum_o[...] += jnp.concatenate(sums + [jnp.zeros((3, cols), F32)], axis=0)
    dpre = taps[0:1, :] * dconv
    edge = jnp.zeros((HALO, cols), F32)
    blank = jnp.zeros((8, cols), F32)
    for j in range(1, 4):
        masked = dconv * masks[j]
        longer = jnp.concatenate([masked, ahead[8 * (j - 1) : 8 * j, :]], axis=0)
        dpre = dpre + taps[j : j + 1, :] * pltpu.roll(longer, SPAN + 8 - j, axis=0)[:SPAN, :]
        opening = masked[:8, :]
        ahead[8 * (j - 1) : 8 * j, :] = opening
        before = pltpu.roll(jnp.concatenate([blank, blank, opening], axis=0), 24 - j, axis=0)[:HALO, :]
        edge = edge + taps[j : j + 1, :] * before
    dx_o[pl.ds(pl.multiple_of(HALO + c * SPAN, HALO), SPAN), :] = dpre.astype(BF16)

    @pl.when(c == 0)
    def _():
        dx_o[:HALO, :] = edge.astype(BF16)

    @pl.when(n == 2 * chunks - 1)
    def _():
        for h in range(2):
            scat_z.fold(h, stages - 1)
            home_z.start(h)
        for s, to in mates():
            branch_copy(s, to).wait_recv()
        own_rows = pl.ds(pl.multiple_of(place * local_rows, 16), local_rows)
        total = inputs[...].astype(F32) + branch[own_rows, :].astype(F32)
        for s in range(1, hp):
            total = total + arrived[s - 1].astype(F32)
        out_o[...] = total.astype(BF16)
        home_o.wait()
        go_o[...] = oz[0].astype(F32) + oz[1].astype(F32)
        home_z.wait()
        gz_o[...] = zz[0].astype(F32) + zz[1].astype(F32)
        for item in (scat_o, scat_z, home_o, home_z):
            item.finish()
        for s, to in mates():
            branch_copy(s, to).wait_send()

        @pl.when(part == 1)
        def _():
            grad_state().wait_send()


def run_pull(
    sc, xs, dy, bc, dtin, dt, lc, lr, em, et, kd, st, sin, ds, pre, taps, bias, skip, alog,
    first, inputs, mixed, wo, gz, go, ha, ig, size, parts,
):
    count, inner = xs.shape
    local_rows, width = inputs.shape
    total = count + HALO
    chunks = count // SPAN
    wrows = width // size
    hp = parts // 2

    def rev(step):
        return chunks - 1 - step

    tile = pl.BlockSpec((SPAN, ig), lambda b, i: (rev(i), b))
    per_block = pl.BlockSpec((1, SPAN, LANES), lambda b, i: (b, rev(i), 0))
    states = pl.BlockSpec((1, LANES, ig), lambda b, i: (rev(i), 0, b))
    edge = pl.BlockSpec((LANES, ig), lambda b, i: (0, b))
    row = pl.BlockSpec((1, ig), lambda b, i: (0, b))
    full = pl.BlockSpec((total, ig), lambda b, i: (0, b))
    anywhere = pl.BlockSpec(memory_space=pl.ANY)
    shape = jax.ShapeDtypeStruct
    vm = pltpu.VMEM
    dma = pltpu.SemaphoreType.DMA
    blocks, links = size // 2, max(size // 2 - 1, 1)
    scratch = dict(
        cbt=vm((SPAN, SPAN), F32),
        off=vm((SPAN, SPAN), F32),
        dcb=vm((SPAN, SPAN), F32),
        ahead=vm((24, ig), F32),
        dxi=vm((SPAN, ig), F32),
        rsum=vm((LANES, SPAN), F32),
        dsin=vm((LANES, inner), BF16),
        mixed=vm((count, inner), BF16),
        wo=vm((width, inner), BF16),
        branch=vm((count, width), BF16),
        arrived=vm((hp - 1, local_rows, width), BF16),
        zacc=vm((blocks, wrows, inner), BF16),
        oacc=vm((blocks, wrows, inner), BF16),
        zcore=[vm((blocks, wrows, ig), BF16)] * 2,
        ocore=[vm((blocks, wrows, ig), BF16)] * 2,
        zlink=[vm((links, wrows, ig), BF16)] * 2,
        olink=[vm((links, wrows, ig), BF16)] * 2,
        zz=vm((2, wrows, ig), BF16),
        oz=vm((2, wrows, ig), BF16),
        loads=dma((2,)),
        zls=dma((2, blocks)),
        ols=dma((2, blocks)),
        ccs=dma((2, 2, blocks)),
        ccr=dma((2, 2, blocks)),
        cls=dma((2, 2, links)),
        clr=dma((2, 2, links)),
        hs=dma((4,)),
        hr=dma((4,)),
        ho=dma((2,)),
        ds_s=dma((1,)),
        ds_r=dma((1,)),
        bs=dma((hp - 1,)),
        br=dma((hp - 1,)),
    )
    return pl.pallas_call(
        partial(pull_body, size, parts, ha, wrows),
        grid=(2, chunks),
        out_shape=(
            shape((total, inner), BF16),
            shape((count, 2 * LANES), F32),
            shape((2, count, LANES), F32),
            shape((8, inner), F32),
            shape((2, 8, LANES), F32),
            shape((local_rows, width), BF16),
            shape((wrows, ig), F32),
            shape((wrows, ig), F32),
        ),
        in_specs=[
            scalars(),
            tile,
            tile,
            pl.BlockSpec((SPAN, 2 * LANES), lambda b, i: (rev(i), 0)),
            per_block,
            per_block,
            per_block,
            pl.BlockSpec((1, 16, SPAN), lambda b, i: (b, 0, rev(i))),
            per_block,
            per_block,
            pl.BlockSpec((1, 24, LANES), lambda b, i: (b, 0, 0)),
            states,
            edge,
            states,
            full,
            pl.BlockSpec((4, ig), lambda b, i: (0, b)),
            row,
            row,
            pl.BlockSpec((1, 1, LANES), lambda b, i: (b, 0, 0)),
            anywhere,
            whole(),
            anywhere,
            anywhere,
            anywhere,
            anywhere,
        ],
        out_specs=(
            full,
            pl.BlockSpec((count, 2 * LANES), lambda b, i: (0, 0)),
            per_block,
            pl.BlockSpec((8, ig), lambda b, i: (0, b)),
            pl.BlockSpec((1, 8, LANES), lambda b, i: (b, 0, 0)),
            whole(),
            whole(),
            whole(),
        ),
        scratch_shapes=list(scratch.values()),
        compiler_params=pltpu.CompilerParams(vmem_limit_bytes=VMEM_BYTES, collective_id=3, has_side_effects=True),
        cost_estimate=cost(20e9, 30e6),
        name="pull",
    )(
        sc, xs, dy, bc, dtin, dt, lc, lr, em, et, kd, st, sin, ds, pre, taps, bias, skip, alog,
        first, inputs, mixed, wo, gz, go,
    )


def last_body(
    size, parts, rows, ha, ig,
    ends, inputs, cot, ngain, tok_h, dz_h, dx_h, wz_h, wx_h, ws_h, dbc, ddt, pre, taps, bias, csum, gsum, hsum,
    gin_o, gx_o, gdt_o, gbc_o, chan_o, rep_o,
    tok, dz, dx, wz, wx, ws, gx, gsm, dsm, conv, dlow, dother, dn_out, dn_in, dn_own, edge_out, edge_in,
    xcore, xlink, score, slink, xz, dtz, bcz, chan, chan_in, chan_z, rep, rep_in,
    loads, ccs, ccr, cls, clr, zs, zr, zo, bs, br, ds, dr, ns, nr, es, er, ts, tr,
):
    p = lax.axis_index("tensor")
    me = lax.axis_index("dp")
    hp = parts // 2
    place = lax.rem(p, hp)
    half = p // hp
    inner = 2 * ig
    local_rows, width = inputs.shape
    count = local_rows * hp
    total = count + HALO
    base = half * count
    own_at = pl.multiple_of(HALO + place * local_rows, 16)

    greet(size, parts)
    moving = [
        pltpu.make_async_copy(src, dst, loads.at[i])
        for i, (src, dst) in enumerate(((tok_h, tok), (dx_h, dx), (wx_h, wx), (dz_h, dz), (wz_h, wz), (ws_h, ws)))
    ]
    for copy in moving:
        copy.start()

    def mates():
        return [(s, half * hp + lax.rem(place + s, hp)) for s in range(1, hp)]

    dlow[...] = dbc[...].astype(BF16)

    def maps_copy(s, to):
        return remote(dlow, dother.at[s - 1], ds.at[s], dr.at[s], tensor=to)

    for s, to in mates():
        maps_copy(s, to).start()

    dp_steps = [("dp", 1)] + [("dp", bit) for bit in link_bits(size)]
    z_steps = []
    bit = 1
    while bit < parts:
        z_steps.append(("tensor", bit))
        bit *= 2
    chan[0:5, :] = csum[0:5, :]
    chan[5:7, :] = gsum[0:2, :]
    chan[7:8, :] = jnp.zeros((1, inner), F32)
    for b in range(2):
        for i in range(2):
            at = b * ig + i * LANES
            chan[7:8, at : at + LANES] = hsum[b, i : i + 1, :]
    sum_chan = Butterfly(0, chan, chan_in, dp_steps, bs, br)
    sum_rep = Butterfly(1, rep, rep_in, dp_steps + z_steps, bs, br)
    sum_chan.push(0)

    def x_block(h, v):
        return sharded_rows(gx, me, v, rows, halves(ig, inner)[h])

    def s_block(h, v):
        return sharded_rows(gsm, me, v, rows, halves(2 * LANES, 4 * LANES)[h])

    scat_x = Scatter(0, x_block, lambda h, u: x_block(h, 2 * u), None, size, xcore, xlink, ccs, ccr, cls, clr)
    scat_s = Scatter(1, s_block, lambda h, u: s_block(h, 2 * u), None, size, score, slink, ccs, ccr, cls, clr)
    stages = scat_x.stages()
    home_x = FromHeads(0, lambda side: x_block(side, 0), xz, parts, zs, zr, zo)
    home_dt = FromHeads(
        1,
        lambda side: sharded_rows(gsm, me, 0, rows, (side * LANES, (side + 1) * LANES)),
        dtz, parts, zs, zr, zo,
    )
    home_chan = FromHeads(2, lambda side: chan.at[:, pl.ds(side * ig, ig)], chan_z, parts, zs, zr, zo)

    cols = col_tile(ig)
    moving[0].wait()
    moving[1].wait()

    def grad_x(j, carry):
        lanes = pl.ds(pl.multiple_of(j * cols, cols), cols)
        gx[:, lanes] = tn(tok[...], dx[:, lanes]).astype(BF16)
        return carry

    per_half = ig // cols
    lax.fori_loop(0, per_half, grad_x, 0)
    scat_x.start(0)
    sum_chan.fold(0)
    if len(dp_steps) > 1:
        sum_chan.push(1)
    lax.fori_loop(per_half, 2 * per_half, grad_x, 0)
    scat_x.start(1)

    for s, to in mates():
        maps_copy(s, to).wait_recv()
    upstream = dlow[...].astype(F32)
    for s in range(1, hp):
        upstream = upstream + dother[s - 1].astype(F32)
    pos = base + iota((count, 1), 0)
    masks = [same_as_behind(ends, pos, j) for j in range(4)]
    lagged = [pre[HALO - j : HALO - j + count, :] * masks[j] for j in range(1, 4)]
    lagged = [pre[HALO:, :]] + lagged
    through = bias[...]
    for j in range(4):
        through = through + taps[j : j + 1, :] * lagged[j]
    sig = sigmoid(through)
    dconv = upstream * (sig * (1.0 + through * (1.0 - sig)))
    rep[...] = jnp.zeros_like(rep)
    for j in range(5):
        value = dconv * lagged[j] if j < 4 else dconv
        rep[1:2, j * 2 * LANES : (j + 1) * 2 * LANES] = jnp.sum(value, axis=0, keepdims=True) / hp
    conv[...] = jnp.zeros_like(conv)
    dpre = jnp.zeros((total, 2 * LANES), F32)
    for j in range(4):
        conv[HALO : HALO + count, :] = dconv * masks[j] if j else dconv
        dpre = dpre + taps[j : j + 1, :] * conv[j : j + total, :]
    dsm[:, 2 * LANES :] = dpre.astype(BF16)
    dsm[:HALO, : 2 * LANES] = jnp.zeros((HALO, 2 * LANES), BF16)
    for b in range(2):
        dsm[HALO:, b * LANES : (b + 1) * LANES] = ddt[b].astype(BF16)

    scat_x.fold_core(0)
    scat_x.send(0, 0)
    scat_x.fold_core(1)
    scat_x.send(1, 0)
    for i in range(1, len(dp_steps)):
        sum_chan.fold(i)
        if i + 1 < len(dp_steps):
            sum_chan.push(i + 1)
    home_chan.start(0)
    home_chan.start(1)
    gsm[...] = tn(tok[...], dsm[...]).astype(BF16)
    scat_s.start(0)
    scat_s.start(1)
    for copy in moving[2:]:
        copy.wait()

    tile = 256

    def dn_tile(start, n, at, with_z):
        span = pl.ds(start, n)
        value = (
            nt(dx[span, :], wx[at, :])
            + nt(dsm[span, : 2 * LANES], ws[at, : 2 * LANES])
            + nt(dsm[span, 2 * LANES :], ws[at, 2 * LANES :]) * (1.0 / hp)
        )
        if with_z:
            value = value + nt(dz[pl.ds(start - HALO, n), :], wz[at, :])
        rep[0:1, at] += jnp.sum(value * tok[span, at].astype(F32), axis=0, keepdims=True)
        return value

    def dn_copy(s, to):
        return remote(dn_out.at[s - 1], dn_in.at[s - 1], ns.at[s], nr.at[s], tensor=to)

    def edge_copy(k):
        return remote(edge_out, edge_in.at[k], es.at[0], er.at[k], tensor=hp - 1)

    for s, to in mates():
        there = pl.multiple_of(HALO + lax.rem(place + s, hp) * local_rows, 16)

        def other_rows(j, carry, s=s, there=there):
            at = pl.ds(pl.multiple_of(j * tile, tile), tile)
            dn_out[s - 1, :, at] = dn_tile(there, local_rows, at, True).astype(BF16)
            return carry

        lax.fori_loop(0, width // tile, other_rows, 0)
        dn_copy(s, to).start()

    scat_s.fold_core(0)
    scat_s.send(0, 0)
    scat_s.fold_core(1)
    scat_s.send(1, 0)

    def edge_rows(j, carry):
        at = pl.ds(pl.multiple_of(j * tile, tile), tile)
        edge_out[:, at] = dn_tile(0, HALO, at, False).astype(BF16)
        return carry

    lax.fori_loop(0, width // tile, edge_rows, 0)
    for k in range(hp):

        @pl.when(p == hp + k)
        def _(k=k):
            edge_copy(k).start()

    def own_rows(j, carry):
        at = pl.ds(pl.multiple_of(j * tile, tile), tile)
        dn_own[:, at] = dn_tile(own_at, local_rows, at, True)
        return carry

    lax.fori_loop(0, width // tile, own_rows, 0)
    sum_rep.push(0)
    for s in range(stages):
        for scat in (scat_x, scat_s):
            for h in range(2):
                scat.fold(h, s)
                if s + 1 < stages:
                    scat.send(h, s + 1)
        sum_rep.fold(s)
        sum_rep.push(s + 1)
    home_x.start(0)
    home_x.start(1)
    home_dt.start(0)
    home_dt.start(1)
    bc_mine = sharded_rows(gsm, me, 0, rows, (2 * LANES, 4 * LANES))
    bc_copy = remote(bc_mine, bcz, ts.at[0], tr.at[0], tensor=lax.rem(p + hp, parts))
    bc_copy.start()
    for i in range(stages, len(sum_rep.steps)):
        sum_rep.fold(i)
        if i + 1 < len(sum_rep.steps):
            sum_rep.push(i + 1)
    rep_o[...] = rep[...]
    home_chan.wait()
    chan_o[...] = chan_z[0] + chan_z[1]

    for s, to in mates():
        dn_copy(s, to).wait_recv()

    @pl.when(p == hp - 1)
    def _():
        for k in range(hp):
            edge_copy(k).wait_recv()
        last = local_rows - HALO
        for k in range(hp):
            dn_own[last:, :] += edge_in[k].astype(F32)

    dnormed = dn_own[...]
    for s in range(1, hp):
        dnormed = dnormed + dn_in[s - 1].astype(F32)
    values = inputs[...].astype(F32)
    scale = lax.rsqrt(jnp.mean(values * values, axis=1, keepdims=True) + EPS)
    side = dnormed * ngain[...]
    pull = scale * scale * scale * (jnp.sum(side * values, axis=1, keepdims=True) / width)
    gin_o[...] = (scale * side - values * pull + cot[...].astype(F32)).astype(BF16)

    home_dt.wait()
    gdt_o[...] = dtz[0].astype(F32) + dtz[1].astype(F32)
    bc_copy.wait_recv()
    gbc_o[...] = bc_mine[...].astype(F32) + bcz[...].astype(F32)
    home_x.wait()
    gx_o[...] = xz[0].astype(F32) + xz[1].astype(F32)
    for item in (scat_x, scat_s, home_x, home_dt, home_chan):
        item.finish()
    for s, to in mates():
        maps_copy(s, to).wait_send()
        dn_copy(s, to).wait_send()
    bc_copy.wait_send()

    @pl.when(half == 1)
    def _():
        edge_copy(0).wait_send()


def run_last(
    ends, inputs, cot, ngain, tok, dz, dx, wz, wx, ws, dbc, ddt, pre, taps, bias, csum, gsum, hsum, size, parts, ha, ig
):
    local_rows, width = inputs.shape
    total = tok.shape[0]
    count = total - HALO
    inner = 2 * ig
    hp = parts // 2
    rows = width // size
    shape = jax.ShapeDtypeStruct
    anywhere = pl.BlockSpec(memory_space=pl.ANY)
    dma = pltpu.SemaphoreType.DMA
    blocks, links = size // 2, max(size // 2 - 1, 1)
    steps = size.bit_length() - 1 + parts.bit_length() - 1
    vm = pltpu.VMEM

    def pair(n, cols):
        return [vm((n, rows, cols), BF16), vm((n, rows, cols), BF16)]

    scratch = dict(
        tok=vm(tok.shape, BF16),
        dz=vm(dz.shape, BF16),
        dx=vm(dx.shape, BF16),
        wz=vm(wz.shape, BF16),
        wx=vm(wx.shape, BF16),
        ws=vm(ws.shape, BF16),
        gx=vm((width, inner), BF16),
        gsm=vm((width, 4 * LANES), BF16),
        dsm=vm((total, 4 * LANES), BF16),
        conv=vm((total + 8, 2 * LANES), F32),
        dlow=vm((count, 2 * LANES), BF16),
        dother=vm((hp - 1, count, 2 * LANES), BF16),
        dn_out=vm((hp - 1, local_rows, width), BF16),
        dn_in=vm((hp - 1, local_rows, width), BF16),
        dn_own=vm((local_rows, width), F32),
        edge_out=vm((HALO, width), BF16),
        edge_in=vm((hp, HALO, width), BF16),
        xcore=pair(blocks, ig),
        xlink=pair(links, ig),
        score=pair(blocks, 2 * LANES),
        slink=pair(links, 2 * LANES),
        xz=vm((2, rows, ig), BF16),
        dtz=vm((2, rows, LANES), BF16),
        bcz=vm((rows, 2 * LANES), BF16),
        chan=vm((8, inner), F32),
        chan_in=vm((steps, 8, inner), F32),
        chan_z=vm((2, 8, ig), F32),
        rep=vm((8, width), F32),
        rep_in=vm((steps, 8, width), F32),
        loads=dma((6,)),
        ccs=dma((2, 2, blocks)),
        ccr=dma((2, 2, blocks)),
        cls=dma((2, 2, links)),
        clr=dma((2, 2, links)),
        zs=dma((6,)),
        zr=dma((6,)),
        zo=dma((3,)),
        bs=dma((2, steps)),
        br=dma((2, steps)),
        ds=dma((hp,)),
        dr=dma((hp,)),
        ns=dma((hp,)),
        nr=dma((hp,)),
        es=dma((1,)),
        er=dma((hp,)),
        ts=dma((1,)),
        tr=dma((1,)),
    )
    return pl.pallas_call(
        partial(last_body, size, parts, rows, ha, ig),
        out_shape=(
            shape((local_rows, width), BF16),
            shape((rows, ig), F32),
            shape((rows, LANES), F32),
            shape((rows, 2 * LANES), F32),
            shape((8, ig), F32),
            shape((8, width), F32),
        ),
        in_specs=[scalars(), whole(), whole(), whole()] + [anywhere] * 6 + [whole()] * 8,
        out_specs=[whole()] * 6,
        scratch_shapes=list(scratch.values()),
        compiler_params=pltpu.CompilerParams(vmem_limit_bytes=VMEM_BYTES, collective_id=1, has_side_effects=True),
        cost_estimate=cost(2 * total * width * (3 * inner + 1024), 40e6),
        name="last",
    )(ends, inputs, cot, ngain, tok, dz, dx, wz, wx, ws, dbc, ddt, pre, taps, bias, csum, gsum, hsum)


def local(
    inputs,
    cotangent,
    seq_lengths,
    norm_gain,
    w_z,
    w_x,
    w_bc,
    w_dt,
    conv_x,
    conv_x_bias,
    conv_bc,
    conv_bc_bias,
    dt_bias,
    a_log,
    d_skip,
    gate_gain,
    w_out,
):
    parts = lax.axis_size("tensor")
    size = lax.axis_size("dp")
    ha = dt_bias.shape[0]
    ig = w_z.shape[1]
    inner_all = ig * parts
    head_width = ig // ha

    ends = [seq_lengths[0, 0], seq_lengths[0, 0] + seq_lengths[0, 1]]
    ends.append(ends[1] + seq_lengths[0, 2])
    sc = jnp.stack(ends).astype(jnp.int32)

    def pad(v, to):
        return jnp.pad(v, [(0, 0)] * (v.ndim - 1) + [(0, to - v.shape[-1])])

    heads_row = jnp.concatenate([pad(dt_bias, LANES), pad(a_log, LANES)])
    table = jnp.concatenate(
        [conv_x, conv_x_bias[None], gate_gain[None], jnp.repeat(d_skip, head_width)[None], pad(heads_row, ig)[None]]
    )
    (
        tok, pulled, wx, wz, wo, ws, par, pre_bc, bc, dtin, dt, lc, lr, em, et, kd, pre_x, xs, st, sin, z, dm,
    ) = run_first(
        sc, inputs, cotangent, norm_gain[None], w_x, w_z, w_out.T, w_bc, pad(w_dt, LANES), table, conv_bc,
        conv_bc_bias[None], size, parts, ha,
    )
    taps_x, bias_x, gain, skip = par[0:4], par[4:5], par[5:6], par[6:7]
    alog_blocks = jnp.stack([par[7, LANES : 2 * LANES], par[7, ig + LANES : ig + 2 * LANES]])[:, None, :]
    y, stat = run_scan(sc, xs, bc, dt, lc, lr, em, kd, st, sin, z, dm, skip, gain, ig, size, parts)
    mixed, dz, dy, gate_sums, ds, dfirst = run_gate(sc, y, z, dm, stat, xs, gain, bc, em, kd, ig, inner_all)
    gw_o = run_grad(pulled, mixed)
    gw_z = run_grad(tok, dz)
    dx, dbc, ddt, conv_sums, head_sums, outputs, grad_w_z, grad_w_o = run_pull(
        sc, xs, dy, bc, dtin, dt, lc, lr, em, et, kd, st, sin, ds, pre_x, taps_x, bias_x, skip, alog_blocks,
        dfirst, inputs, mixed, wo, gw_z, gw_o, ha, ig, size, parts,
    )
    grad_inputs, grad_w_x, grad_w_dt, grad_w_bc, chan, rep = run_last(
        sc, inputs, cotangent, norm_gain[None], tok, dz, dx, wz, wx, ws, dbc, ddt, pre_bc, conv_bc,
        conv_bc_bias[None], conv_sums, gate_sums, head_sums, size, parts, ha, ig,
    )
    rep_bc = rep[1, : 10 * LANES].reshape(5, 2 * LANES)
    return (
        outputs,
        grad_inputs,
        rep[0] / norm_gain,
        grad_w_z,
        grad_w_x,
        grad_w_bc,
        grad_w_dt[:, :ha],
        chan[:4],
        chan[4],
        rep_bc[:4],
        rep_bc[4],
        chan[7, :ha],
        chan[7, LANES : LANES + ha],
        jnp.sum(chan[6].reshape(ha, head_width), axis=1),
        chan[5],
        grad_w_o.T,
    )


def solution(mesh):
    tokens = P(("dp", "tensor"), None)
    matrix = P("dp", "tensor")
    heads = P("tensor")
    return jax.shard_map(
        local,
        mesh=mesh,
        in_specs=(
            tokens,
            tokens,
            P("dp", None),
            P(),
            matrix,
            matrix,
            P("dp", None),
            matrix,
            P(None, "tensor"),
            heads,
            P(),
            P(),
            heads,
            heads,
            heads,
            heads,
            P("tensor", "dp"),
        ),
        out_specs=(
            tokens,
            tokens,
            P(),
            matrix,
            matrix,
            P("dp", None),
            matrix,
            P(None, "tensor"),
            heads,
            P(),
            P(),
            heads,
            heads,
            heads,
            heads,
            P("tensor", "dp"),
        ),
        check_vma=False,
    )
```

```python
from functools import partial

import jax
import jax.numpy as jnp
from jax import lax
from jax.experimental import pallas as pl
from jax.experimental.pallas import tpu as pltpu
from jax.sharding import PartitionSpec as P

SPAN = 256
HALO = 16
LANES = 128
LOG2E = 1.4426950408889634
EPS = 1e-05
FAR = -1e30
HIGH = lax.Precision.HIGHEST
F32 = jnp.float32
BF16 = jnp.bfloat16
VMEM_BYTES = 60 * 1024 * 1024


def nn(a, b):
    return jnp.dot(a, b, preferred_element_type=F32)


def nt(a, b):
    return lax.dot_general(a, b, (((1,), (1,)), ((), ())), preferred_element_type=F32)


def tn(a, b):
    return lax.dot_general(a, b, (((0,), (0,)), ((), ())), preferred_element_type=F32)


def sigmoid(v):
    return 1.0 / (1.0 + jnp.exp(-v))


def iota(shape, axis):
    return lax.broadcasted_iota(jnp.int32, shape, axis)


def seg_at(lengths, pos):
    end = lengths[0, 0]
    found = (pos >= end).astype(jnp.int32)
    for i in range(1, 3):
        end = end + lengths[0, i]
        found = found + (pos >= end).astype(jnp.int32)
    return jnp.where(pos < 0, -1, found)


def same_as_behind(sc, pos, offset):
    return (seg_at(sc, pos - offset) == seg_at(sc, pos)).astype(F32)


def head_map(cols, start, first, both=True):
    k = iota((LANES, cols), 0)
    if both:
        k = k & 63
    head = ((iota((LANES, cols), 1) + start) >> 6) + first
    return (k == head).astype(BF16)


def expand(values, mapping):
    high = values.astype(BF16).astype(F32)
    low = values - high
    return nn((high + pltpu.roll(low, 64, axis=1)).astype(BF16), mapping)


def whole():
    return pl.BlockSpec(memory_space=pltpu.VMEM)


def scalars():
    return pl.BlockSpec(memory_space=pltpu.SMEM)


def params():
    return pltpu.CompilerParams(vmem_limit_bytes=VMEM_BYTES)


def cost(flops, nbytes):
    return pl.CostEstimate(flops=int(flops), bytes_accessed=int(nbytes), transcendentals=0)


def col_tile(ig):
    return 256 if ig % 256 == 0 else 128


def flip(me, v):
    out = me
    bit = 1
    while bit <= v:
        if v & bit:
            out = out + bit - 2 * bit * lax.rem(me // bit, 2)
        bit *= 2
    return out


def link_bits(size):
    bits = []
    bit = 2
    while bit < size:
        bits.append(bit)
        bit *= 2
    return bits


def remote(src, dst, send, recv, **where):
    return pltpu.make_async_remote_copy(
        src_ref=src, dst_ref=dst, send_sem=send, recv_sem=recv, device_id=where, device_id_type=pl.DeviceIdType.MESH
    )


def greet(bits, partners):
    me = lax.axis_index("dp")
    barrier = pltpu.get_barrier_semaphore()
    for bit in bits:
        pl.semaphore_signal(barrier, inc=1, device_id={"dp": flip(me, bit)}, device_id_type=pl.DeviceIdType.MESH)
    for to in partners:
        pl.semaphore_signal(barrier, inc=1, device_id={"tensor": to}, device_id_type=pl.DeviceIdType.MESH)
    pl.semaphore_wait(barrier, len(bits) + len(partners))


def others(parts):
    p = lax.axis_index("tensor")
    return [lax.rem(p + shift, parts) for shift in range(1, parts)]


def row(ref):
    return jnp.reshape(ref[...], (1, ref.shape[0]))


class ToHeads:
    def __init__(self, k, src, place_of, parts, send, recv, own):
        self.p = lax.axis_index("tensor")
        self.hp = parts // 2
        self.k, self.src, self.place_of = k, src, place_of
        self.send, self.recv, self.own = send, recv, own

    def copy(self, i, side, to):
        return remote(
            self.src, self.place_of(side), self.send.at[2 * self.k + i], self.recv.at[2 * self.k + side], tensor=to
        )

    def local(self, side):
        return pltpu.make_async_copy(self.src, self.place_of(side), self.own.at[self.k])

    def targets(self):
        return [self.p // 2, self.p // 2 + self.hp]

    def start(self):
        side = lax.rem(self.p, 2)
        for i, to in enumerate(self.targets()):

            @pl.when(to != self.p)
            def _(i=i, to=to):
                self.copy(i, side, to).start()

            @pl.when(to == self.p)
            def _():
                self.local(side).start()

    def wait(self):
        q = lax.rem(self.p, self.hp)
        for side in range(2):
            source = 2 * q + side

            @pl.when(source != self.p)
            def _(side=side):
                self.copy(0, side, self.p // 2).wait_recv()

            @pl.when(source == self.p)
            def _(side=side):
                self.local(side).wait()

    def finish(self):
        side = lax.rem(self.p, 2)
        for i, to in enumerate(self.targets()):

            @pl.when(to != self.p)
            def _(i=i, to=to):
                self.copy(i, side, to).wait_send()


class Gather:
    def __init__(self, k, ref, split, rows, size, send, recv):
        self.me = lax.axis_index("dp")
        self.k, self.ref, self.rows, self.size = k, ref, rows, size
        bits = link_bits(size)
        self.orders = [bits, bits[::-1]]
        self.cols = [slice(0, split), slice(split, ref.shape[1])]
        self.send, self.recv = send, recv
        self.sent = []

    def block(self, half, v):
        start = pl.multiple_of(flip(self.me, v) * self.rows, 16)
        cols = self.cols[half]
        return self.ref.at[pl.ds(start, self.rows), pl.ds(cols.start, cols.stop - cols.start)]

    def copy(self, half, v, bit):
        n = bit.bit_length() - 1
        here = self.block(half, v)
        return remote(
            here,
            here,
            self.send.at[self.k, half, v * self.size.bit_length() + n],
            self.recv.at[self.k, half, v ^ bit],
            dp=flip(self.me, bit),
        )

    def push(self, half, v, bits):
        for bit in bits:
            self.copy(half, v, bit).start()
            self.sent.append((half, v, bit))

    def arrive(self, half, v):
        here = self.block(half, v)
        remote(
            here,
            here,
            self.send.at[self.k, half, 0],
            self.recv.at[self.k, half, v],
            dp=flip(self.me, 1),
        ).wait_recv()

    def start(self):
        for half in range(2):
            self.push(half, 0, self.orders[half])
        for half in range(2):
            self.push(half, 0, [1])

    def stage(self, s):
        for half in range(2):
            order = self.orders[half]
            names = [0]
            for bit in order[:s]:
                names = names + [v ^ bit for v in names]
            for v in sorted(n ^ order[s] for n in names):
                self.arrive(half, v)
                self.push(half, v, order[s + 1 :])
                self.push(half, v, [1])

    def stages(self):
        return len(self.orders[0])

    def cores(self):
        for half in range(2):
            for v in range(1, self.size, 2):
                self.arrive(half, v)

    def finish(self):
        for half, v, bit in self.sent:
            self.copy(half, v, bit).wait_send()


class Scatter:
    def __init__(self, k, source, acc, own, size, core_buf, link_buf, cs, cr, ls, lr):
        self.me = lax.axis_index("dp")
        self.k, self.source, self.acc, self.own, self.size = k, source, acc, own, size
        self.core_buf, self.link_buf = core_buf, link_buf
        self.cs, self.cr, self.ls, self.lr = cs, cr, ls, lr
        bits = link_bits(size)
        self.orders = [bits, bits[::-1]]
        self.sent = []

    def core(self, half, u):
        return remote(
            self.source(half, 2 * u + 1),
            self.core_buf[half].at[u],
            self.cs.at[self.k, half, u],
            self.cr.at[self.k, half, u],
            dp=flip(self.me, 1),
        )

    def start(self, half):
        for u in range(self.size // 2):
            self.core(half, u).start()
            if self.own is not None:
                self.own(half, u).start()

    def add(self, half, u, other):
        ref = self.acc(half, u)
        ref[...] = (ref[...].astype(F32) + other[...].astype(F32)).astype(BF16)

    def fold_core(self, half):
        for u in range(self.size // 2):
            self.core(half, u).wait_recv()
            if self.own is not None:
                self.own(half, u).wait()
            self.add(half, u, self.core_buf[half].at[u])

    def plan(self, half, s):
        order = self.orders[half]
        held, slot = list(range(0, self.size, 2)), 0
        for i, bit in enumerate(order):
            away = [v for v in held if v & bit]
            stay = [v for v in held if not v & bit]
            if i == s:
                return bit, away, stay, slot
            held, slot = stay, slot + len(stay)

    def link(self, half, s, i):
        bit, away, stay, slot = self.plan(half, s)
        n = slot + stay.index(away[i] ^ bit)
        return remote(
            self.acc(half, away[i] >> 1),
            self.link_buf[half].at[n],
            self.ls.at[self.k, half, n],
            self.lr.at[self.k, half, n],
            dp=flip(self.me, bit),
        )

    def send(self, half, s):
        for i in range(len(self.plan(half, s)[1])):
            self.link(half, s, i).start()

    def fold(self, half, s):
        bit, away, stay, slot = self.plan(half, s)
        for i in range(len(away)):
            self.link(half, s, i).wait_recv()
        for i, v in enumerate(stay):
            self.add(half, v >> 1, self.link_buf[half].at[slot + i])

    def stages(self):
        return len(self.orders[0])

    def finish(self):
        for half in range(2):
            for u in range(self.size // 2):
                self.core(half, u).wait_send()
            for s in range(self.stages()):
                for i in range(len(self.plan(half, s)[1])):
                    self.link(half, s, i).wait_send()


class FromHeads:
    def __init__(self, k, block, slots, parts, send, recv, own):
        self.p = lax.axis_index("tensor")
        self.hp = parts // 2
        self.k, self.block, self.slots = k, block, slots
        self.send, self.recv, self.own = send, recv, own
        self.half = self.p // self.hp
        self.q = lax.rem(self.p, self.hp)

    def copy(self, side, slot):
        return remote(
            self.block(side),
            self.slots.at[slot],
            self.send.at[2 * self.k + side],
            self.recv.at[2 * self.k + slot],
            tensor=2 * self.q + side,
        )

    def local(self, side, slot):
        return pltpu.make_async_copy(self.block(side), self.slots.at[slot], self.own.at[self.k])

    def start(self, side):
        to = 2 * self.q + side

        @pl.when(to != self.p)
        def _():
            self.copy(side, self.half).start()

        @pl.when(to == self.p)
        def _():
            self.local(side, self.half).start()

    def wait(self):
        for slot in range(2):
            source = self.p // 2 + slot * self.hp

            @pl.when(source != self.p)
            def _(slot=slot):
                self.copy(0, slot).wait_recv()

            @pl.when(source == self.p)
            def _(slot=slot):
                self.local(0, slot).wait()

    def finish(self, sides=(0, 1)):
        for side in sides:

            @pl.when(2 * self.q + side != self.p)
            def _(side=side):
                self.copy(side, self.half).wait_send()


class Butterfly:
    def __init__(self, k, ref, slots, steps, send, recv):
        self.k, self.ref, self.slots, self.steps = k, ref, slots, steps
        self.send, self.recv = send, recv

    def copy(self, i):
        axis, bit = self.steps[i]
        return remote(
            self.ref,
            self.slots.at[i],
            self.send.at[self.k, i],
            self.recv.at[self.k, i],
            **{axis: flip(lax.axis_index(axis), bit)},
        )

    def push(self, i):
        self.copy(i).start()

    def fold(self, i):
        self.copy(i).wait()
        self.ref[...] += self.slots[i]


def sharded_rows(ref, me, v, rows, cols):
    start = pl.multiple_of(flip(me, v) * rows, 16)
    return ref.at[pl.ds(start, rows), pl.ds(cols[0], cols[1] - cols[0])]


def halves(split, total):
    return [(0, split), (split, total)]


def split_of(cols):
    return (cols // 2 + LANES - 1) // LANES * LANES


def first_body(
    size, parts, rows, ha, ig,
    ends, inputs, cot, ngain, w_x, w_z, w_out, w_bc, w_dt, conv_x, conv_x_bias, dt_bias, a_log, d_skip, gate_gain,
    taps_bc, bias_bc,
    tok_h, pulled_h, wx_h, wz_h, wo_h, ws_h, par_h, pre_h, bc_h, dtin_h, dt_h, lc_h, lr_h, em_h, et_h, kd_h,
    prex_h, xs_h, st_h, sin_h, z_h, dm_h,
    tok, pulled, wx, wz, wo, ws, par, pre, bc, dtin, dt, lc, lr, em, et, kd, st, stage, xs_stage, fin, sin,
    lags, w_dt_wide, table,
    zs, zr, zo, gs, gr, ts, tr, cs, cr, hs, hr, ss, sr, local, outs, tiles,
):
    p = lax.axis_index("tensor")
    me = lax.axis_index("dp")
    hp = parts // 2
    place = lax.rem(p, hp)
    half = p // hp
    inner = 2 * ig
    local_rows, width = inputs.shape
    count = local_rows * hp
    total = count + HALO
    base = half * count
    own_rows = pl.multiple_of(place * local_rows, 16)

    def mates():
        return [(s, half * hp + lax.rem(place + s, hp)) for s in range(1, hp)]

    def my_rows():
        return pl.ds(pl.multiple_of(me * rows, 16), rows)

    def wide(ref, cols):
        return lambda side: ref.at[my_rows(), pl.ds(pl.multiple_of(side * cols, LANES), cols)]

    emitted = []

    def emit(src, dst):
        copy = pltpu.make_async_copy(src, dst, outs.at[len(emitted)])
        copy.start()
        emitted.append(copy)

    w_dt_wide[...] = jnp.zeros_like(w_dt_wide)
    w_dt_wide[:, :ha] = w_dt[...].T
    greet([1] + link_bits(size), others(parts))
    to_table = ToHeads(0, table, lambda side: par.at[:, pl.ds(pl.multiple_of(side * ig, LANES), ig)], parts, zs, zr, zo)
    to_dt = ToHeads(1, w_dt_wide, wide(ws, LANES), parts, zs, zr, zo)
    to_x = ToHeads(2, w_x, wide(wx, ig), parts, zs, zr, zo)
    to_z = ToHeads(3, w_z, wide(wz, ig), parts, zs, zr, zo)
    to_o = ToHeads(4, w_out, wide(wo, ig), parts, zs, zr, zo)
    to_dt.start()
    to_x.start()
    bc_copy = pltpu.make_async_copy(w_bc, ws.at[my_rows(), pl.ds(2 * LANES, 2 * LANES)], local.at[0])
    bc_copy.start()
    cot_copy = pltpu.make_async_copy(cot, pulled.at[pl.ds(own_rows, local_rows)], local.at[1])
    cot_copy.start()

    values = inputs[...].astype(F32)
    scale = lax.rsqrt(jnp.mean(values * values, axis=1, keepdims=True) + EPS)
    mine = pl.ds(pl.multiple_of(HALO + own_rows, 16), local_rows)
    tok[mine, :] = (values * scale * row(ngain)).astype(BF16)

    def tok_copy(s, to):
        return remote(tok.at[mine], tok.at[mine], ts.at[s], tr.at[s], tensor=to)

    def tok_arrive(s):
        there = pl.ds(pl.multiple_of(HALO + lax.rem(place + hp - s, hp) * local_rows, 16), local_rows)
        remote(tok.at[there], tok.at[there], ts.at[s], tr.at[s], tensor=p).wait_recv()

    def cot_copy_to(s, to):
        return remote(cot, pulled.at[pl.ds(own_rows, local_rows)], cs.at[s], cr.at[s], tensor=to)

    def cot_arrive(s):
        there = pl.ds(pl.multiple_of(lax.rem(place + hp - s, hp) * local_rows, 16), local_rows)
        remote(pulled.at[there], pulled.at[there], cs.at[s], cr.at[s], tensor=p).wait_recv()

    def halo_copy(k):
        return remote(tok.at[pl.ds(total - HALO, HALO)], tok.at[pl.ds(0, HALO)], hs.at[k], hr.at[0], tensor=hp + k)

    for s, to in mates():
        tok_copy(s, to).start()

    @pl.when(p == hp - 1)
    def _():
        for k in range(hp):
            halo_copy(k).start()

    @pl.when(half == 0)
    def _():
        tok[:HALO, :] = jnp.zeros((HALO, width), BF16)

    table[...] = jnp.zeros_like(table)
    table[0:4, :] = conv_x[...]
    table[4:5, :] = row(conv_x_bias)
    table[5:6, :] = row(gate_gain)
    table[6:7, :ha] = row(d_skip)
    table[7:8, :ha] = row(dt_bias)
    table[7:8, LANES : LANES + ha] = row(a_log)
    to_table.start()

    g_s = Gather(0, ws, 2 * LANES, rows, size, gs, gr)
    g_x = Gather(1, wx, ig, rows, size, gs, gr)
    g_z = Gather(2, wz, ig, rows, size, gs, gr)
    g_o = Gather(3, wo, ig, rows, size, gs, gr)
    stages = g_x.stages()
    to_dt.wait()
    bc_copy.wait()
    g_s.start()
    to_x.wait()
    g_x.start()
    to_z.start()
    for s in range(stages):
        g_s.stage(s)
        g_x.stage(s)
        if s == 0:
            to_z.wait()
            g_z.start()
            to_o.start()
    g_s.cores()
    for s, _ in mates():
        tok_arrive(s)
    for s, to in mates():
        cot_copy_to(s, to).start()

    @pl.when(half == 1)
    def _():
        halo_copy(0).wait_recv()

    emit(tok, tok_h)
    emit(ws, ws_h)

    both = nn(tok[...], ws[...])
    pre[...] = both[:, 2 * LANES :]
    emit(pre, pre_h)
    pos = base + iota((count, 1), 0)
    for j in range(1, 4):
        lags[j - 1] = jnp.broadcast_to(same_as_behind(ends, pos, j), (count, LANES))
    for side in range(2):
        at = slice(side * LANES, (side + 1) * LANES)
        acc = bias_bc[...].reshape(1, 2 * LANES)[:, at] + taps_bc[0:1, at] * pre[HALO : HALO + count, at]
        for j in range(1, 4):
            acc = acc + taps_bc[j : j + 1, at] * pre[HALO - j : HALO - j + count, at] * lags[j - 1]
        bc[:, at] = (acc * sigmoid(acc)).astype(BF16)
    emit(bc, bc_h)
    to_table.wait()
    emit(par, par_h)
    lane = iota((1, LANES), 1)
    keep = ((lane & 15) < ha).astype(F32) * (lane < 32).astype(F32)

    def merge(values):
        return values[0] + pltpu.roll(values[1], 16, axis=1)

    biases = merge([par[7:8, b * ig : b * ig + LANES] for b in range(2)])
    logs_a = merge([par[7:8, b * ig + LANES : b * ig + 2 * LANES] for b in range(2)])
    shifted = merge([both[HALO:, b * LANES : (b + 1) * LANES] for b in range(2)]) + biases
    steps = (jnp.maximum(shifted, 0.0) + jnp.log1p(jnp.exp(-jnp.abs(shifted)))) * keep
    dtin[...] = shifted
    dt[...] = steps
    scaled = steps * (-jnp.exp(logs_a) * LOG2E)
    tri = (iota((SPAN, SPAN), 0) >= iota((SPAN, SPAN), 1)).astype(F32)
    chunks = count // SPAN
    gone = []
    for c in range(chunks):
        span = slice(c * SPAN, (c + 1) * SPAN)
        logs = jnp.dot(tri, scaled[span, :], precision=HIGH, preferred_element_type=F32)
        first, last = base + c * SPAN - 1, base + (c + 1) * SPAN - 1
        here = base + c * SPAN + iota((SPAN, 1), 0)
        seg = seg_at(ends, here)
        seg_first, seg_last = seg_at(ends, first), seg_at(ends, last)
        final = logs[SPAN - 1 : SPAN, :]
        gone.append(jnp.where(seg_first == seg_last, 1.0, 0.0).astype(F32) * jnp.exp2(final) * keep)
        lc[span, :] = logs
        lr[:, span] = logs.T[:32, :]
        em[span, :] = (seg == seg_first).astype(F32) * jnp.exp2(logs) * keep
        et[span, :] = (seg == seg_last).astype(F32) * jnp.exp2(final - logs) * keep
    ahead_of, behind_of = [keep], [keep]
    for c in range(chunks - 1):
        ahead_of.append(ahead_of[-1] * gone[c])
        behind_of.append(behind_of[-1] * gone[chunks - 1 - c])
    behind_of = behind_of[::-1]
    fill = [jnp.zeros((1, LANES), F32)] * (8 - chunks)
    kd[...] = jnp.concatenate(gone + fill + ahead_of + fill + behind_of + fill, axis=0)
    for src, dst in ((dtin, dtin_h), (dt, dt_h), (lc, lc_h), (lr, lr_h), (em, em_h), (et, et_h), (kd, kd_h)):
        emit(src, dst)

    g_x.cores()
    emit(wx, wx_h)
    to_o.wait()
    g_z.stage(0)
    g_o.start()

    cols = col_tile(ig)

    def tile_out(kind, slot, j):
        at = pl.ds(pl.multiple_of(j * cols, cols), cols)
        if kind == 0:
            return pltpu.make_async_copy(stage.at[slot], prex_h.at[:, at], tiles.at[0, slot])
        if kind == 1:
            return pltpu.make_async_copy(xs_stage.at[slot], xs_h.at[:, at], tiles.at[1, slot])
        rows_of = stage.at[slot, pl.ds(0, count)]
        return pltpu.make_async_copy(rows_of, (z_h if kind == 2 else dm_h).at[:, at], tiles.at[kind, slot])

    def xpath(j, carry):
        slot = lax.rem(j, 2)

        @pl.when(j >= 2)
        def _():
            tile_out(0, slot, j).wait()
            tile_out(1, slot, j).wait()

        at = pl.multiple_of(j * cols, cols)
        lanes = pl.ds(at, cols)
        b = at // ig
        stage[slot] = nn(tok[...], wx[:, lanes])
        mapping = head_map(cols, lax.rem(at, ig), b * 16)
        state = jnp.zeros((LANES, cols), F32)
        decay = expand(kd[0:8, :], mapping)
        taps, bias = par[0:4, lanes], par[4:5, lanes]
        for c in range(chunks):
            low = c * SPAN
            weight = expand(dt[low : low + SPAN, :] * et[low : low + SPAN, :], mapping)
            weighted = []
            for side in range(cols // LANES):
                lane_at = slice(side * LANES, (side + 1) * LANES)
                window = stage[slot, low : low + SPAN + HALO, lane_at]
                conv = bias[:, lane_at] + taps[0:1, lane_at] * window[HALO:, :]
                for k in range(1, 4):
                    lag = pltpu.roll(window, k, axis=0)[HALO:, :]
                    conv = conv + taps[k : k + 1, lane_at] * lag * lags[k - 1, low : low + SPAN, :]
                xs = (conv * sigmoid(conv)).astype(BF16)
                xs_stage[slot, low : low + SPAN, lane_at] = xs
                weighted.append((xs.astype(F32) * weight[:, lane_at]).astype(BF16))
            st[c, :, lanes] = state
            fresh = tn(bc[low : low + SPAN, :LANES], jnp.concatenate(weighted, axis=1))
            state = decay[c : c + 1, :] * state + fresh
        fin[:, lanes] = state.astype(BF16)
        tile_out(0, slot, j).start()
        tile_out(1, slot, j).start()
        return carry

    def project(kind, x, skip, w):
        def step(j, carry):
            slot = lax.rem(j, 2)

            @pl.when(j >= 2)
            def _():
                tile_out(kind, slot, j).wait()

            lanes = pl.ds(pl.multiple_of(j * cols, cols), cols)
            stage[slot, :count, :] = nn(x[skip:, :], w[:, lanes])
            tile_out(kind, slot, j).start()
            return carry

        return step

    tiles_all = inner // cols
    middle = tiles_all // 2

    def drain(kind):
        for j in range(tiles_all - 2, tiles_all):
            tile_out(kind, j % 2, j).wait()

    lax.fori_loop(0, middle, xpath, 0)
    for s in range(1, stages):
        g_z.stage(s)
    lax.fori_loop(middle, tiles_all, xpath, 0)
    emit(st, st_h)

    def state_copy():
        return remote(fin, sin, ss.at[0], sr.at[0], tensor=lax.rem(p + hp, parts))

    @pl.when(half == 0)
    def _():
        state_copy().start()

    drain(0)
    drain(1)
    g_z.cores()
    emit(wz, wz_h)
    lax.fori_loop(0, middle, project(2, tok, HALO, wz), 0)
    for s in range(stages):
        g_o.stage(s)
    lax.fori_loop(middle, tiles_all, project(2, tok, HALO, wz), 0)
    drain(2)
    for s, _ in mates():
        cot_arrive(s)
    cot_copy.wait()
    emit(pulled, pulled_h)
    g_o.cores()
    emit(wo, wo_h)
    lax.fori_loop(0, tiles_all, project(3, pulled, 0, wo), 0)

    @pl.when(half == 1)
    def _():
        state_copy().wait_recv()

    @pl.when(half == 0)
    def _():
        sin[...] = jnp.zeros_like(sin)

    emit(sin, sin_h)
    drain(3)
    for item in (to_table, to_dt, to_x, to_z, to_o, g_s, g_x, g_z, g_o):
        item.finish()
    for s, to in mates():
        tok_copy(s, to).wait_send()
        cot_copy_to(s, to).wait_send()

    @pl.when(p == hp - 1)
    def _():
        for k in range(hp):
            halo_copy(k).wait_send()

    @pl.when(half == 0)
    def _():
        state_copy().wait_send()

    for copy in emitted:
        copy.wait()


def run_first(
    ends, inputs, cot, ngain, w_x, w_z, w_out, w_bc, w_dt, conv_x, conv_x_bias, dt_bias, a_log, d_skip, gate_gain,
    taps_bc, bias_bc, size, parts,
):
    ha = dt_bias.shape[0]
    local_rows, width = inputs.shape
    rows, ig = w_x.shape
    inner = 2 * ig
    hp = parts // 2
    count = local_rows * hp
    total = count + HALO
    chunks = count // SPAN
    cols = col_tile(ig)
    shape = jax.ShapeDtypeStruct
    per_block = shape((count, LANES), F32)
    outs = (
        shape((total, width), BF16),
        shape((count, width), BF16),
        shape((width, inner), BF16),
        shape((width, inner), BF16),
        shape((width, inner), BF16),
        shape((width, 4 * LANES), BF16),
        shape((8, inner), F32),
        shape((total, 2 * LANES), F32),
        shape((count, 2 * LANES), BF16),
        per_block,
        per_block,
        per_block,
        shape((32, count), F32),
        per_block,
        per_block,
        shape((24, LANES), F32),
        shape((total, inner), F32),
        shape((count, inner), BF16),
        shape((chunks, LANES, inner), F32),
        shape((LANES, inner), BF16),
        shape((count, inner), F32),
        shape((count, inner), F32),
    )
    anywhere = pl.BlockSpec(memory_space=pl.ANY)
    dma = pltpu.SemaphoreType.DMA
    nbits = size.bit_length()
    scratch = [pltpu.VMEM(o.shape, o.dtype) for o in outs[:16]]
    scratch += [
        pltpu.VMEM((chunks, LANES, inner), F32),
        pltpu.VMEM((2, total, cols), F32),
        pltpu.VMEM((2, count, cols), BF16),
        pltpu.VMEM((LANES, inner), BF16),
        pltpu.VMEM((LANES, inner), BF16),
        pltpu.VMEM((3, count, LANES), F32),
        pltpu.VMEM((rows, LANES), BF16),
        pltpu.VMEM((8, ig), F32),
        dma((10,)),
        dma((10,)),
        dma((5,)),
        dma((4, 2, size * nbits)),
        dma((4, 2, size)),
        dma((hp,)),
        dma((hp,)),
        dma((hp,)),
        dma((hp,)),
        dma((hp,)),
        dma((1,)),
        dma((1,)),
        dma((1,)),
        dma((2,)),
        dma((24,)),
        dma((4, 2)),
    ]
    return pl.pallas_call(
        partial(first_body, size, parts, rows, ha, ig),
        out_shape=outs,
        in_specs=[scalars(), whole(), anywhere, whole(), anywhere, anywhere, anywhere, anywhere] + [whole()] * 9,
        out_specs=[anywhere] * len(outs),
        scratch_shapes=scratch,
        compiler_params=pltpu.CompilerParams(vmem_limit_bytes=VMEM_BYTES, collective_id=0, has_side_effects=True),
        cost_estimate=cost(2 * total * width * (3 * inner + 512), 60e6),
        name="first",
    )(
        ends, inputs, cot, ngain, w_x, w_z, w_out, w_bc, w_dt, conv_x, conv_x_bias, dt_bias, a_log, d_skip,
        gate_gain, taps_bc, bias_bc,
    )


def scan_body(
    size, parts, sc, xs, bc, dt, lc, lr, em, kd, st, sin, z, dm, par, y_o, stat_o, cb, off, stat, mine, theirs, ss, sr
):
    c, b = pl.program_id(0), pl.program_id(1)
    cols = xs.shape[1]
    p = lax.axis_index("tensor")
    hp = parts // 2
    count = stat.shape[0]
    base = (p // hp) * count
    rows_here = pl.ds(pl.multiple_of(c * SPAN, SPAN), SPAN)

    def mate(s):
        return (p // hp) * hp + lax.rem(lax.rem(p, hp) + s, hp)

    @pl.when((c == 0) & (b == 0))
    def _():
        greet([], [mate(s) for s in range(1, hp)])

    @pl.when(b == 0)
    def _():
        cb[...] = nt(bc[:, LANES:], bc[:, :LANES])
        start = base + c * SPAN
        t, s = iota((SPAN, SPAN), 0), iota((SPAN, SPAN), 1)
        seen = (t >= s) & (seg_at(sc, start + t) == seg_at(sc, start + s))
        off[...] = jnp.where(seen, 0.0, FAR)
        stat[rows_here, :] = jnp.zeros((SPAN, LANES), F32)

    mapping = head_map(cols, 0, b * 16)
    scaled = (xs[...].astype(F32) * expand(dt[...], mapping)).astype(BF16)
    carry = expand(kd[8:16, :], mapping)
    rows8 = (iota((8, 1), 0) == c).astype(F32)
    state = st[0] + jnp.sum(carry * rows8, axis=0, keepdims=True) * sin[...].astype(F32)
    skip = expand(jnp.broadcast_to(par[6:7, :LANES], (8, LANES)), head_map(cols, 0, 0))[0:1, :]
    far = nn(bc[:, LANES:], state.astype(BF16)) * expand(em[...], mapping) + skip * xs[...].astype(F32)
    columns = pltpu.roll(lc[...], lax.rem(LANES - 16 * b, LANES), axis=1)
    lane = iota((1, LANES), 1)
    sides = [(lane < 64).astype(BF16), (lane >= 64).astype(BF16)]
    half = SPAN // 2
    square = jnp.zeros((SPAN, 1), F32)
    cross = jnp.zeros((SPAN, 1), F32)
    for k in range(cols // LANES):
        at = slice(k * LANES, (k + 1) * LANES)
        pair = scaled[:, at]
        top = far[:half, at]
        low = far[half:, at]
        for side in range(2):
            h = 2 * k + side
            operand = pair * sides[side]
            column = columns[:, h : h + 1]
            row = lr[h : h + 1, :]
            w_top = cb[:half, :half] * jnp.exp2(column[:half] - row[:, :half] + off[:half, :half])
            top = top + nn(w_top.astype(BF16), operand[:half, :])
            w_low = cb[half:, :] * jnp.exp2(column[half:] - row + off[half:, :])
            low = low + nn(w_low.astype(BF16), operand)
        out = jnp.concatenate([top, low], axis=0)
        y_o[:, at] = out
        gate = z[:, at]
        gated = out * (gate * sigmoid(gate))
        square = square + jnp.sum(gated * gated, axis=1, keepdims=True)
        cross = cross + jnp.sum(gated * (dm[:, at] * par[5:6, at]), axis=1, keepdims=True)
    stat[rows_here, :] += jnp.where(lane == 0, square, 0.0) + jnp.where(lane == 1, cross, 0.0)

    @pl.when((c == pl.num_programs(0) - 1) & (b == 1))
    def _():
        mine[...] = stat[...].T[:8, :]

        def copy(s):
            return remote(mine, theirs.at[s - 1], ss.at[s - 1], sr.at[s - 1], tensor=mate(s))

        for s in range(1, hp):
            copy(s).start()
        for s in range(1, hp):
            copy(s).wait()
        total = mine[...]
        for s in range(1, hp):
            total = total + theirs[s - 1]
        stat_o[...] = jnp.concatenate([total, jnp.zeros((LANES - 8, count), F32)], axis=0).T


def run_scan(sc, xs, bc, dt, lc, lr, em, kd, st, sin, z, dm, par, ig, size, parts):
    count, inner = xs.shape
    chunks = count // SPAN
    tile = pl.BlockSpec((SPAN, ig), lambda c, b: (c, b))
    per_token = pl.BlockSpec((SPAN, LANES), lambda c, b: (c, 0))
    return pl.pallas_call(
        partial(scan_body, size, parts),
        grid=(chunks, 2),
        out_shape=(
            jax.ShapeDtypeStruct((count, inner), F32),
            jax.ShapeDtypeStruct((count, LANES), F32),
        ),
        in_specs=[
            scalars(),
            tile,
            pl.BlockSpec((SPAN, 2 * LANES), lambda c, b: (c, 0)),
            per_token,
            per_token,
            pl.BlockSpec((16, SPAN), lambda c, b: (b, c)),
            per_token,
            whole(),
            pl.BlockSpec((1, LANES, ig), lambda c, b: (c, 0, b)),
            pl.BlockSpec((LANES, ig), lambda c, b: (0, b)),
            tile,
            tile,
            pl.BlockSpec((8, ig), lambda c, b: (0, b)),
        ],
        out_specs=(tile, pl.BlockSpec((count, LANES), lambda c, b: (0, 0))),
        scratch_shapes=[
            pltpu.VMEM((SPAN, SPAN), F32),
            pltpu.VMEM((SPAN, SPAN), F32),
            pltpu.VMEM((count, LANES), F32),
            pltpu.VMEM((8, count), F32),
            pltpu.VMEM((parts // 2 - 1, 8, count), F32),
            pltpu.SemaphoreType.DMA((parts // 2 - 1,)),
            pltpu.SemaphoreType.DMA((parts // 2 - 1,)),
        ],
        compiler_params=pltpu.CompilerParams(vmem_limit_bytes=VMEM_BYTES, collective_id=2, has_side_effects=True),
        cost_estimate=cost(6e9, 20e6),
        name="scan",
    )(sc, xs, bc, dt, lc, lr, em, kd, st, sin, z, dm, par)


def gate_body(
    parts, ig, inner_all, y, z, dm, stats, xs, par, bc, em, kd, tok, pulled,
    mixed_o, dz_o, dy_o, sums_o, ds_o, gz_o, go_o, dsin_o,
    first, dsin, ss, sr,
):
    count, cols = y.shape
    j = pl.program_id(0)
    tiles = pl.num_programs(0)
    p = lax.axis_index("tensor")
    hp = parts // 2
    part = p // hp
    peer = lax.rem(p + hp, parts)

    def state_copy(i):
        at = pl.ds(pl.multiple_of(i * cols, cols), cols)
        return remote(first.at[:, at], dsin.at[:, at], ss.at[i], sr.at[i], tensor=peer)

    @pl.when(j == 0)
    def _():
        greet([], [peer])

    at = j * cols
    mapping = head_map(cols, lax.rem(at, ig), at // ig * 16)
    gone = expand(kd[0:8, :], mapping)
    gain = par[5:6, :]
    grad = jnp.zeros((LANES, cols), F32)
    by_gain = jnp.zeros((1, cols), F32)
    by_skip = jnp.zeros((1, cols), F32)
    for c in range(count // SPAN - 1, -1, -1):
        span = slice(c * SPAN, (c + 1) * SPAN)
        stat = stats[span, :]
        scale = lax.rsqrt(stat[:, 0:1] / inner_all + EPS)
        pull = scale * scale * scale * stat[:, 1:2] / inner_all
        gate = z[span, :]
        sig = sigmoid(gate)
        act = gate * sig
        out = y[span, :]
        gated = out * act
        normal = gated * scale
        mixed = (normal * gain).astype(BF16)
        mixed_o[span, :] = mixed
        upstream = dm[span, :]
        by_gain = by_gain + jnp.sum(upstream * normal, axis=0, keepdims=True)
        dgated = scale * (upstream * gain) - gated * pull
        dz = (dgated * out * (sig * (1.0 + gate * (1.0 - sig)))).astype(BF16)
        dz_o[span, :] = dz
        dy = dgated * act
        by_skip = by_skip + jnp.sum(dy * xs[span, :].astype(F32), axis=0, keepdims=True)
        dy_o[span, :] = dy.astype(BF16)
        ds_o[c] = grad
        lead = (dy * expand(em[span, :], mapping)).astype(BF16)
        grad = gone[c : c + 1, :] * grad + tn(bc[span, LANES:], lead)
    sums_o[...] = jnp.concatenate([by_gain, by_skip, jnp.zeros((6, cols), F32)], axis=0)
    first[:, pl.ds(pl.multiple_of(j * cols, cols), cols)] = grad.astype(BF16)

    @pl.when(part == 1)
    def _():
        state_copy(j).start()

    go_o[...] = tn(pulled[...], mixed_o[...]).astype(BF16)
    gz_o[...] = tn(tok[HALO:, :], dz_o[...]).astype(BF16)

    @pl.when(j == tiles - 1)
    def _():
        def send_done(i, carry):
            state_copy(i).wait_send()
            return carry

        def arrived(i, carry):
            state_copy(i).wait_recv()
            return carry

        @pl.when(part == 1)
        def _():
            lax.fori_loop(0, tiles, send_done, 0)
            dsin_o[...] = jnp.zeros_like(dsin_o)

        @pl.when(part == 0)
        def _():
            lax.fori_loop(0, tiles, arrived, 0)
            dsin_o[...] = dsin[...]


def run_gate(y, z, dm, stat, xs, par, bc, em, kd, tok, pulled, ig, inner_all, parts):
    count, inner = y.shape
    width = tok.shape[1]
    cols = col_tile(ig)
    tiles = inner // cols
    chunks = count // SPAN

    tile = pl.BlockSpec((count, cols), lambda j: (0, j))
    grads = pl.BlockSpec((width, cols), lambda j: (0, j))
    low = jax.ShapeDtypeStruct((count, inner), BF16)
    shape = jax.ShapeDtypeStruct
    return pl.pallas_call(
        partial(gate_body, parts, ig, inner_all),
        grid=(tiles,),
        out_shape=(
            low,
            low,
            low,
            shape((8, inner), F32),
            shape((chunks, LANES, inner), F32),
            shape((width, inner), BF16),
            shape((width, inner), BF16),
            shape((LANES, inner), BF16),
        ),
        in_specs=[
            tile,
            tile,
            tile,
            whole(),
            tile,
            pl.BlockSpec((8, cols), lambda j: (0, j)),
            whole(),
            whole(),
            whole(),
            whole(),
            whole(),
        ],
        out_specs=(
            tile,
            tile,
            tile,
            pl.BlockSpec((8, cols), lambda j: (0, j)),
            pl.BlockSpec((chunks, LANES, cols), lambda j: (0, 0, j)),
            grads,
            grads,
            whole(),
        ),
        scratch_shapes=[
            pltpu.VMEM((LANES, inner), BF16),
            pltpu.VMEM((LANES, inner), BF16),
            pltpu.SemaphoreType.DMA((tiles,)),
            pltpu.SemaphoreType.DMA((tiles,)),
        ],
        compiler_params=pltpu.CompilerParams(vmem_limit_bytes=VMEM_BYTES, collective_id=4, has_side_effects=True),
        cost_estimate=cost(12e9, 30e6),
        name="gate",
    )(y, z, dm, stat, xs, par, bc, em, kd, tok, pulled)


def pull_body(
    size, parts, ha, wrows,
    sc, xs, dy, bc, dtin, dt, lc, lr, em, et, kd, st, sin, ds, dsin, pre, par,
    inputs, mixed_h, wo_h, gz_h, go_h, tok_h,
    dx_o, dbc_o, ddt_o, csum_o, hsum_o, out_o, gz_o, go_o, ga_o,
    cbt, off, dcb, ahead, dxi, rsum, mixed, wo, branch, arrived, tok, ga, dlow, dother,
    zacc, oacc, zcore, ocore, acore, zlink, olink, alink, zz, oz, az,
    loads, zls, ols, ccs, ccr, cls, clr, hs, hr, ho, ms, mr, bs, br,
):
    b, step = pl.program_id(0), pl.program_id(1)
    chunks = pl.num_programs(1)
    c = chunks - 1 - step
    cols = xs.shape[1]
    half = SPAN // 2
    p = lax.axis_index("tensor")
    me = lax.axis_index("dp")
    hp = parts // 2
    place = lax.rem(p, hp)
    part = p // hp
    count = dbc_o.shape[0]
    local_rows = inputs.shape[0]
    start = part * count + c * SPAN
    n = b * chunks + step
    rows_here = pl.ds(pl.multiple_of(c * SPAN, SPAN), SPAN)

    def scatter(k, src, acc, core_buf, link_buf, own_sem):
        columns = halves(cols, 2 * cols)
        return Scatter(
            k,
            lambda h, v: sharded_rows(src, me, v, wrows, columns[h]),
            lambda h, u: acc.at[u, :, pl.ds(columns[h][0], cols)],
            lambda h, u: pltpu.make_async_copy(
                sharded_rows(src, me, 2 * u, wrows, columns[h]),
                acc.at[u, :, pl.ds(columns[h][0], cols)],
                own_sem.at[h, u],
            ),
            size, core_buf, link_buf, ccs, ccr, cls, clr,
        )

    def a_block(h, v):
        return sharded_rows(ga, me, v, wrows, halves(split_of(cols), cols)[h])

    scat_o = scatter(0, go_h, oacc, ocore, olink, ols)
    scat_z = scatter(1, gz_h, zacc, zcore, zlink, zls)
    scat_a = Scatter(2, a_block, lambda h, u: a_block(h, 2 * u), None, size, acore, alink, ccs, ccr, cls, clr)
    home_o = FromHeads(0, lambda side: oacc.at[0, :, pl.ds(side * cols, cols)], oz, parts, hs, hr, ho)
    home_z = FromHeads(1, lambda side: zacc.at[0, :, pl.ds(side * cols, cols)], zz, parts, hs, hr, ho)
    home_a = FromHeads(2, lambda side: sharded_rows(ga, me, 0, wrows, (0, cols)), az, parts, hs, hr, ho)
    stages = scat_o.stages()

    def mates():
        return [(s, part * hp + lax.rem(place + s, hp)) for s in range(1, hp)]

    def branch_copy(s, to):
        rows_to = pl.ds(pl.multiple_of(lax.rem(place + s, hp) * local_rows, 16), local_rows)
        return remote(branch.at[rows_to], arrived.at[s - 1], bs.at[s - 1], br.at[s - 1], tensor=to)

    def maps_copy(s, to, i):
        at = pl.ds(pl.multiple_of(i * SPAN, SPAN), SPAN)
        return remote(dlow.at[at], dother.at[s - 1, at], ms.at[s - 1, i], mr.at[s - 1, i], tensor=to)

    @pl.when(n == 0)
    def _():
        load_mixed = pltpu.make_async_copy(mixed_h, mixed, loads.at[0])
        load_wo = pltpu.make_async_copy(wo_h, wo, loads.at[1])
        load_mixed.start()
        load_wo.start()
        greet([1] + link_bits(size), others(parts))
        for h in range(2):
            scat_o.start(h)
        for h in range(2):
            scat_z.start(h)
        load_mixed.wait()
        load_wo.wait()

        def out_tile(j, carry):
            at = pl.ds(pl.multiple_of(j * SPAN, SPAN), SPAN)
            branch[:, at] = nt(mixed[...], wo[at, :]).astype(BF16)
            return carry

        lax.fori_loop(0, wo.shape[0] // SPAN, out_tile, 0)
        for s, to in mates():
            branch_copy(s, to).start()
        pltpu.make_async_copy(tok_h, tok, loads.at[2]).start()
        for h in range(2):
            scat_o.fold_core(h)
            scat_o.send(h, 0)

    @pl.when(n == 1)
    def _():
        for h in range(2):
            scat_z.fold_core(h)
            scat_z.send(h, 0)

    @pl.when(n == 3)
    def _():
        for s in range(stages - 1):
            for h in range(2):
                scat_o.fold(h, s)
                scat_o.send(h, s + 1)

    @pl.when(n == 4)
    def _():
        for s in range(stages - 1):
            for h in range(2):
                scat_z.fold(h, s)
                scat_z.send(h, s + 1)
        for h in range(2):
            scat_o.fold(h, stages - 1)
            home_o.start(h)

    @pl.when(n == chunks + 1)
    def _():
        for h in range(2):
            scat_a.fold_core(h)
            scat_a.send(h, 0)

    @pl.when(n == chunks + 2)
    def _():
        for h in range(2):
            scat_z.fold(h, stages - 1)
            home_z.start(h)
        for s in range(stages - 1):
            for h in range(2):
                scat_a.fold(h, s)
                scat_a.send(h, s + 1)

    b_map, c_map = bc[:, :LANES], bc[:, LANES:]
    cbt[...] = nt(b_map, c_map)
    s, t = iota((SPAN, SPAN), 0), iota((SPAN, SPAN), 1)
    seen = (t >= s) & (seg_at(sc, start + t) == seg_at(sc, start + s))
    off[...] = jnp.where(seen, 0.0, FAR)
    dcb[...] = jnp.zeros_like(dcb)

    @pl.when(step == 0)
    def _():
        ahead[...] = jnp.zeros_like(ahead)
        csum_o[...] = jnp.zeros_like(csum_o)
        hsum_o[...] = jnp.zeros_like(hsum_o)
        rsum[...] = jnp.zeros_like(rsum)

    lane = iota((1, LANES), 1)
    taps, bias = par[0:4, :], par[4:5, :]
    skip = expand(jnp.broadcast_to(par[6:7, :LANES], (8, LANES)), head_map(cols, 0, 0))[0:1, :]
    mapping = head_map(cols, 0, b * 16)
    single = head_map(cols, 0, 0, both=False)
    columns = pltpu.roll(lc[...], lax.rem(LANES - 16 * b, LANES), axis=1)

    def mine(values):
        return pltpu.roll(values, lax.rem(LANES - 16 * b, LANES), axis=1) * (lane < ha).astype(F32)

    sides = [(lane < 64).astype(BF16), (lane >= 64).astype(BF16)]
    steps_wide = expand(dt[...], mapping)
    steps = mine(dt[...])
    xf = xs[...].astype(F32)
    scaled = (xf * steps_wide).astype(BF16)
    dyl = dy[...]
    csums = jnp.zeros((SPAN, LANES), F32)
    for k in range(cols // LANES):
        at = slice(k * LANES, (k + 1) * LANES)
        x_pair, dy_pair = scaled[:, at], dyl[:, at]
        top = jnp.zeros((half, LANES), F32)
        low = jnp.zeros((half, LANES), F32)
        for side in range(2):
            h = 2 * k + side
            x_one = x_pair * sides[side]
            dy_one = dy_pair * sides[side]
            column = columns[:, h : h + 1]
            row = lr[h : h + 1, :]
            decay = jnp.exp2(row - column[:half] + off[:half, :])
            top = top + nn((cbt[:half, :] * decay).astype(BF16), dy_one)
            share = nt(x_one[:half, :], dy_pair) * decay
            dcb[:half, :] += share
            both = share * cbt[:half, :]
            row_sum = jnp.sum(both, axis=0, keepdims=True)
            col_top = jnp.sum(both, axis=1, keepdims=True)
            decay = jnp.exp2(row[:, half:] - column[half:] + off[half:, half:])
            low = low + nn((cbt[half:, half:] * decay).astype(BF16), dy_one[half:, :])
            share = nt(x_one[half:, :], dy_pair[half:, :]) * decay
            dcb[half:, half:] += share
            both = share * cbt[half:, half:]
            rsum[h : h + 1, :half] = row_sum[:, :half]
            rsum[h : h + 1, half:] = row_sum[:, half:] + jnp.sum(both, axis=0, keepdims=True)
            col_low = jnp.sum(both, axis=1, keepdims=True)
            csums = csums + jnp.where(lane == h, jnp.concatenate([col_top, col_low], axis=0), 0.0)
        dxi[:half, at] = top
        dxi[half:, at] = low
    lead_wide = expand(em[...], mapping)
    tail_wide = expand(et[...], mapping)
    decays = expand(kd[...], mapping)
    pick = (iota((8, 1), 0) == c).astype(F32)
    state = st[0] + jnp.sum(decays[8:16] * pick, axis=0, keepdims=True) * sin[...].astype(F32)
    dstate = ds[0] + jnp.sum(decays[16:24] * pick, axis=0, keepdims=True) * dsin[...].astype(F32)
    state_l, dstate_l = state.astype(BF16), dstate.astype(BF16)
    dyf = dyl.astype(F32)
    led = dyf * lead_wide
    read = nn(c_map, state_l)
    dx_far = nn(b_map, dstate_l) * tail_wide
    db = nn(dcb[...].astype(BF16), c_map) + nt((scaled.astype(F32) * tail_wide).astype(BF16), dstate_l)
    dc = tn(dcb[...].astype(BF16), b_map) + nt(led.astype(BF16), state_l)

    @pl.when(b == 0)
    def _():
        dbc_o[rows_here, :LANES] = db
        dbc_o[rows_here, LANES:] = dc

    @pl.when(b > 0)
    def _():
        dlow[rows_here, :LANES] = (dbc_o[rows_here, :LANES] + db).astype(BF16)
        dlow[rows_here, LANES:] = (dbc_o[rows_here, LANES:] + dc).astype(BF16)
        for s, to in mates():
            maps_copy(s, to, c).start()

    near = dxi[...]
    from_near = nt((xf * near).astype(BF16), single)
    from_far = nt((xf * dx_far).astype(BF16), single)
    reads = nt((led * read).astype(BF16), single)
    crossing = jnp.sum(state * dstate, axis=0, keepdims=True)
    held = lax.dot_general(
        jnp.broadcast_to(crossing, (8, cols)),
        single.astype(F32),
        (((1,), (1,)), ((), ())),
        precision=HIGH,
        preferred_element_type=F32,
    )[0:1, :]
    held = held * mine(jnp.broadcast_to(jnp.sum(kd[0:8, :] * pick, axis=0, keepdims=True), (8, LANES)))[0:1, :]
    lower = (s > t).astype(F32)
    upper = (s <= t).astype(F32)
    dlog = (
        jnp.dot(upper, rsum[...].T - csums + reads, precision=HIGH, preferred_element_type=F32)
        + jnp.dot(lower, steps * from_far, precision=HIGH, preferred_element_type=F32)
        + held
    )
    rates = jnp.concatenate([par[7:8, LANES : 2 * LANES], jnp.zeros((7, LANES), F32)], axis=0)
    rate = -jnp.exp(rates)[0:1, :]
    dstep = from_near + from_far + dlog * rate
    ddt = dstep * mine(sigmoid(dtin[...]))
    ddt_o[0] = ddt
    hsum_o[0, 0:1, :] += jnp.sum(ddt, axis=0, keepdims=True)
    hsum_o[0, 1:2, :] += jnp.sum(dlog * steps * rate, axis=0, keepdims=True)

    dxs = (near + dx_far) * steps_wide + dyf * skip[...]
    window = pre[pl.ds(pl.multiple_of(c * SPAN, SPAN), SPAN + HALO), :]
    pos = start + iota((SPAN, 1), 0)
    masks = [same_as_behind(sc, pos, j) for j in range(4)]
    lagged = [window[HALO:, :]]
    for j in range(1, 4):
        lagged.append(pltpu.roll(window, j, axis=0)[HALO:, :] * masks[j])
    conv = bias[...]
    for j in range(4):
        conv = conv + taps[j : j + 1, :] * lagged[j]
    sig = sigmoid(conv)
    dconv = dxs * (sig * (1.0 + conv * (1.0 - sig)))
    sums = [jnp.sum(dconv * lagged[j], axis=0, keepdims=True) for j in range(4)]
    sums.append(jnp.sum(dconv, axis=0, keepdims=True))
    csum_o[...] += jnp.concatenate(sums + [jnp.zeros((3, cols), F32)], axis=0)
    dpre = taps[0:1, :] * dconv
    edge = jnp.zeros((HALO, cols), F32)
    blank = jnp.zeros((8, cols), F32)
    for j in range(1, 4):
        masked = dconv * masks[j]
        longer = jnp.concatenate([masked, ahead[8 * (j - 1) : 8 * j, :]], axis=0)
        dpre = dpre + taps[j : j + 1, :] * pltpu.roll(longer, SPAN + 8 - j, axis=0)[:SPAN, :]
        opening = masked[:8, :]
        ahead[8 * (j - 1) : 8 * j, :] = opening
        before = pltpu.roll(jnp.concatenate([blank, blank, opening], axis=0), 24 - j, axis=0)[:HALO, :]
        edge = edge + taps[j : j + 1, :] * before
    dx_o[pl.ds(pl.multiple_of(HALO + c * SPAN, HALO), SPAN), :] = dpre.astype(BF16)

    @pl.when(c == 0)
    def _():
        dx_o[:HALO, :] = edge.astype(BF16)

    @pl.when(n == chunks - 1)
    def _():
        pltpu.make_async_copy(tok_h, tok, loads.at[2]).wait()
        wide = col_tile(cols)

        def grad_tile(j, carry):
            at = pl.ds(pl.multiple_of(j * wide, wide), wide)
            ga[:, at] = tn(tok[...], dx_o[:, at]).astype(BF16)
            return carry

        lax.fori_loop(0, cols // wide, grad_tile, 0)
        for h in range(2):
            scat_a.start(h)

    @pl.when(n == 2 * chunks - 1)
    def _():
        for h in range(2):
            scat_a.fold(h, stages - 1)
        home_a.start(0)
        for s, to in mates():
            branch_copy(s, to).wait_recv()
        own_rows = pl.ds(pl.multiple_of(place * local_rows, 16), local_rows)
        total = inputs[...].astype(F32) + branch[own_rows, :].astype(F32)
        for s in range(1, hp):
            total = total + arrived[s - 1].astype(F32)
        out_o[...] = total.astype(BF16)
        home_o.wait()
        go_o[...] = oz[0].astype(F32) + oz[1].astype(F32)
        home_z.wait()
        gz_o[...] = zz[0].astype(F32) + zz[1].astype(F32)

        @pl.when(lax.rem(p, 2) == 0)
        def _():
            home_a.wait()
            ga_o[...] = az[0].astype(F32) + az[1].astype(F32)

        @pl.when(lax.rem(p, 2) == 1)
        def _():
            ga_o[...] = jnp.zeros_like(ga_o)

        for s, to in mates():
            for i in range(count // SPAN):
                maps_copy(s, to, i).wait_recv()
        summed = dlow[...].astype(F32)
        for s in range(1, hp):
            summed = summed + dother[s - 1].astype(F32)
        dbc_o[...] = summed
        for item in (scat_o, scat_z, scat_a, home_o, home_z):
            item.finish()
        home_a.finish((0,))
        for s, to in mates():
            branch_copy(s, to).wait_send()
            for i in range(count // SPAN):
                maps_copy(s, to, i).wait_send()


def run_pull(
    sc, xs, dy, bc, dtin, dt, lc, lr, em, et, kd, st, sin, ds, dsin, pre, par,
    inputs, mixed, wo, gz, go, tok, ha, ig, size, parts,
):
    count, inner = xs.shape
    local_rows, width = inputs.shape
    total = count + HALO
    chunks = count // SPAN
    wrows = width // size
    hp = parts // 2

    def rev(step):
        return chunks - 1 - step

    tile = pl.BlockSpec((SPAN, ig), lambda b, i: (rev(i), b))
    per_token = pl.BlockSpec((SPAN, LANES), lambda b, i: (rev(i), 0))
    states = pl.BlockSpec((1, LANES, ig), lambda b, i: (rev(i), 0, b))
    edge = pl.BlockSpec((LANES, ig), lambda b, i: (0, b))
    full = pl.BlockSpec((total, ig), lambda b, i: (0, b))
    anywhere = pl.BlockSpec(memory_space=pl.ANY)
    shape = jax.ShapeDtypeStruct
    vm = pltpu.VMEM
    dma = pltpu.SemaphoreType.DMA
    blocks, links = size // 2, max(size // 2 - 1, 1)
    splits = [split_of(ig), ig - split_of(ig)]
    scratch = dict(
        cbt=vm((SPAN, SPAN), F32),
        off=vm((SPAN, SPAN), F32),
        dcb=vm((SPAN, SPAN), F32),
        ahead=vm((24, ig), F32),
        dxi=vm((SPAN, ig), F32),
        rsum=vm((LANES, SPAN), F32),
        mixed=vm((count, inner), BF16),
        wo=vm((width, inner), BF16),
        branch=vm((count, width), BF16),
        arrived=vm((hp - 1, local_rows, width), BF16),
        tok=vm((total, width), BF16),
        ga=vm((width, ig), BF16),
        dlow=vm((count, 2 * LANES), BF16),
        dother=vm((hp - 1, count, 2 * LANES), BF16),
        zacc=vm((blocks, wrows, inner), BF16),
        oacc=vm((blocks, wrows, inner), BF16),
        zcore=[vm((blocks, wrows, ig), BF16)] * 2,
        ocore=[vm((blocks, wrows, ig), BF16)] * 2,
        acore=[vm((blocks, wrows, w), BF16) for w in splits],
        zlink=[vm((links, wrows, ig), BF16)] * 2,
        olink=[vm((links, wrows, ig), BF16)] * 2,
        alink=[vm((links, wrows, w), BF16) for w in splits],
        zz=vm((2, wrows, ig), BF16),
        oz=vm((2, wrows, ig), BF16),
        az=vm((2, wrows, ig), BF16),
        loads=dma((3,)),
        zls=dma((2, blocks)),
        ols=dma((2, blocks)),
        ccs=dma((3, 2, blocks)),
        ccr=dma((3, 2, blocks)),
        cls=dma((3, 2, links)),
        clr=dma((3, 2, links)),
        hs=dma((6,)),
        hr=dma((6,)),
        ho=dma((3,)),
        ms=dma((hp - 1, chunks)),
        mr=dma((hp - 1, chunks)),
        bs=dma((hp - 1,)),
        br=dma((hp - 1,)),
    )
    return pl.pallas_call(
        partial(pull_body, size, parts, ha, wrows),
        grid=(2, chunks),
        out_shape=(
            shape((total, inner), BF16),
            shape((count, 2 * LANES), F32),
            shape((2, count, LANES), F32),
            shape((8, inner), F32),
            shape((2, 8, LANES), F32),
            shape((local_rows, width), BF16),
            shape((wrows, ig), F32),
            shape((wrows, ig), F32),
            shape((wrows, ig), F32),
        ),
        in_specs=[
            scalars(),
            tile,
            tile,
            pl.BlockSpec((SPAN, 2 * LANES), lambda b, i: (rev(i), 0)),
            per_token,
            per_token,
            per_token,
            pl.BlockSpec((16, SPAN), lambda b, i: (b, rev(i))),
            per_token,
            per_token,
            whole(),
            states,
            edge,
            states,
            edge,
            full,
            pl.BlockSpec((8, ig), lambda b, i: (0, b)),
            whole(),
        ]
        + [anywhere] * 5,
        out_specs=(
            full,
            whole(),
            pl.BlockSpec((1, SPAN, LANES), lambda b, i: (b, rev(i), 0)),
            pl.BlockSpec((8, ig), lambda b, i: (0, b)),
            pl.BlockSpec((1, 8, LANES), lambda b, i: (b, 0, 0)),
            whole(),
            whole(),
            whole(),
            whole(),
        ),
        scratch_shapes=list(scratch.values()),
        compiler_params=pltpu.CompilerParams(vmem_limit_bytes=VMEM_BYTES, collective_id=3, has_side_effects=True),
        cost_estimate=cost(20e9, 30e6),
        name="pull",
    )(
        sc, xs, dy, bc, dtin, dt, lc, lr, em, et, kd, st, sin, ds, dsin, pre, par,
        inputs, mixed, wo, gz, go, tok,
    )


def last_body(
    size, parts, rows, ha, ig,
    ends, inputs, cot, ngain, tok_h, dz_h, dx_h, wz_h, wx_h, ws_h, dbc, ddt, pre, taps, bias, csum, gsum, hsum, ga,
    gin_o, gx_o, gdt_o, gbc_o, chan_o, rep_o,
    tok, dz, dx, wz, wx, ws, gx, gsm, dsm, conv, dn_out, dn_in, dn_own, edge_out, edge_in,
    xcore, xlink, score, slink, xz, dtz, bcz, chan, chan_in, chan_z, rep, rep_in,
    loads, ccs, ccr, cls, clr, zs, zr, zo, bs, br, ns, nr, es, er, ts, tr,
):
    p = lax.axis_index("tensor")
    me = lax.axis_index("dp")
    hp = parts // 2
    place = lax.rem(p, hp)
    half = p // hp
    inner = 2 * ig
    local_rows, width = inputs.shape
    count = local_rows * hp
    total = count + HALO
    base = half * count
    own_at = pl.multiple_of(HALO + place * local_rows, 16)

    moving = [
        pltpu.make_async_copy(src, dst, loads.at[i])
        for i, (src, dst) in enumerate(((tok_h, tok), (dx_h, dx), (wx_h, wx), (dz_h, dz), (wz_h, wz), (ws_h, ws)))
    ]
    for copy in moving:
        copy.start()
    greet([1] + link_bits(size), others(parts))

    def mates():
        return [(s, half * hp + lax.rem(place + s, hp)) for s in range(1, hp)]

    dp_steps = [("dp", 1)] + [("dp", bit) for bit in link_bits(size)]
    z_steps = []
    bit = 1
    while bit < parts:
        z_steps.append(("tensor", bit))
        bit *= 2
    chan[0:5, :] = csum[0:5, :]
    chan[5:7, :] = gsum[0:2, :]
    chan[7:8, :] = jnp.zeros((1, inner), F32)
    for b in range(2):
        for i in range(2):
            at = b * ig + i * LANES
            chan[7:8, at : at + LANES] = hsum[b, i : i + 1, :]
    sum_chan = Butterfly(0, chan, chan_in, dp_steps, bs, br)
    sum_rep = Butterfly(1, rep, rep_in, dp_steps + z_steps, bs, br)
    sum_chan.push(0)

    def x_block(h, v):
        return sharded_rows(gx, me, v, rows, halves(split_of(ig), ig)[h])

    def s_block(h, v):
        return sharded_rows(gsm, me, v, rows, halves(2 * LANES, 4 * LANES)[h])

    scat_x = Scatter(0, x_block, lambda h, u: x_block(h, 2 * u), None, size, xcore, xlink, ccs, ccr, cls, clr)
    scat_s = Scatter(1, s_block, lambda h, u: s_block(h, 2 * u), None, size, score, slink, ccs, ccr, cls, clr)
    stages = scat_x.stages()
    home_x = FromHeads(0, lambda side: sharded_rows(gx, me, 0, rows, (0, ig)), xz, parts, zs, zr, zo)
    home_dt = FromHeads(
        1,
        lambda side: sharded_rows(gsm, me, 0, rows, (side * LANES, (side + 1) * LANES)),
        dtz, parts, zs, zr, zo,
    )
    home_chan = FromHeads(2, lambda side: chan.at[:, pl.ds(side * ig, ig)], chan_z, parts, zs, zr, zo)

    cols = col_tile(ig)
    moving[0].wait()
    moving[1].wait()

    def grad_x(j, carry):
        at = pl.multiple_of(j * cols, cols)
        gx[:, pl.ds(at, cols)] = tn(tok[...], dx[:, pl.ds(ig + at, cols)]).astype(BF16)
        return carry

    lax.fori_loop(0, ig // cols, grad_x, 0)
    for h in range(2):
        scat_x.start(h)
    sum_chan.fold(0)
    if len(dp_steps) > 1:
        sum_chan.push(1)

    upstream = dbc[...]
    pos = base + iota((count, 1), 0)
    masks = [same_as_behind(ends, pos, j) for j in range(4)]
    lagged = [pre[HALO - j : HALO - j + count, :] * masks[j] for j in range(1, 4)]
    lagged = [pre[HALO:, :]] + lagged
    through = bias[...].reshape(1, 2 * LANES)
    for j in range(4):
        through = through + taps[j : j + 1, :] * lagged[j]
    sig = sigmoid(through)
    dconv = upstream * (sig * (1.0 + through * (1.0 - sig)))
    rep[...] = jnp.zeros_like(rep)
    for j in range(5):
        value = dconv * lagged[j] if j < 4 else dconv
        rep[1:2, j * 2 * LANES : (j + 1) * 2 * LANES] = jnp.sum(value, axis=0, keepdims=True) / hp
    conv[...] = jnp.zeros_like(conv)
    dpre = jnp.zeros((total, 2 * LANES), F32)
    for j in range(4):
        conv[HALO : HALO + count, :] = dconv * masks[j] if j else dconv
        dpre = dpre + taps[j : j + 1, :] * conv[j : j + total, :]
    dsm[:, 2 * LANES :] = dpre.astype(BF16)
    dsm[:HALO, : 2 * LANES] = jnp.zeros((HALO, 2 * LANES), BF16)
    for b in range(2):
        dsm[HALO:, b * LANES : (b + 1) * LANES] = ddt[b].astype(BF16)

    for h in range(2):
        scat_x.fold_core(h)
        scat_x.send(h, 0)
    for i in range(1, len(dp_steps)):
        sum_chan.fold(i)
        if i + 1 < len(dp_steps):
            sum_chan.push(i + 1)
    home_chan.start(0)
    home_chan.start(1)
    for copy in moving[2:]:
        copy.wait()

    tile = 256

    def dn_tile(start, n, at, with_z):
        span = pl.ds(start, n)
        value = (
            nt(dx[span, :], wx[at, :])
            + nt(dsm[span, : 2 * LANES], ws[at, : 2 * LANES])
            + nt(dsm[span, 2 * LANES :], ws[at, 2 * LANES :]) * (1.0 / hp)
        )
        if with_z:
            value = value + nt(dz[pl.ds(start - HALO, n), :], wz[at, :])
        rep[0:1, at] += jnp.sum(value * tok[span, at].astype(F32), axis=0, keepdims=True)
        return value

    def dn_copy(s, to, j):
        at = pl.ds(pl.multiple_of(j * tile, tile), tile)
        return remote(dn_out.at[s - 1, :, at], dn_in.at[s - 1, :, at], ns.at[s - 1, j], nr.at[s - 1, j], tensor=to)

    def edge_copy(k):
        return remote(edge_out, edge_in.at[k], es.at[0], er.at[k], tensor=hp - 1)

    def other_rows(s, to):
        there = pl.multiple_of(HALO + lax.rem(place + s, hp) * local_rows, 16)

        def step(j, carry):
            at = pl.ds(pl.multiple_of(j * tile, tile), tile)
            dn_out[s - 1, :, at] = dn_tile(there, local_rows, at, True).astype(BF16)
            dn_copy(s, to, j).start()
            return carry

        return step

    dn_tiles = width // tile
    middle = dn_tiles // 2
    for s, to in mates():
        lax.fori_loop(0, middle, other_rows(s, to), 0)
    gsm[...] = tn(tok[...], dsm[...]).astype(BF16)
    scat_s.start(0)
    scat_s.start(1)
    for s, to in mates():
        lax.fori_loop(middle, dn_tiles, other_rows(s, to), 0)

    def edge_rows(j, carry):
        at = pl.ds(pl.multiple_of(j * tile, tile), tile)
        edge_out[:, at] = dn_tile(0, HALO, at, False).astype(BF16)
        return carry

    lax.fori_loop(0, dn_tiles, edge_rows, 0)
    for k in range(hp):

        @pl.when(p == hp + k)
        def _(k=k):
            edge_copy(k).start()

    for h in range(2):
        scat_s.fold_core(h)
        scat_s.send(h, 0)
    for s in range(stages - 1):
        for h in range(2):
            scat_x.fold(h, s)
            scat_x.send(h, s + 1)

    def own_rows(j, carry):
        at = pl.ds(pl.multiple_of(j * tile, tile), tile)
        dn_own[:, at] = dn_tile(own_at, local_rows, at, True)
        return carry

    lax.fori_loop(0, middle, own_rows, 0)
    for h in range(2):
        scat_x.fold(h, stages - 1)
    home_x.start(1)
    for s in range(stages - 1):
        for h in range(2):
            scat_s.fold(h, s)
            scat_s.send(h, s + 1)
    lax.fori_loop(middle, dn_tiles, own_rows, 0)
    sum_rep.push(0)
    for h in range(2):
        scat_s.fold(h, stages - 1)
    home_dt.start(0)
    home_dt.start(1)
    bc_mine = sharded_rows(gsm, me, 0, rows, (2 * LANES, 4 * LANES))
    bc_copy = remote(bc_mine, bcz, ts.at[0], tr.at[0], tensor=lax.rem(p + hp, parts))
    bc_copy.start()
    for i in range(len(sum_rep.steps)):
        sum_rep.fold(i)
        if i + 1 < len(sum_rep.steps):
            sum_rep.push(i + 1)
    rep_o[...] = rep[...]
    home_chan.wait()
    chan_o[...] = chan_z[0] + chan_z[1]

    for s, to in mates():
        for j in range(dn_tiles):
            dn_copy(s, to, j).wait_recv()

    @pl.when(p == hp - 1)
    def _():
        for k in range(hp):
            edge_copy(k).wait_recv()
        last = local_rows - HALO
        for k in range(hp):
            dn_own[last:, :] += edge_in[k].astype(F32)

    dnormed = dn_own[...]
    for s in range(1, hp):
        dnormed = dnormed + dn_in[s - 1].astype(F32)
    values = inputs[...].astype(F32)
    scale = lax.rsqrt(jnp.mean(values * values, axis=1, keepdims=True) + EPS)
    side = dnormed * row(ngain)
    pull = scale * scale * scale * (jnp.sum(side * values, axis=1, keepdims=True) / width)
    gin_o[...] = (scale * side - values * pull + cot[...].astype(F32)).astype(BF16)

    home_dt.wait()
    gdt_o[...] = dtz[0].astype(F32) + dtz[1].astype(F32)
    bc_copy.wait_recv()
    gbc_o[...] = bc_mine[...].astype(F32) + bcz[...].astype(F32)

    @pl.when(lax.rem(p, 2) == 1)
    def _():
        home_x.wait()
        gx_o[...] = xz[0].astype(F32) + xz[1].astype(F32)

    @pl.when(lax.rem(p, 2) == 0)
    def _():
        gx_o[...] = ga[...]

    home_x.finish((1,))
    for item in (scat_x, scat_s, home_dt, home_chan):
        item.finish()
    for s, to in mates():
        for j in range(dn_tiles):
            dn_copy(s, to, j).wait_send()
    bc_copy.wait_send()

    @pl.when(half == 1)
    def _():
        edge_copy(0).wait_send()


def run_last(
    ends, inputs, cot, ngain, tok, dz, dx, wz, wx, ws, dbc, ddt, pre, taps, bias, csum, gsum, hsum, ga,
    size, parts, ha, ig,
):
    local_rows, width = inputs.shape
    total = tok.shape[0]
    count = total - HALO
    inner = 2 * ig
    hp = parts // 2
    rows = width // size
    shape = jax.ShapeDtypeStruct
    anywhere = pl.BlockSpec(memory_space=pl.ANY)
    dma = pltpu.SemaphoreType.DMA
    blocks, links = size // 2, max(size // 2 - 1, 1)
    steps = size.bit_length() - 1 + parts.bit_length() - 1
    vm = pltpu.VMEM

    splits = [split_of(ig), ig - split_of(ig)]

    def pair(n, cols):
        return [vm((n, rows, cols), BF16), vm((n, rows, cols), BF16)]

    scratch = dict(
        tok=vm(tok.shape, BF16),
        dz=vm(dz.shape, BF16),
        dx=vm(dx.shape, BF16),
        wz=vm(wz.shape, BF16),
        wx=vm(wx.shape, BF16),
        ws=vm(ws.shape, BF16),
        gx=vm((width, ig), BF16),
        gsm=vm((width, 4 * LANES), BF16),
        dsm=vm((total, 4 * LANES), BF16),
        conv=vm((total + 8, 2 * LANES), F32),
        dn_out=vm((hp - 1, local_rows, width), BF16),
        dn_in=vm((hp - 1, local_rows, width), BF16),
        dn_own=vm((local_rows, width), F32),
        edge_out=vm((HALO, width), BF16),
        edge_in=vm((hp, HALO, width), BF16),
        xcore=[vm((blocks, rows, w), BF16) for w in splits],
        xlink=[vm((links, rows, w), BF16) for w in splits],
        score=pair(blocks, 2 * LANES),
        slink=pair(links, 2 * LANES),
        xz=vm((2, rows, ig), BF16),
        dtz=vm((2, rows, LANES), BF16),
        bcz=vm((rows, 2 * LANES), BF16),
        chan=vm((8, inner), F32),
        chan_in=vm((steps, 8, inner), F32),
        chan_z=vm((2, 8, ig), F32),
        rep=vm((8, width), F32),
        rep_in=vm((steps, 8, width), F32),
        loads=dma((6,)),
        ccs=dma((2, 2, blocks)),
        ccr=dma((2, 2, blocks)),
        cls=dma((2, 2, links)),
        clr=dma((2, 2, links)),
        zs=dma((6,)),
        zr=dma((6,)),
        zo=dma((3,)),
        bs=dma((2, steps)),
        br=dma((2, steps)),
        ns=dma((hp - 1, width // 256)),
        nr=dma((hp - 1, width // 256)),
        es=dma((1,)),
        er=dma((hp,)),
        ts=dma((1,)),
        tr=dma((1,)),
    )
    return pl.pallas_call(
        partial(last_body, size, parts, rows, ha, ig),
        out_shape=(
            shape((local_rows, width), BF16),
            shape((rows, ig), F32),
            shape((rows, LANES), F32),
            shape((rows, 2 * LANES), F32),
            shape((8, ig), F32),
            shape((8, width), F32),
        ),
        in_specs=[scalars(), whole(), whole(), whole()] + [anywhere] * 6 + [whole()] * 9,
        out_specs=[whole()] * 6,
        scratch_shapes=list(scratch.values()),
        compiler_params=pltpu.CompilerParams(vmem_limit_bytes=VMEM_BYTES, collective_id=1, has_side_effects=True),
        cost_estimate=cost(2 * total * width * (3 * inner + 1024), 40e6),
        name="last",
    )(ends, inputs, cot, ngain, tok, dz, dx, wz, wx, ws, dbc, ddt, pre, taps, bias, csum, gsum, hsum, ga)


def finish_body(
    ha, out, gin, rep, ngain, gz, gx, gbc, gdt, chan, go,
    out_o, gin_o, gnorm_o, gz_o, gx_o, gbc_o, gdt_o, gcx_o, gcxb_o, gcb_o, gcbb_o, gdtb_o, galog_o, gskip_o, ggain_o, go_o,
):
    width = ngain.shape[0]
    ig = chan.shape[1]
    out_o[...] = out[...]
    gin_o[...] = gin[...]
    gnorm_o[...] = rep[0:1, :].reshape(width) / ngain[...]
    gz_o[...] = gz[...]
    gx_o[...] = gx[...]
    gbc_o[...] = gbc[...]
    gdt_o[...] = gdt[...].T[:ha, :]
    gcx_o[...] = chan[0:4, :]
    gcxb_o[...] = chan[4:5, :].reshape(ig)
    ggain_o[...] = chan[5:6, :].reshape(ig)
    heads = lax.dot_general(
        chan[...],
        head_map(ig, 0, 0, both=False).astype(F32),
        (((1,), (1,)), ((), ())),
        precision=HIGH,
        preferred_element_type=F32,
    )
    gskip_o[...] = heads[6:7, :ha].reshape(ha)
    gdtb_o[...] = chan[7:8, :ha].reshape(ha)
    galog_o[...] = chan[7:8, LANES : LANES + ha].reshape(ha)
    for j in range(4):
        gcb_o[j : j + 1, :] = rep[1:2, j * 2 * LANES : (j + 1) * 2 * LANES]
    gcbb_o[...] = rep[1:2, 8 * LANES : 10 * LANES].reshape(2 * LANES)
    go_o[...] = go[...]


def run_finish(out, gin, rep, ngain, gz, gx, gbc, gdt, chan, go, ha):
    shape = jax.ShapeDtypeStruct
    rows, ig = gz.shape
    return pl.pallas_call(
        partial(finish_body, ha),
        out_shape=(
            shape(out.shape, BF16),
            shape(gin.shape, BF16),
            shape(ngain.shape, F32),
            shape((rows, ig), F32),
            shape((rows, ig), F32),
            shape(gbc.shape, F32),
            shape((ha, rows), F32),
            shape((4, ig), F32),
            shape((ig,), F32),
            shape((4, 2 * LANES), F32),
            shape((2 * LANES,), F32),
            shape((ha,), F32),
            shape((ha,), F32),
            shape((ha,), F32),
            shape((ig,), F32),
            shape((rows, ig), F32),
        ),
        in_specs=[whole()] * 10,
        out_specs=[whole()] * 16,
        compiler_params=params(),
        cost_estimate=cost(1e7, 8e6),
        name="finish",
    )(out, gin, rep, ngain, gz, gx, gbc, gdt, chan, go)


def local(
    inputs,
    cotangent,
    seq_lengths,
    norm_gain,
    w_z,
    w_x,
    w_bc,
    w_dt,
    conv_x,
    conv_x_bias,
    conv_bc,
    conv_bc_bias,
    dt_bias,
    a_log,
    d_skip,
    gate_gain,
    w_out,
):
    parts = lax.axis_size("tensor")
    size = lax.axis_size("dp")
    ha = dt_bias.shape[0]
    ig = w_z.shape[1]
    (
        tok, pulled, wx, wz, wo, ws, par, pre_bc, bc, dtin, dt, lc, lr, em, et, kd, pre_x, xs, st, sin, z, dm,
    ) = run_first(
        seq_lengths, inputs, cotangent, norm_gain, w_x, w_z, w_out.T, w_bc, w_dt.T, conv_x, conv_x_bias, dt_bias, a_log,
        d_skip, gate_gain, conv_bc, conv_bc_bias, size, parts,
    )
    y, stat = run_scan(seq_lengths, xs, bc, dt, lc, lr, em, kd, st, sin, z, dm, par, ig, size, parts)
    mixed, dz, dy, gate_sums, ds, gw_z, gw_o, dsin = run_gate(
        y, z, dm, stat, xs, par, bc, em, kd, tok, pulled, ig, ig * parts, parts
    )
    dx, dbc, ddt, conv_sums, head_sums, outputs, grad_w_z, grad_w_o, grad_w_a = run_pull(
        seq_lengths, xs, dy, bc, dtin, dt, lc, lr, em, et, kd, st, sin, ds, dsin, pre_x, par,
        inputs, mixed, wo, gw_z, gw_o, tok, ha, ig, size, parts,
    )
    grad_inputs, grad_w_x, grad_w_dt, grad_w_bc, chan, rep = run_last(
        seq_lengths, inputs, cotangent, norm_gain, tok, dz, dx, wz, wx, ws, dbc, ddt, pre_bc, conv_bc,
        conv_bc_bias, conv_sums, gate_sums, head_sums, grad_w_a, size, parts, ha, ig,
    )
    done = run_finish(
        outputs, grad_inputs, rep, norm_gain, grad_w_z, grad_w_x, grad_w_bc, grad_w_dt, chan, grad_w_o, ha
    )
    return (*done[:6], done[6].T, *done[7:15], done[15].T)


def solution(mesh):
    tokens = P(("dp", "tensor"), None)
    matrix = P("dp", "tensor")
    heads = P("tensor")
    return jax.shard_map(
        local,
        mesh=mesh,
        in_specs=(
            tokens,
            tokens,
            P("dp", None),
            P(),
            matrix,
            matrix,
            P("dp", None),
            matrix,
            P(None, "tensor"),
            heads,
            P(),
            P(),
            heads,
            heads,
            heads,
            heads,
            P("tensor", "dp"),
        ),
        out_specs=(
            tokens,
            tokens,
            P(),
            matrix,
            matrix,
            P("dp", None),
            matrix,
            P(None, "tensor"),
            heads,
            P(),
            P(),
            heads,
            heads,
            heads,
            heads,
            P("tensor", "dp"),
        ),
        check_vma=False,
    )
```

```python
from functools import partial

import jax
import jax.numpy as jnp
from jax import lax
from jax.experimental import pallas as pl
from jax.experimental.pallas import tpu as pltpu
from jax.sharding import PartitionSpec as P

SPAN = 256
HALO = 16
LANES = 128
LOG2E = 1.4426950408889634
EPS = 1e-05
FAR = -1e30
HIGH = lax.Precision.HIGHEST
F32 = jnp.float32
BF16 = jnp.bfloat16
VMEM_BYTES = 60 * 1024 * 1024


def nn(a, b):
    return jnp.dot(a, b, preferred_element_type=F32)


def nt(a, b):
    return lax.dot_general(a, b, (((1,), (1,)), ((), ())), preferred_element_type=F32)


def tn(a, b):
    return lax.dot_general(a, b, (((0,), (0,)), ((), ())), preferred_element_type=F32)


def sigmoid(v):
    return 1.0 / (1.0 + jnp.exp(-v))


def iota(shape, axis):
    return lax.broadcasted_iota(jnp.int32, shape, axis)


def seg_at(lengths, pos):
    end = lengths[0, 0]
    found = (pos >= end).astype(jnp.int32)
    for i in range(1, 3):
        end = end + lengths[0, i]
        found = found + (pos >= end).astype(jnp.int32)
    return jnp.where(pos < 0, -1, found)


def same_as_behind(sc, pos, offset):
    return (seg_at(sc, pos - offset) == seg_at(sc, pos)).astype(F32)


def head_map(cols, start, first, both=True):
    k = iota((LANES, cols), 0)
    if both:
        k = k & 63
    head = ((iota((LANES, cols), 1) + start) >> 6) + first
    return (k == head).astype(BF16)


def expand(values, mapping):
    high = values.astype(BF16).astype(F32)
    low = values - high
    return nn((high + pltpu.roll(low, 64, axis=1)).astype(BF16), mapping)


def thirds(values):
    high = values.astype(BF16).astype(F32)
    left = values - high
    middle = left.astype(BF16).astype(F32)
    return (high + pltpu.roll(middle, 16, axis=1) + pltpu.roll(left - middle, 32, axis=1)).astype(BF16)


def joined(values):
    return values + pltpu.roll(values, LANES - 16, axis=1) + pltpu.roll(values, LANES - 32, axis=1)


def whole():
    return pl.BlockSpec(memory_space=pltpu.VMEM)


def scalars():
    return pl.BlockSpec(memory_space=pltpu.SMEM)


def params():
    return pltpu.CompilerParams(vmem_limit_bytes=VMEM_BYTES)


def cost(flops, nbytes):
    return pl.CostEstimate(flops=int(flops), bytes_accessed=int(nbytes), transcendentals=0)


def col_tile(ig):
    return 256 if ig % 256 == 0 else 128


def flip(me, v):
    out = me
    bit = 1
    while bit <= v:
        if v & bit:
            out = out + bit - 2 * bit * lax.rem(me // bit, 2)
        bit *= 2
    return out


def link_bits(size):
    bits = []
    bit = 2
    while bit < size:
        bits.append(bit)
        bit *= 2
    return bits


def remote(src, dst, send, recv, **where):
    return pltpu.make_async_remote_copy(
        src_ref=src, dst_ref=dst, send_sem=send, recv_sem=recv, device_id=where, device_id_type=pl.DeviceIdType.MESH
    )


def greet(bits, partners):
    me = lax.axis_index("dp")
    barrier = pltpu.get_barrier_semaphore()
    for bit in bits:
        pl.semaphore_signal(barrier, inc=1, device_id={"dp": flip(me, bit)}, device_id_type=pl.DeviceIdType.MESH)
    for to in partners:
        pl.semaphore_signal(barrier, inc=1, device_id={"tensor": to}, device_id_type=pl.DeviceIdType.MESH)
    pl.semaphore_wait(barrier, len(bits) + len(partners))


def others(parts):
    p = lax.axis_index("tensor")
    return [lax.rem(p + shift, parts) for shift in range(1, parts)]


def row(ref):
    return jnp.reshape(ref[...], (1, ref.shape[0]))


class ToHeads:
    def __init__(self, k, src, place_of, parts, send, recv, own):
        self.p = lax.axis_index("tensor")
        self.hp = parts // 2
        self.k, self.src, self.place_of = k, src, place_of
        self.send, self.recv, self.own = send, recv, own

    def copy(self, i, side, to):
        return remote(
            self.src, self.place_of(side), self.send.at[2 * self.k + i], self.recv.at[2 * self.k + side], tensor=to
        )

    def local(self, side):
        return pltpu.make_async_copy(self.src, self.place_of(side), self.own.at[self.k])

    def targets(self):
        return [self.p // 2, self.p // 2 + self.hp]

    def start(self):
        side = lax.rem(self.p, 2)
        for i, to in enumerate(self.targets()):

            @pl.when(to != self.p)
            def _(i=i, to=to):
                self.copy(i, side, to).start()

            @pl.when(to == self.p)
            def _():
                self.local(side).start()

    def wait(self):
        q = lax.rem(self.p, self.hp)
        for side in range(2):
            source = 2 * q + side

            @pl.when(source != self.p)
            def _(side=side):
                self.copy(0, side, self.p // 2).wait_recv()

            @pl.when(source == self.p)
            def _(side=side):
                self.local(side).wait()

    def finish(self):
        side = lax.rem(self.p, 2)
        for i, to in enumerate(self.targets()):

            @pl.when(to != self.p)
            def _(i=i, to=to):
                self.copy(i, side, to).wait_send()


class Gather:
    def __init__(self, k, ref, split, rows, size, send, recv):
        self.me = lax.axis_index("dp")
        self.k, self.ref, self.rows, self.size = k, ref, rows, size
        bits = link_bits(size)
        self.orders = [bits, bits[::-1]]
        self.cols = [slice(0, split), slice(split, ref.shape[1])]
        self.send, self.recv = send, recv
        self.sent = []

    def block(self, half, v):
        start = pl.multiple_of(flip(self.me, v) * self.rows, 16)
        cols = self.cols[half]
        return self.ref.at[pl.ds(start, self.rows), pl.ds(cols.start, cols.stop - cols.start)]

    def copy(self, half, v, bit):
        n = bit.bit_length() - 1
        here = self.block(half, v)
        return remote(
            here,
            here,
            self.send.at[self.k, half, v * self.size.bit_length() + n],
            self.recv.at[self.k, half, v ^ bit],
            dp=flip(self.me, bit),
        )

    def push(self, half, v, bits):
        for bit in bits:
            self.copy(half, v, bit).start()
            self.sent.append((half, v, bit))

    def arrive(self, half, v):
        here = self.block(half, v)
        remote(
            here,
            here,
            self.send.at[self.k, half, 0],
            self.recv.at[self.k, half, v],
            dp=flip(self.me, 1),
        ).wait_recv()

    def start(self):
        for half in range(2):
            self.push(half, 0, self.orders[half])
        for half in range(2):
            self.push(half, 0, [1])

    def stage(self, s):
        for half in range(2):
            order = self.orders[half]
            names = [0]
            for bit in order[:s]:
                names = names + [v ^ bit for v in names]
            for v in sorted(n ^ order[s] for n in names):
                self.arrive(half, v)
                self.push(half, v, order[s + 1 :])
                self.push(half, v, [1])

    def stages(self):
        return len(self.orders[0])

    def cores(self):
        for half in range(2):
            for v in range(1, self.size, 2):
                self.arrive(half, v)

    def finish(self):
        for half, v, bit in self.sent:
            self.copy(half, v, bit).wait_send()


class Scatter:
    def __init__(self, k, source, acc, own, size, core_buf, link_buf, cs, cr, ls, lr):
        self.me = lax.axis_index("dp")
        self.k, self.source, self.acc, self.own, self.size = k, source, acc, own, size
        self.core_buf, self.link_buf = core_buf, link_buf
        self.cs, self.cr, self.ls, self.lr = cs, cr, ls, lr
        bits = link_bits(size)
        self.orders = [bits, bits[::-1]]
        self.sent = []

    def core(self, half, u):
        return remote(
            self.source(half, 2 * u + 1),
            self.core_buf[half].at[u],
            self.cs.at[self.k, half, u],
            self.cr.at[self.k, half, u],
            dp=flip(self.me, 1),
        )

    def start(self, half):
        for u in range(self.size // 2):
            self.core(half, u).start()
            if self.own is not None:
                self.own(half, u).start()

    def add(self, half, u, other):
        ref = self.acc(half, u)
        ref[...] = ref[...] + other[...]

    def fold_core(self, half):
        for u in range(self.size // 2):
            self.core(half, u).wait_recv()
            if self.own is not None:
                self.own(half, u).wait()
            self.add(half, u, self.core_buf[half].at[u])

    def plan(self, half, s):
        order = self.orders[half]
        held, slot = list(range(0, self.size, 2)), 0
        for i, bit in enumerate(order):
            away = [v for v in held if v & bit]
            stay = [v for v in held if not v & bit]
            if i == s:
                return bit, away, stay, slot
            held, slot = stay, slot + len(stay)

    def link(self, half, s, i):
        bit, away, stay, slot = self.plan(half, s)
        n = slot + stay.index(away[i] ^ bit)
        return remote(
            self.acc(half, away[i] >> 1),
            self.link_buf[half].at[n],
            self.ls.at[self.k, half, n],
            self.lr.at[self.k, half, n],
            dp=flip(self.me, bit),
        )

    def send(self, half, s):
        for i in range(len(self.plan(half, s)[1])):
            self.link(half, s, i).start()

    def fold(self, half, s):
        bit, away, stay, slot = self.plan(half, s)
        for i in range(len(away)):
            self.link(half, s, i).wait_recv()
        for i, v in enumerate(stay):
            self.add(half, v >> 1, self.link_buf[half].at[slot + i])

    def stages(self):
        return len(self.orders[0])

    def finish(self):
        for half in range(2):
            for u in range(self.size // 2):
                self.core(half, u).wait_send()
            for s in range(self.stages()):
                for i in range(len(self.plan(half, s)[1])):
                    self.link(half, s, i).wait_send()


class FromHeads:
    def __init__(self, k, block, slots, parts, send, recv, own):
        self.p = lax.axis_index("tensor")
        self.hp = parts // 2
        self.k, self.block, self.slots = k, block, slots
        self.send, self.recv, self.own = send, recv, own
        self.half = self.p // self.hp
        self.q = lax.rem(self.p, self.hp)

    def copy(self, side, slot):
        return remote(
            self.block(side),
            self.slots.at[slot],
            self.send.at[2 * self.k + side],
            self.recv.at[2 * self.k + slot],
            tensor=2 * self.q + side,
        )

    def local(self, side, slot):
        return pltpu.make_async_copy(self.block(side), self.slots.at[slot], self.own.at[self.k])

    def start(self, side):
        to = 2 * self.q + side

        @pl.when(to != self.p)
        def _():
            self.copy(side, self.half).start()

        @pl.when(to == self.p)
        def _():
            self.local(side, self.half).start()

    def wait(self):
        for slot in range(2):
            source = self.p // 2 + slot * self.hp

            @pl.when(source != self.p)
            def _(slot=slot):
                self.copy(0, slot).wait_recv()

            @pl.when(source == self.p)
            def _(slot=slot):
                self.local(0, slot).wait()

    def finish(self, sides=(0, 1)):
        for side in sides:

            @pl.when(2 * self.q + side != self.p)
            def _(side=side):
                self.copy(side, self.half).wait_send()


class Butterfly:
    def __init__(self, k, ref, slots, steps, send, recv):
        self.k, self.ref, self.slots, self.steps = k, ref, slots, steps
        self.send, self.recv = send, recv

    def copy(self, i):
        axis, bit = self.steps[i]
        return remote(
            self.ref,
            self.slots.at[i],
            self.send.at[self.k, i],
            self.recv.at[self.k, i],
            **{axis: flip(lax.axis_index(axis), bit)},
        )

    def push(self, i):
        self.copy(i).start()

    def fold(self, i):
        self.copy(i).wait()
        self.ref[...] += self.slots[i]


class AllZ:
    def __init__(self, ref, slots, parts, send, recv, own):
        self.p = lax.axis_index("tensor")
        self.ref, self.slots, self.parts = ref, slots, parts
        self.send, self.recv, self.own = send, recv, own

    def copy(self, shift):
        to = lax.rem(self.p + shift, self.parts)
        return remote(
            self.ref, self.slots.at[self.p], self.send.at[shift], self.recv.at[shift], tensor=to
        )

    def arrival(self, shift):
        there = self.slots.at[lax.rem(self.p + self.parts - shift, self.parts)]
        return remote(self.ref, there, self.send.at[shift], self.recv.at[shift], tensor=self.p)

    def mine(self):
        return pltpu.make_async_copy(self.ref, self.slots.at[self.p], self.own.at[0])

    def start(self):
        self.mine().start()
        for shift in range(1, self.parts):
            self.copy(shift).start()

    def total(self):
        self.mine().wait()
        for shift in range(1, self.parts):
            self.arrival(shift).wait_recv()
        value = self.slots[0]
        for i in range(1, self.parts):
            value = value + self.slots[i]
        return value

    def finish(self):
        for shift in range(1, self.parts):
            self.copy(shift).wait_send()


def sharded_rows(ref, me, v, rows, cols):
    start = pl.multiple_of(flip(me, v) * rows, 16)
    return ref.at[pl.ds(start, rows), pl.ds(cols[0], cols[1] - cols[0])]


def halves(split, total):
    return [(0, split), (split, total)]


def split_of(cols):
    return (cols // 2 + LANES - 1) // LANES * LANES


def first_body(
    size, parts, rows, ha, ig,
    ends, inputs, cot, ngain, w_x, w_z, w_out, w_bc, w_dt, conv_x, conv_x_bias, dt_bias, a_log, d_skip, gate_gain,
    taps_bc, bias_bc,
    tok_h, pulled_h, wx_h, wz_h, wo_h, ws_h, par_h, pre_h, bc_h, dtin_h, dt_h, lc_h, lr_h, em_h, et_h, kd_h,
    prex_h, xs_h, st_h, sin_h, z_h, dm_h, y_h, stat_o,
    tok, pulled, wx, wz, wo, ws, par, pre, bc, dtin, dt, lc, lr, em, et, kd, st, stage, xs, fin, sin, z, gated_s, y_stage, cb, off, stat, sums_out, sums_in,
    lags, w_dt_wide, table, maps_in,
    zs, zr, zo, gs, gr, ts, tr, cs, cr, hs, hr, ss, sr, ms, mr, local, outs, tiles,
):
    p = lax.axis_index("tensor")
    me = lax.axis_index("dp")
    hp = parts // 2
    place = lax.rem(p, hp)
    half = p // hp
    inner = 2 * ig
    local_rows, width = inputs.shape
    count = local_rows * hp
    total = count + HALO
    base = half * count
    own_rows = pl.multiple_of(place * local_rows, 16)

    def mates():
        return [(s, half * hp + lax.rem(place + s, hp)) for s in range(1, hp)]

    def my_rows():
        return pl.ds(pl.multiple_of(me * rows, 16), rows)

    def wide(ref, cols):
        return lambda side: ref.at[my_rows(), pl.ds(pl.multiple_of(side * cols, LANES), cols)]

    emitted = []

    def emit(src, dst):
        copy = pltpu.make_async_copy(src, dst, outs.at[len(emitted)])
        copy.start()
        emitted.append(copy)

    w_dt_wide[...] = jnp.zeros_like(w_dt_wide)
    w_dt_wide[:, :ha] = w_dt[...].T
    greet([1] + link_bits(size), others(parts))
    to_table = ToHeads(0, table, lambda side: par.at[:, pl.ds(pl.multiple_of(side * ig, LANES), ig)], parts, zs, zr, zo)
    to_dt = ToHeads(1, w_dt_wide, wide(ws, LANES), parts, zs, zr, zo)
    to_x = ToHeads(2, w_x, wide(wx, ig), parts, zs, zr, zo)
    to_z = ToHeads(3, w_z, wide(wz, ig), parts, zs, zr, zo)
    to_o = ToHeads(4, w_out, wide(wo, ig), parts, zs, zr, zo)
    to_dt.start()
    to_x.start()
    bc_copy = pltpu.make_async_copy(w_bc, ws.at[my_rows(), pl.ds(2 * LANES, 2 * LANES)], local.at[0])
    bc_copy.start()
    cot_copy = pltpu.make_async_copy(cot, pulled.at[pl.ds(own_rows, local_rows)], local.at[1])
    cot_copy.start()

    values = inputs[...].astype(F32)
    scale = lax.rsqrt(jnp.mean(values * values, axis=1, keepdims=True) + EPS)
    mine = pl.ds(pl.multiple_of(HALO + own_rows, 16), local_rows)
    tok[mine, :] = (values * scale * row(ngain)).astype(BF16)

    def tok_copy(s, to):
        return remote(tok.at[mine], tok.at[mine], ts.at[s], tr.at[s], tensor=to)

    def tok_arrive(s):
        there = pl.ds(pl.multiple_of(HALO + lax.rem(place + hp - s, hp) * local_rows, 16), local_rows)
        remote(tok.at[there], tok.at[there], ts.at[s], tr.at[s], tensor=p).wait_recv()

    def cot_copy_to(s, to):
        return remote(cot, pulled.at[pl.ds(own_rows, local_rows)], cs.at[s], cr.at[s], tensor=to)

    def cot_arrive(s):
        there = pl.ds(pl.multiple_of(lax.rem(place + hp - s, hp) * local_rows, 16), local_rows)
        remote(pulled.at[there], pulled.at[there], cs.at[s], cr.at[s], tensor=p).wait_recv()

    def halo_copy(k):
        return remote(tok.at[pl.ds(total - HALO, HALO)], tok.at[pl.ds(0, HALO)], hs.at[k], hr.at[0], tensor=hp + k)

    for s, to in mates():
        tok_copy(s, to).start()

    @pl.when(p == hp - 1)
    def _():
        for k in range(hp):
            halo_copy(k).start()

    @pl.when(half == 0)
    def _():
        tok[:HALO, :] = jnp.zeros((HALO, width), BF16)

    for b in range(2):
        maps_in[b] = head_map(ig, 0, b * 16)
    table[...] = jnp.zeros_like(table)
    table[0:4, :] = conv_x[...]
    table[4:5, :] = row(conv_x_bias)
    table[5:6, :] = row(gate_gain)
    table[6:7, :ha] = row(d_skip)
    table[7:8, :ha] = row(dt_bias)
    table[7:8, LANES : LANES + ha] = row(a_log)
    to_table.start()

    g_s = Gather(0, ws, 2 * LANES, rows, size, gs, gr)
    g_x = Gather(1, wx, ig, rows, size, gs, gr)
    g_z = Gather(2, wz, ig, rows, size, gs, gr)
    g_o = Gather(3, wo, ig, rows, size, gs, gr)
    stages = g_x.stages()
    to_dt.wait()
    bc_copy.wait()
    g_s.start()
    to_x.wait()
    g_x.start()
    to_z.start()
    for s in range(stages):
        g_s.stage(s)
        g_x.stage(s)
        if s == 0:
            to_z.wait()
            g_z.start()
            to_o.start()
    g_s.cores()
    for s, _ in mates():
        tok_arrive(s)
    for s, to in mates():
        cot_copy_to(s, to).start()

    @pl.when(half == 1)
    def _():
        halo_copy(0).wait_recv()

    emit(tok, tok_h)
    emit(ws, ws_h)

    both = nn(tok[...], ws[...])
    pre[...] = both[:, 2 * LANES :]
    emit(pre, pre_h)
    pos = base + iota((count, 1), 0)
    for j in range(1, 4):
        lags[j - 1] = jnp.broadcast_to(same_as_behind(ends, pos, j), (count, LANES))
    for side in range(2):
        at = slice(side * LANES, (side + 1) * LANES)
        acc = bias_bc[...].reshape(1, 2 * LANES)[:, at] + taps_bc[0:1, at] * pre[HALO : HALO + count, at]
        for j in range(1, 4):
            acc = acc + taps_bc[j : j + 1, at] * pre[HALO - j : HALO - j + count, at] * lags[j - 1]
        bc[:, at] = (acc * sigmoid(acc)).astype(BF16)
    emit(bc, bc_h)
    to_table.wait()
    emit(par, par_h)
    lane = iota((1, LANES), 1)
    keep = ((lane & 15) < ha).astype(F32) * (lane < 32).astype(F32)

    def merge(values):
        return values[0] + pltpu.roll(values[1], 16, axis=1)

    biases = merge([par[7:8, b * ig : b * ig + LANES] for b in range(2)])
    logs_a = merge([par[7:8, b * ig + LANES : b * ig + 2 * LANES] for b in range(2)])
    shifted = merge([both[HALO:, b * LANES : (b + 1) * LANES] for b in range(2)]) + biases
    steps = (jnp.maximum(shifted, 0.0) + jnp.log1p(jnp.exp(-jnp.abs(shifted)))) * keep
    dtin[...] = shifted
    dt[...] = steps
    scaled = steps * (-jnp.exp(logs_a) * LOG2E)
    tri = (iota((SPAN, SPAN), 0) >= iota((SPAN, SPAN), 1)).astype(F32)
    chunks = count // SPAN
    gone = []
    for c in range(chunks):
        span = slice(c * SPAN, (c + 1) * SPAN)
        logs = jnp.dot(tri, scaled[span, :], precision=HIGH, preferred_element_type=F32)
        first, last = base + c * SPAN - 1, base + (c + 1) * SPAN - 1
        here = base + c * SPAN + iota((SPAN, 1), 0)
        seg = seg_at(ends, here)
        seg_first, seg_last = seg_at(ends, first), seg_at(ends, last)
        final = logs[SPAN - 1 : SPAN, :]
        gone.append(jnp.where(seg_first == seg_last, 1.0, 0.0).astype(F32) * jnp.exp2(final) * keep)
        lc[span, :] = logs
        lr[:, span] = logs.T[:32, :]
        em[span, :] = (seg == seg_first).astype(F32) * jnp.exp2(logs) * keep
        et[span, :] = (seg == seg_last).astype(F32) * jnp.exp2(final - logs) * keep
    ahead_of, behind_of = [keep], [keep]
    for c in range(chunks - 1):
        ahead_of.append(ahead_of[-1] * gone[c])
        behind_of.append(behind_of[-1] * gone[chunks - 1 - c])
    behind_of = behind_of[::-1]
    fill = [jnp.zeros((1, LANES), F32)] * (8 - chunks)
    kd[...] = jnp.concatenate(gone + fill + ahead_of + fill + behind_of + fill, axis=0)
    for src, dst in ((dtin, dtin_h), (dt, dt_h), (lc, lc_h), (lr, lr_h), (em, em_h), (et, et_h), (kd, kd_h)):
        emit(src, dst)

    g_x.cores()
    emit(wx, wx_h)
    g_z.stage(0)

    cols = col_tile(ig)

    def state_copy(j):
        at = pl.ds(pl.multiple_of(j * cols, cols), cols)
        return remote(fin.at[:, at], sin.at[:, at], ss.at[j], sr.at[j], tensor=lax.rem(p + hp, parts))

    def tile_out(kind, slot, j):
        at = pl.ds(pl.multiple_of(j * cols, cols), cols)
        if kind == 0:
            return pltpu.make_async_copy(stage.at[slot], prex_h.at[:, at], tiles.at[0, slot])
        return pltpu.make_async_copy(stage.at[slot, pl.ds(0, count)], dm_h.at[:, at], tiles.at[kind, slot])

    def xpath(j, carry):
        slot = lax.rem(j, 2)

        @pl.when(j >= 2)
        def _():
            tile_out(0, slot, j).wait()

        at = pl.multiple_of(j * cols, cols)
        lanes = pl.ds(at, cols)
        b = at // ig
        stage[slot] = nn(tok[...], wx[:, lanes])
        mapping = maps_in[b, :, pl.ds(pl.multiple_of(lax.rem(at, ig), LANES), cols)]
        state = jnp.zeros((LANES, cols), F32)
        decay = expand(kd[0:8, :], mapping)
        taps, bias = par[0:4, lanes], par[4:5, lanes]
        for c in range(chunks):
            low = c * SPAN
            weight = expand(dt[low : low + SPAN, :] * et[low : low + SPAN, :], mapping)
            weighted = []
            for side in range(cols // LANES):
                lane_at = slice(side * LANES, (side + 1) * LANES)
                window = stage[slot, low : low + SPAN + HALO, lane_at]
                conv = bias[:, lane_at] + taps[0:1, lane_at] * window[HALO:, :]
                for k in range(1, 4):
                    lag = pltpu.roll(window, k, axis=0)[HALO:, :]
                    conv = conv + taps[k : k + 1, lane_at] * lag * lags[k - 1, low : low + SPAN, :]
                value = (conv * sigmoid(conv)).astype(BF16)
                xs[low : low + SPAN, pl.ds(pl.multiple_of(at + side * LANES, LANES), LANES)] = value
                weighted.append((value.astype(F32) * weight[:, lane_at]).astype(BF16))
            st[c, :, lanes] = state
            fresh = tn(bc[low : low + SPAN, :LANES], jnp.concatenate(weighted, axis=1))
            state = decay[c : c + 1, :] * state + fresh
        fin[:, lanes] = state.astype(BF16)

        @pl.when(half == 0)
        def _():
            state_copy(j).start()

        tile_out(0, slot, j).start()
        return carry

    def project(j, carry):
        lanes = pl.ds(pl.multiple_of(j * cols, cols), cols)
        z[:, lanes] = nn(tok[HALO:, :], wz[:, lanes])
        return carry

    lane_row = iota((1, LANES), 1)
    sides = [(lane_row < 64).astype(BF16), (lane_row >= 64).astype(BF16)]
    middle_of = SPAN // 2

    def y_out(i):
        c, b = i // 2, lax.rem(i, 2)
        rows_to = pl.ds(pl.multiple_of(c * SPAN, SPAN), SPAN)
        lanes_to = pl.ds(pl.multiple_of(b * ig, LANES), ig)
        return pltpu.make_async_copy(y_stage.at[b], y_h.at[rows_to, lanes_to], tiles.at[2, b])

    def scan(i, carry):
        c, b = i // 2, lax.rem(i, 2)
        rows_here = pl.ds(pl.multiple_of(c * SPAN, SPAN), SPAN)
        lanes_b = pl.ds(pl.multiple_of(b * ig, LANES), ig)

        @pl.when(i >= 2)
        def _():
            y_out(i).wait()

        b_map, c_map = bc[rows_here, :LANES], bc[rows_here, LANES:]
        cb[...] = nt(c_map, b_map)
        start = base + c * SPAN
        t, s = iota((SPAN, SPAN), 0), iota((SPAN, SPAN), 1)
        seg_row, seg_col = seg_at(ends, start + iota((1, SPAN), 1)), seg_at(ends, start + iota((SPAN, 1), 0))
        off[...] = jnp.where((t >= s) & (seg_col == seg_row), 0.0, FAR)
        mapping = maps_in[b]
        steps_wide = expand(dt[rows_here, :], mapping)
        lead_wide = expand(em[rows_here, :], mapping)
        arriving = expand(kd[8:16, :], mapping) * (iota((8, 1), 0) == c).astype(F32)
        state = st[c, :, lanes_b] + jnp.sum(arriving, axis=0, keepdims=True) * sin[:, lanes_b].astype(F32)
        skips = par[6:7, pl.ds(pl.multiple_of(b * ig, LANES), LANES)]
        skip = expand(jnp.broadcast_to(skips, (8, LANES)), maps_in[0])[0:1, :]
        read = nn(c_map, state.astype(BF16))
        columns = pltpu.roll(lc[rows_here, :], lax.rem(LANES - 16 * b, LANES), axis=1)
        lines = lr[pl.ds(pl.multiple_of(b * 16, 16), 16), rows_here]
        square = jnp.zeros((SPAN, LANES), F32)
        for k in range(ig // LANES):
            at = slice(k * LANES, (k + 1) * LANES)
            there = pl.ds(pl.multiple_of(b * ig + k * LANES, LANES), LANES)
            xf = xs[rows_here, there].astype(F32)
            pair = (xf * steps_wide[:, at]).astype(BF16)
            far = read[:, at] * lead_wide[:, at] + skip[:, at] * xf
            top = far[:middle_of]
            low = far[middle_of:]
            for side in range(2):
                h = 2 * k + side
                operand = pair * sides[side]
                column = columns[:, h : h + 1]
                line = lines[h : h + 1, :]
                gap = column[:middle_of] - line[:, :middle_of] + off[:middle_of, :middle_of]
                w_top = cb[:middle_of, :middle_of] * jnp.exp2(gap)
                top = top + nn(w_top.astype(BF16), operand[:middle_of, :])
                w_low = cb[middle_of:, :] * jnp.exp2(column[middle_of:] - line + off[middle_of:, :])
                low = low + nn(w_low.astype(BF16), operand)
            out = jnp.concatenate([top, low], axis=0)
            y_stage[b, :, at] = out
            gate = z[rows_here, there]
            gated = out * (gate * sigmoid(gate))
            gated_s[rows_here, there] = gated
            square = square + gated * gated
        y_out(i).start()
        held = jnp.where(b == 0, 0.0, stat[rows_here, :])
        stat[rows_here, :] = held + jnp.where(lane_row == 0, jnp.sum(square, axis=1, keepdims=True), 0.0)
        return carry

    def dm_tile(j, cross):
        slot = lax.rem(j, 2)

        @pl.when(j >= 2)
        def _():
            tile_out(1, slot, j).wait()

        lanes = pl.ds(pl.multiple_of(j * cols, cols), cols)
        value = nn(pulled[...], wo[:, lanes])
        stage[slot, :count, :] = value
        tile_out(1, slot, j).start()
        share = value * gated_s[:, lanes] * par[5:6, lanes]
        for i in range(cols // LANES):
            cross = cross + share[:, i * LANES : (i + 1) * LANES]
        return cross

    tiles_all = inner // cols
    middle = tiles_all // 2

    def drain(kind):
        for j in range(tiles_all - 2, tiles_all):
            tile_out(kind, j % 2, j).wait()

    lax.fori_loop(0, middle, xpath, 0)
    for s in range(1, stages):
        g_z.stage(s)
    lax.fori_loop(middle, tiles_all, xpath, 0)
    emit(xs, xs_h)
    emit(st, st_h)
    to_o.wait()
    g_o.start()
    drain(0)
    g_z.cores()
    emit(wz, wz_h)
    lax.fori_loop(0, tiles_all, project, 0)
    emit(z, z_h)

    @pl.when(half == 1)
    def _():
        for j in range(tiles_all):
            state_copy(j).wait_recv()

    @pl.when(half == 0)
    def _():
        sin[...] = jnp.zeros_like(sin)

    emit(sin, sin_h)
    lax.fori_loop(0, chunks, scan, 0)
    for s in range(stages - 1):
        g_o.stage(s)
    lax.fori_loop(chunks, 2 * chunks, scan, 0)
    g_o.stage(stages - 1)
    g_o.cores()
    emit(wo, wo_h)
    for s, _ in mates():
        cot_arrive(s)
    cot_copy.wait()
    emit(pulled, pulled_h)
    cross = lax.fori_loop(0, tiles_all, dm_tile, jnp.zeros((count, LANES), F32))
    stat[...] += jnp.where(lane_row == 1, jnp.sum(cross, axis=1, keepdims=True), 0.0)
    sums_out[...] = stat[...].T[:8, :]

    def stat_copy(s, to):
        return remote(sums_out, sums_in.at[s - 1], ms.at[s - 1], mr.at[s - 1], tensor=to)

    for s, to in mates():
        stat_copy(s, to).start()
    drain(1)
    for i in range(2 * chunks - 2, 2 * chunks):
        y_out(i).wait()
    for s, to in mates():
        stat_copy(s, to).wait()
    summed = sums_out[...]
    for s in range(1, hp):
        summed = summed + sums_in[s - 1]
    stat_o[...] = jnp.concatenate([summed, jnp.zeros((LANES - 8, count), F32)], axis=0).T
    for item in (to_table, to_dt, to_x, to_z, to_o, g_s, g_x, g_z, g_o):
        item.finish()
    for s, to in mates():
        tok_copy(s, to).wait_send()
        cot_copy_to(s, to).wait_send()

    @pl.when(p == hp - 1)
    def _():
        for k in range(hp):
            halo_copy(k).wait_send()

    @pl.when(half == 0)
    def _():
        for j in range(tiles_all):
            state_copy(j).wait_send()

    for copy in emitted:
        copy.wait()


def run_first(
    ends, inputs, cot, ngain, w_x, w_z, w_out, w_bc, w_dt, conv_x, conv_x_bias, dt_bias, a_log, d_skip, gate_gain,
    taps_bc, bias_bc, size, parts,
):
    ha = dt_bias.shape[0]
    local_rows, width = inputs.shape
    rows, ig = w_x.shape
    inner = 2 * ig
    hp = parts // 2
    count = local_rows * hp
    total = count + HALO
    chunks = count // SPAN
    cols = col_tile(ig)
    shape = jax.ShapeDtypeStruct
    per_block = shape((count, LANES), F32)
    outs = (
        shape((total, width), BF16),
        shape((count, width), BF16),
        shape((width, inner), BF16),
        shape((width, inner), BF16),
        shape((width, inner), BF16),
        shape((width, 4 * LANES), BF16),
        shape((8, inner), F32),
        shape((total, 2 * LANES), F32),
        shape((count, 2 * LANES), BF16),
        per_block,
        per_block,
        per_block,
        shape((32, count), F32),
        per_block,
        per_block,
        shape((24, LANES), F32),
        shape((total, inner), F32),
        shape((count, inner), BF16),
        shape((chunks, LANES, inner), F32),
        shape((LANES, inner), BF16),
        shape((count, inner), F32),
        shape((count, inner), F32),
        shape((count, inner), F32),
        shape((count, LANES), F32),
    )
    anywhere = pl.BlockSpec(memory_space=pl.ANY)
    dma = pltpu.SemaphoreType.DMA
    nbits = size.bit_length()
    scratch = [pltpu.VMEM(o.shape, o.dtype) for o in outs[:16]]
    scratch += [
        pltpu.VMEM((chunks, LANES, inner), F32),
        pltpu.VMEM((2, total, cols), F32),
        pltpu.VMEM((count, inner), BF16),
        pltpu.VMEM((LANES, inner), BF16),
        pltpu.VMEM((LANES, inner), BF16),
        pltpu.VMEM((count, inner), F32),
        pltpu.VMEM((count, inner), F32),
        pltpu.VMEM((2, SPAN, ig), F32),
        pltpu.VMEM((SPAN, SPAN), F32),
        pltpu.VMEM((SPAN, SPAN), F32),
        pltpu.VMEM((count, LANES), F32),
        pltpu.VMEM((8, count), F32),
        pltpu.VMEM((hp - 1, 8, count), F32),
        pltpu.VMEM((3, count, LANES), F32),
        pltpu.VMEM((rows, LANES), BF16),
        pltpu.VMEM((8, ig), F32),
        pltpu.VMEM((2, LANES, ig), BF16),
        dma((10,)),
        dma((10,)),
        dma((5,)),
        dma((4, 2, size * nbits)),
        dma((4, 2, size)),
        dma((hp,)),
        dma((hp,)),
        dma((hp,)),
        dma((hp,)),
        dma((hp,)),
        dma((1,)),
        dma((inner // cols,)),
        dma((inner // cols,)),
        dma((hp - 1,)),
        dma((hp - 1,)),
        dma((2,)),
        dma((24,)),
        dma((3, 2)),
    ]
    return pl.pallas_call(
        partial(first_body, size, parts, rows, ha, ig),
        out_shape=outs,
        in_specs=[scalars(), whole(), anywhere, whole(), anywhere, anywhere, anywhere, anywhere] + [whole()] * 9,
        out_specs=[anywhere] * (len(outs) - 1) + [whole()],
        scratch_shapes=scratch,
        compiler_params=pltpu.CompilerParams(vmem_limit_bytes=VMEM_BYTES, collective_id=0, has_side_effects=True),
        cost_estimate=cost(2 * total * width * (3 * inner + 512), 60e6),
        name="first",
    )(
        ends, inputs, cot, ngain, w_x, w_z, w_out, w_bc, w_dt, conv_x, conv_x_bias, dt_bias, a_log, d_skip,
        gate_gain, taps_bc, bias_bc,
    )


def gate_body(
    parts, ig, inner_all, y, z, dm, stats, xs, par, bc, em, kd, tok_h, pulled_h,
    mixed_o, dz_o, dy_o, sums_o, ds_o, gz_o, go_o, dsin_o,
    first, dsin, tok, pulled, mixed_s, dz_s, loads, ss, sr,
):
    count, cols = y.shape
    j = pl.program_id(0)
    tiles = pl.num_programs(0) // 2
    p = lax.axis_index("tensor")
    hp = parts // 2
    part = p // hp
    peer = lax.rem(p + hp, parts)

    def state_copy(i):
        at = pl.ds(pl.multiple_of(i * cols, cols), cols)
        return remote(first.at[:, at], dsin.at[:, at], ss.at[i], sr.at[i], tensor=peer)

    def elementwise():
        at = j * cols
        here = pl.ds(pl.multiple_of(at, cols), cols)
        mapping = head_map(cols, lax.rem(at, ig), at // ig * 16)
        gone = expand(kd[0:8, :], mapping)
        gain = par[5:6, :]
        grad = jnp.zeros((LANES, cols), F32)
        by_gain = jnp.zeros((1, cols), F32)
        by_skip = jnp.zeros((1, cols), F32)
        for c in range(count // SPAN - 1, -1, -1):
            span = slice(c * SPAN, (c + 1) * SPAN)
            stat = stats[span, :]
            scale = lax.rsqrt(stat[:, 0:1] / inner_all + EPS)
            pull = scale * scale * scale * stat[:, 1:2] / inner_all
            gate = z[span, :]
            sig = sigmoid(gate)
            act = gate * sig
            out = y[span, :]
            gated = out * act
            normal = gated * scale
            mixed = (normal * gain).astype(BF16)
            mixed_o[span, :] = mixed
            mixed_s[span, here] = mixed
            upstream = dm[span, :]
            by_gain = by_gain + jnp.sum(upstream * normal, axis=0, keepdims=True)
            dgated = scale * (upstream * gain) - gated * pull
            dz = (dgated * out * (sig * (1.0 + gate * (1.0 - sig)))).astype(BF16)
            dz_o[span, :] = dz
            dz_s[span, here] = dz
            dy = dgated * act
            by_skip = by_skip + jnp.sum(dy * xs[span, :].astype(F32), axis=0, keepdims=True)
            dy_o[span, :] = dy.astype(BF16)
            ds_o[c] = grad
            lead = (dy * expand(em[span, :], mapping)).astype(BF16)
            grad = gone[c : c + 1, :] * grad + tn(bc[span, LANES:], lead)
        sums_o[...] = jnp.concatenate([by_gain, by_skip, jnp.zeros((6, cols), F32)], axis=0)
        first[:, pl.ds(pl.multiple_of(j * cols, cols), cols)] = grad.astype(BF16)

        @pl.when(part == 1)
        def _():
            state_copy(j).start()

    def load(i):
        src, dst = ((pulled_h, pulled), (tok_h, tok))[i]
        return pltpu.make_async_copy(src, dst, loads.at[i])

    @pl.when(j == 0)
    def _():
        greet([], [peer])
        load(0).start()
        load(1).start()

    @pl.when(j < tiles)
    def _():
        elementwise()

    @pl.when(j == tiles)
    def _():
        load(0).wait()
        load(1).wait()

    @pl.when(j >= tiles)
    def _():
        here = pl.ds(pl.multiple_of((j - tiles) * cols, cols), cols)
        go_o[...] = tn(pulled[...], mixed_s[:, here]).astype(BF16)
        gz_o[...] = tn(tok[HALO:, :], dz_s[:, here]).astype(BF16)

    @pl.when(j == 2 * tiles - 1)
    def _():
        def send_done(i, carry):
            state_copy(i).wait_send()
            return carry

        def arrived(i, carry):
            state_copy(i).wait_recv()
            return carry

        @pl.when(part == 1)
        def _():
            lax.fori_loop(0, tiles, send_done, 0)
            dsin_o[...] = jnp.zeros_like(dsin_o)

        @pl.when(part == 0)
        def _():
            lax.fori_loop(0, tiles, arrived, 0)
            dsin_o[...] = dsin[...]


def run_gate(y, z, dm, stat, xs, par, bc, em, kd, tok, pulled, ig, inner_all, parts):
    count, inner = y.shape
    width = tok.shape[1]
    cols = col_tile(ig)
    tiles = inner // cols
    chunks = count // SPAN

    def now(j):
        return jnp.minimum(j, tiles - 1)

    tile = pl.BlockSpec((count, cols), lambda j: (0, now(j)))
    grads = pl.BlockSpec((width, cols), lambda j: (0, jnp.maximum(j - tiles, 0)))
    low = jax.ShapeDtypeStruct((count, inner), BF16)
    shape = jax.ShapeDtypeStruct
    return pl.pallas_call(
        partial(gate_body, parts, ig, inner_all),
        grid=(2 * tiles,),
        out_shape=(
            low,
            low,
            low,
            shape((8, inner), F32),
            shape((chunks, LANES, inner), F32),
            shape((width, inner), BF16),
            shape((width, inner), BF16),
            shape((LANES, inner), BF16),
        ),
        in_specs=[
            tile,
            tile,
            tile,
            whole(),
            tile,
            pl.BlockSpec((8, cols), lambda j: (0, now(j))),
            whole(),
            whole(),
            whole(),
            pl.BlockSpec(memory_space=pl.ANY),
            pl.BlockSpec(memory_space=pl.ANY),
        ],
        out_specs=(
            tile,
            tile,
            tile,
            pl.BlockSpec((8, cols), lambda j: (0, now(j))),
            pl.BlockSpec((chunks, LANES, cols), lambda j: (0, 0, now(j))),
            grads,
            grads,
            whole(),
        ),
        scratch_shapes=[
            pltpu.VMEM((LANES, inner), BF16),
            pltpu.VMEM((LANES, inner), BF16),
            pltpu.VMEM(tok.shape, BF16),
            pltpu.VMEM(pulled.shape, BF16),
            pltpu.VMEM((count, inner), BF16),
            pltpu.VMEM((count, inner), BF16),
            pltpu.SemaphoreType.DMA((2,)),
            pltpu.SemaphoreType.DMA((tiles,)),
            pltpu.SemaphoreType.DMA((tiles,)),
        ],
        compiler_params=pltpu.CompilerParams(vmem_limit_bytes=VMEM_BYTES, collective_id=4, has_side_effects=True),
        cost_estimate=cost(12e9, 30e6),
        name="gate",
    )(y, z, dm, stat, xs, par, bc, em, kd, tok, pulled)


def pull_body(
    size, parts, ha, wrows,
    sc, xs, dy, bc, dtin, dt, lc, lr, em, et, kd, st, sin, ds, dsin, pre, par,
    inputs, mixed_h, wo_h, gz_h, go_h, tok_h,
    dx_o, dbc_o, ddt_o, csum_o, hsum_o, out_o, gz_o, go_o, ga_o,
    cbt, off, dcb, ahead, lags, products, tails, leads, rsum, maps_in, maps_out, skips, mixed, wo, branch, arrived, tok, ga, dlow, dother,
    zacc, oacc, zcore, ocore, acore, zlink, olink, alink, zz, oz,
    loads, zls, ols, ccs, ccr, cls, clr, hs, hr, ho, ms, mr, bs, br,
):
    b, step = pl.program_id(0), pl.program_id(1)
    chunks = pl.num_programs(1)
    c = chunks - 1 - step
    cols = xs.shape[1]
    half = SPAN // 2
    p = lax.axis_index("tensor")
    me = lax.axis_index("dp")
    hp = parts // 2
    place = lax.rem(p, hp)
    part = p // hp
    count = dbc_o.shape[0]
    local_rows = inputs.shape[0]
    start = part * count + c * SPAN
    n = b * chunks + step
    rows_here = pl.ds(pl.multiple_of(c * SPAN, SPAN), SPAN)

    def scatter(k, src, acc, core_buf, link_buf, own_sem):
        columns = halves(cols, 2 * cols)
        return Scatter(
            k,
            lambda h, v: sharded_rows(src, me, v, wrows, columns[h]),
            lambda h, u: acc.at[u, :, pl.ds(columns[h][0], cols)],
            lambda h, u: pltpu.make_async_copy(
                sharded_rows(src, me, 2 * u, wrows, columns[h]),
                acc.at[u, :, pl.ds(columns[h][0], cols)],
                own_sem.at[h, u],
            ),
            size, core_buf, link_buf, ccs, ccr, cls, clr,
        )

    def a_block(h, v):
        return sharded_rows(ga, me, v, wrows, halves(split_of(cols), cols)[h])

    scat_o = scatter(0, go_h, oacc, ocore, olink, ols)
    scat_z = scatter(1, gz_h, zacc, zcore, zlink, zls)
    scat_a = Scatter(2, a_block, lambda h, u: a_block(h, 2 * u), None, size, acore, alink, ccs, ccr, cls, clr)
    home_o = FromHeads(0, lambda side: oacc.at[0, :, pl.ds(side * cols, cols)], oz, parts, hs, hr, ho)
    home_z = FromHeads(1, lambda side: zacc.at[0, :, pl.ds(side * cols, cols)], zz, parts, hs, hr, ho)
    stages = scat_o.stages()

    def mates():
        return [(s, part * hp + lax.rem(place + s, hp)) for s in range(1, hp)]

    def branch_copy(s, to):
        rows_to = pl.ds(pl.multiple_of(lax.rem(place + s, hp) * local_rows, 16), local_rows)
        return remote(branch.at[rows_to], arrived.at[s - 1], bs.at[s - 1], br.at[s - 1], tensor=to)

    def maps_copy(s, to, i):
        at = pl.ds(pl.multiple_of(i * SPAN, SPAN), SPAN)
        return remote(dlow.at[at], dother.at[s - 1, at], ms.at[s - 1, i], mr.at[s - 1, i], tensor=to)

    @pl.when(n == 0)
    def _():
        load_mixed = pltpu.make_async_copy(mixed_h, mixed, loads.at[0])
        load_mixed.start()

        def wo_copy(j):
            slot = lax.rem(j, 2)
            from_rows = pl.ds(pl.multiple_of(j * SPAN, SPAN), SPAN)
            return pltpu.make_async_copy(wo_h.at[from_rows], wo.at[slot], loads.at[1 + slot])

        wo_copy(0).start()
        greet([1] + link_bits(size), others(parts))
        for h in range(2):
            scat_o.start(h)
        for h in range(2):
            scat_z.start(h)
        load_mixed.wait()
        out_tiles = wo_h.shape[0] // SPAN

        def out_tile(j, carry):
            @pl.when(j + 1 < out_tiles)
            def _():
                wo_copy(j + 1).start()

            wo_copy(j).wait()
            at = pl.ds(pl.multiple_of(j * SPAN, SPAN), SPAN)
            branch[:, at] = nt(mixed[...], wo[lax.rem(j, 2)]).astype(BF16)
            return carry

        lax.fori_loop(0, out_tiles, out_tile, 0)
        for s, to in mates():
            branch_copy(s, to).start()
        pltpu.make_async_copy(tok_h, tok, loads.at[3]).start()
        for h in range(2):
            scat_o.fold_core(h)
            scat_o.send(h, 0)

    @pl.when(n == 1)
    def _():
        for h in range(2):
            scat_z.fold_core(h)
            scat_z.send(h, 0)

    @pl.when(n == 3)
    def _():
        for s in range(stages - 1):
            for h in range(2):
                scat_o.fold(h, s)
                scat_o.send(h, s + 1)

    @pl.when(n == 4)
    def _():
        for s in range(stages - 1):
            for h in range(2):
                scat_z.fold(h, s)
                scat_z.send(h, s + 1)
        for h in range(2):
            scat_o.fold(h, stages - 1)
            home_o.start(h)

    @pl.when(n == chunks + 1)
    def _():
        for h in range(2):
            scat_a.fold_core(h)
            scat_a.send(h, 0)

    @pl.when(n == chunks + 2)
    def _():
        for h in range(2):
            scat_z.fold(h, stages - 1)
            home_z.start(h)
        for s in range(stages - 1):
            for h in range(2):
                scat_a.fold(h, s)
                scat_a.send(h, s + 1)

    b_map, c_map = bc[:, :LANES], bc[:, LANES:]
    cbt[...] = nt(b_map, c_map)
    s, t = iota((SPAN, SPAN), 0), iota((SPAN, SPAN), 1)
    seg_row, seg_col = seg_at(sc, start + iota((1, SPAN), 1)), seg_at(sc, start + iota((SPAN, 1), 0))
    off[...] = jnp.where((t >= s) & (seg_col == seg_row), 0.0, FAR)
    here = start + iota((SPAN, LANES), 0)
    for j in range(1, 4):
        lags[j - 1] = same_as_behind(sc, here, j)
    dcb[...] = jnp.zeros_like(dcb)

    @pl.when(step == 0)
    def _():
        ahead[...] = jnp.zeros_like(ahead)
        csum_o[...] = jnp.zeros_like(csum_o)
        hsum_o[...] = jnp.zeros_like(hsum_o)
        rsum[...] = jnp.zeros_like(rsum)
        maps_in[...] = head_map(cols, 0, b * 16)
        maps_out[...] = head_map(cols, 0, 0, both=False)
        skips[...] = expand(jnp.broadcast_to(par[6:7, :LANES], (8, LANES)), head_map(cols, 0, 0))

    lane = iota((1, LANES), 1)
    taps, bias = par[0:4, :], par[4:5, :]
    skip = skips[0:1, :]
    mapping = maps_in[...]
    single = maps_out[...]
    columns = pltpu.roll(lc[...], lax.rem(LANES - 16 * b, LANES), axis=1)

    def mine(values):
        return pltpu.roll(values, lax.rem(LANES - 16 * b, LANES), axis=1) * (lane < ha).astype(F32)

    sides = [(lane < 64).astype(BF16), (lane >= 64).astype(BF16)]
    steps = mine(dt[...])
    steps_wide = expand(dt[...], mapping)
    lead_wide = expand(em[...], mapping)
    tail_wide = expand(et[...], mapping)
    decays = expand(kd[...], mapping)
    pick = (iota((8, 1), 0) == c).astype(F32)
    state = st[0] + jnp.sum(decays[8:16] * pick, axis=0, keepdims=True) * sin[...].astype(F32)
    dstate = ds[0] + jnp.sum(decays[16:24] * pick, axis=0, keepdims=True) * dsin[...].astype(F32)
    state_l, dstate_l = state.astype(BF16), dstate.astype(BF16)
    crossing = jnp.sum(state * dstate, axis=0, keepdims=True)
    read = nn(c_map, state_l)
    far = nn(b_map, dstate_l)
    csums = jnp.zeros((SPAN, LANES), F32)
    blank = jnp.zeros((8, LANES), F32)
    window_at = pl.ds(pl.multiple_of(c * SPAN, SPAN), SPAN + HALO)
    out_at = pl.ds(pl.multiple_of(HALO + c * SPAN, HALO), SPAN)
    for k in range(cols // LANES):
        at = slice(k * LANES, (k + 1) * LANES)
        xf = xs[:, at].astype(F32)
        wide = steps_wide[:, at]
        x_pair, dy_pair = (xf * wide).astype(BF16), dy[:, at]
        top = jnp.zeros((half, LANES), F32)
        low = jnp.zeros((half, LANES), F32)
        for side in range(2):
            h = 2 * k + side
            x_one = x_pair * sides[side]
            dy_one = dy_pair * sides[side]
            column = columns[:, h : h + 1]
            row = lr[h : h + 1, :]
            decay = jnp.exp2(row - column[:half] + off[:half, :])
            top = top + nn((cbt[:half, :] * decay).astype(BF16), dy_one)
            share = nt(x_one[:half, :], dy_pair) * decay
            dcb[:half, :] += share
            both = share * cbt[:half, :]
            row_sum = jnp.sum(both, axis=0, keepdims=True)
            col_top = jnp.sum(both, axis=1, keepdims=True)
            decay = jnp.exp2(row[:, half:] - column[half:] + off[half:, half:])
            low = low + nn((cbt[half:, half:] * decay).astype(BF16), dy_one[half:, :])
            share = nt(x_one[half:, :], dy_pair[half:, :]) * decay
            dcb[half:, half:] += share
            both = share * cbt[half:, half:]
            rsum[h : h + 1, :half] = row_sum[:, :half]
            rsum[h : h + 1, half:] = row_sum[:, half:] + jnp.sum(both, axis=0, keepdims=True)
            col_low = jnp.sum(both, axis=1, keepdims=True)
            csums = csums + jnp.where(lane == h, jnp.concatenate([col_top, col_low], axis=0), 0.0)
        near = jnp.concatenate([top, low], axis=0)
        tail = tail_wide[:, at]
        dx_far = far[:, at] * tail
        tails[:, at] = (x_pair.astype(F32) * tail).astype(BF16)
        dyf = dy_pair.astype(F32)
        led = dyf * lead_wide[:, at]
        leads[:, at] = led.astype(BF16)
        products[0, :, at] = (xf * near).astype(BF16)
        products[1, :, at] = (xf * dx_far).astype(BF16)
        products[2, :, at] = (led * read[:, at]).astype(BF16)
        dxs = (near + dx_far) * wide + dyf * skip[:, at]

        window = pre[window_at, at]
        lagged = [window[HALO:, :]]
        for j in range(1, 4):
            lagged.append(pltpu.roll(window, j, axis=0)[HALO:, :] * lags[j - 1])
        conv = bias[:, at]
        for j in range(4):
            conv = conv + taps[j : j + 1, at] * lagged[j]
        sig = sigmoid(conv)
        dconv = dxs * (sig * (1.0 + conv * (1.0 - sig)))
        sums = [jnp.sum(dconv * lagged[j], axis=0, keepdims=True) for j in range(4)]
        sums.append(jnp.sum(dconv, axis=0, keepdims=True))
        csum_o[:, at] += jnp.concatenate(sums + [jnp.zeros((3, LANES), F32)], axis=0)
        dpre = taps[0:1, at] * dconv
        edge = jnp.zeros((HALO, LANES), F32)
        for j in range(1, 4):
            masked = dconv * lags[j - 1]
            longer = jnp.concatenate([masked, ahead[8 * (j - 1) : 8 * j, at]], axis=0)
            dpre = dpre + taps[j : j + 1, at] * pltpu.roll(longer, SPAN + 8 - j, axis=0)[:SPAN, :]
            opening = masked[:8, :]
            ahead[8 * (j - 1) : 8 * j, at] = opening
            before = pltpu.roll(jnp.concatenate([blank, blank, opening], axis=0), 24 - j, axis=0)[:HALO, :]
            edge = edge + taps[j : j + 1, at] * before
        dx_o[out_at, at] = dpre.astype(BF16)
        dx_o[:HALO, at] = edge.astype(BF16)
    db = nn(dcb[...].astype(BF16), c_map) + nt(tails[...], dstate_l)
    dc = tn(dcb[...].astype(BF16), b_map) + nt(leads[...], state_l)

    @pl.when(b == 0)
    def _():
        dbc_o[rows_here, :LANES] = db
        dbc_o[rows_here, LANES:] = dc

    @pl.when(b > 0)
    def _():
        dlow[rows_here, :LANES] = (dbc_o[rows_here, :LANES] + db).astype(BF16)
        dlow[rows_here, LANES:] = (dbc_o[rows_here, LANES:] + dc).astype(BF16)
        for s, to in mates():
            maps_copy(s, to, c).start()

    from_near = nt(products[0], single)
    from_far = nt(products[1], single)
    reads = nt(products[2], single)
    high = crossing.astype(BF16).astype(F32)
    middle = (crossing - high).astype(BF16).astype(F32)
    pieces = jnp.concatenate([high, middle, crossing - high - middle, jnp.zeros((5, cols), F32)], axis=0)
    held = jnp.sum(nt(pieces.astype(BF16), single), axis=0, keepdims=True)
    held = held * mine(jnp.broadcast_to(jnp.sum(kd[0:8, :] * pick, axis=0, keepdims=True), (8, LANES)))[0:1, :]
    lower = (s > t).astype(BF16)
    upper = (s <= t).astype(BF16)
    dlog = joined(nn(upper, thirds(rsum[...].T - csums + reads)) + nn(lower, thirds(steps * from_far))) + held
    rates = jnp.concatenate([par[7:8, LANES : 2 * LANES], jnp.zeros((7, LANES), F32)], axis=0)
    rate = -jnp.exp(rates)[0:1, :]
    dstep = from_near + from_far + dlog * rate
    ddt = dstep * mine(sigmoid(dtin[...]))
    ddt_o[0] = ddt
    hsum_o[0, 0:1, :] += jnp.sum(ddt, axis=0, keepdims=True)
    hsum_o[0, 1:2, :] += jnp.sum(dlog * steps * rate, axis=0, keepdims=True)

    @pl.when(n == chunks - 1)
    def _():
        pltpu.make_async_copy(tok_h, tok, loads.at[3]).wait()
        wide = col_tile(cols)

        def grad_tile(j, carry):
            at = pl.ds(pl.multiple_of(j * wide, wide), wide)
            ga[:, at] = tn(tok[...], dx_o[:, at]).astype(BF16)
            return carry

        lax.fori_loop(0, cols // wide, grad_tile, 0)
        for h in range(2):
            scat_a.start(h)

    @pl.when(n == 2 * chunks - 1)
    def _():
        for s, to in mates():
            branch_copy(s, to).wait_recv()
        own_rows = pl.ds(pl.multiple_of(place * local_rows, 16), local_rows)
        total = inputs[...].astype(F32) + branch[own_rows, :].astype(F32)
        for s in range(1, hp):
            total = total + arrived[s - 1].astype(F32)
        out_o[...] = total.astype(BF16)
        home_o.wait()
        go_o[...] = oz[0].astype(F32) + oz[1].astype(F32)
        home_z.wait()
        gz_o[...] = zz[0].astype(F32) + zz[1].astype(F32)

        for h in range(2):
            scat_a.fold(h, stages - 1)
        ga_o[...] = sharded_rows(ga, me, 0, wrows, (0, cols))[...]
        for s, to in mates():
            for i in range(count // SPAN):
                maps_copy(s, to, i).wait_recv()
        summed = dlow[...].astype(F32)
        for s in range(1, hp):
            summed = summed + dother[s - 1].astype(F32)
        dbc_o[...] = summed
        for item in (scat_o, scat_z, scat_a, home_o, home_z):
            item.finish()
        for s, to in mates():
            branch_copy(s, to).wait_send()
            for i in range(count // SPAN):
                maps_copy(s, to, i).wait_send()


def run_pull(
    sc, xs, dy, bc, dtin, dt, lc, lr, em, et, kd, st, sin, ds, dsin, pre, par,
    inputs, mixed, wo, gz, go, tok, ha, ig, size, parts,
):
    count, inner = xs.shape
    local_rows, width = inputs.shape
    total = count + HALO
    chunks = count // SPAN
    wrows = width // size
    hp = parts // 2

    def rev(step):
        return chunks - 1 - step

    tile = pl.BlockSpec((SPAN, ig), lambda b, i: (rev(i), b))
    per_token = pl.BlockSpec((SPAN, LANES), lambda b, i: (rev(i), 0))
    states = pl.BlockSpec((1, LANES, ig), lambda b, i: (rev(i), 0, b))
    edge = pl.BlockSpec((LANES, ig), lambda b, i: (0, b))
    full = pl.BlockSpec((total, ig), lambda b, i: (0, b))
    anywhere = pl.BlockSpec(memory_space=pl.ANY)
    shape = jax.ShapeDtypeStruct
    vm = pltpu.VMEM
    dma = pltpu.SemaphoreType.DMA
    blocks, links = size // 2, max(size // 2 - 1, 1)
    splits = [split_of(ig), ig - split_of(ig)]
    scratch = dict(
        cbt=vm((SPAN, SPAN), F32),
        off=vm((SPAN, SPAN), F32),
        dcb=vm((SPAN, SPAN), F32),
        ahead=vm((24, ig), F32),
        lags=vm((3, SPAN, LANES), F32),
        products=vm((3, SPAN, ig), BF16),
        tails=vm((SPAN, ig), BF16),
        leads=vm((SPAN, ig), BF16),
        rsum=vm((LANES, SPAN), F32),
        maps_in=vm((LANES, ig), BF16),
        maps_out=vm((LANES, ig), BF16),
        skips=vm((8, ig), F32),
        mixed=vm((count, inner), BF16),
        wo=vm((2, SPAN, inner), BF16),
        branch=vm((count, width), BF16),
        arrived=vm((hp - 1, local_rows, width), BF16),
        tok=vm((total, width), BF16),
        ga=vm((width, ig), BF16),
        dlow=vm((count, 2 * LANES), BF16),
        dother=vm((hp - 1, count, 2 * LANES), BF16),
        zacc=vm((blocks, wrows, inner), BF16),
        oacc=vm((blocks, wrows, inner), BF16),
        zcore=[vm((blocks, wrows, ig), BF16)] * 2,
        ocore=[vm((blocks, wrows, ig), BF16)] * 2,
        acore=[vm((blocks, wrows, w), BF16) for w in splits],
        zlink=[vm((links, wrows, ig), BF16)] * 2,
        olink=[vm((links, wrows, ig), BF16)] * 2,
        alink=[vm((links, wrows, w), BF16) for w in splits],
        zz=vm((2, wrows, ig), BF16),
        oz=vm((2, wrows, ig), BF16),
        loads=dma((4,)),
        zls=dma((2, blocks)),
        ols=dma((2, blocks)),
        ccs=dma((3, 2, blocks)),
        ccr=dma((3, 2, blocks)),
        cls=dma((3, 2, links)),
        clr=dma((3, 2, links)),
        hs=dma((4,)),
        hr=dma((4,)),
        ho=dma((2,)),
        ms=dma((hp - 1, chunks)),
        mr=dma((hp - 1, chunks)),
        bs=dma((hp - 1,)),
        br=dma((hp - 1,)),
    )
    return pl.pallas_call(
        partial(pull_body, size, parts, ha, wrows),
        grid=(2, chunks),
        out_shape=(
            shape((total, inner), BF16),
            shape((count, 2 * LANES), F32),
            shape((2, count, LANES), F32),
            shape((8, inner), F32),
            shape((2, 8, LANES), F32),
            shape((local_rows, width), BF16),
            shape((wrows, ig), F32),
            shape((wrows, ig), F32),
            shape((wrows, ig), BF16),
        ),
        in_specs=[
            scalars(),
            tile,
            tile,
            pl.BlockSpec((SPAN, 2 * LANES), lambda b, i: (rev(i), 0)),
            per_token,
            per_token,
            per_token,
            pl.BlockSpec((16, SPAN), lambda b, i: (b, rev(i))),
            per_token,
            per_token,
            whole(),
            states,
            edge,
            states,
            edge,
            full,
            pl.BlockSpec((8, ig), lambda b, i: (0, b)),
            whole(),
        ]
        + [anywhere] * 5,
        out_specs=(
            full,
            whole(),
            pl.BlockSpec((1, SPAN, LANES), lambda b, i: (b, rev(i), 0)),
            pl.BlockSpec((8, ig), lambda b, i: (0, b)),
            pl.BlockSpec((1, 8, LANES), lambda b, i: (b, 0, 0)),
            whole(),
            whole(),
            whole(),
            whole(),
        ),
        scratch_shapes=list(scratch.values()),
        compiler_params=pltpu.CompilerParams(vmem_limit_bytes=VMEM_BYTES, collective_id=3, has_side_effects=True),
        cost_estimate=cost(20e9, 30e6),
        name="pull",
    )(
        sc, xs, dy, bc, dtin, dt, lc, lr, em, et, kd, st, sin, ds, dsin, pre, par,
        inputs, mixed, wo, gz, go, tok,
    )


def last_body(
    size, parts, rows, ha, ig,
    ends, inputs, cot, ngain, tok_h, dz_h, dx_h, wz_h, wx_h, ws_h, dbc, ddt, pre, taps, bias, csum, gsum, hsum, ga,
    gin_o, gx_o, gdt_o, gbc_o, chan_o, rep_o,
    tok, dz, dx, wz, wx, ws, gx, gsm, dsm, conv, dn_out, dn_in, dn_own, edge_out, edge_in,
    xcore, xlink, score, slink, xz, dtz, bcz, chan, chan_in, chan_z, rep, rep_in, rep_z,
    loads, ccs, ccr, cls, clr, zs, zr, zo, bs, br, ns, nr, es, er, ts, tr, rs, rr, ro,
):
    p = lax.axis_index("tensor")
    me = lax.axis_index("dp")
    hp = parts // 2
    place = lax.rem(p, hp)
    half = p // hp
    inner = 2 * ig
    local_rows, width = inputs.shape
    count = local_rows * hp
    total = count + HALO
    base = half * count
    own_at = pl.multiple_of(HALO + place * local_rows, 16)

    moving = [
        pltpu.make_async_copy(src, dst, loads.at[i])
        for i, (src, dst) in enumerate(((dx_h, dx), (tok_h, tok), (wx_h, wx), (dz_h, dz), (wz_h, wz), (ws_h, ws)))
    ]
    for copy in moving:
        copy.start()
    greet([1] + link_bits(size), others(parts))

    def mates():
        return [(s, half * hp + lax.rem(place + s, hp)) for s in range(1, hp)]

    dp_steps = [("dp", 1)] + [("dp", bit) for bit in link_bits(size)]
    chan[0:5, :] = csum[0:5, :]
    chan[5:7, :] = gsum[0:2, :]
    chan[7:8, :] = jnp.zeros((1, inner), F32)
    for b in range(2):
        for i in range(2):
            at = b * ig + i * LANES
            chan[7:8, at : at + LANES] = hsum[b, i : i + 1, :]
    sum_chan = Butterfly(0, chan, chan_in, dp_steps, bs, br)
    sum_rep = Butterfly(1, rep, rep_in, dp_steps, bs, br)
    all_rep = AllZ(rep, rep_z, parts, rs, rr, ro)
    sum_chan.push(0)

    def x_block(h, v):
        return sharded_rows(gx, me, v, rows, halves(split_of(ig), ig)[h])

    def s_block(h, v):
        return sharded_rows(gsm, me, v, rows, halves(2 * LANES, 4 * LANES)[h])

    scat_x = Scatter(0, x_block, lambda h, u: x_block(h, 2 * u), None, size, xcore, xlink, ccs, ccr, cls, clr)
    scat_s = Scatter(1, s_block, lambda h, u: s_block(h, 2 * u), None, size, score, slink, ccs, ccr, cls, clr)
    stages = scat_x.stages()
    home_x = FromHeads(0, lambda side: sharded_rows(gx, me, 0, rows, (0, ig)) if side else ga, xz, parts, zs, zr, zo)
    home_dt = FromHeads(
        1,
        lambda side: sharded_rows(gsm, me, 0, rows, (side * LANES, (side + 1) * LANES)),
        dtz, parts, zs, zr, zo,
    )
    home_x.start(0)
    home_chan = FromHeads(2, lambda side: chan.at[:, pl.ds(side * ig, ig)], chan_z, parts, zs, zr, zo)

    cols = col_tile(ig)
    rep[...] = jnp.zeros_like(rep)
    dsm[:HALO, : 2 * LANES] = jnp.zeros((HALO, 2 * LANES), BF16)
    for b in range(2):
        dsm[HALO:, b * LANES : (b + 1) * LANES] = ddt[b].astype(BF16)
    for copy in moving[:2]:
        copy.wait()

    def grad_x(j, carry):
        at = pl.multiple_of(j * cols, cols)
        gx[:, pl.ds(at, cols)] = tn(tok[...], dx[:, pl.ds(ig + at, cols)]).astype(BF16)
        return carry

    def fold_cores(*scats):
        for scat in scats:
            for h in range(2):
                scat.fold_core(h)
                scat.send(h, 0)

    def relay(scat, s):
        for h in range(2):
            scat.fold(h, s)
            if s + 1 < stages:
                scat.send(h, s + 1)

    lax.fori_loop(0, ig // cols, grad_x, 0)
    for h in range(2):
        scat_x.start(h)
    for copy in moving[2:]:
        copy.wait()

    tile = 256

    def dn_tile(j, start, n, at, with_z, share):
        span = pl.ds(start, n)
        value = nt(dx[span, :], wx[at, :]) + nt(dsm[span, : 2 * LANES], ws[at, : 2 * LANES])
        if share:
            value = value + nt(dsm[span, 2 * LANES :], ws[at, 2 * LANES :]) * share
        if with_z:
            value = value + nt(dz[pl.ds(start - HALO, n), :], wz[at, :])
        rep[pl.ds(j, 1), :] += jnp.sum(value * tok[span, at].astype(F32), axis=0, keepdims=True)
        return value

    def dn_copy(s, to, j):
        at = pl.ds(pl.multiple_of(j * tile, tile), tile)
        return remote(dn_out.at[s - 1, :, at], dn_in.at[s - 1, :, at], ns.at[s - 1, j], nr.at[s - 1, j], tensor=to)

    def edge_copy(k):
        return remote(edge_out, edge_in.at[k], es.at[0], er.at[k], tensor=hp - 1)

    def other_rows(s, to):
        there = pl.multiple_of(HALO + lax.rem(place + s, hp) * local_rows, 16)

        def step(j, carry):
            at = pl.ds(pl.multiple_of(j * tile, tile), tile)
            dn_out[s - 1, :, at] = dn_tile(j, there, local_rows, at, True, 0.0).astype(BF16)
            dn_copy(s, to, j).start()
            return carry

        return step

    dn_tiles = width // tile
    middle = dn_tiles // 2
    for s, to in mates():
        lax.fori_loop(0, middle, other_rows(s, to), 0)
    fold_cores(scat_x)
    sum_chan.fold(0)
    if len(dp_steps) > 1:
        sum_chan.push(1)
    for s, to in mates():
        lax.fori_loop(middle, dn_tiles, other_rows(s, to), 0)

    upstream = dbc[...]
    pos = base + iota((count, 1), 0)
    masks = [same_as_behind(ends, pos, j) for j in range(4)]
    lagged = [pre[HALO - j : HALO - j + count, :] * masks[j] for j in range(1, 4)]
    lagged = [pre[HALO:, :]] + lagged
    through = bias[...].reshape(1, 2 * LANES)
    for j in range(4):
        through = through + taps[j : j + 1, :] * lagged[j]
    sig = sigmoid(through)
    dconv = upstream * (sig * (1.0 + through * (1.0 - sig)))
    for j in range(5):
        value = dconv * lagged[j] if j < 4 else dconv
        rep[8 + j : 9 + j, :] = jnp.sum(value, axis=0, keepdims=True) / hp
    conv[...] = jnp.zeros_like(conv)
    dpre = jnp.zeros((total, 2 * LANES), F32)
    for j in range(4):
        conv[HALO : HALO + count, :] = dconv * masks[j] if j else dconv
        dpre = dpre + taps[j : j + 1, :] * conv[j : j + total, :]
    dsm[:, 2 * LANES :] = dpre.astype(BF16)
    gsm[...] = tn(tok[...], dsm[...]).astype(BF16)
    scat_s.start(0)
    scat_s.start(1)
    for i in range(1, len(dp_steps)):
        sum_chan.fold(i)
        if i + 1 < len(dp_steps):
            sum_chan.push(i + 1)
    home_chan.start(0)
    home_chan.start(1)

    def edge_rows(j, carry):
        at = pl.ds(pl.multiple_of(j * tile, tile), tile)
        edge_out[:, at] = dn_tile(j, 0, HALO, at, False, 1.0 / hp).astype(BF16)
        return carry

    lax.fori_loop(0, dn_tiles, edge_rows, 0)
    for k in range(hp):

        @pl.when(p == hp + k)
        def _(k=k):
            edge_copy(k).start()

    def own_rows(j, carry):
        at = pl.ds(pl.multiple_of(j * tile, tile), tile)
        dn_own[:, at] = dn_tile(j, own_at, local_rows, at, True, 1.0)
        return carry

    third = (dn_tiles + 2) // 3
    lax.fori_loop(0, third, own_rows, 0)
    fold_cores(scat_s)
    for s in range(stages - 1):
        relay(scat_x, s)
    lax.fori_loop(third, 2 * third, own_rows, 0)
    for s in range(stages - 1):
        relay(scat_s, s)
    lax.fori_loop(2 * third, dn_tiles, own_rows, 0)
    sum_rep.push(0)
    relay(scat_x, stages - 1)
    home_x.start(1)
    relay(scat_s, stages - 1)
    home_dt.start(0)
    home_dt.start(1)
    bc_mine = sharded_rows(gsm, me, 0, rows, (2 * LANES, 4 * LANES))
    bc_copy = remote(bc_mine, bcz, ts.at[0], tr.at[0], tensor=lax.rem(p + hp, parts))
    bc_copy.start()
    for i in range(len(dp_steps)):
        sum_rep.fold(i)
        if i + 1 < len(dp_steps):
            sum_rep.push(i + 1)
    all_rep.start()
    home_chan.wait()
    chan_o[...] = chan_z[0] + chan_z[1]

    for s, to in mates():
        for j in range(dn_tiles):
            dn_copy(s, to, j).wait_recv()

    @pl.when(p == hp - 1)
    def _():
        for k in range(hp):
            edge_copy(k).wait_recv()
        last = local_rows - HALO
        for k in range(hp):
            dn_own[last:, :] += edge_in[k].astype(F32)

    dnormed = dn_own[...]
    for s in range(1, hp):
        dnormed = dnormed + dn_in[s - 1].astype(F32)
    values = inputs[...].astype(F32)
    scale = lax.rsqrt(jnp.mean(values * values, axis=1, keepdims=True) + EPS)
    side = dnormed * row(ngain)
    pull = scale * scale * scale * (jnp.sum(side * values, axis=1, keepdims=True) / width)
    gin_o[...] = (scale * side - values * pull + cot[...].astype(F32)).astype(BF16)

    rep_o[...] = all_rep.total()
    home_dt.wait()
    gdt_o[...] = dtz[0].astype(F32) + dtz[1].astype(F32)
    bc_copy.wait_recv()
    gbc_o[...] = bc_mine[...].astype(F32) + bcz[...].astype(F32)
    home_x.wait()
    gx_o[...] = xz[0].astype(F32) + xz[1].astype(F32)
    for item in (scat_x, scat_s, home_x, home_dt, home_chan, all_rep):
        item.finish()
    for s, to in mates():
        for j in range(dn_tiles):
            dn_copy(s, to, j).wait_send()
    bc_copy.wait_send()

    @pl.when(half == 1)
    def _():
        edge_copy(0).wait_send()


def run_last(
    ends, inputs, cot, ngain, tok, dz, dx, wz, wx, ws, dbc, ddt, pre, taps, bias, csum, gsum, hsum, ga,
    size, parts, ha, ig,
):
    local_rows, width = inputs.shape
    total = tok.shape[0]
    count = total - HALO
    inner = 2 * ig
    hp = parts // 2
    rows = width // size
    shape = jax.ShapeDtypeStruct
    anywhere = pl.BlockSpec(memory_space=pl.ANY)
    dma = pltpu.SemaphoreType.DMA
    blocks, links = size // 2, max(size // 2 - 1, 1)
    steps = size.bit_length() - 1
    vm = pltpu.VMEM

    splits = [split_of(ig), ig - split_of(ig)]

    def pair(n, cols):
        return [vm((n, rows, cols), BF16), vm((n, rows, cols), BF16)]

    scratch = dict(
        tok=vm(tok.shape, BF16),
        dz=vm(dz.shape, BF16),
        dx=vm(dx.shape, BF16),
        wz=vm(wz.shape, BF16),
        wx=vm(wx.shape, BF16),
        ws=vm(ws.shape, BF16),
        gx=vm((width, ig), BF16),
        gsm=vm((width, 4 * LANES), BF16),
        dsm=vm((total, 4 * LANES), BF16),
        conv=vm((total + 8, 2 * LANES), F32),
        dn_out=vm((hp - 1, local_rows, width), BF16),
        dn_in=vm((hp - 1, local_rows, width), BF16),
        dn_own=vm((local_rows, width), F32),
        edge_out=vm((HALO, width), BF16),
        edge_in=vm((hp, HALO, width), BF16),
        xcore=[vm((blocks, rows, w), BF16) for w in splits],
        xlink=[vm((links, rows, w), BF16) for w in splits],
        score=pair(blocks, 2 * LANES),
        slink=pair(links, 2 * LANES),
        xz=vm((2, rows, ig), BF16),
        dtz=vm((2, rows, LANES), BF16),
        bcz=vm((rows, 2 * LANES), BF16),
        chan=vm((8, inner), F32),
        chan_in=vm((steps, 8, inner), F32),
        chan_z=vm((2, 8, ig), F32),
        rep=vm((16, 2 * LANES), F32),
        rep_in=vm((steps, 16, 2 * LANES), F32),
        rep_z=vm((parts, 16, 2 * LANES), F32),
        loads=dma((6,)),
        ccs=dma((2, 2, blocks)),
        ccr=dma((2, 2, blocks)),
        cls=dma((2, 2, links)),
        clr=dma((2, 2, links)),
        zs=dma((6,)),
        zr=dma((6,)),
        zo=dma((3,)),
        bs=dma((2, steps)),
        br=dma((2, steps)),
        ns=dma((hp - 1, width // 256)),
        nr=dma((hp - 1, width // 256)),
        es=dma((1,)),
        er=dma((hp,)),
        ts=dma((1,)),
        tr=dma((1,)),
        rs=dma((parts,)),
        rr=dma((parts,)),
        ro=dma((1,)),
    )
    return pl.pallas_call(
        partial(last_body, size, parts, rows, ha, ig),
        out_shape=(
            shape((local_rows, width), BF16),
            shape((rows, ig), F32),
            shape((rows, LANES), F32),
            shape((rows, 2 * LANES), F32),
            shape((8, ig), F32),
            shape((16, 2 * LANES), F32),
        ),
        in_specs=[scalars(), whole(), whole(), whole()] + [anywhere] * 6 + [whole()] * 9,
        out_specs=[whole()] * 6,
        scratch_shapes=list(scratch.values()),
        compiler_params=pltpu.CompilerParams(vmem_limit_bytes=VMEM_BYTES, collective_id=1, has_side_effects=True),
        cost_estimate=cost(2 * total * width * (3 * inner + 1024), 40e6),
        name="last",
    )(ends, inputs, cot, ngain, tok, dz, dx, wz, wx, ws, dbc, ddt, pre, taps, bias, csum, gsum, hsum, ga)


def finish_body(
    ha, out, gin, rep, ngain, gz, gx, gbc, gdt, chan, go,
    out_o, gin_o, gnorm_o, gz_o, gx_o, gbc_o, gdt_o, gcx_o, gcxb_o, gcb_o, gcbb_o, gdtb_o, galog_o, gskip_o, ggain_o, go_o,
):
    width = ngain.shape[0]
    ig = chan.shape[1]
    out_o[...] = out[...]
    gin_o[...] = gin[...]
    gains = jnp.concatenate([rep[j : j + 1, :] for j in range(width // (2 * LANES))], axis=1)
    gnorm_o[...] = gains.reshape(width) / ngain[...]
    gz_o[...] = gz[...]
    gx_o[...] = gx[...]
    gbc_o[...] = gbc[...]
    gdt_o[...] = gdt[...].T[:ha, :]
    gcx_o[...] = chan[0:4, :]
    gcxb_o[...] = chan[4:5, :].reshape(ig)
    ggain_o[...] = chan[5:6, :].reshape(ig)
    heads = lax.dot_general(
        chan[...],
        head_map(ig, 0, 0, both=False).astype(F32),
        (((1,), (1,)), ((), ())),
        precision=HIGH,
        preferred_element_type=F32,
    )
    gskip_o[...] = heads[6:7, :ha].reshape(ha)
    gdtb_o[...] = chan[7:8, :ha].reshape(ha)
    galog_o[...] = chan[7:8, LANES : LANES + ha].reshape(ha)
    for j in range(4):
        gcb_o[j : j + 1, :] = rep[8 + j : 9 + j, :]
    gcbb_o[...] = rep[12:13, :].reshape(2 * LANES)
    go_o[...] = go[...]


def run_finish(out, gin, rep, ngain, gz, gx, gbc, gdt, chan, go, ha):
    shape = jax.ShapeDtypeStruct
    rows, ig = gz.shape
    return pl.pallas_call(
        partial(finish_body, ha),
        out_shape=(
            shape(out.shape, BF16),
            shape(gin.shape, BF16),
            shape(ngain.shape, F32),
            shape((rows, ig), F32),
            shape((rows, ig), F32),
            shape(gbc.shape, F32),
            shape((ha, rows), F32),
            shape((4, ig), F32),
            shape((ig,), F32),
            shape((4, 2 * LANES), F32),
            shape((2 * LANES,), F32),
            shape((ha,), F32),
            shape((ha,), F32),
            shape((ha,), F32),
            shape((ig,), F32),
            shape((rows, ig), F32),
        ),
        in_specs=[whole()] * 10,
        out_specs=[whole()] * 16,
        compiler_params=params(),
        cost_estimate=cost(1e7, 8e6),
        name="finish",
    )(out, gin, rep, ngain, gz, gx, gbc, gdt, chan, go)


def local(
    inputs,
    cotangent,
    seq_lengths,
    norm_gain,
    w_z,
    w_x,
    w_bc,
    w_dt,
    conv_x,
    conv_x_bias,
    conv_bc,
    conv_bc_bias,
    dt_bias,
    a_log,
    d_skip,
    gate_gain,
    w_out,
):
    parts = lax.axis_size("tensor")
    size = lax.axis_size("dp")
    ha = dt_bias.shape[0]
    ig = w_z.shape[1]
    (
        tok, pulled, wx, wz, wo, ws, par, pre_bc, bc, dtin, dt, lc, lr, em, et, kd, pre_x, xs, st, sin, z, dm, y, stat,
    ) = run_first(
        seq_lengths, inputs, cotangent, norm_gain, w_x, w_z, w_out.T, w_bc, w_dt.T, conv_x, conv_x_bias, dt_bias, a_log,
        d_skip, gate_gain, conv_bc, conv_bc_bias, size, parts,
    )
    mixed, dz, dy, gate_sums, ds, gw_z, gw_o, dsin = run_gate(
        y, z, dm, stat, xs, par, bc, em, kd, tok, pulled, ig, ig * parts, parts
    )
    dx, dbc, ddt, conv_sums, head_sums, outputs, grad_w_z, grad_w_o, grad_w_a = run_pull(
        seq_lengths, xs, dy, bc, dtin, dt, lc, lr, em, et, kd, st, sin, ds, dsin, pre_x, par,
        inputs, mixed, wo, gw_z, gw_o, tok, ha, ig, size, parts,
    )
    grad_inputs, grad_w_x, grad_w_dt, grad_w_bc, chan, rep = run_last(
        seq_lengths, inputs, cotangent, norm_gain, tok, dz, dx, wz, wx, ws, dbc, ddt, pre_bc, conv_bc,
        conv_bc_bias, conv_sums, gate_sums, head_sums, grad_w_a, size, parts, ha, ig,
    )
    done = run_finish(
        outputs, grad_inputs, rep, norm_gain, grad_w_z, grad_w_x, grad_w_bc, grad_w_dt, chan, grad_w_o, ha
    )
    return (*done[:6], done[6].T, *done[7:15], done[15].T)


def solution(mesh):
    tokens = P(("dp", "tensor"), None)
    matrix = P("dp", "tensor")
    heads = P("tensor")
    return jax.shard_map(
        local,
        mesh=mesh,
        in_specs=(
            tokens,
            tokens,
            P("dp", None),
            P(),
            matrix,
            matrix,
            P("dp", None),
            matrix,
            P(None, "tensor"),
            heads,
            P(),
            P(),
            heads,
            heads,
            heads,
            heads,
            P("tensor", "dp"),
        ),
        out_specs=(
            tokens,
            tokens,
            P(),
            matrix,
            matrix,
            P("dp", None),
            matrix,
            P(None, "tensor"),
            heads,
            P(),
            P(),
            heads,
            heads,
            heads,
            heads,
            P("tensor", "dp"),
        ),
        check_vma=False,
    )
```

```python
from functools import partial

import jax
import jax.numpy as jnp
from jax import lax
from jax.experimental import pallas as pl
from jax.experimental.pallas import tpu as pltpu
from jax.sharding import PartitionSpec as P

SPAN = 256
HALO = 16
LANES = 128
LOG2E = 1.4426950408889634
EPS = 1e-05
FAR = -1e30
HIGH = lax.Precision.HIGHEST
F32 = jnp.float32
BF16 = jnp.bfloat16
VMEM_BYTES = 60 * 1024 * 1024


def nn(a, b):
    return jnp.dot(a, b, preferred_element_type=F32)


def nt(a, b):
    return lax.dot_general(a, b, (((1,), (1,)), ((), ())), preferred_element_type=F32)


def tn(a, b):
    return lax.dot_general(a, b, (((0,), (0,)), ((), ())), preferred_element_type=F32)


def sigmoid(v):
    return 1.0 / (1.0 + jnp.exp(-v))


def iota(shape, axis):
    return lax.broadcasted_iota(jnp.int32, shape, axis)


def seg_at(lengths, pos):
    end = lengths[0, 0]
    found = (pos >= end).astype(jnp.int32)
    for i in range(1, 3):
        end = end + lengths[0, i]
        found = found + (pos >= end).astype(jnp.int32)
    return jnp.where(pos < 0, -1, found)


def same_as_behind(sc, pos, offset):
    return (seg_at(sc, pos - offset) == seg_at(sc, pos)).astype(F32)


def head_map(cols, start, first, both=True):
    k = iota((LANES, cols), 0)
    if both:
        k = k & 63
    head = ((iota((LANES, cols), 1) + start) >> 6) + first
    return (k == head).astype(BF16)


def expand(values, mapping):
    high = values.astype(BF16).astype(F32)
    low = values - high
    return nn((high + pltpu.roll(low, 64, axis=1)).astype(BF16), mapping)


def thirds(values):
    high = values.astype(BF16).astype(F32)
    left = values - high
    middle = left.astype(BF16).astype(F32)
    return (high + pltpu.roll(middle, 16, axis=1) + pltpu.roll(left - middle, 32, axis=1)).astype(BF16)


def joined(values):
    return values + pltpu.roll(values, LANES - 16, axis=1) + pltpu.roll(values, LANES - 32, axis=1)


def whole():
    return pl.BlockSpec(memory_space=pltpu.VMEM)


def scalars():
    return pl.BlockSpec(memory_space=pltpu.SMEM)


def params():
    return pltpu.CompilerParams(vmem_limit_bytes=VMEM_BYTES)


def cost(flops, nbytes):
    return pl.CostEstimate(flops=int(flops), bytes_accessed=int(nbytes), transcendentals=0)


def col_tile(ig):
    return 256 if ig % 256 == 0 else 128


def flip(me, v):
    out = me
    bit = 1
    while bit <= v:
        if v & bit:
            out = out + bit - 2 * bit * lax.rem(me // bit, 2)
        bit *= 2
    return out


def link_bits(size):
    bits = []
    bit = 2
    while bit < size:
        bits.append(bit)
        bit *= 2
    return bits


def remote(src, dst, send, recv, **where):
    return pltpu.make_async_remote_copy(
        src_ref=src, dst_ref=dst, send_sem=send, recv_sem=recv, device_id=where, device_id_type=pl.DeviceIdType.MESH
    )


def greet(bits, partners):
    me = lax.axis_index("dp")
    barrier = pltpu.get_barrier_semaphore()
    for bit in bits:
        pl.semaphore_signal(barrier, inc=1, device_id={"dp": flip(me, bit)}, device_id_type=pl.DeviceIdType.MESH)
    for to in partners:
        pl.semaphore_signal(barrier, inc=1, device_id={"tensor": to}, device_id_type=pl.DeviceIdType.MESH)
    pl.semaphore_wait(barrier, len(bits) + len(partners))


def others(parts):
    p = lax.axis_index("tensor")
    return [lax.rem(p + shift, parts) for shift in range(1, parts)]


def row(ref):
    return jnp.reshape(ref[...], (1, ref.shape[0]))


class ToHeads:
    def __init__(self, k, src, place_of, parts, send, recv, own):
        self.p = lax.axis_index("tensor")
        self.hp = parts // 2
        self.k, self.src, self.place_of = k, src, place_of
        self.send, self.recv, self.own = send, recv, own

    def copy(self, i, side, to):
        return remote(
            self.src, self.place_of(side), self.send.at[2 * self.k + i], self.recv.at[2 * self.k + side], tensor=to
        )

    def local(self, side):
        return pltpu.make_async_copy(self.src, self.place_of(side), self.own.at[self.k])

    def targets(self):
        return [self.p // 2, self.p // 2 + self.hp]

    def start(self):
        side = lax.rem(self.p, 2)
        for i, to in enumerate(self.targets()):

            @pl.when(to != self.p)
            def _(i=i, to=to):
                self.copy(i, side, to).start()

            @pl.when(to == self.p)
            def _():
                self.local(side).start()

    def wait(self):
        q = lax.rem(self.p, self.hp)
        for side in range(2):
            source = 2 * q + side

            @pl.when(source != self.p)
            def _(side=side):
                self.copy(0, side, self.p // 2).wait_recv()

            @pl.when(source == self.p)
            def _(side=side):
                self.local(side).wait()

    def finish(self):
        side = lax.rem(self.p, 2)
        for i, to in enumerate(self.targets()):

            @pl.when(to != self.p)
            def _(i=i, to=to):
                self.copy(i, side, to).wait_send()


class Gather:
    def __init__(self, k, ref, split, rows, size, send, recv):
        self.me = lax.axis_index("dp")
        self.k, self.ref, self.rows, self.size = k, ref, rows, size
        bits = link_bits(size)
        self.orders = [bits, bits[::-1]]
        self.cols = [slice(0, split), slice(split, ref.shape[1])]
        self.send, self.recv = send, recv
        self.sent = []

    def block(self, half, v):
        start = pl.multiple_of(flip(self.me, v) * self.rows, 16)
        cols = self.cols[half]
        return self.ref.at[pl.ds(start, self.rows), pl.ds(cols.start, cols.stop - cols.start)]

    def copy(self, half, v, bit):
        n = bit.bit_length() - 1
        here = self.block(half, v)
        return remote(
            here,
            here,
            self.send.at[self.k, half, v * self.size.bit_length() + n],
            self.recv.at[self.k, half, v ^ bit],
            dp=flip(self.me, bit),
        )

    def push(self, half, v, bits):
        for bit in bits:
            self.copy(half, v, bit).start()
            self.sent.append((half, v, bit))

    def arrive(self, half, v):
        here = self.block(half, v)
        remote(
            here,
            here,
            self.send.at[self.k, half, 0],
            self.recv.at[self.k, half, v],
            dp=flip(self.me, 1),
        ).wait_recv()

    def start(self):
        for half in range(2):
            self.push(half, 0, self.orders[half])
        for half in range(2):
            self.push(half, 0, [1])

    def stage(self, s):
        for half in range(2):
            order = self.orders[half]
            names = [0]
            for bit in order[:s]:
                names = names + [v ^ bit for v in names]
            for v in sorted(n ^ order[s] for n in names):
                self.arrive(half, v)
                self.push(half, v, order[s + 1 :])
                self.push(half, v, [1])

    def stages(self):
        return len(self.orders[0])

    def cores(self):
        for half in range(2):
            for v in range(1, self.size, 2):
                self.arrive(half, v)

    def finish(self):
        for half, v, bit in self.sent:
            self.copy(half, v, bit).wait_send()


class Scatter:
    def __init__(self, k, source, acc, own, size, core_buf, link_buf, cs, cr, ls, lr):
        self.me = lax.axis_index("dp")
        self.k, self.source, self.acc, self.own, self.size = k, source, acc, own, size
        self.core_buf, self.link_buf = core_buf, link_buf
        self.cs, self.cr, self.ls, self.lr = cs, cr, ls, lr
        bits = link_bits(size)
        self.orders = [bits, bits[::-1]]
        self.sent = []

    def core(self, half, u):
        return remote(
            self.source(half, 2 * u + 1),
            self.core_buf[half].at[u],
            self.cs.at[self.k, half, u],
            self.cr.at[self.k, half, u],
            dp=flip(self.me, 1),
        )

    def start(self, half):
        for u in range(self.size // 2):
            self.core(half, u).start()
            if self.own is not None:
                self.own(half, u).start()

    def add(self, half, u, other):
        ref = self.acc(half, u)
        ref[...] = ref[...] + other[...]

    def fold_core(self, half):
        for u in range(self.size // 2):
            self.core(half, u).wait_recv()
            if self.own is not None:
                self.own(half, u).wait()
            self.add(half, u, self.core_buf[half].at[u])

    def plan(self, half, s):
        order = self.orders[half]
        held, slot = list(range(0, self.size, 2)), 0
        for i, bit in enumerate(order):
            away = [v for v in held if v & bit]
            stay = [v for v in held if not v & bit]
            if i == s:
                return bit, away, stay, slot
            held, slot = stay, slot + len(stay)

    def link(self, half, s, i):
        bit, away, stay, slot = self.plan(half, s)
        n = slot + stay.index(away[i] ^ bit)
        return remote(
            self.acc(half, away[i] >> 1),
            self.link_buf[half].at[n],
            self.ls.at[self.k, half, n],
            self.lr.at[self.k, half, n],
            dp=flip(self.me, bit),
        )

    def send(self, half, s):
        for i in range(len(self.plan(half, s)[1])):
            self.link(half, s, i).start()

    def fold(self, half, s):
        bit, away, stay, slot = self.plan(half, s)
        for i in range(len(away)):
            self.link(half, s, i).wait_recv()
        for i, v in enumerate(stay):
            self.add(half, v >> 1, self.link_buf[half].at[slot + i])

    def stages(self):
        return len(self.orders[0])

    def finish_core(self):
        for half in range(2):
            for u in range(self.size // 2):
                self.core(half, u).wait_send()

    def finish_links(self):
        for half in range(2):
            for s in range(self.stages()):
                for i in range(len(self.plan(half, s)[1])):
                    self.link(half, s, i).wait_send()

    def finish(self):
        self.finish_core()
        self.finish_links()


class FromHeads:
    def __init__(self, k, block, slots, parts, send, recv, own):
        self.p = lax.axis_index("tensor")
        self.hp = parts // 2
        self.k, self.block, self.slots = k, block, slots
        self.send, self.recv, self.own = send, recv, own
        self.half = self.p // self.hp
        self.q = lax.rem(self.p, self.hp)

    def copy(self, side, slot):
        return remote(
            self.block(side),
            self.slots.at[slot],
            self.send.at[2 * self.k + side],
            self.recv.at[2 * self.k + slot],
            tensor=2 * self.q + side,
        )

    def local(self, side, slot):
        return pltpu.make_async_copy(self.block(side), self.slots.at[slot], self.own.at[self.k])

    def start(self, side):
        to = 2 * self.q + side

        @pl.when(to != self.p)
        def _():
            self.copy(side, self.half).start()

        @pl.when(to == self.p)
        def _():
            self.local(side, self.half).start()

    def wait(self):
        for slot in range(2):
            source = self.p // 2 + slot * self.hp

            @pl.when(source != self.p)
            def _(slot=slot):
                self.copy(0, slot).wait_recv()

            @pl.when(source == self.p)
            def _(slot=slot):
                self.local(0, slot).wait()

    def finish(self, sides=(0, 1)):
        for side in sides:

            @pl.when(2 * self.q + side != self.p)
            def _(side=side):
                self.copy(side, self.half).wait_send()


class Butterfly:
    def __init__(self, k, ref, slots, steps, send, recv):
        self.k, self.ref, self.slots, self.steps = k, ref, slots, steps
        self.send, self.recv = send, recv

    def copy(self, i):
        axis, bit = self.steps[i]
        return remote(
            self.ref,
            self.slots.at[i],
            self.send.at[self.k, i],
            self.recv.at[self.k, i],
            **{axis: flip(lax.axis_index(axis), bit)},
        )

    def push(self, i):
        self.copy(i).start()

    def fold(self, i):
        self.copy(i).wait()
        self.ref[...] += self.slots[i]


class AllZ:
    def __init__(self, ref, slots, parts, send, recv, own):
        self.p = lax.axis_index("tensor")
        self.ref, self.slots, self.parts = ref, slots, parts
        self.send, self.recv, self.own = send, recv, own

    def copy(self, shift):
        to = lax.rem(self.p + shift, self.parts)
        return remote(
            self.ref, self.slots.at[self.p], self.send.at[shift], self.recv.at[shift], tensor=to
        )

    def arrival(self, shift):
        there = self.slots.at[lax.rem(self.p + self.parts - shift, self.parts)]
        return remote(self.ref, there, self.send.at[shift], self.recv.at[shift], tensor=self.p)

    def mine(self):
        return pltpu.make_async_copy(self.ref, self.slots.at[self.p], self.own.at[0])

    def start(self):
        self.mine().start()
        for shift in range(1, self.parts):
            self.copy(shift).start()

    def total(self):
        self.mine().wait()
        for shift in range(1, self.parts):
            self.arrival(shift).wait_recv()
        value = self.slots[0]
        for i in range(1, self.parts):
            value = value + self.slots[i]
        return value

    def finish(self):
        for shift in range(1, self.parts):
            self.copy(shift).wait_send()


def sharded_rows(ref, me, v, rows, cols):
    start = pl.multiple_of(flip(me, v) * rows, 16)
    return ref.at[pl.ds(start, rows), pl.ds(cols[0], cols[1] - cols[0])]


def halves(split, total):
    return [(0, split), (split, total)]


def split_of(cols):
    return (cols // 2 + LANES - 1) // LANES * LANES


def first_body(
    size, parts, rows, ha, ig,
    ends, inputs, cot, ngain, w_x, w_z, w_out, w_bc, w_dt, conv_x, conv_x_bias, dt_bias, a_log, d_skip, gate_gain,
    taps_bc, bias_bc,
    tok_h, pulled_h, wx_h, wz_h, wo_h, ws_h, par_h, pre_h, bc_h, dtin_h, dt_h, lc_h, lr_h, em_h, et_h, kd_h,
    prex_h, xs_h, st_h, sin_h, z_h, dm_h, y_h, stat_o,
    tok, pulled, wx, wz, wo, ws, par, pre, bc, dtin, dt, lc, lr, em, et, kd, st, stage, xs, fin, sin, z, gated_s, y_stage, cb, off, stat, sums_out, sums_in,
    lags, w_dt_wide, table, maps_in,
    zs, zr, zo, gs, gr, ts, tr, cs, cr, hs, hr, ss, sr, ms, mr, local, outs, tiles,
):
    p = lax.axis_index("tensor")
    me = lax.axis_index("dp")
    hp = parts // 2
    place = lax.rem(p, hp)
    half = p // hp
    inner = 2 * ig
    local_rows, width = inputs.shape
    count = local_rows * hp
    total = count + HALO
    base = half * count
    own_rows = pl.multiple_of(place * local_rows, 16)

    def mates():
        return [(s, half * hp + lax.rem(place + s, hp)) for s in range(1, hp)]

    def my_rows():
        return pl.ds(pl.multiple_of(me * rows, 16), rows)

    def wide(ref, cols):
        return lambda side: ref.at[my_rows(), pl.ds(pl.multiple_of(side * cols, LANES), cols)]

    emitted = []

    def emit(src, dst):
        copy = pltpu.make_async_copy(src, dst, outs.at[len(emitted)])
        copy.start()
        emitted.append(copy)

    w_dt_wide[...] = jnp.zeros_like(w_dt_wide)
    w_dt_wide[:, :ha] = w_dt[...].T
    greet([1] + link_bits(size), others(parts))
    to_table = ToHeads(0, table, lambda side: par.at[:, pl.ds(pl.multiple_of(side * ig, LANES), ig)], parts, zs, zr, zo)
    to_dt = ToHeads(1, w_dt_wide, wide(ws, LANES), parts, zs, zr, zo)
    to_x = ToHeads(2, w_x, wide(wx, ig), parts, zs, zr, zo)
    to_z = ToHeads(3, w_z, wide(wz, ig), parts, zs, zr, zo)
    to_o = ToHeads(4, w_out, wide(wo, ig), parts, zs, zr, zo)
    to_dt.start()
    to_x.start()
    bc_copy = pltpu.make_async_copy(w_bc, ws.at[my_rows(), pl.ds(2 * LANES, 2 * LANES)], local.at[0])
    bc_copy.start()
    cot_copy = pltpu.make_async_copy(cot, pulled.at[pl.ds(own_rows, local_rows)], local.at[1])
    cot_copy.start()

    values = inputs[...].astype(F32)
    scale = lax.rsqrt(jnp.mean(values * values, axis=1, keepdims=True) + EPS)
    mine = pl.ds(pl.multiple_of(HALO + own_rows, 16), local_rows)
    tok[mine, :] = (values * scale * row(ngain)).astype(BF16)

    def tok_copy(s, to):
        return remote(tok.at[mine], tok.at[mine], ts.at[s], tr.at[s], tensor=to)

    def tok_arrive(s):
        there = pl.ds(pl.multiple_of(HALO + lax.rem(place + hp - s, hp) * local_rows, 16), local_rows)
        remote(tok.at[there], tok.at[there], ts.at[s], tr.at[s], tensor=p).wait_recv()

    piece = local_rows // 2

    def cot_copy_to(s, to, i):
        there = pl.ds(pl.multiple_of(own_rows + i * piece, 16), piece)
        return remote(cot.at[pl.ds(i * piece, piece)], pulled.at[there], cs.at[i, s], cr.at[i, s], tensor=to)

    def cot_arrive(s, i):
        start = lax.rem(place + hp - s, hp) * local_rows + i * piece
        there = pl.ds(pl.multiple_of(start, 16), piece)
        remote(pulled.at[there], pulled.at[there], cs.at[i, s], cr.at[i, s], tensor=p).wait_recv()

    def halo_copy(k):
        return remote(tok.at[pl.ds(total - HALO, HALO)], tok.at[pl.ds(0, HALO)], hs.at[k], hr.at[0], tensor=hp + k)

    for s, to in mates():
        tok_copy(s, to).start()

    @pl.when(p == hp - 1)
    def _():
        for k in range(hp):
            halo_copy(k).start()

    @pl.when(half == 0)
    def _():
        tok[:HALO, :] = jnp.zeros((HALO, width), BF16)

    for b in range(2):
        maps_in[b] = head_map(ig, 0, b * 16)
    table[...] = jnp.zeros_like(table)
    table[0:4, :] = conv_x[...]
    table[4:5, :] = row(conv_x_bias)
    table[5:6, :] = row(gate_gain)
    table[6:7, :ha] = row(d_skip)
    table[7:8, :ha] = row(dt_bias)
    table[7:8, LANES : LANES + ha] = row(a_log)
    to_table.start()

    g_s = Gather(0, ws, 2 * LANES, rows, size, gs, gr)
    g_x = Gather(1, wx, ig, rows, size, gs, gr)
    g_z = Gather(2, wz, ig, rows, size, gs, gr)
    g_o = Gather(3, wo, ig, rows, size, gs, gr)
    stages = g_x.stages()
    to_dt.wait()
    bc_copy.wait()
    g_s.start()
    to_x.wait()
    g_x.start()
    to_z.start()
    for s in range(stages):
        g_x.stage(s)
        g_s.stage(s)
        if s == 0:
            to_o.start()
    to_z.wait()
    g_z.start()
    g_s.cores()
    for s, _ in mates():
        tok_arrive(s)
    for s, to in mates():
        cot_copy_to(s, to, 0).start()

    @pl.when(half == 1)
    def _():
        halo_copy(0).wait_recv()

    emit(tok, tok_h)
    emit(ws, ws_h)

    both = nn(tok[...], ws[...])
    pre[...] = both[:, 2 * LANES :]
    emit(pre, pre_h)
    pos = base + iota((count, 1), 0)
    for j in range(1, 4):
        lags[j - 1] = jnp.broadcast_to(same_as_behind(ends, pos, j), (count, LANES))
    for side in range(2):
        at = slice(side * LANES, (side + 1) * LANES)
        acc = bias_bc[...].reshape(1, 2 * LANES)[:, at] + taps_bc[0:1, at] * pre[HALO : HALO + count, at]
        for j in range(1, 4):
            acc = acc + taps_bc[j : j + 1, at] * pre[HALO - j : HALO - j + count, at] * lags[j - 1]
        bc[:, at] = (acc * sigmoid(acc)).astype(BF16)
    emit(bc, bc_h)
    to_table.wait()
    emit(par, par_h)
    lane = iota((1, LANES), 1)
    keep = ((lane & 15) < ha).astype(F32) * (lane < 32).astype(F32)

    def merge(values):
        return values[0] + pltpu.roll(values[1], 16, axis=1)

    biases = merge([par[7:8, b * ig : b * ig + LANES] for b in range(2)])
    logs_a = merge([par[7:8, b * ig + LANES : b * ig + 2 * LANES] for b in range(2)])
    shifted = merge([both[HALO:, b * LANES : (b + 1) * LANES] for b in range(2)]) + biases
    steps = (jnp.maximum(shifted, 0.0) + jnp.log1p(jnp.exp(-jnp.abs(shifted)))) * keep
    dtin[...] = shifted
    dt[...] = steps
    scaled = steps * (-jnp.exp(logs_a) * LOG2E)
    tri = (iota((SPAN, SPAN), 0) >= iota((SPAN, SPAN), 1)).astype(F32)
    chunks = count // SPAN
    gone = []
    for c in range(chunks):
        span = slice(c * SPAN, (c + 1) * SPAN)
        logs = jnp.dot(tri, scaled[span, :], precision=HIGH, preferred_element_type=F32)
        first, last = base + c * SPAN - 1, base + (c + 1) * SPAN - 1
        here = base + c * SPAN + iota((SPAN, 1), 0)
        seg = seg_at(ends, here)
        seg_first, seg_last = seg_at(ends, first), seg_at(ends, last)
        final = logs[SPAN - 1 : SPAN, :]
        gone.append(jnp.where(seg_first == seg_last, 1.0, 0.0).astype(F32) * jnp.exp2(final) * keep)
        lc[span, :] = logs
        lr[:, span] = logs.T[:32, :]
        em[span, :] = (seg == seg_first).astype(F32) * jnp.exp2(logs) * keep
        et[span, :] = (seg == seg_last).astype(F32) * jnp.exp2(final - logs) * keep
    ahead_of, behind_of = [keep], [keep]
    for c in range(chunks - 1):
        ahead_of.append(ahead_of[-1] * gone[c])
        behind_of.append(behind_of[-1] * gone[chunks - 1 - c])
    behind_of = behind_of[::-1]
    fill = [jnp.zeros((1, LANES), F32)] * (8 - chunks)
    kd[...] = jnp.concatenate(gone + fill + ahead_of + fill + behind_of + fill, axis=0)
    for src, dst in ((dtin, dtin_h), (dt, dt_h), (lc, lc_h), (lr, lr_h), (em, em_h), (et, et_h), (kd, kd_h)):
        emit(src, dst)

    g_x.cores()
    emit(wx, wx_h)

    cols = col_tile(ig)

    def state_copy(j):
        at = pl.ds(pl.multiple_of(j * cols, cols), cols)
        return remote(fin.at[:, at], sin.at[:, at], ss.at[j], sr.at[j], tensor=lax.rem(p + hp, parts))

    def tile_out(kind, slot, j):
        at = pl.ds(pl.multiple_of(j * cols, cols), cols)
        if kind == 0:
            return pltpu.make_async_copy(stage.at[slot], prex_h.at[:, at], tiles.at[0, slot])
        return pltpu.make_async_copy(stage.at[slot, pl.ds(0, count)], dm_h.at[:, at], tiles.at[kind, slot])

    def xpath(j, carry):
        slot = lax.rem(j, 2)

        @pl.when(j >= 2)
        def _():
            tile_out(0, slot, j).wait()

        at = pl.multiple_of(j * cols, cols)
        lanes = pl.ds(at, cols)
        b = at // ig
        stage[slot] = nn(tok[...], wx[:, lanes])
        mapping = maps_in[b, :, pl.ds(pl.multiple_of(lax.rem(at, ig), LANES), cols)]
        state = jnp.zeros((LANES, cols), F32)
        decay = expand(kd[0:8, :], mapping)
        taps, bias = par[0:4, lanes], par[4:5, lanes]
        for c in range(chunks):
            low = c * SPAN
            weight = expand(dt[low : low + SPAN, :] * et[low : low + SPAN, :], mapping)
            weighted = []
            for side in range(cols // LANES):
                lane_at = slice(side * LANES, (side + 1) * LANES)
                window = stage[slot, low : low + SPAN + HALO, lane_at]
                conv = bias[:, lane_at] + taps[0:1, lane_at] * window[HALO:, :]
                for k in range(1, 4):
                    lag = pltpu.roll(window, k, axis=0)[HALO:, :]
                    conv = conv + taps[k : k + 1, lane_at] * lag * lags[k - 1, low : low + SPAN, :]
                value = (conv * sigmoid(conv)).astype(BF16)
                xs[low : low + SPAN, pl.ds(pl.multiple_of(at + side * LANES, LANES), LANES)] = value
                weighted.append((value.astype(F32) * weight[:, lane_at]).astype(BF16))
            st[c, :, lanes] = state
            fresh = tn(bc[low : low + SPAN, :LANES], jnp.concatenate(weighted, axis=1))
            state = decay[c : c + 1, :] * state + fresh
        fin[:, lanes] = state.astype(BF16)

        @pl.when(half == 0)
        def _():
            state_copy(j).start()

        tile_out(0, slot, j).start()
        return carry

    def project(j, carry):
        lanes = pl.ds(pl.multiple_of(j * cols, cols), cols)
        z[:, lanes] = nn(tok[HALO:, :], wz[:, lanes])
        return carry

    lane_row = iota((1, LANES), 1)
    sides = [(lane_row < 64).astype(BF16), (lane_row >= 64).astype(BF16)]
    middle_of = SPAN // 2

    def y_out(i):
        c, b = i // 2, lax.rem(i, 2)
        rows_to = pl.ds(pl.multiple_of(c * SPAN, SPAN), SPAN)
        lanes_to = pl.ds(pl.multiple_of(b * ig, LANES), ig)
        return pltpu.make_async_copy(y_stage.at[b], y_h.at[rows_to, lanes_to], tiles.at[2, b])

    def scan(i, carry):
        c, b = i // 2, lax.rem(i, 2)
        rows_here = pl.ds(pl.multiple_of(c * SPAN, SPAN), SPAN)
        lanes_b = pl.ds(pl.multiple_of(b * ig, LANES), ig)

        @pl.when(i >= 2)
        def _():
            y_out(i).wait()

        b_map, c_map = bc[rows_here, :LANES], bc[rows_here, LANES:]
        cb[...] = nt(c_map, b_map)
        start = base + c * SPAN
        t, s = iota((SPAN, SPAN), 0), iota((SPAN, SPAN), 1)
        seg_row, seg_col = seg_at(ends, start + iota((1, SPAN), 1)), seg_at(ends, start + iota((SPAN, 1), 0))
        off[...] = jnp.where((t >= s) & (seg_col == seg_row), 0.0, FAR)
        mapping = maps_in[b]
        steps_wide = expand(dt[rows_here, :], mapping)
        lead_wide = expand(em[rows_here, :], mapping)
        arriving = expand(kd[8:16, :], mapping) * (iota((8, 1), 0) == c).astype(F32)
        state = st[c, :, lanes_b] + jnp.sum(arriving, axis=0, keepdims=True) * sin[:, lanes_b].astype(F32)
        skips = par[6:7, pl.ds(pl.multiple_of(b * ig, LANES), LANES)]
        skip = expand(jnp.broadcast_to(skips, (8, LANES)), maps_in[0])[0:1, :]
        read = nn(c_map, state.astype(BF16))
        columns = pltpu.roll(lc[rows_here, :], lax.rem(LANES - 16 * b, LANES), axis=1)
        lines = lr[pl.ds(pl.multiple_of(b * 16, 16), 16), rows_here]
        square = jnp.zeros((SPAN, LANES), F32)
        for k in range(ig // LANES):
            at = slice(k * LANES, (k + 1) * LANES)
            there = pl.ds(pl.multiple_of(b * ig + k * LANES, LANES), LANES)
            xf = xs[rows_here, there].astype(F32)
            pair = (xf * steps_wide[:, at]).astype(BF16)
            far = read[:, at] * lead_wide[:, at] + skip[:, at] * xf
            top = far[:middle_of]
            low = far[middle_of:]
            for side in range(2):
                h = 2 * k + side
                operand = pair * sides[side]
                column = columns[:, h : h + 1]
                line = lines[h : h + 1, :]
                gap = column[:middle_of] - line[:, :middle_of] + off[:middle_of, :middle_of]
                w_top = cb[:middle_of, :middle_of] * jnp.exp2(gap)
                top = top + nn(w_top.astype(BF16), operand[:middle_of, :])
                w_low = cb[middle_of:, :] * jnp.exp2(column[middle_of:] - line + off[middle_of:, :])
                low = low + nn(w_low.astype(BF16), operand)
            out = jnp.concatenate([top, low], axis=0)
            y_stage[b, :, at] = out
            gate = z[rows_here, there]
            gated = out * (gate * sigmoid(gate))
            gated_s[rows_here, there] = gated
            square = square + gated * gated
        y_out(i).start()
        held = jnp.where(b == 0, 0.0, stat[rows_here, :])
        stat[rows_here, :] = held + jnp.where(lane_row == 0, jnp.sum(square, axis=1, keepdims=True), 0.0)
        return carry

    def dm_tile(j, cross):
        slot = lax.rem(j, 2)

        @pl.when(j >= 2)
        def _():
            tile_out(1, slot, j).wait()

        lanes = pl.ds(pl.multiple_of(j * cols, cols), cols)
        value = nn(pulled[...], wo[:, lanes])
        stage[slot, :count, :] = value
        tile_out(1, slot, j).start()
        share = value * gated_s[:, lanes] * par[5:6, lanes]
        for i in range(cols // LANES):
            cross = cross + share[:, i * LANES : (i + 1) * LANES]
        return cross

    tiles_all = inner // cols
    middle = tiles_all // 2

    def drain(kind):
        for j in range(tiles_all - 2, tiles_all):
            tile_out(kind, j % 2, j).wait()

    lax.fori_loop(0, middle, xpath, 0)
    for s in range(stages - 1):
        g_z.stage(s)
    lax.fori_loop(middle, tiles_all, xpath, 0)
    for s, to in mates():
        cot_copy_to(s, to, 1).start()
    emit(xs, xs_h)
    emit(st, st_h)
    g_z.stage(stages - 1)
    to_o.wait()
    g_o.start()
    drain(0)
    g_z.cores()
    emit(wz, wz_h)
    lax.fori_loop(0, tiles_all, project, 0)
    emit(z, z_h)

    @pl.when(half == 1)
    def _():
        for j in range(tiles_all):
            state_copy(j).wait_recv()

    @pl.when(half == 0)
    def _():
        sin[...] = jnp.zeros_like(sin)

    emit(sin, sin_h)
    lax.fori_loop(0, chunks, scan, 0)
    for s in range(stages - 1):
        g_o.stage(s)
    lax.fori_loop(chunks, 2 * chunks, scan, 0)
    g_o.stage(stages - 1)
    g_o.cores()
    emit(wo, wo_h)
    for s, _ in mates():
        for i in range(2):
            cot_arrive(s, i)
    cot_copy.wait()
    emit(pulled, pulled_h)
    cross = lax.fori_loop(0, tiles_all, dm_tile, jnp.zeros((count, LANES), F32))
    stat[...] += jnp.where(lane_row == 1, jnp.sum(cross, axis=1, keepdims=True), 0.0)
    sums_out[...] = stat[...].T[:8, :]

    def stat_copy(s, to):
        return remote(sums_out, sums_in.at[s - 1], ms.at[s - 1], mr.at[s - 1], tensor=to)

    for s, to in mates():
        stat_copy(s, to).start()
    drain(1)
    for i in range(2 * chunks - 2, 2 * chunks):
        y_out(i).wait()
    for s, to in mates():
        stat_copy(s, to).wait()
    summed = sums_out[...]
    for s in range(1, hp):
        summed = summed + sums_in[s - 1]
    stat_o[...] = jnp.concatenate([summed, jnp.zeros((LANES - 8, count), F32)], axis=0).T
    for item in (to_table, to_dt, to_x, to_z, to_o, g_s, g_x, g_z, g_o):
        item.finish()
    for s, to in mates():
        tok_copy(s, to).wait_send()
        for i in range(2):
            cot_copy_to(s, to, i).wait_send()

    @pl.when(p == hp - 1)
    def _():
        for k in range(hp):
            halo_copy(k).wait_send()

    @pl.when(half == 0)
    def _():
        for j in range(tiles_all):
            state_copy(j).wait_send()

    for copy in emitted:
        copy.wait()


def run_first(
    ends, inputs, cot, ngain, w_x, w_z, w_out, w_bc, w_dt, conv_x, conv_x_bias, dt_bias, a_log, d_skip, gate_gain,
    taps_bc, bias_bc, size, parts,
):
    ha = dt_bias.shape[0]
    local_rows, width = inputs.shape
    rows, ig = w_x.shape
    inner = 2 * ig
    hp = parts // 2
    count = local_rows * hp
    total = count + HALO
    chunks = count // SPAN
    cols = col_tile(ig)
    shape = jax.ShapeDtypeStruct
    per_block = shape((count, LANES), F32)
    outs = (
        shape((total, width), BF16),
        shape((count, width), BF16),
        shape((width, inner), BF16),
        shape((width, inner), BF16),
        shape((width, inner), BF16),
        shape((width, 4 * LANES), BF16),
        shape((8, inner), F32),
        shape((total, 2 * LANES), F32),
        shape((count, 2 * LANES), BF16),
        per_block,
        per_block,
        per_block,
        shape((32, count), F32),
        per_block,
        per_block,
        shape((24, LANES), F32),
        shape((total, inner), F32),
        shape((count, inner), BF16),
        shape((chunks, LANES, inner), F32),
        shape((LANES, inner), BF16),
        shape((count, inner), F32),
        shape((count, inner), F32),
        shape((count, inner), F32),
        shape((count, LANES), F32),
    )
    anywhere = pl.BlockSpec(memory_space=pl.ANY)
    dma = pltpu.SemaphoreType.DMA
    nbits = size.bit_length()
    scratch = [pltpu.VMEM(o.shape, o.dtype) for o in outs[:16]]
    scratch += [
        pltpu.VMEM((chunks, LANES, inner), F32),
        pltpu.VMEM((2, total, cols), F32),
        pltpu.VMEM((count, inner), BF16),
        pltpu.VMEM((LANES, inner), BF16),
        pltpu.VMEM((LANES, inner), BF16),
        pltpu.VMEM((count, inner), F32),
        pltpu.VMEM((count, inner), F32),
        pltpu.VMEM((2, SPAN, ig), F32),
        pltpu.VMEM((SPAN, SPAN), F32),
        pltpu.VMEM((SPAN, SPAN), F32),
        pltpu.VMEM((count, LANES), F32),
        pltpu.VMEM((8, count), F32),
        pltpu.VMEM((hp - 1, 8, count), F32),
        pltpu.VMEM((3, count, LANES), F32),
        pltpu.VMEM((rows, LANES), BF16),
        pltpu.VMEM((8, ig), F32),
        pltpu.VMEM((2, LANES, ig), BF16),
        dma((10,)),
        dma((10,)),
        dma((5,)),
        dma((4, 2, size * nbits)),
        dma((4, 2, size)),
        dma((hp,)),
        dma((hp,)),
        dma((2, hp)),
        dma((2, hp)),
        dma((hp,)),
        dma((1,)),
        dma((inner // cols,)),
        dma((inner // cols,)),
        dma((hp - 1,)),
        dma((hp - 1,)),
        dma((2,)),
        dma((24,)),
        dma((3, 2)),
    ]
    return pl.pallas_call(
        partial(first_body, size, parts, rows, ha, ig),
        out_shape=outs,
        in_specs=[scalars(), whole(), anywhere, whole(), anywhere, anywhere, anywhere, anywhere] + [whole()] * 9,
        out_specs=[anywhere] * (len(outs) - 1) + [whole()],
        scratch_shapes=scratch,
        compiler_params=pltpu.CompilerParams(vmem_limit_bytes=VMEM_BYTES, collective_id=0, has_side_effects=True),
        cost_estimate=cost(2 * total * width * (3 * inner + 512), 60e6),
        name="first",
    )(
        ends, inputs, cot, ngain, w_x, w_z, w_out, w_bc, w_dt, conv_x, conv_x_bias, dt_bias, a_log, d_skip,
        gate_gain, taps_bc, bias_bc,
    )


def gate_body(
    size, parts, ig, inner_all, gz_tiles, y, z, dm, stats, xs, par, bc, em, kd, tok_h, pulled_h, wo,
    dz_o, dy_o, sums_o, ds_o, gz_h, go_h, dsin_o, branch_o,
    first, dsin, tok, pulled, mixed_s, dz_s, gz, go, zcore, ocore, loads, ss, sr, ccs, ccr, outs,
):
    count, cols = y.shape
    j = pl.program_id(0)
    tiles = gz_tiles
    p = lax.axis_index("tensor")
    hp = parts // 2
    part = p // hp
    peer = lax.rem(p + hp, parts)

    me = lax.axis_index("dp")
    rows = go.shape[0] // size

    def scatter(k, ref, core_buf):
        columns = halves(ig, 2 * ig)

        def block(h, v):
            return sharded_rows(ref, me, v, rows, columns[h])

        return Scatter(k, block, lambda h, u: block(h, 2 * u), None, size, core_buf, None, ccs, ccr, None, None)

    scat_o, scat_z = scatter(0, go, ocore), scatter(1, gz, zcore)

    def sums_out(k, ref, dst):
        return [
            pltpu.make_async_copy(sharded_rows(ref, me, 2 * u, rows, (0, 2 * ig)), dst.at[u], outs.at[k, u])
            for u in range(size // 2)
        ]

    def state_copy(i):
        at = pl.ds(pl.multiple_of(i * cols, cols), cols)
        return remote(first.at[:, at], dsin.at[:, at], ss.at[i], sr.at[i], tensor=peer)

    def elementwise():
        at = j * cols
        here = pl.ds(pl.multiple_of(at, cols), cols)
        mapping = head_map(cols, lax.rem(at, ig), at // ig * 16)
        gone = expand(kd[0:8, :], mapping)
        gain = par[5:6, :]
        grad = jnp.zeros((LANES, cols), F32)
        by_gain = jnp.zeros((1, cols), F32)
        by_skip = jnp.zeros((1, cols), F32)
        for c in range(count // SPAN - 1, -1, -1):
            span = slice(c * SPAN, (c + 1) * SPAN)
            stat = stats[span, :]
            scale = lax.rsqrt(stat[:, 0:1] / inner_all + EPS)
            pull = scale * scale * scale * stat[:, 1:2] / inner_all
            gate = z[span, :]
            sig = sigmoid(gate)
            act = gate * sig
            out = y[span, :]
            gated = out * act
            normal = gated * scale
            mixed = (normal * gain).astype(BF16)
            mixed_s[span, here] = mixed
            upstream = dm[span, :]
            by_gain = by_gain + jnp.sum(upstream * normal, axis=0, keepdims=True)
            dgated = scale * (upstream * gain) - gated * pull
            dz = (dgated * out * (sig * (1.0 + gate * (1.0 - sig)))).astype(BF16)
            dz_o[span, :] = dz
            dz_s[span, here] = dz
            dy = dgated * act
            by_skip = by_skip + jnp.sum(dy * xs[span, :].astype(F32), axis=0, keepdims=True)
            dy_o[span, :] = dy.astype(BF16)
            ds_o[c] = grad
            lead = (dy * expand(em[span, :], mapping)).astype(BF16)
            grad = gone[c : c + 1, :] * grad + tn(bc[span, LANES:], lead)
        sums_o[...] = jnp.concatenate([by_gain, by_skip, jnp.zeros((6, cols), F32)], axis=0)
        first[:, pl.ds(pl.multiple_of(j * cols, cols), cols)] = grad.astype(BF16)

        @pl.when(part == 1)
        def _():
            state_copy(j).start()

    def load(i):
        src, dst = ((pulled_h, pulled), (tok_h, tok))[i]
        return pltpu.make_async_copy(src, dst, loads.at[i])

    @pl.when(j == 0)
    def _():
        greet([1], [peer])
        load(0).start()
        load(1).start()

    @pl.when(j < tiles)
    def _():
        elementwise()

    @pl.when(j == tiles)
    def _():
        load(0).wait()
        load(1).wait()

    @pl.when((j >= tiles) & (j < 2 * tiles))
    def _():
        here = pl.ds(pl.multiple_of((j - tiles) * cols, cols), cols)
        go[:, here] = tn(pulled[...], mixed_s[:, here]).astype(BF16)
        gz[:, here] = tn(tok[HALO:, :], dz_s[:, here]).astype(BF16)

    for h in range(2):

        @pl.when(j == tiles + (h + 1) * (tiles // 2) - 1)
        def _(h=h):
            scat_o.start(h)
            scat_z.start(h)

    @pl.when(j >= 2 * tiles)
    def _():
        branch_o[...] = nt(mixed_s[...], wo[...]).astype(BF16)

    last = pl.num_programs(0) - 1
    for h in range(2):

        @pl.when(j == 2 * tiles + h * 2 + 1)
        def _(h=h):
            scat_o.fold_core(h)

        @pl.when(j == 2 * tiles + h * 2 + 2)
        def _(h=h):
            scat_z.fold_core(h)

    @pl.when(j == last - 1)
    def _():
        for copy in sums_out(0, go, go_h):
            copy.start()

    @pl.when(j == last)
    def _():
        for copy in sums_out(1, gz, gz_h):
            copy.start()

    @pl.when(j == last)
    def _():
        scat_o.finish_core()
        scat_z.finish_core()
        for copy in sums_out(0, go, go_h) + sums_out(1, gz, gz_h):
            copy.wait()

        def send_done(i, carry):
            state_copy(i).wait_send()
            return carry

        def arrived(i, carry):
            state_copy(i).wait_recv()
            return carry

        @pl.when(part == 1)
        def _():
            lax.fori_loop(0, tiles, send_done, 0)
            dsin_o[...] = jnp.zeros_like(dsin_o)

        @pl.when(part == 0)
        def _():
            lax.fori_loop(0, tiles, arrived, 0)
            dsin_o[...] = dsin[...]


def run_gate(y, z, dm, stat, xs, par, bc, em, kd, tok, pulled, wo, ig, inner_all, size, parts):
    count, inner = y.shape
    width = tok.shape[1]
    cols = col_tile(ig)
    tiles = inner // cols
    chunks = count // SPAN

    def now(j):
        return jnp.minimum(j, tiles - 1)

    tile = pl.BlockSpec((count, cols), lambda j: (0, now(j)))
    grads = pl.BlockSpec(memory_space=pl.ANY)
    rows = width // size
    blocks = size // 2

    def out(j):
        return jnp.maximum(j - 2 * tiles, 0)

    low = jax.ShapeDtypeStruct((count, inner), BF16)
    shape = jax.ShapeDtypeStruct
    return pl.pallas_call(
        partial(gate_body, size, parts, ig, inner_all, tiles),
        grid=(2 * tiles + width // SPAN,),
        out_shape=(
            low,
            low,
            shape((8, inner), F32),
            shape((chunks, LANES, inner), F32),
            shape((blocks, rows, inner), BF16),
            shape((blocks, rows, inner), BF16),
            shape((LANES, inner), BF16),
            shape((count, width), BF16),
        ),
        in_specs=[
            tile,
            tile,
            tile,
            whole(),
            tile,
            pl.BlockSpec((8, cols), lambda j: (0, now(j))),
            whole(),
            whole(),
            whole(),
            pl.BlockSpec(memory_space=pl.ANY),
            pl.BlockSpec(memory_space=pl.ANY),
            pl.BlockSpec((SPAN, inner), lambda j: (out(j), 0)),
        ],
        out_specs=(
            tile,
            tile,
            pl.BlockSpec((8, cols), lambda j: (0, now(j))),
            pl.BlockSpec((chunks, LANES, cols), lambda j: (0, 0, now(j))),
            grads,
            grads,
            whole(),
            pl.BlockSpec((count, SPAN), lambda j: (0, out(j))),
        ),
        scratch_shapes=[
            pltpu.VMEM((LANES, inner), BF16),
            pltpu.VMEM((LANES, inner), BF16),
            pltpu.VMEM(tok.shape, BF16),
            pltpu.VMEM(pulled.shape, BF16),
            pltpu.VMEM((count, inner), BF16),
            pltpu.VMEM((count, inner), BF16),
            pltpu.VMEM((width, inner), BF16),
            pltpu.VMEM((width, inner), BF16),
            [pltpu.VMEM((blocks, rows, ig), BF16)] * 2,
            [pltpu.VMEM((blocks, rows, ig), BF16)] * 2,
            pltpu.SemaphoreType.DMA((2,)),
            pltpu.SemaphoreType.DMA((tiles,)),
            pltpu.SemaphoreType.DMA((tiles,)),
            pltpu.SemaphoreType.DMA((2, 2, blocks)),
            pltpu.SemaphoreType.DMA((2, 2, blocks)),
            pltpu.SemaphoreType.DMA((2, blocks)),
        ],
        compiler_params=pltpu.CompilerParams(vmem_limit_bytes=VMEM_BYTES, collective_id=4, has_side_effects=True),
        cost_estimate=cost(12e9, 30e6),
        name="gate",
    )(y, z, dm, stat, xs, par, bc, em, kd, tok, pulled, wo)


def pull_body(
    size, parts, ha, wrows,
    sc, xs, dy, bc, dtin, dt, lc, lr, em, et, kd, st, sin, ds, dsin, pre, par,
    inputs_h, branch_h, gz_h, go_h, tok_h,
    dx_o, dbc_o, ddt_o, csum_o, hsum_o, out_o, gz_o, go_o, ga_o,
    cbt, off, dcb, ahead, lags, products, tails, leads, rsum, maps_in, maps_out, skips, inputs, branch, arrived, tok, ga, dlow, dother,
    zacc, oacc, acore, zlink, olink, alink, zz, oz,
    loads, ccs, ccr, cls, clr, hs, hr, ho, ms, mr, bs, br,
):
    b, step = pl.program_id(0), pl.program_id(1)
    chunks = pl.num_programs(1)
    c = chunks - 1 - step
    cols = xs.shape[1]
    half = SPAN // 2
    p = lax.axis_index("tensor")
    me = lax.axis_index("dp")
    hp = parts // 2
    place = lax.rem(p, hp)
    part = p // hp
    count = dbc_o.shape[0]
    local_rows = inputs.shape[0]
    start = part * count + c * SPAN
    n = b * chunks + step
    rows_here = pl.ds(pl.multiple_of(c * SPAN, SPAN), SPAN)

    def scatter(k, acc, link_buf):
        columns = halves(cols, 2 * cols)
        return Scatter(
            k, None, lambda h, u: acc.at[u, :, pl.ds(columns[h][0], cols)], None, size, None, link_buf, ccs, ccr, cls, clr
        )

    def a_block(h, v):
        return sharded_rows(ga, me, v, wrows, halves(split_of(cols), cols)[h])

    scat_o = scatter(0, oacc, olink)
    scat_z = scatter(1, zacc, zlink)
    scat_a = Scatter(2, a_block, lambda h, u: a_block(h, 2 * u), None, size, acore, alink, ccs, ccr, cls, clr)
    home_o = FromHeads(0, lambda side: oacc.at[0, :, pl.ds(side * cols, cols)], oz, parts, hs, hr, ho)
    home_z = FromHeads(1, lambda side: zacc.at[0, :, pl.ds(side * cols, cols)], zz, parts, hs, hr, ho)
    stages = scat_o.stages()

    def mates():
        return [(s, part * hp + lax.rem(place + s, hp)) for s in range(1, hp)]

    def branch_copy(s, to):
        rows_to = pl.ds(pl.multiple_of(lax.rem(place + s, hp) * local_rows, 16), local_rows)
        return remote(branch_h.at[rows_to], arrived.at[s - 1], bs.at[s - 1], br.at[s - 1], tensor=to)

    def maps_copy(s, to, i):
        at = pl.ds(pl.multiple_of(i * SPAN, SPAN), SPAN)
        return remote(dlow.at[at], dother.at[s - 1, at], ms.at[s - 1, i], mr.at[s - 1, i], tensor=to)

    def branch_own():
        own = pl.ds(pl.multiple_of(place * local_rows, 16), local_rows)
        return pltpu.make_async_copy(branch_h.at[own], branch, loads.at[0])

    def inputs_load():
        return pltpu.make_async_copy(inputs_h, inputs, loads.at[4])

    def tok_load():
        return pltpu.make_async_copy(tok_h, tok, loads.at[1])

    @pl.when(n == 0)
    def _():
        sums = [pltpu.make_async_copy(src, dst, loads.at[2 + i]) for i, (src, dst) in enumerate(((go_h, oacc), (gz_h, zacc)))]
        for copy in sums:
            copy.start()
        greet([1] + link_bits(size), others(parts))
        for s, to in mates():
            branch_copy(s, to).start()
        for copy in sums:
            copy.wait()
        for h in range(2):
            scat_o.send(h, 0)
        branch_own().start()
        inputs_load().start()
        tok_load().start()

    @pl.when(n == 1)
    def _():
        for h in range(2):
            scat_z.send(h, 0)

    @pl.when(n == 2)
    def _():
        for s in range(stages - 1):
            for h in range(2):
                scat_o.fold(h, s)
                scat_o.send(h, s + 1)

    @pl.when(n == 3)
    def _():
        for h in range(2):
            scat_o.fold(h, stages - 1)
            home_o.start(h)
        for s in range(stages - 1):
            for h in range(2):
                scat_z.fold(h, s)
                scat_z.send(h, s + 1)

    @pl.when(n == 4)
    def _():
        for h in range(2):
            scat_z.fold(h, stages - 1)
            home_z.start(h)

    @pl.when(n == chunks + 1)
    def _():
        for h in range(2):
            scat_a.fold_core(h)
            scat_a.send(h, 0)

    @pl.when(n == chunks + 2)
    def _():
        for s in range(stages - 1):
            for h in range(2):
                scat_a.fold(h, s)
                scat_a.send(h, s + 1)

    b_map, c_map = bc[:, :LANES], bc[:, LANES:]
    cbt[...] = nt(b_map, c_map)
    s, t = iota((SPAN, SPAN), 0), iota((SPAN, SPAN), 1)
    seg_row, seg_col = seg_at(sc, start + iota((1, SPAN), 1)), seg_at(sc, start + iota((SPAN, 1), 0))
    off[...] = jnp.where((t >= s) & (seg_col == seg_row), 0.0, FAR)
    here = start + iota((SPAN, LANES), 0)
    for j in range(1, 4):
        lags[j - 1] = same_as_behind(sc, here, j)
    dcb[...] = jnp.zeros_like(dcb)

    @pl.when(step == 0)
    def _():
        ahead[...] = jnp.zeros_like(ahead)
        csum_o[...] = jnp.zeros_like(csum_o)
        hsum_o[...] = jnp.zeros_like(hsum_o)
        rsum[...] = jnp.zeros_like(rsum)
        maps_in[...] = head_map(cols, 0, b * 16)
        maps_out[...] = head_map(cols, 0, 0, both=False)
        skips[...] = expand(jnp.broadcast_to(par[6:7, :LANES], (8, LANES)), head_map(cols, 0, 0))

    lane = iota((1, LANES), 1)
    taps, bias = par[0:4, :], par[4:5, :]
    skip = skips[0:1, :]
    mapping = maps_in[...]
    single = maps_out[...]
    columns = pltpu.roll(lc[...], lax.rem(LANES - 16 * b, LANES), axis=1)

    def mine(values):
        return pltpu.roll(values, lax.rem(LANES - 16 * b, LANES), axis=1) * (lane < ha).astype(F32)

    sides = [(lane < 64).astype(BF16), (lane >= 64).astype(BF16)]
    steps = mine(dt[...])
    steps_wide = expand(dt[...], mapping)
    lead_wide = expand(em[...], mapping)
    tail_wide = expand(et[...], mapping)
    decays = expand(kd[...], mapping)
    pick = (iota((8, 1), 0) == c).astype(F32)
    state = st[0] + jnp.sum(decays[8:16] * pick, axis=0, keepdims=True) * sin[...].astype(F32)
    dstate = ds[0] + jnp.sum(decays[16:24] * pick, axis=0, keepdims=True) * dsin[...].astype(F32)
    state_l, dstate_l = state.astype(BF16), dstate.astype(BF16)
    crossing = jnp.sum(state * dstate, axis=0, keepdims=True)
    read = nn(c_map, state_l)
    far = nn(b_map, dstate_l)
    csums = jnp.zeros((SPAN, LANES), F32)
    blank = jnp.zeros((8, LANES), F32)
    window_at = pl.ds(pl.multiple_of(c * SPAN, SPAN), SPAN + HALO)
    out_at = pl.ds(pl.multiple_of(HALO + c * SPAN, HALO), SPAN)
    for k in range(cols // LANES):
        at = slice(k * LANES, (k + 1) * LANES)
        xf = xs[:, at].astype(F32)
        wide = steps_wide[:, at]
        x_pair, dy_pair = (xf * wide).astype(BF16), dy[:, at]
        top = jnp.zeros((half, LANES), F32)
        low = jnp.zeros((half, LANES), F32)
        for side in range(2):
            h = 2 * k + side
            x_one = x_pair * sides[side]
            dy_one = dy_pair * sides[side]
            column = columns[:, h : h + 1]
            row = lr[h : h + 1, :]
            decay = jnp.exp2(row - column[:half] + off[:half, :])
            top = top + nn((cbt[:half, :] * decay).astype(BF16), dy_one)
            share = nt(x_one[:half, :], dy_pair) * decay
            dcb[:half, :] += share
            both = share * cbt[:half, :]
            row_sum = jnp.sum(both, axis=0, keepdims=True)
            col_top = jnp.sum(both, axis=1, keepdims=True)
            decay = jnp.exp2(row[:, half:] - column[half:] + off[half:, half:])
            low = low + nn((cbt[half:, half:] * decay).astype(BF16), dy_one[half:, :])
            share = nt(x_one[half:, :], dy_pair[half:, :]) * decay
            dcb[half:, half:] += share
            both = share * cbt[half:, half:]
            rsum[h : h + 1, :half] = row_sum[:, :half]
            rsum[h : h + 1, half:] = row_sum[:, half:] + jnp.sum(both, axis=0, keepdims=True)
            col_low = jnp.sum(both, axis=1, keepdims=True)
            csums = csums + jnp.where(lane == h, jnp.concatenate([col_top, col_low], axis=0), 0.0)
        near = jnp.concatenate([top, low], axis=0)
        tail = tail_wide[:, at]
        dx_far = far[:, at] * tail
        tails[:, at] = (x_pair.astype(F32) * tail).astype(BF16)
        dyf = dy_pair.astype(F32)
        led = dyf * lead_wide[:, at]
        leads[:, at] = led.astype(BF16)
        products[0, :, at] = (xf * near).astype(BF16)
        products[1, :, at] = (xf * dx_far).astype(BF16)
        products[2, :, at] = (led * read[:, at]).astype(BF16)
        dxs = (near + dx_far) * wide + dyf * skip[:, at]

        window = pre[window_at, at]
        lagged = [window[HALO:, :]]
        for j in range(1, 4):
            lagged.append(pltpu.roll(window, j, axis=0)[HALO:, :] * lags[j - 1])
        conv = bias[:, at]
        for j in range(4):
            conv = conv + taps[j : j + 1, at] * lagged[j]
        sig = sigmoid(conv)
        dconv = dxs * (sig * (1.0 + conv * (1.0 - sig)))
        sums = [jnp.sum(dconv * lagged[j], axis=0, keepdims=True) for j in range(4)]
        sums.append(jnp.sum(dconv, axis=0, keepdims=True))
        csum_o[:, at] += jnp.concatenate(sums + [jnp.zeros((3, LANES), F32)], axis=0)
        dpre = taps[0:1, at] * dconv
        edge = jnp.zeros((HALO, LANES), F32)
        for j in range(1, 4):
            masked = dconv * lags[j - 1]
            longer = jnp.concatenate([masked, ahead[8 * (j - 1) : 8 * j, at]], axis=0)
            dpre = dpre + taps[j : j + 1, at] * pltpu.roll(longer, SPAN + 8 - j, axis=0)[:SPAN, :]
            opening = masked[:8, :]
            ahead[8 * (j - 1) : 8 * j, at] = opening
            before = pltpu.roll(jnp.concatenate([blank, blank, opening], axis=0), 24 - j, axis=0)[:HALO, :]
            edge = edge + taps[j : j + 1, at] * before
        dx_o[out_at, at] = dpre.astype(BF16)
        dx_o[:HALO, at] = edge.astype(BF16)
    db = nn(dcb[...].astype(BF16), c_map) + nt(tails[...], dstate_l)
    dc = tn(dcb[...].astype(BF16), b_map) + nt(leads[...], state_l)

    @pl.when(b == 0)
    def _():
        dbc_o[rows_here, :LANES] = db
        dbc_o[rows_here, LANES:] = dc

    @pl.when(b > 0)
    def _():
        dlow[rows_here, :LANES] = (dbc_o[rows_here, :LANES] + db).astype(BF16)
        dlow[rows_here, LANES:] = (dbc_o[rows_here, LANES:] + dc).astype(BF16)
        for s, to in mates():
            maps_copy(s, to, c).start()

    from_near = nt(products[0], single)
    from_far = nt(products[1], single)
    reads = nt(products[2], single)
    high = crossing.astype(BF16).astype(F32)
    middle = (crossing - high).astype(BF16).astype(F32)
    pieces = jnp.concatenate([high, middle, crossing - high - middle, jnp.zeros((5, cols), F32)], axis=0)
    held = jnp.sum(nt(pieces.astype(BF16), single), axis=0, keepdims=True)
    held = held * mine(jnp.broadcast_to(jnp.sum(kd[0:8, :] * pick, axis=0, keepdims=True), (8, LANES)))[0:1, :]
    lower = (s > t).astype(BF16)
    upper = (s <= t).astype(BF16)
    dlog = joined(nn(upper, thirds(rsum[...].T - csums + reads)) + nn(lower, thirds(steps * from_far))) + held
    rates = jnp.concatenate([par[7:8, LANES : 2 * LANES], jnp.zeros((7, LANES), F32)], axis=0)
    rate = -jnp.exp(rates)[0:1, :]
    dstep = from_near + from_far + dlog * rate
    ddt = dstep * mine(sigmoid(dtin[...]))
    ddt_o[0] = ddt
    hsum_o[0, 0:1, :] += jnp.sum(ddt, axis=0, keepdims=True)
    hsum_o[0, 1:2, :] += jnp.sum(dlog * steps * rate, axis=0, keepdims=True)

    @pl.when(n == chunks - 1)
    def _():
        tok_load().wait()
        wide = col_tile(cols)

        def grad_tile(j, carry):
            at = pl.ds(pl.multiple_of(j * wide, wide), wide)
            ga[:, at] = tn(tok[...], dx_o[:, at]).astype(BF16)
            return carry

        lax.fori_loop(0, cols // wide, grad_tile, 0)
        for h in range(2):
            scat_a.start(h)

    @pl.when(n == 2 * chunks - 1)
    def _():
        for s, to in mates():
            branch_copy(s, to).wait_recv()
        branch_own().wait()
        inputs_load().wait()
        total = inputs[...].astype(F32) + branch[...].astype(F32)
        for s in range(1, hp):
            total = total + arrived[s - 1].astype(F32)
        out_o[...] = total.astype(BF16)
        home_o.wait()
        go_o[...] = oz[0].astype(F32) + oz[1].astype(F32)
        home_z.wait()
        gz_o[...] = zz[0].astype(F32) + zz[1].astype(F32)

        for h in range(2):
            scat_a.fold(h, stages - 1)
        ga_o[...] = sharded_rows(ga, me, 0, wrows, (0, cols))[...]
        for s, to in mates():
            for i in range(count // SPAN):
                maps_copy(s, to, i).wait_recv()
        summed = dlow[...].astype(F32)
        for s in range(1, hp):
            summed = summed + dother[s - 1].astype(F32)
        dbc_o[...] = summed
        for item in (scat_a, home_o, home_z):
            item.finish()
        scat_o.finish_links()
        scat_z.finish_links()
        for s, to in mates():
            branch_copy(s, to).wait_send()
            for i in range(count // SPAN):
                maps_copy(s, to, i).wait_send()


def run_pull(
    sc, xs, dy, bc, dtin, dt, lc, lr, em, et, kd, st, sin, ds, dsin, pre, par,
    inputs, branch, gz, go, tok, ha, ig, size, parts,
):
    count, inner = xs.shape
    local_rows, width = inputs.shape
    total = count + HALO
    chunks = count // SPAN
    wrows = width // size
    hp = parts // 2

    def rev(step):
        return chunks - 1 - step

    tile = pl.BlockSpec((SPAN, ig), lambda b, i: (rev(i), b))
    per_token = pl.BlockSpec((SPAN, LANES), lambda b, i: (rev(i), 0))
    states = pl.BlockSpec((1, LANES, ig), lambda b, i: (rev(i), 0, b))
    edge = pl.BlockSpec((LANES, ig), lambda b, i: (0, b))
    full = pl.BlockSpec((total, ig), lambda b, i: (0, b))
    anywhere = pl.BlockSpec(memory_space=pl.ANY)
    shape = jax.ShapeDtypeStruct
    vm = pltpu.VMEM
    dma = pltpu.SemaphoreType.DMA
    blocks, links = size // 2, max(size // 2 - 1, 1)
    splits = [split_of(ig), ig - split_of(ig)]
    scratch = dict(
        cbt=vm((SPAN, SPAN), F32),
        off=vm((SPAN, SPAN), F32),
        dcb=vm((SPAN, SPAN), F32),
        ahead=vm((24, ig), F32),
        lags=vm((3, SPAN, LANES), F32),
        products=vm((3, SPAN, ig), BF16),
        tails=vm((SPAN, ig), BF16),
        leads=vm((SPAN, ig), BF16),
        rsum=vm((LANES, SPAN), F32),
        maps_in=vm((LANES, ig), BF16),
        maps_out=vm((LANES, ig), BF16),
        skips=vm((8, ig), F32),
        inputs=vm((local_rows, width), BF16),
        branch=vm((local_rows, width), BF16),
        arrived=vm((hp - 1, local_rows, width), BF16),
        tok=vm((total, width), BF16),
        ga=vm((width, ig), BF16),
        dlow=vm((count, 2 * LANES), BF16),
        dother=vm((hp - 1, count, 2 * LANES), BF16),
        zacc=vm((blocks, wrows, inner), BF16),
        oacc=vm((blocks, wrows, inner), BF16),
        acore=[vm((blocks, wrows, w), BF16) for w in splits],
        zlink=[vm((links, wrows, ig), BF16)] * 2,
        olink=[vm((links, wrows, ig), BF16)] * 2,
        alink=[vm((links, wrows, w), BF16) for w in splits],
        zz=vm((2, wrows, ig), BF16),
        oz=vm((2, wrows, ig), BF16),
        loads=dma((5,)),
        ccs=dma((3, 2, blocks)),
        ccr=dma((3, 2, blocks)),
        cls=dma((3, 2, links)),
        clr=dma((3, 2, links)),
        hs=dma((4,)),
        hr=dma((4,)),
        ho=dma((2,)),
        ms=dma((hp - 1, chunks)),
        mr=dma((hp - 1, chunks)),
        bs=dma((hp - 1,)),
        br=dma((hp - 1,)),
    )
    return pl.pallas_call(
        partial(pull_body, size, parts, ha, wrows),
        grid=(2, chunks),
        out_shape=(
            shape((total, inner), BF16),
            shape((count, 2 * LANES), F32),
            shape((2, count, LANES), F32),
            shape((8, inner), F32),
            shape((2, 8, LANES), F32),
            shape((local_rows, width), BF16),
            shape((wrows, ig), F32),
            shape((wrows, ig), F32),
            shape((wrows, ig), BF16),
        ),
        in_specs=[
            scalars(),
            tile,
            tile,
            pl.BlockSpec((SPAN, 2 * LANES), lambda b, i: (rev(i), 0)),
            per_token,
            per_token,
            per_token,
            pl.BlockSpec((16, SPAN), lambda b, i: (b, rev(i))),
            per_token,
            per_token,
            whole(),
            states,
            edge,
            states,
            edge,
            full,
            pl.BlockSpec((8, ig), lambda b, i: (0, b)),
        ]
        + [anywhere] * 5,
        out_specs=(
            full,
            whole(),
            pl.BlockSpec((1, SPAN, LANES), lambda b, i: (b, rev(i), 0)),
            pl.BlockSpec((8, ig), lambda b, i: (0, b)),
            pl.BlockSpec((1, 8, LANES), lambda b, i: (b, 0, 0)),
            whole(),
            whole(),
            whole(),
            whole(),
        ),
        scratch_shapes=list(scratch.values()),
        compiler_params=pltpu.CompilerParams(vmem_limit_bytes=VMEM_BYTES, collective_id=3, has_side_effects=True),
        cost_estimate=cost(20e9, 30e6),
        name="pull",
    )(
        sc, xs, dy, bc, dtin, dt, lc, lr, em, et, kd, st, sin, ds, dsin, pre, par,
        inputs, branch, gz, go, tok,
    )


def last_body(
    size, parts, rows, ha, ig,
    ends, inputs_h, cot_h, ngain, tok_h, dz_h, dx_h, wz_h, wx_h, ws_h, dbc_h, ddt, pre_h, taps, bias, csum, gsum, hsum, ga,
    gin_o, gx_o, gdt_o, gbc_o, chan_o, rep_o,
    inputs, cot, dbc, pre, tok, dz, dx, wz, wx, ws, gx, gsm, dsm, conv, dn_out, dn_in, dn_own, edge_out, edge_in,
    xcore, xlink, score, slink, xz, dtz, bcz, chan, chan_in, chan_z, rep, rep_in, rep_z,
    loads, ccs, ccr, cls, clr, zs, zr, zo, bs, br, ns, nr, es, er, ts, tr, rs, rr, ro,
):
    p = lax.axis_index("tensor")
    me = lax.axis_index("dp")
    hp = parts // 2
    place = lax.rem(p, hp)
    half = p // hp
    inner = 2 * ig
    local_rows, width = inputs.shape
    count = local_rows * hp
    total = count + HALO
    base = half * count
    own_at = pl.multiple_of(HALO + place * local_rows, 16)

    moving = [
        pltpu.make_async_copy(src, dst, loads.at[i])
        for i, (src, dst) in enumerate((
            (dx_h, dx), (tok_h, tok), (wx_h, wx), (dz_h, dz), (wz_h, wz), (ws_h, ws),
            (dbc_h, dbc), (pre_h, pre), (inputs_h, inputs), (cot_h, cot),
        ))
    ]
    for copy in moving:
        copy.start()
    greet([1] + link_bits(size), others(parts))

    def mates():
        return [(s, half * hp + lax.rem(place + s, hp)) for s in range(1, hp)]

    dp_steps = [("dp", 1)] + [("dp", bit) for bit in link_bits(size)]
    chan[0:5, :] = csum[0:5, :]
    chan[5:7, :] = gsum[0:2, :]
    chan[7:8, :] = jnp.zeros((1, inner), F32)
    for b in range(2):
        for i in range(2):
            at = b * ig + i * LANES
            chan[7:8, at : at + LANES] = hsum[b, i : i + 1, :]
    sum_chan = Butterfly(0, chan, chan_in, dp_steps, bs, br)
    sum_rep = Butterfly(1, rep, rep_in, dp_steps, bs, br)
    all_rep = AllZ(rep, rep_z, parts, rs, rr, ro)
    sum_chan.push(0)

    def x_block(h, v):
        return sharded_rows(gx, me, v, rows, halves(split_of(ig), ig)[h])

    def s_block(h, v):
        return sharded_rows(gsm, me, v, rows, halves(2 * LANES, 4 * LANES)[h])

    scat_x = Scatter(0, x_block, lambda h, u: x_block(h, 2 * u), None, size, xcore, xlink, ccs, ccr, cls, clr)
    scat_s = Scatter(1, s_block, lambda h, u: s_block(h, 2 * u), None, size, score, slink, ccs, ccr, cls, clr)
    stages = scat_x.stages()
    home_x = FromHeads(0, lambda side: sharded_rows(gx, me, 0, rows, (0, ig)) if side else ga, xz, parts, zs, zr, zo)
    home_dt = FromHeads(
        1,
        lambda side: sharded_rows(gsm, me, 0, rows, (side * LANES, (side + 1) * LANES)),
        dtz, parts, zs, zr, zo,
    )
    home_x.start(0)
    home_chan = FromHeads(2, lambda side: chan.at[:, pl.ds(side * ig, ig)], chan_z, parts, zs, zr, zo)

    cols = col_tile(ig)
    rep[...] = jnp.zeros_like(rep)
    dsm[:HALO, : 2 * LANES] = jnp.zeros((HALO, 2 * LANES), BF16)
    for b in range(2):
        dsm[HALO:, b * LANES : (b + 1) * LANES] = ddt[b].astype(BF16)
    for copy in moving[:2]:
        copy.wait()

    def grad_x(j, carry):
        at = pl.multiple_of(j * cols, cols)
        gx[:, pl.ds(at, cols)] = tn(tok[...], dx[:, pl.ds(ig + at, cols)]).astype(BF16)
        return carry

    def fold_cores(*scats):
        for scat in scats:
            for h in range(2):
                scat.fold_core(h)
                scat.send(h, 0)

    def relay(scat, s):
        for h in range(2):
            scat.fold(h, s)
            if s + 1 < stages:
                scat.send(h, s + 1)

    lax.fori_loop(0, ig // cols, grad_x, 0)
    for h in range(2):
        scat_x.start(h)
    for copy in moving[2:6]:
        copy.wait()

    tile = 256

    def dn_tile(j, start, n, at, with_z, share):
        span = pl.ds(start, n)
        value = nt(dx[span, :], wx[at, :]) + nt(dsm[span, : 2 * LANES], ws[at, : 2 * LANES])
        if share:
            value = value + nt(dsm[span, 2 * LANES :], ws[at, 2 * LANES :]) * share
        if with_z:
            value = value + nt(dz[pl.ds(start - HALO, n), :], wz[at, :])
        rep[pl.ds(j, 1), :] += jnp.sum(value * tok[span, at].astype(F32), axis=0, keepdims=True)
        return value

    def dn_copy(s, to, j):
        at = pl.ds(pl.multiple_of(j * tile, tile), tile)
        return remote(dn_out.at[s - 1, :, at], dn_in.at[s - 1, :, at], ns.at[s - 1, j], nr.at[s - 1, j], tensor=to)

    def edge_copy(k):
        return remote(edge_out, edge_in.at[k], es.at[0], er.at[k], tensor=hp - 1)

    def other_rows(s, to):
        there = pl.multiple_of(HALO + lax.rem(place + s, hp) * local_rows, 16)

        def step(j, carry):
            at = pl.ds(pl.multiple_of(j * tile, tile), tile)
            dn_out[s - 1, :, at] = dn_tile(j, there, local_rows, at, True, 0.0).astype(BF16)
            dn_copy(s, to, j).start()
            return carry

        return step

    dn_tiles = width // tile
    middle = dn_tiles // 2
    for s, to in mates():
        lax.fori_loop(0, middle, other_rows(s, to), 0)
    fold_cores(scat_x)
    sum_chan.fold(0)
    if len(dp_steps) > 1:
        sum_chan.push(1)
    for s, to in mates():
        lax.fori_loop(middle, dn_tiles, other_rows(s, to), 0)

    for copy in moving[6:]:
        copy.wait()
    upstream = dbc[...]
    pos = base + iota((count, 1), 0)
    masks = [same_as_behind(ends, pos, j) for j in range(4)]
    lagged = [pre[HALO - j : HALO - j + count, :] * masks[j] for j in range(1, 4)]
    lagged = [pre[HALO:, :]] + lagged
    through = bias[...].reshape(1, 2 * LANES)
    for j in range(4):
        through = through + taps[j : j + 1, :] * lagged[j]
    sig = sigmoid(through)
    dconv = upstream * (sig * (1.0 + through * (1.0 - sig)))
    for j in range(5):
        value = dconv * lagged[j] if j < 4 else dconv
        rep[8 + j : 9 + j, :] = jnp.sum(value, axis=0, keepdims=True) / hp
    conv[...] = jnp.zeros_like(conv)
    dpre = jnp.zeros((total, 2 * LANES), F32)
    for j in range(4):
        conv[HALO : HALO + count, :] = dconv * masks[j] if j else dconv
        dpre = dpre + taps[j : j + 1, :] * conv[j : j + total, :]
    dsm[:, 2 * LANES :] = dpre.astype(BF16)
    for s in range(stages - 1):
        relay(scat_x, s)
    gsm[...] = tn(tok[...], dsm[...]).astype(BF16)
    scat_s.start(0)
    scat_s.start(1)
    for i in range(1, len(dp_steps)):
        sum_chan.fold(i)
        if i + 1 < len(dp_steps):
            sum_chan.push(i + 1)
    home_chan.start(0)
    home_chan.start(1)

    def edge_rows(j, carry):
        at = pl.ds(pl.multiple_of(j * tile, tile), tile)
        edge_out[:, at] = dn_tile(j, 0, HALO, at, False, 1.0 / hp).astype(BF16)
        return carry

    lax.fori_loop(0, dn_tiles, edge_rows, 0)
    for k in range(hp):

        @pl.when(p == hp + k)
        def _(k=k):
            edge_copy(k).start()

    def own_rows(j, carry):
        at = pl.ds(pl.multiple_of(j * tile, tile), tile)
        dn_own[:, at] = dn_tile(j, own_at, local_rows, at, True, 1.0)
        return carry

    third = (dn_tiles + 2) // 3
    lax.fori_loop(0, third, own_rows, 0)
    relay(scat_x, stages - 1)
    home_x.start(1)
    fold_cores(scat_s)
    lax.fori_loop(third, 2 * third, own_rows, 0)
    for s in range(stages - 1):
        relay(scat_s, s)
    lax.fori_loop(2 * third, dn_tiles, own_rows, 0)
    sum_rep.push(0)
    relay(scat_s, stages - 1)
    home_dt.start(0)
    home_dt.start(1)
    bc_mine = sharded_rows(gsm, me, 0, rows, (2 * LANES, 4 * LANES))
    bc_copy = remote(bc_mine, bcz, ts.at[0], tr.at[0], tensor=lax.rem(p + hp, parts))
    bc_copy.start()
    for i in range(len(dp_steps)):
        sum_rep.fold(i)
        if i + 1 < len(dp_steps):
            sum_rep.push(i + 1)
    all_rep.start()
    home_chan.wait()
    chan_o[...] = chan_z[0] + chan_z[1]

    for s, to in mates():
        for j in range(dn_tiles):
            dn_copy(s, to, j).wait_recv()

    @pl.when(p == hp - 1)
    def _():
        for k in range(hp):
            edge_copy(k).wait_recv()
        last = local_rows - HALO
        for k in range(hp):
            dn_own[last:, :] += edge_in[k].astype(F32)

    dnormed = dn_own[...]
    for s in range(1, hp):
        dnormed = dnormed + dn_in[s - 1].astype(F32)
    values = inputs[...].astype(F32)
    scale = lax.rsqrt(jnp.mean(values * values, axis=1, keepdims=True) + EPS)
    side = dnormed * row(ngain)
    pull = scale * scale * scale * (jnp.sum(side * values, axis=1, keepdims=True) / width)
    gin_o[...] = (scale * side - values * pull + cot[...].astype(F32)).astype(BF16)

    rep_o[...] = all_rep.total()
    home_dt.wait()
    gdt_o[...] = dtz[0].astype(F32) + dtz[1].astype(F32)
    bc_copy.wait_recv()
    gbc_o[...] = bc_mine[...].astype(F32) + bcz[...].astype(F32)
    home_x.wait()
    gx_o[...] = xz[0].astype(F32) + xz[1].astype(F32)
    for item in (scat_x, scat_s, home_x, home_dt, home_chan, all_rep):
        item.finish()
    for s, to in mates():
        for j in range(dn_tiles):
            dn_copy(s, to, j).wait_send()
    bc_copy.wait_send()

    @pl.when(half == 1)
    def _():
        edge_copy(0).wait_send()


def run_last(
    ends, inputs, cot, ngain, tok, dz, dx, wz, wx, ws, dbc, ddt, pre, taps, bias, csum, gsum, hsum, ga,
    size, parts, ha, ig,
):
    local_rows, width = inputs.shape
    total = tok.shape[0]
    count = total - HALO
    inner = 2 * ig
    hp = parts // 2
    rows = width // size
    shape = jax.ShapeDtypeStruct
    anywhere = pl.BlockSpec(memory_space=pl.ANY)
    dma = pltpu.SemaphoreType.DMA
    blocks, links = size // 2, max(size // 2 - 1, 1)
    steps = size.bit_length() - 1
    vm = pltpu.VMEM

    splits = [split_of(ig), ig - split_of(ig)]

    def pair(n, cols):
        return [vm((n, rows, cols), BF16), vm((n, rows, cols), BF16)]

    scratch = dict(
        inputs=vm(inputs.shape, BF16),
        cot=vm(cot.shape, BF16),
        dbc=vm(dbc.shape, F32),
        pre=vm(pre.shape, F32),
        tok=vm(tok.shape, BF16),
        dz=vm(dz.shape, BF16),
        dx=vm(dx.shape, BF16),
        wz=vm(wz.shape, BF16),
        wx=vm(wx.shape, BF16),
        ws=vm(ws.shape, BF16),
        gx=vm((width, ig), BF16),
        gsm=vm((width, 4 * LANES), BF16),
        dsm=vm((total, 4 * LANES), BF16),
        conv=vm((total + 8, 2 * LANES), F32),
        dn_out=vm((hp - 1, local_rows, width), BF16),
        dn_in=vm((hp - 1, local_rows, width), BF16),
        dn_own=vm((local_rows, width), F32),
        edge_out=vm((HALO, width), BF16),
        edge_in=vm((hp, HALO, width), BF16),
        xcore=[vm((blocks, rows, w), BF16) for w in splits],
        xlink=[vm((links, rows, w), BF16) for w in splits],
        score=pair(blocks, 2 * LANES),
        slink=pair(links, 2 * LANES),
        xz=vm((2, rows, ig), BF16),
        dtz=vm((2, rows, LANES), BF16),
        bcz=vm((rows, 2 * LANES), BF16),
        chan=vm((8, inner), F32),
        chan_in=vm((steps, 8, inner), F32),
        chan_z=vm((2, 8, ig), F32),
        rep=vm((16, 2 * LANES), F32),
        rep_in=vm((steps, 16, 2 * LANES), F32),
        rep_z=vm((parts, 16, 2 * LANES), F32),
        loads=dma((10,)),
        ccs=dma((2, 2, blocks)),
        ccr=dma((2, 2, blocks)),
        cls=dma((2, 2, links)),
        clr=dma((2, 2, links)),
        zs=dma((6,)),
        zr=dma((6,)),
        zo=dma((3,)),
        bs=dma((2, steps)),
        br=dma((2, steps)),
        ns=dma((hp - 1, width // 256)),
        nr=dma((hp - 1, width // 256)),
        es=dma((1,)),
        er=dma((hp,)),
        ts=dma((1,)),
        tr=dma((1,)),
        rs=dma((parts,)),
        rr=dma((parts,)),
        ro=dma((1,)),
    )
    return pl.pallas_call(
        partial(last_body, size, parts, rows, ha, ig),
        out_shape=(
            shape((local_rows, width), BF16),
            shape((rows, ig), F32),
            shape((rows, LANES), F32),
            shape((rows, 2 * LANES), F32),
            shape((8, ig), F32),
            shape((16, 2 * LANES), F32),
        ),
        in_specs=[scalars(), anywhere, anywhere, whole()] + [anywhere] * 7 + [whole(), anywhere] + [whole()] * 6,
        out_specs=[whole()] * 6,
        scratch_shapes=list(scratch.values()),
        compiler_params=pltpu.CompilerParams(vmem_limit_bytes=VMEM_BYTES, collective_id=1, has_side_effects=True),
        cost_estimate=cost(2 * total * width * (3 * inner + 1024), 40e6),
        name="last",
    )(ends, inputs, cot, ngain, tok, dz, dx, wz, wx, ws, dbc, ddt, pre, taps, bias, csum, gsum, hsum, ga)


def finish_body(
    ha, out, gin, rep, ngain, gz, gx, gbc, gdt, chan, go,
    out_o, gin_o, gnorm_o, gz_o, gx_o, gbc_o, gdt_o, gcx_o, gcxb_o, gcb_o, gcbb_o, gdtb_o, galog_o, gskip_o, ggain_o, go_o,
):
    width = ngain.shape[0]
    ig = chan.shape[1]
    out_o[...] = out[...]
    gin_o[...] = gin[...]
    gains = jnp.concatenate([rep[j : j + 1, :] for j in range(width // (2 * LANES))], axis=1)
    gnorm_o[...] = gains.reshape(width) / ngain[...]
    gz_o[...] = gz[...]
    gx_o[...] = gx[...]
    gbc_o[...] = gbc[...]
    gdt_o[...] = gdt[...].T[:ha, :]
    gcx_o[...] = chan[0:4, :]
    gcxb_o[...] = chan[4:5, :].reshape(ig)
    ggain_o[...] = chan[5:6, :].reshape(ig)
    heads = lax.dot_general(
        chan[...],
        head_map(ig, 0, 0, both=False).astype(F32),
        (((1,), (1,)), ((), ())),
        precision=HIGH,
        preferred_element_type=F32,
    )
    gskip_o[...] = heads[6:7, :ha].reshape(ha)
    gdtb_o[...] = chan[7:8, :ha].reshape(ha)
    galog_o[...] = chan[7:8, LANES : LANES + ha].reshape(ha)
    for j in range(4):
        gcb_o[j : j + 1, :] = rep[8 + j : 9 + j, :]
    gcbb_o[...] = rep[12:13, :].reshape(2 * LANES)
    go_o[...] = go[...]


def run_finish(out, gin, rep, ngain, gz, gx, gbc, gdt, chan, go, ha):
    shape = jax.ShapeDtypeStruct
    rows, ig = gz.shape
    return pl.pallas_call(
        partial(finish_body, ha),
        out_shape=(
            shape(out.shape, BF16),
            shape(gin.shape, BF16),
            shape(ngain.shape, F32),
            shape((rows, ig), F32),
            shape((rows, ig), F32),
            shape(gbc.shape, F32),
            shape((ha, rows), F32),
            shape((4, ig), F32),
            shape((ig,), F32),
            shape((4, 2 * LANES), F32),
            shape((2 * LANES,), F32),
            shape((ha,), F32),
            shape((ha,), F32),
            shape((ha,), F32),
            shape((ig,), F32),
            shape((rows, ig), F32),
        ),
        in_specs=[whole()] * 10,
        out_specs=[whole()] * 16,
        compiler_params=params(),
        cost_estimate=cost(1e7, 8e6),
        name="finish",
    )(out, gin, rep, ngain, gz, gx, gbc, gdt, chan, go)


def local(
    inputs,
    cotangent,
    seq_lengths,
    norm_gain,
    w_z,
    w_x,
    w_bc,
    w_dt,
    conv_x,
    conv_x_bias,
    conv_bc,
    conv_bc_bias,
    dt_bias,
    a_log,
    d_skip,
    gate_gain,
    w_out,
):
    parts = lax.axis_size("tensor")
    size = lax.axis_size("dp")
    ha = dt_bias.shape[0]
    ig = w_z.shape[1]
    (
        tok, pulled, wx, wz, wo, ws, par, pre_bc, bc, dtin, dt, lc, lr, em, et, kd, pre_x, xs, st, sin, z, dm, y, stat,
    ) = run_first(
        seq_lengths, inputs, cotangent, norm_gain, w_x, w_z, w_out.T, w_bc, w_dt.T, conv_x, conv_x_bias, dt_bias, a_log,
        d_skip, gate_gain, conv_bc, conv_bc_bias, size, parts,
    )
    dz, dy, gate_sums, ds, gw_z, gw_o, dsin, branch = run_gate(
        y, z, dm, stat, xs, par, bc, em, kd, tok, pulled, wo, ig, ig * parts, size, parts
    )
    dx, dbc, ddt, conv_sums, head_sums, outputs, grad_w_z, grad_w_o, grad_w_a = run_pull(
        seq_lengths, xs, dy, bc, dtin, dt, lc, lr, em, et, kd, st, sin, ds, dsin, pre_x, par,
        inputs, branch, gw_z, gw_o, tok, ha, ig, size, parts,
    )
    grad_inputs, grad_w_x, grad_w_dt, grad_w_bc, chan, rep = run_last(
        seq_lengths, inputs, cotangent, norm_gain, tok, dz, dx, wz, wx, ws, dbc, ddt, pre_bc, conv_bc,
        conv_bc_bias, conv_sums, gate_sums, head_sums, grad_w_a, size, parts, ha, ig,
    )
    done = run_finish(
        outputs, grad_inputs, rep, norm_gain, grad_w_z, grad_w_x, grad_w_bc, grad_w_dt, chan, grad_w_o, ha
    )
    return (*done[:6], done[6].T, *done[7:15], done[15].T)


def solution(mesh):
    tokens = P(("dp", "tensor"), None)
    matrix = P("dp", "tensor")
    heads = P("tensor")
    return jax.shard_map(
        local,
        mesh=mesh,
        in_specs=(
            tokens,
            tokens,
            P("dp", None),
            P(),
            matrix,
            matrix,
            P("dp", None),
            matrix,
            P(None, "tensor"),
            heads,
            P(),
            P(),
            heads,
            heads,
            heads,
            heads,
            P("tensor", "dp"),
        ),
        out_specs=(
            tokens,
            tokens,
            P(),
            matrix,
            matrix,
            P("dp", None),
            matrix,
            P(None, "tensor"),
            heads,
            P(),
            P(),
            heads,
            heads,
            heads,
            heads,
            P("tensor", "dp"),
        ),
        check_vma=False,
    )
```

```python
from functools import partial

import jax
import jax.numpy as jnp
from jax import lax
from jax.experimental import pallas as pl
from jax.experimental.pallas import tpu as pltpu
from jax.sharding import PartitionSpec as P

SPAN = 256
HALO = 16
LANES = 128
LOG2E = 1.4426950408889634
EPS = 1e-05
FAR = -1e30
HIGH = lax.Precision.HIGHEST
F32 = jnp.float32
BF16 = jnp.bfloat16
VMEM_BYTES = 60 * 1024 * 1024


def nn(a, b):
    return jnp.dot(a, b, preferred_element_type=F32)


def nt(a, b):
    return lax.dot_general(a, b, (((1,), (1,)), ((), ())), preferred_element_type=F32)


def tn(a, b):
    return lax.dot_general(a, b, (((0,), (0,)), ((), ())), preferred_element_type=F32)


def sigmoid(v):
    return 1.0 / (1.0 + jnp.exp(-v))


def iota(shape, axis):
    return lax.broadcasted_iota(jnp.int32, shape, axis)


def seg_at(lengths, pos):
    end = lengths[0, 0]
    found = (pos >= end).astype(jnp.int32)
    for i in range(1, 3):
        end = end + lengths[0, i]
        found = found + (pos >= end).astype(jnp.int32)
    return jnp.where(pos < 0, -1, found)


def same_as_behind(sc, pos, offset):
    return (seg_at(sc, pos - offset) == seg_at(sc, pos)).astype(F32)


def head_map(cols, start, first, both=True):
    k = iota((LANES, cols), 0)
    if both:
        k = k & 63
    head = ((iota((LANES, cols), 1) + start) >> 6) + first
    return (k == head).astype(BF16)


def expand(values, mapping):
    high = values.astype(BF16).astype(F32)
    low = values - high
    return nn((high + pltpu.roll(low, 64, axis=1)).astype(BF16), mapping)


def thirds(values):
    high = values.astype(BF16).astype(F32)
    left = values - high
    middle = left.astype(BF16).astype(F32)
    return (high + pltpu.roll(middle, 16, axis=1) + pltpu.roll(left - middle, 32, axis=1)).astype(BF16)


def joined(values):
    return values + pltpu.roll(values, LANES - 16, axis=1) + pltpu.roll(values, LANES - 32, axis=1)


def whole():
    return pl.BlockSpec(memory_space=pltpu.VMEM)


def scalars():
    return pl.BlockSpec(memory_space=pltpu.SMEM)


def params():
    return pltpu.CompilerParams(vmem_limit_bytes=VMEM_BYTES)


def cost(flops, nbytes):
    return pl.CostEstimate(flops=int(flops), bytes_accessed=int(nbytes), transcendentals=0)


def col_tile(ig):
    return 256 if ig % 256 == 0 else 128


def flip(me, v):
    out = me
    bit = 1
    while bit <= v:
        if v & bit:
            out = out + bit - 2 * bit * lax.rem(me // bit, 2)
        bit *= 2
    return out


def link_bits(size):
    bits = []
    bit = 2
    while bit < size:
        bits.append(bit)
        bit *= 2
    return bits


def remote(src, dst, send, recv, **where):
    return pltpu.make_async_remote_copy(
        src_ref=src, dst_ref=dst, send_sem=send, recv_sem=recv, device_id=where, device_id_type=pl.DeviceIdType.MESH
    )


def greet(bits, partners):
    me = lax.axis_index("dp")
    barrier = pltpu.get_barrier_semaphore()
    for bit in bits:
        pl.semaphore_signal(barrier, inc=1, device_id={"dp": flip(me, bit)}, device_id_type=pl.DeviceIdType.MESH)
    for to in partners:
        pl.semaphore_signal(barrier, inc=1, device_id={"tensor": to}, device_id_type=pl.DeviceIdType.MESH)
    pl.semaphore_wait(barrier, len(bits) + len(partners))


def others(parts):
    p = lax.axis_index("tensor")
    return [lax.rem(p + shift, parts) for shift in range(1, parts)]


def row(ref):
    return jnp.reshape(ref[...], (1, ref.shape[0]))


class ToHeads:
    def __init__(self, k, src, place_of, parts, send, recv, own):
        self.p = lax.axis_index("tensor")
        self.hp = parts // 2
        self.k, self.src, self.place_of = k, src, place_of
        self.send, self.recv, self.own = send, recv, own

    def copy(self, i, side, to):
        return remote(
            self.src, self.place_of(side), self.send.at[2 * self.k + i], self.recv.at[2 * self.k + side], tensor=to
        )

    def local(self, side):
        return pltpu.make_async_copy(self.src, self.place_of(side), self.own.at[self.k])

    def targets(self):
        return [self.p // 2, self.p // 2 + self.hp]

    def start(self):
        side = lax.rem(self.p, 2)
        for i, to in enumerate(self.targets()):

            @pl.when(to != self.p)
            def _(i=i, to=to):
                self.copy(i, side, to).start()

            @pl.when(to == self.p)
            def _():
                self.local(side).start()

    def wait(self):
        q = lax.rem(self.p, self.hp)
        for side in range(2):
            source = 2 * q + side

            @pl.when(source != self.p)
            def _(side=side):
                self.copy(0, side, self.p // 2).wait_recv()

            @pl.when(source == self.p)
            def _(side=side):
                self.local(side).wait()

    def finish(self):
        side = lax.rem(self.p, 2)
        for i, to in enumerate(self.targets()):

            @pl.when(to != self.p)
            def _(i=i, to=to):
                self.copy(i, side, to).wait_send()


class Gather:
    def __init__(self, k, ref, split, rows, size, send, recv):
        self.me = lax.axis_index("dp")
        self.k, self.ref, self.rows, self.size = k, ref, rows, size
        bits = link_bits(size)
        self.orders = [bits, bits[::-1]]
        self.cols = [slice(0, split), slice(split, ref.shape[1])]
        self.send, self.recv = send, recv
        self.sent = []

    def block(self, half, v):
        start = pl.multiple_of(flip(self.me, v) * self.rows, 16)
        cols = self.cols[half]
        return self.ref.at[pl.ds(start, self.rows), pl.ds(cols.start, cols.stop - cols.start)]

    def copy(self, half, v, bit):
        n = bit.bit_length() - 1
        here = self.block(half, v)
        return remote(
            here,
            here,
            self.send.at[self.k, half, v * self.size.bit_length() + n],
            self.recv.at[self.k, half, v ^ bit],
            dp=flip(self.me, bit),
        )

    def push(self, half, v, bits):
        for bit in bits:
            self.copy(half, v, bit).start()
            self.sent.append((half, v, bit))

    def arrive(self, half, v):
        here = self.block(half, v)
        remote(
            here,
            here,
            self.send.at[self.k, half, 0],
            self.recv.at[self.k, half, v],
            dp=flip(self.me, 1),
        ).wait_recv()

    def start(self):
        for half in range(2):
            self.push(half, 0, self.orders[half])
        for half in range(2):
            self.push(half, 0, [1])

    def stage(self, s):
        for half in range(2):
            order = self.orders[half]
            names = [0]
            for bit in order[:s]:
                names = names + [v ^ bit for v in names]
            for v in sorted(n ^ order[s] for n in names):
                self.arrive(half, v)
                self.push(half, v, order[s + 1 :])
                self.push(half, v, [1])

    def stages(self):
        return len(self.orders[0])

    def cores(self):
        for half in range(2):
            for v in range(1, self.size, 2):
                self.arrive(half, v)

    def finish(self):
        for half, v, bit in self.sent:
            self.copy(half, v, bit).wait_send()


class Scatter:
    def __init__(self, k, source, acc, own, size, core_buf, link_buf, cs, cr, ls, lr):
        self.me = lax.axis_index("dp")
        self.k, self.source, self.acc, self.own, self.size = k, source, acc, own, size
        self.core_buf, self.link_buf = core_buf, link_buf
        self.cs, self.cr, self.ls, self.lr = cs, cr, ls, lr
        bits = link_bits(size)
        self.orders = [bits, bits[::-1]]
        self.sent = []

    def core(self, half, u):
        return remote(
            self.source(half, 2 * u + 1),
            self.core_buf[half].at[u],
            self.cs.at[self.k, half, u],
            self.cr.at[self.k, half, u],
            dp=flip(self.me, 1),
        )

    def start(self, half):
        for u in range(self.size // 2):
            self.core(half, u).start()
            if self.own is not None:
                self.own(half, u).start()

    def add(self, half, u, other):
        ref = self.acc(half, u)
        ref[...] = ref[...] + other[...]

    def fold_core(self, half):
        for u in range(self.size // 2):
            self.core(half, u).wait_recv()
            if self.own is not None:
                self.own(half, u).wait()
            self.add(half, u, self.core_buf[half].at[u])

    def plan(self, half, s):
        order = self.orders[half]
        held, slot = list(range(0, self.size, 2)), 0
        for i, bit in enumerate(order):
            away = [v for v in held if v & bit]
            stay = [v for v in held if not v & bit]
            if i == s:
                return bit, away, stay, slot
            held, slot = stay, slot + len(stay)

    def link(self, half, s, i):
        bit, away, stay, slot = self.plan(half, s)
        n = slot + stay.index(away[i] ^ bit)
        return remote(
            self.acc(half, away[i] >> 1),
            self.link_buf[half].at[n],
            self.ls.at[self.k, half, n],
            self.lr.at[self.k, half, n],
            dp=flip(self.me, bit),
        )

    def send(self, half, s):
        for i in range(len(self.plan(half, s)[1])):
            self.link(half, s, i).start()

    def fold(self, half, s):
        bit, away, stay, slot = self.plan(half, s)
        for i in range(len(away)):
            self.link(half, s, i).wait_recv()
        for i, v in enumerate(stay):
            self.add(half, v >> 1, self.link_buf[half].at[slot + i])

    def stages(self):
        return len(self.orders[0])

    def finish_core(self):
        for half in range(2):
            for u in range(self.size // 2):
                self.core(half, u).wait_send()

    def finish_links(self):
        for half in range(2):
            for s in range(self.stages()):
                for i in range(len(self.plan(half, s)[1])):
                    self.link(half, s, i).wait_send()

    def finish(self):
        self.finish_core()
        self.finish_links()


class FromHeads:
    def __init__(self, k, block, slots, parts, send, recv, own):
        self.p = lax.axis_index("tensor")
        self.hp = parts // 2
        self.k, self.block, self.slots = k, block, slots
        self.send, self.recv, self.own = send, recv, own
        self.half = self.p // self.hp
        self.q = lax.rem(self.p, self.hp)

    def copy(self, side, slot):
        return remote(
            self.block(side),
            self.slots.at[slot],
            self.send.at[2 * self.k + side],
            self.recv.at[2 * self.k + slot],
            tensor=2 * self.q + side,
        )

    def local(self, side, slot):
        return pltpu.make_async_copy(self.block(side), self.slots.at[slot], self.own.at[self.k])

    def start(self, side):
        to = 2 * self.q + side

        @pl.when(to != self.p)
        def _():
            self.copy(side, self.half).start()

        @pl.when(to == self.p)
        def _():
            self.local(side, self.half).start()

    def wait(self):
        for slot in range(2):
            source = self.p // 2 + slot * self.hp

            @pl.when(source != self.p)
            def _(slot=slot):
                self.copy(0, slot).wait_recv()

            @pl.when(source == self.p)
            def _(slot=slot):
                self.local(0, slot).wait()

    def finish(self, sides=(0, 1)):
        for side in sides:

            @pl.when(2 * self.q + side != self.p)
            def _(side=side):
                self.copy(side, self.half).wait_send()


class Butterfly:
    def __init__(self, k, ref, slots, steps, send, recv):
        self.k, self.ref, self.slots, self.steps = k, ref, slots, steps
        self.send, self.recv = send, recv

    def copy(self, i):
        axis, bit = self.steps[i]
        return remote(
            self.ref,
            self.slots.at[i],
            self.send.at[self.k, i],
            self.recv.at[self.k, i],
            **{axis: flip(lax.axis_index(axis), bit)},
        )

    def push(self, i):
        self.copy(i).start()

    def fold(self, i):
        self.copy(i).wait()
        self.ref[...] += self.slots[i]


class AllZ:
    def __init__(self, ref, slots, parts, send, recv, own):
        self.p = lax.axis_index("tensor")
        self.ref, self.slots, self.parts = ref, slots, parts
        self.send, self.recv, self.own = send, recv, own

    def copy(self, shift):
        to = lax.rem(self.p + shift, self.parts)
        return remote(
            self.ref, self.slots.at[self.p], self.send.at[shift], self.recv.at[shift], tensor=to
        )

    def arrival(self, shift):
        there = self.slots.at[lax.rem(self.p + self.parts - shift, self.parts)]
        return remote(self.ref, there, self.send.at[shift], self.recv.at[shift], tensor=self.p)

    def mine(self):
        return pltpu.make_async_copy(self.ref, self.slots.at[self.p], self.own.at[0])

    def start(self):
        self.mine().start()
        for shift in range(1, self.parts):
            self.copy(shift).start()

    def total(self):
        self.mine().wait()
        for shift in range(1, self.parts):
            self.arrival(shift).wait_recv()
        value = self.slots[0]
        for i in range(1, self.parts):
            value = value + self.slots[i]
        return value

    def finish(self):
        for shift in range(1, self.parts):
            self.copy(shift).wait_send()


def sharded_rows(ref, me, v, rows, cols):
    start = pl.multiple_of(flip(me, v) * rows, 16)
    return ref.at[pl.ds(start, rows), pl.ds(cols[0], cols[1] - cols[0])]


def halves(split, total):
    return [(0, split), (split, total)]


def split_of(cols):
    return (cols // 2 + LANES - 1) // LANES * LANES


def first_body(
    size, parts, rows, ha, ig,
    ends, inputs, cot, ngain, w_x, w_z, w_out, w_bc, w_dt, conv_x, conv_x_bias, dt_bias, a_log, d_skip, gate_gain,
    taps_bc, bias_bc,
    tok_h, pulled_h, wx_h, wz_h, wo_h, ws_h, par_h, pre_h, bc_h, dtin_h, dt_h, lc_h, lr_h, em_h, et_h, kd_h,
    prex_h, xs_h, st_h, sin_h, z_h, dm_h, y_h, stat_o,
    tok, pulled, wx, wz, wo, ws, par, pre, bc, dtin, dt, lc, lr, em, et, kd, st, stage, xs, fin, sin, z, gated_s, y_stage, cb, off, stat, sums_out, sums_in,
    lags, w_dt_wide, table, maps_in,
    zs, zr, zo, gs, gr, ts, tr, cs, cr, hs, hr, ss, sr, ms, mr, local, outs, tiles,
):
    p = lax.axis_index("tensor")
    me = lax.axis_index("dp")
    hp = parts // 2
    place = lax.rem(p, hp)
    half = p // hp
    inner = 2 * ig
    local_rows, width = inputs.shape
    count = local_rows * hp
    total = count + HALO
    base = half * count
    own_rows = pl.multiple_of(place * local_rows, 16)

    def mates():
        return [(s, half * hp + lax.rem(place + s, hp)) for s in range(1, hp)]

    def my_rows():
        return pl.ds(pl.multiple_of(me * rows, 16), rows)

    def wide(ref, cols):
        return lambda side: ref.at[my_rows(), pl.ds(pl.multiple_of(side * cols, LANES), cols)]

    emitted = []

    def emit(src, dst):
        copy = pltpu.make_async_copy(src, dst, outs.at[len(emitted)])
        copy.start()
        emitted.append(copy)

    w_dt_wide[...] = jnp.zeros_like(w_dt_wide)
    w_dt_wide[:, :ha] = w_dt[...].T
    greet([1] + link_bits(size), others(parts))
    to_table = ToHeads(0, table, lambda side: par.at[:, pl.ds(pl.multiple_of(side * ig, LANES), ig)], parts, zs, zr, zo)
    to_dt = ToHeads(1, w_dt_wide, wide(ws, LANES), parts, zs, zr, zo)
    to_x = ToHeads(2, w_x, wide(wx, ig), parts, zs, zr, zo)
    to_z = ToHeads(3, w_z, wide(wz, ig), parts, zs, zr, zo)
    to_o = ToHeads(4, w_out, wide(wo, ig), parts, zs, zr, zo)
    to_dt.start()
    to_x.start()
    bc_copy = pltpu.make_async_copy(w_bc, ws.at[my_rows(), pl.ds(2 * LANES, 2 * LANES)], local.at[0])
    bc_copy.start()
    cot_copy = pltpu.make_async_copy(cot, pulled.at[pl.ds(own_rows, local_rows)], local.at[1])
    cot_copy.start()

    values = inputs[...].astype(F32)
    scale = lax.rsqrt(jnp.mean(values * values, axis=1, keepdims=True) + EPS)
    mine = pl.ds(pl.multiple_of(HALO + own_rows, 16), local_rows)
    tok[mine, :] = (values * scale * row(ngain)).astype(BF16)

    def tok_copy(s, to):
        return remote(tok.at[mine], tok.at[mine], ts.at[s], tr.at[s], tensor=to)

    def tok_arrive(s):
        there = pl.ds(pl.multiple_of(HALO + lax.rem(place + hp - s, hp) * local_rows, 16), local_rows)
        remote(tok.at[there], tok.at[there], ts.at[s], tr.at[s], tensor=p).wait_recv()

    piece = local_rows // 2

    def cot_copy_to(s, to, i):
        there = pl.ds(pl.multiple_of(own_rows + i * piece, 16), piece)
        return remote(cot.at[pl.ds(i * piece, piece)], pulled.at[there], cs.at[i, s], cr.at[i, s], tensor=to)

    def cot_arrive(s, i):
        start = lax.rem(place + hp - s, hp) * local_rows + i * piece
        there = pl.ds(pl.multiple_of(start, 16), piece)
        remote(pulled.at[there], pulled.at[there], cs.at[i, s], cr.at[i, s], tensor=p).wait_recv()

    def halo_copy(k):
        return remote(tok.at[pl.ds(total - HALO, HALO)], tok.at[pl.ds(0, HALO)], hs.at[k], hr.at[0], tensor=hp + k)

    for s, to in mates():
        tok_copy(s, to).start()

    @pl.when(p == hp - 1)
    def _():
        for k in range(hp):
            halo_copy(k).start()

    @pl.when(half == 0)
    def _():
        tok[:HALO, :] = jnp.zeros((HALO, width), BF16)

    for b in range(2):
        maps_in[b] = head_map(ig, 0, b * 16)
    table[...] = jnp.zeros_like(table)
    table[0:4, :] = conv_x[...]
    table[4:5, :] = row(conv_x_bias)
    table[5:6, :] = row(gate_gain)
    table[6:7, :ha] = row(d_skip)
    table[7:8, :ha] = row(dt_bias)
    table[7:8, LANES : LANES + ha] = row(a_log)
    to_table.start()

    g_s = Gather(0, ws, 2 * LANES, rows, size, gs, gr)
    g_x = Gather(1, wx, ig, rows, size, gs, gr)
    g_z = Gather(2, wz, ig, rows, size, gs, gr)
    g_o = Gather(3, wo, ig, rows, size, gs, gr)
    stages = g_x.stages()
    to_dt.wait()
    bc_copy.wait()
    g_s.start()
    to_x.wait()
    g_x.start()
    to_z.start()
    for s in range(stages):
        g_x.stage(s)
        g_s.stage(s)
        if s == 0:
            to_o.start()
    to_z.wait()
    g_z.start()
    g_s.cores()
    for s, _ in mates():
        tok_arrive(s)
    for s, to in mates():
        cot_copy_to(s, to, 0).start()

    @pl.when(half == 1)
    def _():
        halo_copy(0).wait_recv()

    emit(tok, tok_h)
    emit(ws, ws_h)

    both = nn(tok[...], ws[...])
    pre[...] = both[:, 2 * LANES :]
    emit(pre, pre_h)
    pos = base + iota((count, 1), 0)
    for j in range(1, 4):
        lags[j - 1] = jnp.broadcast_to(same_as_behind(ends, pos, j), (count, LANES))
    for side in range(2):
        at = slice(side * LANES, (side + 1) * LANES)
        acc = bias_bc[...].reshape(1, 2 * LANES)[:, at] + taps_bc[0:1, at] * pre[HALO : HALO + count, at]
        for j in range(1, 4):
            acc = acc + taps_bc[j : j + 1, at] * pre[HALO - j : HALO - j + count, at] * lags[j - 1]
        bc[:, at] = (acc * sigmoid(acc)).astype(BF16)
    emit(bc, bc_h)
    to_table.wait()
    emit(par, par_h)
    lane = iota((1, LANES), 1)
    keep = ((lane & 15) < ha).astype(F32) * (lane < 32).astype(F32)

    def merge(values):
        return values[0] + pltpu.roll(values[1], 16, axis=1)

    biases = merge([par[7:8, b * ig : b * ig + LANES] for b in range(2)])
    logs_a = merge([par[7:8, b * ig + LANES : b * ig + 2 * LANES] for b in range(2)])
    shifted = merge([both[HALO:, b * LANES : (b + 1) * LANES] for b in range(2)]) + biases
    steps = (jnp.maximum(shifted, 0.0) + jnp.log1p(jnp.exp(-jnp.abs(shifted)))) * keep
    dtin[...] = shifted
    dt[...] = steps
    scaled = steps * (-jnp.exp(logs_a) * LOG2E)
    tri = (iota((SPAN, SPAN), 0) >= iota((SPAN, SPAN), 1)).astype(F32)
    chunks = count // SPAN
    gone = []
    for c in range(chunks):
        span = slice(c * SPAN, (c + 1) * SPAN)
        logs = jnp.dot(tri, scaled[span, :], precision=HIGH, preferred_element_type=F32)
        first, last = base + c * SPAN - 1, base + (c + 1) * SPAN - 1
        here = base + c * SPAN + iota((SPAN, 1), 0)
        seg = seg_at(ends, here)
        seg_first, seg_last = seg_at(ends, first), seg_at(ends, last)
        final = logs[SPAN - 1 : SPAN, :]
        gone.append(jnp.where(seg_first == seg_last, 1.0, 0.0).astype(F32) * jnp.exp2(final) * keep)
        lc[span, :] = logs
        lr[:, span] = logs.T[:32, :]
        em[span, :] = (seg == seg_first).astype(F32) * jnp.exp2(logs) * keep
        et[span, :] = (seg == seg_last).astype(F32) * jnp.exp2(final - logs) * keep
    ahead_of, behind_of = [keep], [keep]
    for c in range(chunks - 1):
        ahead_of.append(ahead_of[-1] * gone[c])
        behind_of.append(behind_of[-1] * gone[chunks - 1 - c])
    behind_of = behind_of[::-1]
    fill = [jnp.zeros((1, LANES), F32)] * (8 - chunks)
    kd[...] = jnp.concatenate(gone + fill + ahead_of + fill + behind_of + fill, axis=0)
    for src, dst in ((dtin, dtin_h), (dt, dt_h), (lc, lc_h), (lr, lr_h), (em, em_h), (et, et_h), (kd, kd_h)):
        emit(src, dst)

    g_x.cores()
    emit(wx, wx_h)

    cols = col_tile(ig)

    def state_copy(j):
        at = pl.ds(pl.multiple_of(j * cols, cols), cols)
        return remote(fin.at[:, at], sin.at[:, at], ss.at[j], sr.at[j], tensor=lax.rem(p + hp, parts))

    def tile_out(kind, slot, j):
        at = pl.ds(pl.multiple_of(j * cols, cols), cols)
        if kind == 0:
            return pltpu.make_async_copy(stage.at[slot], prex_h.at[:, at], tiles.at[0, slot])
        return pltpu.make_async_copy(stage.at[slot, pl.ds(0, count)], dm_h.at[:, at], tiles.at[kind, slot])

    def xpath(j, carry):
        slot = lax.rem(j, 2)

        @pl.when(j >= 2)
        def _():
            tile_out(0, slot, j).wait()

        at = pl.multiple_of(j * cols, cols)
        lanes = pl.ds(at, cols)
        b = at // ig
        stage[slot] = nn(tok[...], wx[:, lanes])
        mapping = maps_in[b, :, pl.ds(pl.multiple_of(lax.rem(at, ig), LANES), cols)]
        state = jnp.zeros((LANES, cols), F32)
        decay = expand(kd[0:8, :], mapping)
        taps, bias = par[0:4, lanes], par[4:5, lanes]
        for c in range(chunks):
            low = c * SPAN
            weight = expand(dt[low : low + SPAN, :] * et[low : low + SPAN, :], mapping)
            weighted = []
            for side in range(cols // LANES):
                lane_at = slice(side * LANES, (side + 1) * LANES)
                window = stage[slot, low : low + SPAN + HALO, lane_at]
                conv = bias[:, lane_at] + taps[0:1, lane_at] * window[HALO:, :]
                for k in range(1, 4):
                    lag = pltpu.roll(window, k, axis=0)[HALO:, :]
                    conv = conv + taps[k : k + 1, lane_at] * lag * lags[k - 1, low : low + SPAN, :]
                value = (conv * sigmoid(conv)).astype(BF16)
                xs[low : low + SPAN, pl.ds(pl.multiple_of(at + side * LANES, LANES), LANES)] = value
                weighted.append((value.astype(F32) * weight[:, lane_at]).astype(BF16))
            st[c, :, lanes] = state
            fresh = tn(bc[low : low + SPAN, :LANES], jnp.concatenate(weighted, axis=1))
            state = decay[c : c + 1, :] * state + fresh
        fin[:, lanes] = state.astype(BF16)

        @pl.when(half == 0)
        def _():
            state_copy(j).start()

        tile_out(0, slot, j).start()
        return carry

    def project(j, carry):
        lanes = pl.ds(pl.multiple_of(j * cols, cols), cols)
        z[:, lanes] = nn(tok[HALO:, :], wz[:, lanes])
        return carry

    lane_row = iota((1, LANES), 1)
    sides = [(lane_row < 64).astype(BF16), (lane_row >= 64).astype(BF16)]
    middle_of = SPAN // 2

    def y_out(i):
        c, b = i // 2, lax.rem(i, 2)
        rows_to = pl.ds(pl.multiple_of(c * SPAN, SPAN), SPAN)
        lanes_to = pl.ds(pl.multiple_of(b * ig, LANES), ig)
        return pltpu.make_async_copy(y_stage.at[b], y_h.at[rows_to, lanes_to], tiles.at[2, b])

    def scan(i, carry):
        c, b = i // 2, lax.rem(i, 2)
        rows_here = pl.ds(pl.multiple_of(c * SPAN, SPAN), SPAN)
        lanes_b = pl.ds(pl.multiple_of(b * ig, LANES), ig)

        @pl.when(i >= 2)
        def _():
            y_out(i).wait()

        b_map, c_map = bc[rows_here, :LANES], bc[rows_here, LANES:]
        cb[...] = nt(c_map, b_map)
        start = base + c * SPAN
        t, s = iota((SPAN, SPAN), 0), iota((SPAN, SPAN), 1)
        seg_row, seg_col = seg_at(ends, start + iota((1, SPAN), 1)), seg_at(ends, start + iota((SPAN, 1), 0))
        off[...] = jnp.where((t >= s) & (seg_col == seg_row), 0.0, FAR)
        mapping = maps_in[b]
        steps_wide = expand(dt[rows_here, :], mapping)
        lead_wide = expand(em[rows_here, :], mapping)
        arriving = expand(kd[8:16, :], mapping) * (iota((8, 1), 0) == c).astype(F32)
        state = st[c, :, lanes_b] + jnp.sum(arriving, axis=0, keepdims=True) * sin[:, lanes_b].astype(F32)
        skips = par[6:7, pl.ds(pl.multiple_of(b * ig, LANES), LANES)]
        skip = expand(jnp.broadcast_to(skips, (8, LANES)), maps_in[0])[0:1, :]
        read = nn(c_map, state.astype(BF16))
        columns = pltpu.roll(lc[rows_here, :], lax.rem(LANES - 16 * b, LANES), axis=1)
        lines = lr[pl.ds(pl.multiple_of(b * 16, 16), 16), rows_here]
        square = jnp.zeros((SPAN, LANES), F32)
        for k in range(ig // LANES):
            at = slice(k * LANES, (k + 1) * LANES)
            there = pl.ds(pl.multiple_of(b * ig + k * LANES, LANES), LANES)
            xf = xs[rows_here, there].astype(F32)
            pair = (xf * steps_wide[:, at]).astype(BF16)
            far = read[:, at] * lead_wide[:, at] + skip[:, at] * xf
            top = far[:middle_of]
            low = far[middle_of:]
            for side in range(2):
                h = 2 * k + side
                operand = pair * sides[side]
                column = columns[:, h : h + 1]
                line = lines[h : h + 1, :]
                gap = column[:middle_of] - line[:, :middle_of] + off[:middle_of, :middle_of]
                w_top = cb[:middle_of, :middle_of] * jnp.exp2(gap)
                top = top + nn(w_top.astype(BF16), operand[:middle_of, :])
                w_low = cb[middle_of:, :] * jnp.exp2(column[middle_of:] - line + off[middle_of:, :])
                low = low + nn(w_low.astype(BF16), operand)
            out = jnp.concatenate([top, low], axis=0)
            y_stage[b, :, at] = out
            gate = z[rows_here, there]
            gated = out * (gate * sigmoid(gate))
            gated_s[rows_here, there] = gated
            square = square + gated * gated
        y_out(i).start()
        held = jnp.where(b == 0, 0.0, stat[rows_here, :])
        stat[rows_here, :] = held + jnp.where(lane_row == 0, jnp.sum(square, axis=1, keepdims=True), 0.0)
        return carry

    def dm_tile(j, cross):
        slot = lax.rem(j, 2)

        @pl.when(j >= 2)
        def _():
            tile_out(1, slot, j).wait()

        lanes = pl.ds(pl.multiple_of(j * cols, cols), cols)
        value = nn(pulled[...], wo[:, lanes])
        stage[slot, :count, :] = value
        tile_out(1, slot, j).start()
        share = value * gated_s[:, lanes] * par[5:6, lanes]
        for i in range(cols // LANES):
            cross = cross + share[:, i * LANES : (i + 1) * LANES]
        return cross

    tiles_all = inner // cols
    middle = tiles_all // 2

    def drain(kind):
        for j in range(tiles_all - 2, tiles_all):
            tile_out(kind, j % 2, j).wait()

    lax.fori_loop(0, middle, xpath, 0)
    for s in range(stages - 1):
        g_z.stage(s)
    to_o.wait()
    g_o.start()
    lax.fori_loop(middle, tiles_all, xpath, 0)
    for s, to in mates():
        cot_copy_to(s, to, 1).start()
    emit(xs, xs_h)
    emit(st, st_h)
    g_z.stage(stages - 1)
    drain(0)
    g_z.cores()
    emit(wz, wz_h)
    lax.fori_loop(0, tiles_all, project, 0)
    emit(z, z_h)

    @pl.when(half == 1)
    def _():
        for j in range(tiles_all):
            state_copy(j).wait_recv()

    @pl.when(half == 0)
    def _():
        sin[...] = jnp.zeros_like(sin)

    emit(sin, sin_h)
    lax.fori_loop(0, 1, scan, 0)
    for s in range(stages - 1):
        g_o.stage(s)
    lax.fori_loop(1, 2 * chunks, scan, 0)
    g_o.stage(stages - 1)
    g_o.cores()
    emit(wo, wo_h)
    for s, _ in mates():
        for i in range(2):
            cot_arrive(s, i)
    cot_copy.wait()
    emit(pulled, pulled_h)
    cross = lax.fori_loop(0, tiles_all, dm_tile, jnp.zeros((count, LANES), F32))
    stat[...] += jnp.where(lane_row == 1, jnp.sum(cross, axis=1, keepdims=True), 0.0)
    sums_out[...] = stat[...].T[:8, :]

    def stat_copy(s, to):
        return remote(sums_out, sums_in.at[s - 1], ms.at[s - 1], mr.at[s - 1], tensor=to)

    for s, to in mates():
        stat_copy(s, to).start()
    drain(1)
    for i in range(2 * chunks - 2, 2 * chunks):
        y_out(i).wait()
    for s, to in mates():
        stat_copy(s, to).wait()
    summed = sums_out[...]
    for s in range(1, hp):
        summed = summed + sums_in[s - 1]
    stat_o[...] = jnp.concatenate([summed, jnp.zeros((LANES - 8, count), F32)], axis=0).T
    for item in (to_table, to_dt, to_x, to_z, to_o, g_s, g_x, g_z, g_o):
        item.finish()
    for s, to in mates():
        tok_copy(s, to).wait_send()
        for i in range(2):
            cot_copy_to(s, to, i).wait_send()

    @pl.when(p == hp - 1)
    def _():
        for k in range(hp):
            halo_copy(k).wait_send()

    @pl.when(half == 0)
    def _():
        for j in range(tiles_all):
            state_copy(j).wait_send()

    for copy in emitted:
        copy.wait()


def run_first(
    ends, inputs, cot, ngain, w_x, w_z, w_out, w_bc, w_dt, conv_x, conv_x_bias, dt_bias, a_log, d_skip, gate_gain,
    taps_bc, bias_bc, size, parts,
):
    ha = dt_bias.shape[0]
    local_rows, width = inputs.shape
    rows, ig = w_x.shape
    inner = 2 * ig
    hp = parts // 2
    count = local_rows * hp
    total = count + HALO
    chunks = count // SPAN
    cols = col_tile(ig)
    shape = jax.ShapeDtypeStruct
    per_block = shape((count, LANES), F32)
    outs = (
        shape((total, width), BF16),
        shape((count, width), BF16),
        shape((width, inner), BF16),
        shape((width, inner), BF16),
        shape((width, inner), BF16),
        shape((width, 4 * LANES), BF16),
        shape((8, inner), F32),
        shape((total, 2 * LANES), F32),
        shape((count, 2 * LANES), BF16),
        per_block,
        per_block,
        per_block,
        shape((32, count), F32),
        per_block,
        per_block,
        shape((24, LANES), F32),
        shape((total, inner), F32),
        shape((count, inner), BF16),
        shape((chunks, LANES, inner), F32),
        shape((LANES, inner), BF16),
        shape((count, inner), F32),
        shape((count, inner), F32),
        shape((count, inner), F32),
        shape((count, LANES), F32),
    )
    anywhere = pl.BlockSpec(memory_space=pl.ANY)
    dma = pltpu.SemaphoreType.DMA
    nbits = size.bit_length()
    scratch = [pltpu.VMEM(o.shape, o.dtype) for o in outs[:16]]
    scratch += [
        pltpu.VMEM((chunks, LANES, inner), F32),
        pltpu.VMEM((2, total, cols), F32),
        pltpu.VMEM((count, inner), BF16),
        pltpu.VMEM((LANES, inner), BF16),
        pltpu.VMEM((LANES, inner), BF16),
        pltpu.VMEM((count, inner), F32),
        pltpu.VMEM((count, inner), F32),
        pltpu.VMEM((2, SPAN, ig), F32),
        pltpu.VMEM((SPAN, SPAN), F32),
        pltpu.VMEM((SPAN, SPAN), F32),
        pltpu.VMEM((count, LANES), F32),
        pltpu.VMEM((8, count), F32),
        pltpu.VMEM((hp - 1, 8, count), F32),
        pltpu.VMEM((3, count, LANES), F32),
        pltpu.VMEM((rows, LANES), BF16),
        pltpu.VMEM((8, ig), F32),
        pltpu.VMEM((2, LANES, ig), BF16),
        dma((10,)),
        dma((10,)),
        dma((5,)),
        dma((4, 2, size * nbits)),
        dma((4, 2, size)),
        dma((hp,)),
        dma((hp,)),
        dma((2, hp)),
        dma((2, hp)),
        dma((hp,)),
        dma((1,)),
        dma((inner // cols,)),
        dma((inner // cols,)),
        dma((hp - 1,)),
        dma((hp - 1,)),
        dma((2,)),
        dma((24,)),
        dma((3, 2)),
    ]
    return pl.pallas_call(
        partial(first_body, size, parts, rows, ha, ig),
        out_shape=outs,
        in_specs=[scalars(), whole(), anywhere, whole(), anywhere, anywhere, anywhere, anywhere] + [whole()] * 9,
        out_specs=[anywhere] * (len(outs) - 1) + [whole()],
        scratch_shapes=scratch,
        compiler_params=pltpu.CompilerParams(vmem_limit_bytes=VMEM_BYTES, collective_id=0, has_side_effects=True),
        cost_estimate=cost(2 * total * width * (3 * inner + 512), 60e6),
        name="first",
    )(
        ends, inputs, cot, ngain, w_x, w_z, w_out, w_bc, w_dt, conv_x, conv_x_bias, dt_bias, a_log, d_skip,
        gate_gain, taps_bc, bias_bc,
    )


def gate_body(
    size, parts, ig, inner_all, gz_tiles, y, z, dm, stats, xs, par, bc, em, kd, tok_h, pulled_h, wo,
    dz_o, dy_o, sums_o, ds_o, gz_h, go_h, dsin_o, branch_o,
    first, dsin, tok, pulled, mixed_s, dz_s, gz, go, zcore, ocore, loads, ss, sr, ccs, ccr, outs,
):
    count, cols = y.shape
    j = pl.program_id(0)
    tiles = gz_tiles
    p = lax.axis_index("tensor")
    hp = parts // 2
    part = p // hp
    peer = lax.rem(p + hp, parts)

    me = lax.axis_index("dp")
    rows = go.shape[0] // size

    def scatter(k, ref, core_buf):
        columns = halves(ig, 2 * ig)

        def block(h, v):
            return sharded_rows(ref, me, v, rows, columns[h])

        return Scatter(k, block, lambda h, u: block(h, 2 * u), None, size, core_buf, None, ccs, ccr, None, None)

    scat_o, scat_z = scatter(0, go, ocore), scatter(1, gz, zcore)

    def sums_out(k, ref, dst):
        return [
            pltpu.make_async_copy(sharded_rows(ref, me, 2 * u, rows, (0, 2 * ig)), dst.at[u], outs.at[k, u])
            for u in range(size // 2)
        ]

    def state_copy(i):
        at = pl.ds(pl.multiple_of(i * cols, cols), cols)
        return remote(first.at[:, at], dsin.at[:, at], ss.at[i], sr.at[i], tensor=peer)

    def elementwise():
        at = j * cols
        here = pl.ds(pl.multiple_of(at, cols), cols)
        mapping = head_map(cols, lax.rem(at, ig), at // ig * 16)
        gone = expand(kd[0:8, :], mapping)
        gain = par[5:6, :]
        grad = jnp.zeros((LANES, cols), F32)
        by_gain = jnp.zeros((1, cols), F32)
        by_skip = jnp.zeros((1, cols), F32)
        for c in range(count // SPAN - 1, -1, -1):
            span = slice(c * SPAN, (c + 1) * SPAN)
            stat = stats[span, :]
            scale = lax.rsqrt(stat[:, 0:1] / inner_all + EPS)
            pull = scale * scale * scale * stat[:, 1:2] / inner_all
            gate = z[span, :]
            sig = sigmoid(gate)
            act = gate * sig
            out = y[span, :]
            gated = out * act
            normal = gated * scale
            mixed = (normal * gain).astype(BF16)
            mixed_s[span, here] = mixed
            upstream = dm[span, :]
            by_gain = by_gain + jnp.sum(upstream * normal, axis=0, keepdims=True)
            dgated = scale * (upstream * gain) - gated * pull
            dz = (dgated * out * (sig * (1.0 + gate * (1.0 - sig)))).astype(BF16)
            dz_o[span, :] = dz
            dz_s[span, here] = dz
            dy = dgated * act
            by_skip = by_skip + jnp.sum(dy * xs[span, :].astype(F32), axis=0, keepdims=True)
            dy_o[span, :] = dy.astype(BF16)
            ds_o[c] = grad
            lead = (dy * expand(em[span, :], mapping)).astype(BF16)
            grad = gone[c : c + 1, :] * grad + tn(bc[span, LANES:], lead)
        sums_o[...] = jnp.concatenate([by_gain, by_skip, jnp.zeros((6, cols), F32)], axis=0)
        first[:, pl.ds(pl.multiple_of(j * cols, cols), cols)] = grad.astype(BF16)

        @pl.when(part == 1)
        def _():
            state_copy(j).start()

    def load(i):
        src, dst = ((pulled_h, pulled), (tok_h, tok))[i]
        return pltpu.make_async_copy(src, dst, loads.at[i])

    @pl.when(j == 0)
    def _():
        greet([1], [peer])
        load(0).start()
        load(1).start()

    @pl.when(j < tiles)
    def _():
        elementwise()

    @pl.when(j == tiles)
    def _():
        load(0).wait()
        load(1).wait()

    @pl.when((j >= tiles) & (j < 2 * tiles))
    def _():
        here = pl.ds(pl.multiple_of((j - tiles) * cols, cols), cols)
        go[:, here] = tn(pulled[...], mixed_s[:, here]).astype(BF16)
        gz[:, here] = tn(tok[HALO:, :], dz_s[:, here]).astype(BF16)

    for h in range(2):

        @pl.when(j == tiles + (h + 1) * (tiles // 2) - 1)
        def _(h=h):
            scat_o.start(h)
            scat_z.start(h)

    @pl.when(j >= 2 * tiles)
    def _():
        branch_o[...] = nt(mixed_s[...], wo[...]).astype(BF16)

    last = pl.num_programs(0) - 1
    for h in range(2):

        @pl.when(j == 2 * tiles + h * 2 + 1)
        def _(h=h):
            scat_o.fold_core(h)

        @pl.when(j == 2 * tiles + h * 2 + 2)
        def _(h=h):
            scat_z.fold_core(h)

    @pl.when(j == last - 1)
    def _():
        for copy in sums_out(0, go, go_h):
            copy.start()

    @pl.when(j == last)
    def _():
        for copy in sums_out(1, gz, gz_h):
            copy.start()

    @pl.when(j == last)
    def _():
        scat_o.finish_core()
        scat_z.finish_core()
        for copy in sums_out(0, go, go_h) + sums_out(1, gz, gz_h):
            copy.wait()

        def send_done(i, carry):
            state_copy(i).wait_send()
            return carry

        def arrived(i, carry):
            state_copy(i).wait_recv()
            return carry

        @pl.when(part == 1)
        def _():
            lax.fori_loop(0, tiles, send_done, 0)
            dsin_o[...] = jnp.zeros_like(dsin_o)

        @pl.when(part == 0)
        def _():
            lax.fori_loop(0, tiles, arrived, 0)
            dsin_o[...] = dsin[...]


def run_gate(y, z, dm, stat, xs, par, bc, em, kd, tok, pulled, wo, ig, inner_all, size, parts):
    count, inner = y.shape
    width = tok.shape[1]
    cols = col_tile(ig)
    tiles = inner // cols
    chunks = count // SPAN

    def now(j):
        return jnp.minimum(j, tiles - 1)

    tile = pl.BlockSpec((count, cols), lambda j: (0, now(j)))
    grads = pl.BlockSpec(memory_space=pl.ANY)
    rows = width // size
    blocks = size // 2

    def out(j):
        return jnp.maximum(j - 2 * tiles, 0)

    low = jax.ShapeDtypeStruct((count, inner), BF16)
    shape = jax.ShapeDtypeStruct
    return pl.pallas_call(
        partial(gate_body, size, parts, ig, inner_all, tiles),
        grid=(2 * tiles + width // SPAN,),
        out_shape=(
            low,
            low,
            shape((8, inner), F32),
            shape((chunks, LANES, inner), F32),
            shape((blocks, rows, inner), BF16),
            shape((blocks, rows, inner), BF16),
            shape((LANES, inner), BF16),
            shape((count, width), BF16),
        ),
        in_specs=[
            tile,
            tile,
            tile,
            whole(),
            tile,
            pl.BlockSpec((8, cols), lambda j: (0, now(j))),
            whole(),
            whole(),
            whole(),
            pl.BlockSpec(memory_space=pl.ANY),
            pl.BlockSpec(memory_space=pl.ANY),
            pl.BlockSpec((SPAN, inner), lambda j: (out(j), 0)),
        ],
        out_specs=(
            tile,
            tile,
            pl.BlockSpec((8, cols), lambda j: (0, now(j))),
            pl.BlockSpec((chunks, LANES, cols), lambda j: (0, 0, now(j))),
            grads,
            grads,
            whole(),
            pl.BlockSpec((count, SPAN), lambda j: (0, out(j))),
        ),
        scratch_shapes=[
            pltpu.VMEM((LANES, inner), BF16),
            pltpu.VMEM((LANES, inner), BF16),
            pltpu.VMEM(tok.shape, BF16),
            pltpu.VMEM(pulled.shape, BF16),
            pltpu.VMEM((count, inner), BF16),
            pltpu.VMEM((count, inner), BF16),
            pltpu.VMEM((width, inner), BF16),
            pltpu.VMEM((width, inner), BF16),
            [pltpu.VMEM((blocks, rows, ig), BF16)] * 2,
            [pltpu.VMEM((blocks, rows, ig), BF16)] * 2,
            pltpu.SemaphoreType.DMA((2,)),
            pltpu.SemaphoreType.DMA((tiles,)),
            pltpu.SemaphoreType.DMA((tiles,)),
            pltpu.SemaphoreType.DMA((2, 2, blocks)),
            pltpu.SemaphoreType.DMA((2, 2, blocks)),
            pltpu.SemaphoreType.DMA((2, blocks)),
        ],
        compiler_params=pltpu.CompilerParams(vmem_limit_bytes=VMEM_BYTES, collective_id=4, has_side_effects=True),
        cost_estimate=cost(12e9, 30e6),
        name="gate",
    )(y, z, dm, stat, xs, par, bc, em, kd, tok, pulled, wo)


def pull_body(
    size, parts, ha, wrows,
    sc, xs, dy, bc, dtin, dt, lc, lr, em, et, kd, st, sin, ds, dsin, pre, par,
    inputs_h, branch_h, gz_h, go_h, tok_h,
    dx_o, dbc_o, ddt_o, csum_o, hsum_o, out_o, gz_o, go_o, ga_o,
    cbt, off, dcb, ahead, lags, products, tails, leads, rsum, maps_in, maps_out, skips, inputs, branch, arrived, tok, ga, dlow, dother,
    zacc, oacc, acore, zlink, olink, alink, zz, oz,
    loads, ccs, ccr, cls, clr, hs, hr, ho, ms, mr, bs, br,
):
    b, step = pl.program_id(0), pl.program_id(1)
    chunks = pl.num_programs(1)
    c = chunks - 1 - step
    cols = xs.shape[1]
    half = SPAN // 2
    p = lax.axis_index("tensor")
    me = lax.axis_index("dp")
    hp = parts // 2
    place = lax.rem(p, hp)
    part = p // hp
    count = dbc_o.shape[0]
    local_rows = inputs.shape[0]
    start = part * count + c * SPAN
    n = b * chunks + step
    rows_here = pl.ds(pl.multiple_of(c * SPAN, SPAN), SPAN)

    def scatter(k, acc, link_buf):
        columns = halves(cols, 2 * cols)
        return Scatter(
            k, None, lambda h, u: acc.at[u, :, pl.ds(columns[h][0], cols)], None, size, None, link_buf, ccs, ccr, cls, clr
        )

    def a_block(h, v):
        return sharded_rows(ga, me, v, wrows, halves(split_of(cols), cols)[h])

    scat_o = scatter(0, oacc, olink)
    scat_z = scatter(1, zacc, zlink)
    scat_a = Scatter(2, a_block, lambda h, u: a_block(h, 2 * u), None, size, acore, alink, ccs, ccr, cls, clr)
    home_o = FromHeads(0, lambda side: oacc.at[0, :, pl.ds(side * cols, cols)], oz, parts, hs, hr, ho)
    home_z = FromHeads(1, lambda side: zacc.at[0, :, pl.ds(side * cols, cols)], zz, parts, hs, hr, ho)
    stages = scat_o.stages()

    def mates():
        return [(s, part * hp + lax.rem(place + s, hp)) for s in range(1, hp)]

    def branch_copy(s, to):
        rows_to = pl.ds(pl.multiple_of(lax.rem(place + s, hp) * local_rows, 16), local_rows)
        return remote(branch_h.at[rows_to], arrived.at[s - 1], bs.at[s - 1], br.at[s - 1], tensor=to)

    def maps_copy(s, to, i):
        at = pl.ds(pl.multiple_of(i * SPAN, SPAN), SPAN)
        return remote(dlow.at[at], dother.at[s - 1, at], ms.at[s - 1, i], mr.at[s - 1, i], tensor=to)

    def branch_own():
        own = pl.ds(pl.multiple_of(place * local_rows, 16), local_rows)
        return pltpu.make_async_copy(branch_h.at[own], branch, loads.at[0])

    def inputs_load():
        return pltpu.make_async_copy(inputs_h, inputs, loads.at[4])

    def tok_load():
        return pltpu.make_async_copy(tok_h, tok, loads.at[1])

    @pl.when(n == 0)
    def _():
        sums = [pltpu.make_async_copy(src, dst, loads.at[2 + i]) for i, (src, dst) in enumerate(((go_h, oacc), (gz_h, zacc)))]
        for copy in sums:
            copy.start()
        greet([1] + link_bits(size), others(parts))
        for s, to in mates():
            branch_copy(s, to).start()
        for copy in sums:
            copy.wait()
        for h in range(2):
            scat_o.send(h, 0)
        branch_own().start()
        inputs_load().start()
        tok_load().start()

    @pl.when(n == 1)
    def _():
        for h in range(2):
            scat_z.send(h, 0)

    @pl.when(n == 2)
    def _():
        for s in range(stages - 1):
            for h in range(2):
                scat_o.fold(h, s)
                scat_o.send(h, s + 1)

    @pl.when(n == 3)
    def _():
        for s in range(stages - 1):
            for h in range(2):
                scat_z.fold(h, s)
                scat_z.send(h, s + 1)

    @pl.when(n == 4)
    def _():
        for h in range(2):
            scat_o.fold(h, stages - 1)
            home_o.start(h)

    @pl.when(n == 5)
    def _():
        for h in range(2):
            scat_z.fold(h, stages - 1)
            home_z.start(h)

    @pl.when(n == chunks + 1)
    def _():
        for h in range(2):
            scat_a.fold_core(h)
            scat_a.send(h, 0)

    @pl.when(n == chunks + 2)
    def _():
        for s in range(stages - 1):
            for h in range(2):
                scat_a.fold(h, s)
                scat_a.send(h, s + 1)

    b_map, c_map = bc[:, :LANES], bc[:, LANES:]
    cbt[...] = nt(b_map, c_map)
    s, t = iota((SPAN, SPAN), 0), iota((SPAN, SPAN), 1)
    seg_row, seg_col = seg_at(sc, start + iota((1, SPAN), 1)), seg_at(sc, start + iota((SPAN, 1), 0))
    off[...] = jnp.where((t >= s) & (seg_col == seg_row), 0.0, FAR)
    here = start + iota((SPAN, LANES), 0)
    for j in range(1, 4):
        lags[j - 1] = same_as_behind(sc, here, j)
    dcb[...] = jnp.zeros_like(dcb)

    @pl.when(step == 0)
    def _():
        ahead[...] = jnp.zeros_like(ahead)
        csum_o[...] = jnp.zeros_like(csum_o)
        hsum_o[...] = jnp.zeros_like(hsum_o)
        rsum[...] = jnp.zeros_like(rsum)
        maps_in[...] = head_map(cols, 0, b * 16)
        maps_out[...] = head_map(cols, 0, 0, both=False)
        skips[...] = expand(jnp.broadcast_to(par[6:7, :LANES], (8, LANES)), head_map(cols, 0, 0))

    lane = iota((1, LANES), 1)
    taps, bias = par[0:4, :], par[4:5, :]
    skip = skips[0:1, :]
    mapping = maps_in[...]
    single = maps_out[...]
    columns = pltpu.roll(lc[...], lax.rem(LANES - 16 * b, LANES), axis=1)

    def mine(values):
        return pltpu.roll(values, lax.rem(LANES - 16 * b, LANES), axis=1) * (lane < ha).astype(F32)

    sides = [(lane < 64).astype(BF16), (lane >= 64).astype(BF16)]
    steps = mine(dt[...])
    steps_wide = expand(dt[...], mapping)
    lead_wide = expand(em[...], mapping)
    tail_wide = expand(et[...], mapping)
    decays = expand(kd[...], mapping)
    pick = (iota((8, 1), 0) == c).astype(F32)
    state = st[0] + jnp.sum(decays[8:16] * pick, axis=0, keepdims=True) * sin[...].astype(F32)
    dstate = ds[0] + jnp.sum(decays[16:24] * pick, axis=0, keepdims=True) * dsin[...].astype(F32)
    state_l, dstate_l = state.astype(BF16), dstate.astype(BF16)
    crossing = jnp.sum(state * dstate, axis=0, keepdims=True)
    read = nn(c_map, state_l)
    far = nn(b_map, dstate_l)
    csums = jnp.zeros((SPAN, LANES), F32)
    blank = jnp.zeros((8, LANES), F32)
    window_at = pl.ds(pl.multiple_of(c * SPAN, SPAN), SPAN + HALO)
    out_at = pl.ds(pl.multiple_of(HALO + c * SPAN, HALO), SPAN)
    for k in range(cols // LANES):
        at = slice(k * LANES, (k + 1) * LANES)
        xf = xs[:, at].astype(F32)
        wide = steps_wide[:, at]
        x_pair, dy_pair = (xf * wide).astype(BF16), dy[:, at]
        top = jnp.zeros((half, LANES), F32)
        low = jnp.zeros((half, LANES), F32)
        for side in range(2):
            h = 2 * k + side
            x_one = x_pair * sides[side]
            dy_one = dy_pair * sides[side]
            column = columns[:, h : h + 1]
            row = lr[h : h + 1, :]
            decay = jnp.exp2(row - column[:half] + off[:half, :])
            top = top + nn((cbt[:half, :] * decay).astype(BF16), dy_one)
            share = nt(x_one[:half, :], dy_pair) * decay
            dcb[:half, :] += share
            both = share * cbt[:half, :]
            row_sum = jnp.sum(both, axis=0, keepdims=True)
            col_top = jnp.sum(both, axis=1, keepdims=True)
            decay = jnp.exp2(row[:, half:] - column[half:] + off[half:, half:])
            low = low + nn((cbt[half:, half:] * decay).astype(BF16), dy_one[half:, :])
            share = nt(x_one[half:, :], dy_pair[half:, :]) * decay
            dcb[half:, half:] += share
            both = share * cbt[half:, half:]
            rsum[h : h + 1, :half] = row_sum[:, :half]
            rsum[h : h + 1, half:] = row_sum[:, half:] + jnp.sum(both, axis=0, keepdims=True)
            col_low = jnp.sum(both, axis=1, keepdims=True)
            csums = csums + jnp.where(lane == h, jnp.concatenate([col_top, col_low], axis=0), 0.0)
        near = jnp.concatenate([top, low], axis=0)
        tail = tail_wide[:, at]
        dx_far = far[:, at] * tail
        tails[:, at] = (x_pair.astype(F32) * tail).astype(BF16)
        dyf = dy_pair.astype(F32)
        led = dyf * lead_wide[:, at]
        leads[:, at] = led.astype(BF16)
        products[0, :, at] = (xf * near).astype(BF16)
        products[1, :, at] = (xf * dx_far).astype(BF16)
        products[2, :, at] = (led * read[:, at]).astype(BF16)
        dxs = (near + dx_far) * wide + dyf * skip[:, at]

        window = pre[window_at, at]
        lagged = [window[HALO:, :]]
        for j in range(1, 4):
            lagged.append(pltpu.roll(window, j, axis=0)[HALO:, :] * lags[j - 1])
        conv = bias[:, at]
        for j in range(4):
            conv = conv + taps[j : j + 1, at] * lagged[j]
        sig = sigmoid(conv)
        dconv = dxs * (sig * (1.0 + conv * (1.0 - sig)))
        sums = [jnp.sum(dconv * lagged[j], axis=0, keepdims=True) for j in range(4)]
        sums.append(jnp.sum(dconv, axis=0, keepdims=True))
        csum_o[:, at] += jnp.concatenate(sums + [jnp.zeros((3, LANES), F32)], axis=0)
        dpre = taps[0:1, at] * dconv
        edge = jnp.zeros((HALO, LANES), F32)
        for j in range(1, 4):
            masked = dconv * lags[j - 1]
            longer = jnp.concatenate([masked, ahead[8 * (j - 1) : 8 * j, at]], axis=0)
            dpre = dpre + taps[j : j + 1, at] * pltpu.roll(longer, SPAN + 8 - j, axis=0)[:SPAN, :]
            opening = masked[:8, :]
            ahead[8 * (j - 1) : 8 * j, at] = opening
            before = pltpu.roll(jnp.concatenate([blank, blank, opening], axis=0), 24 - j, axis=0)[:HALO, :]
            edge = edge + taps[j : j + 1, at] * before
        dx_o[out_at, at] = dpre.astype(BF16)
        dx_o[:HALO, at] = edge.astype(BF16)
    db = nn(dcb[...].astype(BF16), c_map) + nt(tails[...], dstate_l)
    dc = tn(dcb[...].astype(BF16), b_map) + nt(leads[...], state_l)

    @pl.when(b == 0)
    def _():
        dbc_o[rows_here, :LANES] = db
        dbc_o[rows_here, LANES:] = dc

    @pl.when(b > 0)
    def _():
        dlow[rows_here, :LANES] = (dbc_o[rows_here, :LANES] + db).astype(BF16)
        dlow[rows_here, LANES:] = (dbc_o[rows_here, LANES:] + dc).astype(BF16)
        for s, to in mates():
            maps_copy(s, to, c).start()

    from_near = nt(products[0], single)
    from_far = nt(products[1], single)
    reads = nt(products[2], single)
    high = crossing.astype(BF16).astype(F32)
    middle = (crossing - high).astype(BF16).astype(F32)
    pieces = jnp.concatenate([high, middle, crossing - high - middle, jnp.zeros((5, cols), F32)], axis=0)
    held = jnp.sum(nt(pieces.astype(BF16), single), axis=0, keepdims=True)
    held = held * mine(jnp.broadcast_to(jnp.sum(kd[0:8, :] * pick, axis=0, keepdims=True), (8, LANES)))[0:1, :]
    lower = (s > t).astype(BF16)
    upper = (s <= t).astype(BF16)
    dlog = joined(nn(upper, thirds(rsum[...].T - csums + reads)) + nn(lower, thirds(steps * from_far))) + held
    rates = jnp.concatenate([par[7:8, LANES : 2 * LANES], jnp.zeros((7, LANES), F32)], axis=0)
    rate = -jnp.exp(rates)[0:1, :]
    dstep = from_near + from_far + dlog * rate
    ddt = dstep * mine(sigmoid(dtin[...]))
    ddt_o[0] = ddt
    hsum_o[0, 0:1, :] += jnp.sum(ddt, axis=0, keepdims=True)
    hsum_o[0, 1:2, :] += jnp.sum(dlog * steps * rate, axis=0, keepdims=True)

    @pl.when(n == chunks - 1)
    def _():
        tok_load().wait()
        wide = col_tile(cols)

        def grad_tile(j, carry):
            at = pl.ds(pl.multiple_of(j * wide, wide), wide)
            ga[:, at] = tn(tok[...], dx_o[:, at]).astype(BF16)
            return carry

        lax.fori_loop(0, cols // wide, grad_tile, 0)
        for h in range(2):
            scat_a.start(h)

    @pl.when(n == 2 * chunks - 1)
    def _():
        for s, to in mates():
            branch_copy(s, to).wait_recv()
        branch_own().wait()
        inputs_load().wait()
        total = inputs[...].astype(F32) + branch[...].astype(F32)
        for s in range(1, hp):
            total = total + arrived[s - 1].astype(F32)
        out_o[...] = total.astype(BF16)
        home_o.wait()
        go_o[...] = oz[0].astype(F32) + oz[1].astype(F32)
        home_z.wait()
        gz_o[...] = zz[0].astype(F32) + zz[1].astype(F32)

        for h in range(2):
            scat_a.fold(h, stages - 1)
        ga_o[...] = sharded_rows(ga, me, 0, wrows, (0, cols))[...]
        for s, to in mates():
            for i in range(count // SPAN):
                maps_copy(s, to, i).wait_recv()
        summed = dlow[...].astype(F32)
        for s in range(1, hp):
            summed = summed + dother[s - 1].astype(F32)
        dbc_o[...] = summed
        for item in (scat_a, home_o, home_z):
            item.finish()
        scat_o.finish_links()
        scat_z.finish_links()
        for s, to in mates():
            branch_copy(s, to).wait_send()
            for i in range(count // SPAN):
                maps_copy(s, to, i).wait_send()


def run_pull(
    sc, xs, dy, bc, dtin, dt, lc, lr, em, et, kd, st, sin, ds, dsin, pre, par,
    inputs, branch, gz, go, tok, ha, ig, size, parts,
):
    count, inner = xs.shape
    local_rows, width = inputs.shape
    total = count + HALO
    chunks = count // SPAN
    wrows = width // size
    hp = parts // 2

    def rev(step):
        return chunks - 1 - step

    tile = pl.BlockSpec((SPAN, ig), lambda b, i: (rev(i), b))
    per_token = pl.BlockSpec((SPAN, LANES), lambda b, i: (rev(i), 0))
    states = pl.BlockSpec((1, LANES, ig), lambda b, i: (rev(i), 0, b))
    edge = pl.BlockSpec((LANES, ig), lambda b, i: (0, b))
    full = pl.BlockSpec((total, ig), lambda b, i: (0, b))
    anywhere = pl.BlockSpec(memory_space=pl.ANY)
    shape = jax.ShapeDtypeStruct
    vm = pltpu.VMEM
    dma = pltpu.SemaphoreType.DMA
    blocks, links = size // 2, max(size // 2 - 1, 1)
    splits = [split_of(ig), ig - split_of(ig)]
    scratch = dict(
        cbt=vm((SPAN, SPAN), F32),
        off=vm((SPAN, SPAN), F32),
        dcb=vm((SPAN, SPAN), F32),
        ahead=vm((24, ig), F32),
        lags=vm((3, SPAN, LANES), F32),
        products=vm((3, SPAN, ig), BF16),
        tails=vm((SPAN, ig), BF16),
        leads=vm((SPAN, ig), BF16),
        rsum=vm((LANES, SPAN), F32),
        maps_in=vm((LANES, ig), BF16),
        maps_out=vm((LANES, ig), BF16),
        skips=vm((8, ig), F32),
        inputs=vm((local_rows, width), BF16),
        branch=vm((local_rows, width), BF16),
        arrived=vm((hp - 1, local_rows, width), BF16),
        tok=vm((total, width), BF16),
        ga=vm((width, ig), BF16),
        dlow=vm((count, 2 * LANES), BF16),
        dother=vm((hp - 1, count, 2 * LANES), BF16),
        zacc=vm((blocks, wrows, inner), BF16),
        oacc=vm((blocks, wrows, inner), BF16),
        acore=[vm((blocks, wrows, w), BF16) for w in splits],
        zlink=[vm((links, wrows, ig), BF16)] * 2,
        olink=[vm((links, wrows, ig), BF16)] * 2,
        alink=[vm((links, wrows, w), BF16) for w in splits],
        zz=vm((2, wrows, ig), BF16),
        oz=vm((2, wrows, ig), BF16),
        loads=dma((5,)),
        ccs=dma((3, 2, blocks)),
        ccr=dma((3, 2, blocks)),
        cls=dma((3, 2, links)),
        clr=dma((3, 2, links)),
        hs=dma((4,)),
        hr=dma((4,)),
        ho=dma((2,)),
        ms=dma((hp - 1, chunks)),
        mr=dma((hp - 1, chunks)),
        bs=dma((hp - 1,)),
        br=dma((hp - 1,)),
    )
    return pl.pallas_call(
        partial(pull_body, size, parts, ha, wrows),
        grid=(2, chunks),
        out_shape=(
            shape((total, inner), BF16),
            shape((count, 2 * LANES), F32),
            shape((2, count, LANES), F32),
            shape((8, inner), F32),
            shape((2, 8, LANES), F32),
            shape((local_rows, width), BF16),
            shape((wrows, ig), F32),
            shape((wrows, ig), F32),
            shape((wrows, ig), BF16),
        ),
        in_specs=[
            scalars(),
            tile,
            tile,
            pl.BlockSpec((SPAN, 2 * LANES), lambda b, i: (rev(i), 0)),
            per_token,
            per_token,
            per_token,
            pl.BlockSpec((16, SPAN), lambda b, i: (b, rev(i))),
            per_token,
            per_token,
            whole(),
            states,
            edge,
            states,
            edge,
            full,
            pl.BlockSpec((8, ig), lambda b, i: (0, b)),
        ]
        + [anywhere] * 5,
        out_specs=(
            full,
            whole(),
            pl.BlockSpec((1, SPAN, LANES), lambda b, i: (b, rev(i), 0)),
            pl.BlockSpec((8, ig), lambda b, i: (0, b)),
            pl.BlockSpec((1, 8, LANES), lambda b, i: (b, 0, 0)),
            whole(),
            whole(),
            whole(),
            whole(),
        ),
        scratch_shapes=list(scratch.values()),
        compiler_params=pltpu.CompilerParams(vmem_limit_bytes=VMEM_BYTES, collective_id=3, has_side_effects=True),
        cost_estimate=cost(20e9, 30e6),
        name="pull",
    )(
        sc, xs, dy, bc, dtin, dt, lc, lr, em, et, kd, st, sin, ds, dsin, pre, par,
        inputs, branch, gz, go, tok,
    )


def last_body(
    size, parts, rows, ha, ig,
    ends, inputs_h, cot_h, ngain, tok_h, dz_h, dx_h, wz_h, wx_h, ws_h, dbc_h, ddt, pre_h, taps, bias, csum, gsum, hsum, ga,
    gin_o, gx_o, gdt_o, gbc_o, chan_o, rep_o,
    inputs, cot, dbc, pre, tok, dz, dx, wz, wx, ws, gx, gsm, dsm, conv, dn_out, dn_in, dn_own, edge_out, edge_in,
    xcore, xlink, score, slink, xz, dtz, bcz, chan, chan_in, chan_z, rep, rep_in, rep_z,
    loads, ccs, ccr, cls, clr, zs, zr, zo, bs, br, ns, nr, es, er, ts, tr, rs, rr, ro,
):
    p = lax.axis_index("tensor")
    me = lax.axis_index("dp")
    hp = parts // 2
    place = lax.rem(p, hp)
    half = p // hp
    inner = 2 * ig
    local_rows, width = inputs.shape
    count = local_rows * hp
    total = count + HALO
    base = half * count
    own_at = pl.multiple_of(HALO + place * local_rows, 16)

    moving = [
        pltpu.make_async_copy(src, dst, loads.at[i])
        for i, (src, dst) in enumerate((
            (dx_h, dx), (tok_h, tok), (wx_h, wx), (dz_h, dz), (wz_h, wz), (ws_h, ws),
            (dbc_h, dbc), (pre_h, pre), (inputs_h, inputs), (cot_h, cot),
        ))
    ]
    for copy in moving:
        copy.start()
    greet([1] + link_bits(size), others(parts))

    def mates():
        return [(s, half * hp + lax.rem(place + s, hp)) for s in range(1, hp)]

    dp_steps = [("dp", 1)] + [("dp", bit) for bit in link_bits(size)]
    chan[0:5, :] = csum[0:5, :]
    chan[5:7, :] = gsum[0:2, :]
    chan[7:8, :] = jnp.zeros((1, inner), F32)
    for b in range(2):
        for i in range(2):
            at = b * ig + i * LANES
            chan[7:8, at : at + LANES] = hsum[b, i : i + 1, :]
    sum_chan = Butterfly(0, chan, chan_in, dp_steps, bs, br)
    sum_rep = Butterfly(1, rep, rep_in, dp_steps, bs, br)
    all_rep = AllZ(rep, rep_z, parts, rs, rr, ro)
    sum_chan.push(0)

    def x_block(h, v):
        return sharded_rows(gx, me, v, rows, halves(split_of(ig), ig)[h])

    def s_block(h, v):
        return sharded_rows(gsm, me, v, rows, halves(2 * LANES, 4 * LANES)[h])

    scat_x = Scatter(0, x_block, lambda h, u: x_block(h, 2 * u), None, size, xcore, xlink, ccs, ccr, cls, clr)
    scat_s = Scatter(1, s_block, lambda h, u: s_block(h, 2 * u), None, size, score, slink, ccs, ccr, cls, clr)
    stages = scat_x.stages()
    home_x = FromHeads(0, lambda side: sharded_rows(gx, me, 0, rows, (0, ig)) if side else ga, xz, parts, zs, zr, zo)
    home_dt = FromHeads(
        1,
        lambda side: sharded_rows(gsm, me, 0, rows, (side * LANES, (side + 1) * LANES)),
        dtz, parts, zs, zr, zo,
    )
    home_x.start(0)
    home_chan = FromHeads(2, lambda side: chan.at[:, pl.ds(side * ig, ig)], chan_z, parts, zs, zr, zo)

    cols = col_tile(ig)
    rep[...] = jnp.zeros_like(rep)
    dsm[:HALO, : 2 * LANES] = jnp.zeros((HALO, 2 * LANES), BF16)
    for b in range(2):
        dsm[HALO:, b * LANES : (b + 1) * LANES] = ddt[b].astype(BF16)
    for copy in moving[:2]:
        copy.wait()

    def grad_x(j, carry):
        at = pl.multiple_of(j * cols, cols)
        gx[:, pl.ds(at, cols)] = tn(tok[...], dx[:, pl.ds(ig + at, cols)]).astype(BF16)
        return carry

    def fold_cores(*scats):
        for scat in scats:
            for h in range(2):
                scat.fold_core(h)
                scat.send(h, 0)

    def relay(scat, s):
        for h in range(2):
            scat.fold(h, s)
            if s + 1 < stages:
                scat.send(h, s + 1)

    lax.fori_loop(0, ig // cols, grad_x, 0)
    for h in range(2):
        scat_x.start(h)
    for copy in moving[2:6]:
        copy.wait()

    tile = 256

    def dn_tile(j, start, n, at, with_z, share):
        span = pl.ds(start, n)
        value = nt(dx[span, :], wx[at, :]) + nt(dsm[span, : 2 * LANES], ws[at, : 2 * LANES])
        if share:
            value = value + nt(dsm[span, 2 * LANES :], ws[at, 2 * LANES :]) * share
        if with_z:
            value = value + nt(dz[pl.ds(start - HALO, n), :], wz[at, :])
        rep[pl.ds(j, 1), :] += jnp.sum(value * tok[span, at].astype(F32), axis=0, keepdims=True)
        return value

    def dn_copy(s, to, j):
        at = pl.ds(pl.multiple_of(j * tile, tile), tile)
        return remote(dn_out.at[s - 1, :, at], dn_in.at[s - 1, :, at], ns.at[s - 1, j], nr.at[s - 1, j], tensor=to)

    def edge_copy(k):
        return remote(edge_out, edge_in.at[k], es.at[0], er.at[k], tensor=hp - 1)

    def other_rows(s, to):
        there = pl.multiple_of(HALO + lax.rem(place + s, hp) * local_rows, 16)

        def step(j, carry):
            at = pl.ds(pl.multiple_of(j * tile, tile), tile)
            dn_out[s - 1, :, at] = dn_tile(j, there, local_rows, at, True, 0.0).astype(BF16)
            dn_copy(s, to, j).start()
            return carry

        return step

    dn_tiles = width // tile
    middle = dn_tiles // 2
    for s, to in mates():
        lax.fori_loop(0, middle, other_rows(s, to), 0)
    fold_cores(scat_x)
    sum_chan.fold(0)
    if len(dp_steps) > 1:
        sum_chan.push(1)
    for s, to in mates():
        lax.fori_loop(middle, dn_tiles, other_rows(s, to), 0)

    for copy in moving[6:]:
        copy.wait()
    upstream = dbc[...]
    pos = base + iota((count, 1), 0)
    masks = [same_as_behind(ends, pos, j) for j in range(4)]
    lagged = [pre[HALO - j : HALO - j + count, :] * masks[j] for j in range(1, 4)]
    lagged = [pre[HALO:, :]] + lagged
    through = bias[...].reshape(1, 2 * LANES)
    for j in range(4):
        through = through + taps[j : j + 1, :] * lagged[j]
    sig = sigmoid(through)
    dconv = upstream * (sig * (1.0 + through * (1.0 - sig)))
    for j in range(5):
        value = dconv * lagged[j] if j < 4 else dconv
        rep[8 + j : 9 + j, :] = jnp.sum(value, axis=0, keepdims=True) / hp
    conv[...] = jnp.zeros_like(conv)
    dpre = jnp.zeros((total, 2 * LANES), F32)
    for j in range(4):
        conv[HALO : HALO + count, :] = dconv * masks[j] if j else dconv
        dpre = dpre + taps[j : j + 1, :] * conv[j : j + total, :]
    dsm[:, 2 * LANES :] = dpre.astype(BF16)
    for s in range(stages - 1):
        relay(scat_x, s)
    gsm[...] = tn(tok[...], dsm[...]).astype(BF16)
    scat_s.start(0)
    scat_s.start(1)
    for i in range(1, len(dp_steps)):
        sum_chan.fold(i)
        if i + 1 < len(dp_steps):
            sum_chan.push(i + 1)
    home_chan.start(0)
    home_chan.start(1)

    def edge_rows(j, carry):
        at = pl.ds(pl.multiple_of(j * tile, tile), tile)
        edge_out[:, at] = dn_tile(j, 0, HALO, at, False, 1.0 / hp).astype(BF16)
        return carry

    lax.fori_loop(0, dn_tiles, edge_rows, 0)
    for k in range(hp):

        @pl.when(p == hp + k)
        def _(k=k):
            edge_copy(k).start()

    def own_rows(j, carry):
        at = pl.ds(pl.multiple_of(j * tile, tile), tile)
        dn_own[:, at] = dn_tile(j, own_at, local_rows, at, True, 1.0)
        return carry

    third = (dn_tiles + 2) // 3
    lax.fori_loop(0, third, own_rows, 0)
    relay(scat_x, stages - 1)
    home_x.start(1)
    fold_cores(scat_s)
    lax.fori_loop(third, 2 * third, own_rows, 0)
    for s in range(stages - 1):
        relay(scat_s, s)
    lax.fori_loop(2 * third, dn_tiles, own_rows, 0)
    sum_rep.push(0)
    relay(scat_s, stages - 1)
    home_dt.start(0)
    home_dt.start(1)
    bc_mine = sharded_rows(gsm, me, 0, rows, (2 * LANES, 4 * LANES))
    bc_copy = remote(bc_mine, bcz, ts.at[0], tr.at[0], tensor=lax.rem(p + hp, parts))
    bc_copy.start()
    for i in range(len(dp_steps)):
        sum_rep.fold(i)
        if i + 1 < len(dp_steps):
            sum_rep.push(i + 1)
    all_rep.start()
    home_chan.wait()
    chan_o[...] = chan_z[0] + chan_z[1]

    for s, to in mates():
        for j in range(dn_tiles):
            dn_copy(s, to, j).wait_recv()

    @pl.when(p == hp - 1)
    def _():
        for k in range(hp):
            edge_copy(k).wait_recv()
        last = local_rows - HALO
        for k in range(hp):
            dn_own[last:, :] += edge_in[k].astype(F32)

    dnormed = dn_own[...]
    for s in range(1, hp):
        dnormed = dnormed + dn_in[s - 1].astype(F32)
    values = inputs[...].astype(F32)
    scale = lax.rsqrt(jnp.mean(values * values, axis=1, keepdims=True) + EPS)
    side = dnormed * row(ngain)
    pull = scale * scale * scale * (jnp.sum(side * values, axis=1, keepdims=True) / width)
    gin_o[...] = (scale * side - values * pull + cot[...].astype(F32)).astype(BF16)

    rep_o[...] = all_rep.total()
    home_dt.wait()
    gdt_o[...] = dtz[0].astype(F32) + dtz[1].astype(F32)
    bc_copy.wait_recv()
    gbc_o[...] = bc_mine[...].astype(F32) + bcz[...].astype(F32)
    home_x.wait()
    gx_o[...] = xz[0].astype(F32) + xz[1].astype(F32)
    for item in (scat_x, scat_s, home_x, home_dt, home_chan, all_rep):
        item.finish()
    for s, to in mates():
        for j in range(dn_tiles):
            dn_copy(s, to, j).wait_send()
    bc_copy.wait_send()

    @pl.when(half == 1)
    def _():
        edge_copy(0).wait_send()


def run_last(
    ends, inputs, cot, ngain, tok, dz, dx, wz, wx, ws, dbc, ddt, pre, taps, bias, csum, gsum, hsum, ga,
    size, parts, ha, ig,
):
    local_rows, width = inputs.shape
    total = tok.shape[0]
    count = total - HALO
    inner = 2 * ig
    hp = parts // 2
    rows = width // size
    shape = jax.ShapeDtypeStruct
    anywhere = pl.BlockSpec(memory_space=pl.ANY)
    dma = pltpu.SemaphoreType.DMA
    blocks, links = size // 2, max(size // 2 - 1, 1)
    steps = size.bit_length() - 1
    vm = pltpu.VMEM

    splits = [split_of(ig), ig - split_of(ig)]

    def pair(n, cols):
        return [vm((n, rows, cols), BF16), vm((n, rows, cols), BF16)]

    scratch = dict(
        inputs=vm(inputs.shape, BF16),
        cot=vm(cot.shape, BF16),
        dbc=vm(dbc.shape, F32),
        pre=vm(pre.shape, F32),
        tok=vm(tok.shape, BF16),
        dz=vm(dz.shape, BF16),
        dx=vm(dx.shape, BF16),
        wz=vm(wz.shape, BF16),
        wx=vm(wx.shape, BF16),
        ws=vm(ws.shape, BF16),
        gx=vm((width, ig), BF16),
        gsm=vm((width, 4 * LANES), BF16),
        dsm=vm((total, 4 * LANES), BF16),
        conv=vm((total + 8, 2 * LANES), F32),
        dn_out=vm((hp - 1, local_rows, width), BF16),
        dn_in=vm((hp - 1, local_rows, width), BF16),
        dn_own=vm((local_rows, width), F32),
        edge_out=vm((HALO, width), BF16),
        edge_in=vm((hp, HALO, width), BF16),
        xcore=[vm((blocks, rows, w), BF16) for w in splits],
        xlink=[vm((links, rows, w), BF16) for w in splits],
        score=pair(blocks, 2 * LANES),
        slink=pair(links, 2 * LANES),
        xz=vm((2, rows, ig), BF16),
        dtz=vm((2, rows, LANES), BF16),
        bcz=vm((rows, 2 * LANES), BF16),
        chan=vm((8, inner), F32),
        chan_in=vm((steps, 8, inner), F32),
        chan_z=vm((2, 8, ig), F32),
        rep=vm((16, 2 * LANES), F32),
        rep_in=vm((steps, 16, 2 * LANES), F32),
        rep_z=vm((parts, 16, 2 * LANES), F32),
        loads=dma((10,)),
        ccs=dma((2, 2, blocks)),
        ccr=dma((2, 2, blocks)),
        cls=dma((2, 2, links)),
        clr=dma((2, 2, links)),
        zs=dma((6,)),
        zr=dma((6,)),
        zo=dma((3,)),
        bs=dma((2, steps)),
        br=dma((2, steps)),
        ns=dma((hp - 1, width // 256)),
        nr=dma((hp - 1, width // 256)),
        es=dma((1,)),
        er=dma((hp,)),
        ts=dma((1,)),
        tr=dma((1,)),
        rs=dma((parts,)),
        rr=dma((parts,)),
        ro=dma((1,)),
    )
    return pl.pallas_call(
        partial(last_body, size, parts, rows, ha, ig),
        out_shape=(
            shape((local_rows, width), BF16),
            shape((rows, ig), F32),
            shape((rows, LANES), F32),
            shape((rows, 2 * LANES), F32),
            shape((8, ig), F32),
            shape((16, 2 * LANES), F32),
        ),
        in_specs=[scalars(), anywhere, anywhere, whole()] + [anywhere] * 7 + [whole(), anywhere] + [whole()] * 6,
        out_specs=[whole()] * 6,
        scratch_shapes=list(scratch.values()),
        compiler_params=pltpu.CompilerParams(vmem_limit_bytes=VMEM_BYTES, collective_id=1, has_side_effects=True),
        cost_estimate=cost(2 * total * width * (3 * inner + 1024), 40e6),
        name="last",
    )(ends, inputs, cot, ngain, tok, dz, dx, wz, wx, ws, dbc, ddt, pre, taps, bias, csum, gsum, hsum, ga)


def finish_body(
    ha, out, gin, rep, ngain, gz, gx, gbc, gdt, chan, go,
    out_o, gin_o, gnorm_o, gz_o, gx_o, gbc_o, gdt_o, gcx_o, gcxb_o, gcb_o, gcbb_o, gdtb_o, galog_o, gskip_o, ggain_o, go_o,
):
    width = ngain.shape[0]
    ig = chan.shape[1]
    out_o[...] = out[...]
    gin_o[...] = gin[...]
    gains = jnp.concatenate([rep[j : j + 1, :] for j in range(width // (2 * LANES))], axis=1)
    gnorm_o[...] = gains.reshape(width) / ngain[...]
    gz_o[...] = gz[...]
    gx_o[...] = gx[...]
    gbc_o[...] = gbc[...]
    gdt_o[...] = gdt[...].T[:ha, :]
    gcx_o[...] = chan[0:4, :]
    gcxb_o[...] = chan[4:5, :].reshape(ig)
    ggain_o[...] = chan[5:6, :].reshape(ig)
    heads = lax.dot_general(
        chan[...],
        head_map(ig, 0, 0, both=False).astype(F32),
        (((1,), (1,)), ((), ())),
        precision=HIGH,
        preferred_element_type=F32,
    )
    gskip_o[...] = heads[6:7, :ha].reshape(ha)
    gdtb_o[...] = chan[7:8, :ha].reshape(ha)
    galog_o[...] = chan[7:8, LANES : LANES + ha].reshape(ha)
    for j in range(4):
        gcb_o[j : j + 1, :] = rep[8 + j : 9 + j, :]
    gcbb_o[...] = rep[12:13, :].reshape(2 * LANES)
    go_o[...] = go[...]


def run_finish(out, gin, rep, ngain, gz, gx, gbc, gdt, chan, go, ha):
    shape = jax.ShapeDtypeStruct
    rows, ig = gz.shape
    return pl.pallas_call(
        partial(finish_body, ha),
        out_shape=(
            shape(out.shape, BF16),
            shape(gin.shape, BF16),
            shape(ngain.shape, F32),
            shape((rows, ig), F32),
            shape((rows, ig), F32),
            shape(gbc.shape, F32),
            shape((ha, rows), F32),
            shape((4, ig), F32),
            shape((ig,), F32),
            shape((4, 2 * LANES), F32),
            shape((2 * LANES,), F32),
            shape((ha,), F32),
            shape((ha,), F32),
            shape((ha,), F32),
            shape((ig,), F32),
            shape((rows, ig), F32),
        ),
        in_specs=[whole()] * 10,
        out_specs=[whole()] * 16,
        compiler_params=params(),
        cost_estimate=cost(1e7, 8e6),
        name="finish",
    )(out, gin, rep, ngain, gz, gx, gbc, gdt, chan, go)


def local(
    inputs,
    cotangent,
    seq_lengths,
    norm_gain,
    w_z,
    w_x,
    w_bc,
    w_dt,
    conv_x,
    conv_x_bias,
    conv_bc,
    conv_bc_bias,
    dt_bias,
    a_log,
    d_skip,
    gate_gain,
    w_out,
):
    parts = lax.axis_size("tensor")
    size = lax.axis_size("dp")
    ha = dt_bias.shape[0]
    ig = w_z.shape[1]
    (
        tok, pulled, wx, wz, wo, ws, par, pre_bc, bc, dtin, dt, lc, lr, em, et, kd, pre_x, xs, st, sin, z, dm, y, stat,
    ) = run_first(
        seq_lengths, inputs, cotangent, norm_gain, w_x, w_z, w_out.T, w_bc, w_dt.T, conv_x, conv_x_bias, dt_bias, a_log,
        d_skip, gate_gain, conv_bc, conv_bc_bias, size, parts,
    )
    dz, dy, gate_sums, ds, gw_z, gw_o, dsin, branch = run_gate(
        y, z, dm, stat, xs, par, bc, em, kd, tok, pulled, wo, ig, ig * parts, size, parts
    )
    dx, dbc, ddt, conv_sums, head_sums, outputs, grad_w_z, grad_w_o, grad_w_a = run_pull(
        seq_lengths, xs, dy, bc, dtin, dt, lc, lr, em, et, kd, st, sin, ds, dsin, pre_x, par,
        inputs, branch, gw_z, gw_o, tok, ha, ig, size, parts,
    )
    grad_inputs, grad_w_x, grad_w_dt, grad_w_bc, chan, rep = run_last(
        seq_lengths, inputs, cotangent, norm_gain, tok, dz, dx, wz, wx, ws, dbc, ddt, pre_bc, conv_bc,
        conv_bc_bias, conv_sums, gate_sums, head_sums, grad_w_a, size, parts, ha, ig,
    )
    done = run_finish(
        outputs, grad_inputs, rep, norm_gain, grad_w_z, grad_w_x, grad_w_bc, grad_w_dt, chan, grad_w_o, ha
    )
    return (*done[:6], done[6].T, *done[7:15], done[15].T)


def solution(mesh):
    tokens = P(("dp", "tensor"), None)
    matrix = P("dp", "tensor")
    heads = P("tensor")
    return jax.shard_map(
        local,
        mesh=mesh,
        in_specs=(
            tokens,
            tokens,
            P("dp", None),
            P(),
            matrix,
            matrix,
            P("dp", None),
            matrix,
            P(None, "tensor"),
            heads,
            P(),
            P(),
            heads,
            heads,
            heads,
            heads,
            P("tensor", "dp"),
        ),
        out_specs=(
            tokens,
            tokens,
            P(),
            matrix,
            matrix,
            P("dp", None),
            matrix,
            P(None, "tensor"),
            heads,
            P(),
            P(),
            heads,
            heads,
            heads,
            heads,
            P("tensor", "dp"),
        ),
        check_vma=False,
    )
```
